32 devices in a mesh: section: 2 (over core), dp: 8 (over z, y), tensor: 2 (over x).
Axes of the slice: x: 2, y: 2, z: 4, core: 2. Of those that a mesh axis runs over, the one named last changes fastest.
Arguments:
- clips: bfloat16 [16, 1024, 768], P('dp', 'tensor'), may hold values from -6 to 6
- cotangent: bfloat16 [16, 1024, 768], P('dp', 'tensor'), may hold values from -6 to 6
- ln_gains: bfloat16 [2, 2, 768], P('section', None, 'dp'), may hold values from 0.099609375 to 1.8984375
- row_biases: bfloat16 [2, 4, 768], P('section', None, 'dp'), may hold values from -2 to 2
- w_qkv: bfloat16 [2, 3, 768, 768], P('section', None, 'dp', 'tensor'), may hold values from -0.21875 to 0.21875
- b_qv: bfloat16 [2, 2, 12, 64], P('section', None, 'tensor', 'dp'), may hold values from -2 to 2
- w_o: bfloat16 [2, 768, 768], P('section', 'tensor', 'dp'), may hold values from -2.5 to 2.5
- w_up: bfloat16 [2, 768, 3072], P('section', 'dp', 'tensor'), may hold values from -0.21875 to 0.21875
- b_ff: bfloat16 [2, 48, 64], P('section', 'tensor', 'dp'), may hold values from -2 to 2
- w_down: bfloat16 [2, 3072, 768], P('section', 'tensor', 'dp'), may hold values from -0.109375 to 0.109375
Outputs:
- section_out: bfloat16 [2, 16, 1024, 768], P('section', 'dp', 'tensor')
- section_in_grad: bfloat16 [2, 16, 1024, 768], P('section', 'dp', 'tensor')
- grad_ln_gains: float32 [2, 2, 768], P('section', None, ('dp', 'tensor'))
- grad_row_biases: float32 [2, 4, 768], P('section', None, ('dp', 'tensor'))
- grad_w_qkv: float32 [2, 3, 768, 768], P('section', None, 'dp', 'tensor')
- grad_b_qv: float32 [2, 2, 12, 64], P('section', None, 'tensor', 'dp')
- grad_w_o: float32 [2, 768, 768], P('section', 'tensor', 'dp')
- grad_w_up: float32 [2, 768, 3072], P('section', 'dp', 'tensor')
- grad_b_ff: float32 [2, 48, 64], P('section', 'tensor', 'dp')
- grad_w_down: float32 [2, 3072, 768], P('section', 'tensor', 'dp')
The draws below stay inside these ranges and needn't reach their ends.
All inputs are finite; a program needn't handle non-finite values.
Results may differ from the reference program's by a relative error of at most 0.02.
Values may be sent and summed in bfloat16 or wider, within the bound.
A program may use at most 384 MiB of HBM per device.

```python
import jax
import jax.numpy as jnp
from jax import lax

D = 768
HEADS = 12
FF = 3072
HEAD = 64
LEN = 1024
CLIPS = 16


def levels(rng, dims, shards, least, high):
    loudness = 1.0
    for dim, shards_of in shards:
        draws = jax.random.uniform(jax.random.fold_in(jax.random.fold_in(rng, 6), dim), (shards_of,), jnp.float32, least / len(shards), high / len(shards))
        loudness = loudness * jnp.repeat(jnp.exp(draws), dims[dim] // shards_of).reshape((-1,) + (1,) * (len(dims) - 1 - dim))
    return loudness


def noise(own_key, shape, scale, reach, cuts=(), held_as=jnp.bfloat16):
    factor_of = levels(own_key, shape, cuts, -0.22, 0.18) if cuts else 1.0
    array = jax.random.normal(own_key, shape, jnp.float32) * scale * factor_of
    return jnp.minimum(jnp.maximum(array, -reach), reach).astype(held_as)


def setup_inputs(seed: int = 0) -> dict:
    seeds = jax.random.split(jax.random.key(seed), 11)
    clips = noise(seeds[0], (CLIPS, LEN, D), 1.0, 6.0, ((0, 8), (1, 2)))
    cotangent = noise(seeds[1], (CLIPS, LEN, D), 1.0, 6.0, ((0, 8), (1, 2)))
    ln_gains = jnp.clip(1.0 + 0.18 * jax.random.normal(seeds[2], (2, 2, D), jnp.float32), 0.099609375, 1.8984375).astype(jnp.bfloat16)
    row_biases = noise(seeds[3], (2, 4, D), 0.3, 2.0, ((0, 2), (2, 8)))
    w_qkv = noise(seeds[4], (2, 3, D, D), D ** -0.5, 0.21875, ((0, 2), (2, 8), (3, 2)))
    b_qv = noise(seeds[5], (2, 2, HEADS, HEAD), 0.3, 2.0, ((0, 2), (2, 2), (3, 8)))
    w_o = noise(seeds[6], (2, D, D), (D * 8 // LEN) ** -0.5, 2.5, ((0, 2), (1, 2), (2, 8)))
    w_up = noise(seeds[7], (2, D, FF), D ** -0.5, 0.21875, ((0, 2), (1, 8), (2, 2)))
    b_ff = noise(seeds[8], (2, FF // 64, 64), 0.3, 2.0, ((0, 2), (1, 2), (2, 8)))
    w_down = noise(seeds[9], (2, FF, D), FF ** -0.5, 0.109375, ((0, 2), (1, 2), (2, 8)))
    return dict(clips=clips, cotangent=cotangent, ln_gains=ln_gains, row_biases=row_biases, w_qkv=w_qkv, b_qv=b_qv, w_o=w_o, w_up=w_up, b_ff=b_ff, w_down=w_down)


HIGHEST = lax.Precision.HIGHEST
EPSILON = 1e-05

@jax.custom_vjp
def low(v):
    return lax.optimization_barrier(v.astype(jnp.bfloat16)).astype(jnp.float32)

@jax.custom_vjp
def low_back(v):
    return v

def low_keep(v):
    return (low(v), None)

def low_pass(kept, grad):
    return (grad,)

def back_keep(v):
    return (v, None)

def back_low(kept, grad):
    return (low(grad),)
low.defvjp(low_keep, low_pass)
low_back.defvjp(back_keep, back_low)

def normalize(rows_in, gain_in, shift_in):
    centre = lax.optimization_barrier(jnp.mean(rows_in, -1, keepdims=True))
    centered = rows_in - centre
    variance = lax.optimization_barrier(jnp.mean(centered * centered, -1, keepdims=True))
    return centered * lax.rsqrt(variance + EPSILON) * gain_in + shift_in

def product(left_side, right_side):
    return jnp.dot(left_side, right_side, precision=HIGHEST, preferred_element_type=jnp.float32)

def attention(queries, keys_all, values_all):
    block_rows = min(512, LEN)
    scaling = HEAD ** (-0.5)
    query_heads = queries.reshape(LEN // block_rows, block_rows, HEADS, HEAD)
    key_heads = keys_all.reshape(LEN, HEADS, HEAD)
    value_heads = values_all.reshape(LEN, HEADS, HEAD)

    def one_block(query_block):
        scores = low_back(jnp.einsum('qhd,khd->hqk', query_block, key_heads, precision=HIGHEST) * scaling)
        softened = jax.nn.softmax(scores, axis=-1)
        return jnp.einsum('hqk,khd->qhd', low(softened), value_heads, precision=HIGHEST)
    context = lax.map(jax.checkpoint(one_block), query_heads)
    return context.reshape(LEN, D)

def layer(params, rows_in):
    gains_all, biases_all, qkv_w, qv_b, out_w, up_w, ff_b, down_w = params
    first_norm = low(normalize(rows_in, gains_all[0], biases_all[0]))
    queries = low_back(low(product(first_norm, qkv_w[0]) + qv_b[0].reshape(D)))
    keys_all = low_back(low(product(first_norm, qkv_w[1])))
    values_all = low_back(low(product(first_norm, qkv_w[2]) + qv_b[1].reshape(D)))
    context = low_back(low(attention(queries, keys_all, values_all)))
    hidden_res = rows_in + low_back(product(context, out_w) + biases_all[1])
    second_norm = low(normalize(hidden_res, gains_all[1], biases_all[2]))
    pre_act = low_back(product(second_norm, up_w) + ff_b.reshape(FF))
    activated = low(jax.nn.gelu(pre_act, approximate=False))
    return hidden_res + low_back(product(activated, down_w) + biases_all[3])

def reference(clips, cotangent, ln_gains, row_biases, w_qkv, b_qv, w_o, w_up, b_ff, w_down):
    weights = tuple((array_in.astype(jnp.float32) for array_in in (ln_gains, row_biases, w_qkv, b_qv, w_o, w_up, b_ff, w_down)))

    def two_layers(weights_all, inputs, bump_rows):
        first_params = tuple((array_in[0] for array_in in weights_all))
        second_params = tuple((array_in[1] for array_in in weights_all))

        def per_clip(clip_pair):
            clip_rows, bump_clip = clip_pair
            middle = layer(first_params, clip_rows)
            passed = low_back(low(middle)) + bump_clip
            return (middle, layer(second_params, passed))
        return lax.map(jax.checkpoint(per_clip), (inputs, bump_rows))
    inputs = clips.astype(jnp.float32)
    bump_rows = jnp.zeros(inputs.shape, jnp.float32)
    (middle, final), pullback = jax.vjp(two_layers, weights, inputs, bump_rows)
    weight_grads, input_grad, passed_grad = pullback((jnp.zeros_like(middle), cotangent.astype(jnp.float32)))
    section_out = jnp.stack([middle, final]).astype(jnp.bfloat16)
    section_in_grad = jnp.stack([input_grad, passed_grad]).astype(jnp.bfloat16)
    return (section_out, section_in_grad, weight_grads[0], weight_grads[1], weight_grads[2], weight_grads[3], weight_grads[4], weight_grads[5], weight_grads[6], weight_grads[7])
```

```python
import functools

import jax
import jax.numpy as jnp
from jax import lax
from jax.experimental import pallas as pl
from jax.experimental.pallas import tpu as pltpu
from jax.sharding import PartitionSpec as P

BF = jnp.bfloat16
F32 = jnp.float32
MESH = pl.DeviceIdType.MESH
EPSILON = 1e-05
HEAD = 64
GROUPS = 8
LINES = 4
BLOCK = 256
VMEM_LIMIT = 62 * 1024 * 1024

VEC = 0
QKV = 128
OUT = 1280
UP = 1664
DOWN = 3200
END = 4736
SPLIT = 64
FWD_CHUNKS = ((VEC, UP), (UP, DOWN), (DOWN, END))


def mm(left, right):
    return jnp.dot(left, right, preferred_element_type=F32)


def mmt(left, right):
    return lax.dot_general(left, right, (((1,), (1,)), ((), ())), preferred_element_type=F32)


class Place:
    def __init__(self, share):
        self.s = lax.axis_index("section")
        self.d = lax.axis_index("dp")
        self.t = lax.axis_index("tensor")
        group = self.d // share
        self.rest = self.d - group * share
        self.share = share
        self.e = group // 2
        self.y = group - self.e * 2
        self.primary = self.s == self.t
        self.core = (1 - self.s, self.d, self.t)
        self.across = (self.s, self.d, 1 - self.t)
        self.beside = (self.s, self.row_of(self.e, 1 - self.y), self.t)

    def row_of(self, line, y):
        return (line * 2 + y) * self.share + self.rest

    def line(self, step):
        return lax.rem(self.e + step, LINES)

    def greet(self):
        barrier = pltpu.get_barrier_semaphore()
        peers = [self.core, self.across, self.beside]
        for step in range(1, LINES):
            for section in range(2):
                peers.append((section, self.row_of(self.line(step), self.y), self.t))
        for peer in peers:
            pl.semaphore_signal(barrier, inc=1, device_id=peer, device_id_type=MESH)
        pl.semaphore_wait(barrier, len(peers))


def remote(src, dst, send_sem, recv_sem, device):
    return pltpu.make_async_remote_copy(
        src_ref=src,
        dst_ref=dst,
        send_sem=send_sem,
        recv_sem=recv_sem,
        device_id=device,
        device_id_type=MESH,
    )


def await_bytes(ref, sem):
    pltpu.make_async_copy(ref, ref, sem).wait()


def centre(rows_in):
    mean = jnp.mean(rows_in, 0, keepdims=True)
    centred = rows_in - mean
    variance = jnp.mean(centred * centred, 0, keepdims=True)
    scale = lax.rsqrt(variance + EPSILON)
    return centred * scale, scale


def gelu_parts(values):
    bell = jnp.exp(-0.5 * values * values)
    reach = jnp.abs(values) * 0.7071067811865476
    inv = 1.0 / (1.0 + 0.3275911 * reach)
    poly = inv * (
        0.254829592
        + inv * (-0.284496736 + inv * (1.421413741 + inv * (-1.453152027 + inv * 1.061405429)))
    )
    tail = 0.5 * poly * bell
    cdf = jnp.where(values >= 0.0, 1.0 - tail, tail)
    return values * cdf, cdf + values * bell * 0.3989422804014327


def block_of(index):
    return pl.ds(pl.multiple_of(index * BLOCK, BLOCK), BLOCK)


def flip_weights(w, wt, layer, start, width, target=0):
    def body(index, carry):
        cols = pl.ds(pl.multiple_of(start + index * 128, 128), 128)
        rows = pl.ds(pl.multiple_of(target + index * 128, 128), 128)
        tile = w[layer, :, :, :, cols]
        wt[rows, :] = tile.reshape(tile.shape[0] * tile.shape[1] * tile.shape[2], 128).T
        return carry

    lax.fori_loop(0, width // 128, body, 0)


def whole(w, layer, start, width):
    tile = w[layer, :, :, :, start : start + width]
    return tile.reshape(tile.shape[0] * tile.shape[1] * tile.shape[2], width)


def spread_biases(vecs, spread, rows):
    def body(group, carry):
        source = group * rows
        for kind in range(2):
            for head in range(6):
                to = pl.ds(pl.multiple_of(kind * 384 + head * HEAD + group * 8, 8), 8)
                at = pl.ds(pl.multiple_of(source + kind * 48 + head * 8, 8), 8)
                spread[to, :] = vecs[at, :]
        for unit in range(24):
            to = pl.ds(pl.multiple_of(768 + unit * HEAD + group * 8, 8), 8)
            at = pl.ds(pl.multiple_of(source + (unit % 12) * 8, 8), 8)
            spread[to, :] = vecs[at, :]
        return carry

    lax.fori_loop(0, GROUPS, body, 0)


def forward_kernel(
    share,
    clips,
    cot,
    shard,
    out,
    cot_other,
    w_hbm,
    x_hbm,
    n1_hbm,
    qkv_hbm,
    ctx_hbm,
    lse_hbm,
    h_hbm,
    n2_hbm,
    act_hbm,
    slope_hbm,
    w,
    res,
    xs,
    n1,
    n2,
    qkv,
    ctx,
    act,
    slope,
    lse,
    wt,
    xin,
    send,
    recv,
    vecs,
    spread,
    stage,
    z_send,
    z_recv,
    x_send,
    x_recv,
    xb_send,
    xb_recv,
    y_send,
    y_recv,
    ya_send,
    ya_recv,
    e_send,
    e_recv,
    in_sem,
    cot_sem,
    out_sem,
    save_sem,
):
    place = Place(share)
    s, t, e, y = place.s, place.t, place.e, place.y
    primary, secondary = place.primary, jnp.logical_not(place.primary)
    frames = res.shape[1]
    blocks = frames // BLOCK
    half = frames // 2
    quarter = half // 2
    rows = w.shape[3]
    chunk_count = len(FWD_CHUNKS)

    def cols_of(chunk):
        start, stop = FWD_CHUNKS[chunk % chunk_count]
        return pl.ds(start, stop - start)

    place.greet()

    def z_copies(piece):
        cols = cols_of(piece)
        copies = []
        for step in range(LINES):
            device = (t, place.row_of(place.line(step), y), t)
            copies.append(
                remote(
                    shard.at[:, cols],
                    w.at[s, e, y, :, cols],
                    z_send.at[piece, step],
                    z_recv.at[s, piece, e],
                    device,
                )
            )
        local = pltpu.make_async_copy(
            shard.at[:, cols], w.at[s, e, y, :, cols], z_recv.at[s, piece, e]
        )
        return copies, local

    def z_start(piece, section):
        @pl.when(s == section)
        def _():
            copies, local = z_copies(piece)

            @pl.when(primary)
            def _():
                local.start()

            @pl.when(secondary)
            def _():
                copies[0].start()

            for copy in copies[1:]:
                copy.start()

    def z_finish():
        for piece in range(chunk_count):
            copies, _ = z_copies(piece)

            @pl.when(secondary)
            def _():
                copies[0].wait_send()

            for copy in copies[1:]:
                copy.wait_send()

    def x_copy(chunk):
        part = w.at[chunk // chunk_count, :, y, :, cols_of(chunk)]
        return remote(part, part, x_send.at[chunk], x_recv.at[chunk], place.across)

    def y_copy(chunk):
        part = w.at[chunk // chunk_count, :, y, :, cols_of(chunk)]
        return remote(part, part, y_send.at[chunk], y_recv.at[chunk], place.beside)

    def xb_copy(chunk):
        part = w.at[chunk // chunk_count, :, 1 - y, pl.ds(SPLIT, rows - SPLIT), cols_of(chunk)]
        return remote(part, part, xb_send.at[chunk], xb_recv.at[chunk], place.across)

    def ya_copy(chunk):
        part = w.at[chunk // chunk_count, :, y, pl.ds(0, SPLIT), cols_of(chunk)]
        return remote(part, part, ya_send.at[chunk], ya_recv.at[chunk], place.beside)

    def step_z(chunk):
        @pl.when(primary)
        def _():
            layer, piece = chunk // chunk_count, chunk % chunk_count
            for line in range(LINES):
                await_bytes(w.at[layer, line, y, :, cols_of(chunk)], z_recv.at[layer, piece, line])
            x_copy(chunk).start()
            y_copy(chunk).start()

    def step_plane(chunk):
        @pl.when(primary)
        def _():
            part = w.at[chunk // chunk_count, :, 1 - y, :, cols_of(chunk)]
            await_bytes(part, y_recv.at[chunk])
            xb_copy(chunk).start()

        @pl.when(secondary)
        def _():
            part = w.at[chunk // chunk_count, :, y, :, cols_of(chunk)]
            await_bytes(part, x_recv.at[chunk])
            ya_copy(chunk).start()

    def complete(chunk):
        layer = chunk // chunk_count

        @pl.when(secondary)
        def _():
            await_bytes(
                w.at[layer, :, 1 - y, pl.ds(SPLIT, rows - SPLIT), cols_of(chunk)], xb_recv.at[chunk]
            )
            await_bytes(w.at[layer, :, 1 - y, pl.ds(0, SPLIT), cols_of(chunk)], ya_recv.at[chunk])

        save_weights(chunk).start()

    def save_weights(chunk):
        layer = chunk // chunk_count
        part = (layer, slice(None), slice(None), slice(None), cols_of(chunk))
        return pltpu.make_async_copy(w.at[part], w_hbm.at[part], save_sem.at[9, chunk])

    saves = {
        "x": (xs, x_hbm, 0),
        "n1": (n1, n1_hbm, 1),
        "qkv": (qkv, qkv_hbm, 2),
        "ctx": (ctx, ctx_hbm, 3),
        "lse": (lse, lse_hbm, 4),
        "h": (res, h_hbm, 5),
        "n2": (n2, n2_hbm, 6),
        "act": (act, act_hbm, 7),
        "slope": (slope, slope_hbm, 8),
    }

    def save(name, layer):
        src, dst, index = saves[name]
        return pltpu.make_async_copy(src, dst.at[layer], save_sem.at[index, layer])

    def swap_first(src, dst, sems):
        mine = pl.ds(s * quarter, quarter)
        return remote(src.at[1 - t, mine, :], dst.at[mine, :], sems.at[0], sems.at[1], place.across)

    def swap_second(dst, sems):
        mine = pl.ds(s * quarter, quarter)
        return remote(dst.at[mine, :], dst.at[mine, :], sems.at[2], sems.at[3], place.core)

    z_start(0, 0)
    clip_first = swap_first(clips, xin.at[0], in_sem)
    clip_first.start()
    own_clip = pltpu.make_async_copy(clips.at[t], xin.at[1], in_sem.at[4])
    own_clip.start()
    z_start(1, 0)
    cot_first = swap_first(cot, cot_other, cot_sem)
    cot_first.start()

    def take_rows(slot, which):
        for index in range(half // BLOCK):
            tile = xin[slot, index * BLOCK : (index + 1) * BLOCK, :].T
            to = pl.ds(pl.multiple_of(which * half + index * BLOCK, BLOCK), BLOCK)
            xs[:, to] = tile
            res[:, to] = tile.astype(F32)

    own_clip.wait()
    take_rows(1, t)
    clip_first.wait()
    clip_second = swap_second(xin.at[0], in_sem)
    clip_second.start()
    clip_second.wait()
    take_rows(0, 1 - t)
    save("x", 0).start()

    step_z(0)
    z_start(2, 0)
    z_start(0, 1)
    cot_first.wait()
    cot_second = swap_second(cot_other, cot_sem)
    cot_second.start()
    step_plane(0)
    step_z(1)

    def exchange(layer, kind, index):
        return remote(
            send.at[kind, index],
            recv.at[2 * layer + kind, index],
            e_send.at[2 * layer + kind, index],
            e_recv.at[2 * layer + kind, index],
            place.core,
        )

    def joined(layer, kind, index):
        exchange(layer, kind, index).wait()
        return send[kind, index].astype(F32) + recv[2 * layer + kind, index].astype(F32)

    def project(layer, index, rows_in):
        normed = centre(rows_in)[0] * vecs[:, 0:1] + vecs[:, 2:3]
        normed = normed.astype(BF)
        cols = block_of(index)
        n1[:, cols] = normed
        for part in range(3):
            value = mm(wt[part * 384 : (part + 1) * 384, :], normed)
            if part == 0:
                value = (value + spread[0:384, 6:7]) * 0.125
            if part == 2:
                value = value + spread[384:768, 6:7]
            qkv[part * 384 : (part + 1) * 384, cols] = value.astype(BF)

    def attend(layer):
        def one_head(head, carry):
            base = head * HEAD
            keys = qkv[pl.ds(pl.multiple_of(384 + base, HEAD), HEAD), :].T
            values = qkv[pl.ds(pl.multiple_of(768 + base, HEAD), HEAD), :]
            queries = pl.ds(pl.multiple_of(base, HEAD), HEAD)
            for index in range(blocks):
                cols = slice(index * BLOCK, (index + 1) * BLOCK)
                scores = mm(keys, qkv[queries, cols])
                top = jnp.max(scores, 0, keepdims=True)
                soft = jnp.exp(scores - top)
                total = jnp.sum(soft, 0, keepdims=True)
                mixed = mm(values, soft.astype(BF)) / total
                ctx[queries, cols] = mixed.astype(BF)
                lse[pl.ds(head, 1), cols] = top + jnp.log(total)
            return carry

        lax.fori_loop(0, ctx.shape[0] // HEAD, one_head, 0)

    def out_project(layer):
        def body(index, carry):
            part = mm(whole(w, layer, OUT, 384), ctx[:, block_of(index)])
            send[0, index] = part.astype(BF)
            exchange(layer, 0, index).start()
            return carry

        lax.fori_loop(0, blocks, body, 0)

    def hidden(layer):
        def body(index, carry):
            cols = block_of(index)
            rows_in = res[:, cols] + joined(layer, 0, index) + vecs[:, 3:4]
            res[:, cols] = rows_in
            normed = (centre(rows_in)[0] * vecs[:, 1:2] + vecs[:, 4:5]).astype(BF)
            n2[:, cols] = normed
            for part in range(4):
                units = slice(part * 384, (part + 1) * 384)
                lane = 7 if part < 2 else 8
                pre = mm(wt[units, :], normed) + spread[
                    768 + part * 384 : 768 + (part + 1) * 384, lane : lane + 1
                ]
                value, steep = gelu_parts(pre)
                act[units, cols] = value.astype(BF)
                slope[units, cols] = steep.astype(BF)
            return carry

        lax.fori_loop(0, blocks, body, 0)

    def down_project(layer):
        def body(index, carry):
            part = mm(whole(w, layer, DOWN, 1536), act[:, block_of(index)])
            send[1, index] = part.astype(BF)
            exchange(layer, 1, index).start()
            return carry

        lax.fori_loop(0, blocks, body, 0)

    def layer_end(layer, index):
        cols = block_of(index)
        return (res[:, cols] + joined(layer, 1, index) + vecs[:, 5:6]).astype(BF)

    def out_copies(layer):
        mine = pl.ds(pl.multiple_of(t * half, half), half)
        theirs = pl.ds(pl.multiple_of((1 - t) * half, half), half)
        local = pltpu.make_async_copy(stage.at[mine, :], out.at[0, t], out_sem.at[0])
        away = remote(
            stage.at[theirs, :], out.at[0, t], out_sem.at[1], out_sem.at[2], place.across
        )
        return local, away

    def emit(layer):
        @pl.when(s == layer)
        def _():
            for copy in out_copies(layer):
                copy.start()

    def take_vectors(layer):
        vecs[...] = whole(w, layer, VEC, 128).astype(F32)
        spread_biases(vecs, spread, rows)

    complete(0)
    take_vectors(0)
    flip_weights(w, wt, 0, QKV, 1152)

    def start_body(index, carry):
        project(0, index, res[:, block_of(index)])
        return carry

    lax.fori_loop(0, blocks, start_body, 0)
    save("n1", 0).start()
    save("qkv", 0).start()
    step_plane(1)
    step_z(2)
    z_start(1, 1)
    attend(0)
    save("ctx", 0).start()
    save("lse", 0).start()
    out_project(0)
    step_plane(2)
    complete(1)
    flip_weights(w, wt, 0, UP, 1536)
    step_z(3)
    z_start(2, 1)
    hidden(0)
    save("h", 0).start()
    save("n2", 0).start()
    save("act", 0).start()
    save("slope", 0).start()
    step_plane(3)
    step_z(4)
    complete(2)
    down_project(0)
    complete(3)
    flip_weights(w, wt, 1, QKV, 1152)
    for name in ("x", "n1", "qkv", "h"):
        save(name, 0).wait()

    def finish_body(index, carry):
        rows_out = layer_end(0, index)
        cols = block_of(index)
        xs[:, cols] = rows_out
        res[:, cols] = rows_out.astype(F32)

        @pl.when(s == 0)
        def _():
            stage[cols, :] = rows_out.T

        return carry

    lax.fori_loop(0, blocks, finish_body, 0)
    emit(0)
    save("x", 1).start()
    take_vectors(1)

    def middle_body(index, carry):
        project(1, index, res[:, block_of(index)])
        return carry

    lax.fori_loop(0, blocks, middle_body, 0)
    save("n1", 1).start()
    save("qkv", 1).start()
    step_plane(4)
    step_z(5)
    save("ctx", 0).wait()
    save("lse", 0).wait()
    attend(1)
    save("ctx", 1).start()
    save("lse", 1).start()
    out_project(1)
    step_plane(5)
    complete(4)
    flip_weights(w, wt, 1, UP, 1536)
    for name in ("n2", "act", "slope"):
        save(name, 0).wait()
    hidden(1)
    for name in ("h", "n2", "act", "slope"):
        save(name, 1).start()
    complete(5)
    down_project(1)

    def last_body(index, carry):
        rows_out = layer_end(1, index)

        @pl.when(s == 1)
        def _():
            stage[block_of(index), :] = rows_out.T

        return carry

    lax.fori_loop(0, blocks, last_body, 0)
    emit(1)

    z_finish()
    for chunk in range(2 * chunk_count):

        @pl.when(primary)
        def _():
            x_copy(chunk).wait_send()
            y_copy(chunk).wait_send()
            xb_copy(chunk).wait_send()

        @pl.when(secondary)
        def _():
            ya_copy(chunk).wait_send()

        save_weights(chunk).wait()
    for name in saves:
        save(name, 1).wait()
    cot_second.wait()
    local, away = out_copies(0)
    local.wait()
    away.wait()


def forward_call(share, clips, cotangent, shard, dims):
    width, frames, hidden_units, heads_width = dims
    rows = shard.shape[0]
    sem = pltpu.SemaphoreType.DMA
    packed = (2, LINES, 2, rows, END)
    hbm = [
        jax.ShapeDtypeStruct((1,) + clips.shape, BF),
        jax.ShapeDtypeStruct(clips.shape[1:], BF),
        jax.ShapeDtypeStruct(packed, BF),
        jax.ShapeDtypeStruct((2, width, frames), BF),
        jax.ShapeDtypeStruct((2, width, frames), BF),
        jax.ShapeDtypeStruct((2, 3 * heads_width, frames), BF),
        jax.ShapeDtypeStruct((2, heads_width, frames), BF),
        jax.ShapeDtypeStruct((2, 8, frames), F32),
        jax.ShapeDtypeStruct((2, width, frames), F32),
        jax.ShapeDtypeStruct((2, width, frames), BF),
        jax.ShapeDtypeStruct((2, hidden_units, frames), BF),
        jax.ShapeDtypeStruct((2, hidden_units, frames), BF),
    ]
    blocks = frames // BLOCK
    chunks = 2 * len(FWD_CHUNKS)
    scratch = [
        pltpu.VMEM(packed, BF),
        pltpu.VMEM((width, frames), F32),
        pltpu.VMEM((width, frames), BF),
        pltpu.VMEM((width, frames), BF),
        pltpu.VMEM((width, frames), BF),
        pltpu.VMEM((3 * heads_width, frames), BF),
        pltpu.VMEM((heads_width, frames), BF),
        pltpu.VMEM((hidden_units, frames), BF),
        pltpu.VMEM((hidden_units, frames), BF),
        pltpu.VMEM((8, frames), F32),
        pltpu.VMEM((hidden_units, width), BF),
        pltpu.VMEM((2, frames // 2, width), BF),
        pltpu.VMEM((2, blocks, width, BLOCK), BF),
        pltpu.VMEM((4, blocks, width, BLOCK), BF),
        pltpu.VMEM((width, 128), F32),
        pltpu.VMEM((2 * heads_width + hidden_units, 128), F32),
        pltpu.VMEM((frames, width), BF),
        sem((len(FWD_CHUNKS), LINES)),
        sem((2, len(FWD_CHUNKS), LINES)),
        sem((chunks,)),
        sem((chunks,)),
        sem((chunks,)),
        sem((chunks,)),
        sem((chunks,)),
        sem((chunks,)),
        sem((chunks,)),
        sem((chunks,)),
        sem((4, blocks)),
        sem((4, blocks)),
        sem((5,)),
        sem((4,)),
        sem((3,)),
        sem((10, chunks)),
    ]
    anywhere = pl.BlockSpec(memory_space=pl.ANY)
    return pl.pallas_call(
        functools.partial(forward_kernel, share),
        out_shape=hbm,
        in_specs=[anywhere] * 3,
        out_specs=[anywhere] * len(hbm),
        scratch_shapes=scratch,
        compiler_params=pltpu.CompilerParams(
            collective_id=0, has_side_effects=True, vmem_limit_bytes=VMEM_LIMIT
        ),
        cost_estimate=pl.CostEstimate(
            flops=20_000_000_000, bytes_accessed=60_000_000, transcendentals=0
        ),
    )(clips, cotangent, shard)


BWD_CHUNKS = ((DOWN, END), (UP, DOWN), (OUT, UP), (VEC, OUT))


def backward_kernel(
    share,
    cot,
    cot_other,
    w_hbm,
    x_hbm,
    n1_hbm,
    qkv_hbm,
    ctx_hbm,
    lse_hbm,
    h_hbm,
    n2_hbm,
    act_hbm,
    slope_hbm,
    out,
    landed,
    w,
    dy,
    act,
    slope,
    h_in,
    n2,
    qkv,
    ctx,
    dctx,
    low,
    lse,
    wt,
    send,
    recv,
    vecs,
    vec_grads,
    sums,
    spread,
    stage,
    land_a,
    land_b,
    land_y,
    ya_send,
    ya_recv,
    xb_send,
    xb_recv,
    x_send,
    x_recv,
    y_send,
    y_recv,
    z_send,
    z_recv,
    e_send,
    e_recv,
    w_sem,
    load_sem,
    h_sem,
    out_sem,
    ya_free,
    xb_free,
    x_free,
    y_free,
):
    place = Place(share)
    s, t, e, y = place.s, place.t, place.e, place.y
    primary, secondary = place.primary, jnp.logical_not(place.primary)
    frames = dy.shape[1]
    width = dy.shape[0]
    blocks = frames // BLOCK
    half = frames // 2
    rows = w.shape[3]
    chunk_count = len(BWD_CHUNKS)

    place.greet()

    def cols_of(chunk):
        start, stop = BWD_CHUNKS[chunk % chunk_count]
        return pl.ds(start, stop - start)

    def layer_of(chunk):
        return 1 - chunk // chunk_count

    def load_weights(chunk):
        part = (layer_of(chunk), slice(None), slice(None), slice(None), cols_of(chunk))
        return pltpu.make_async_copy(w_hbm.at[part], w.at[part], w_sem.at[chunk])

    loads = {
        "act": (act_hbm, act, 0),
        "slope": (slope_hbm, slope, 1),
        "n2": (n2_hbm, n2, 2),
        "ctx": (ctx_hbm, ctx, 3),
        "qkv": (qkv_hbm, qkv, 4),
        "lse": (lse_hbm, lse, 5),
        "n1": (n1_hbm, act.at[pl.ds(0, width), :], 6),
        "x": (x_hbm, act.at[pl.ds(width, width), :], 7),
    }

    def load(name, layer):
        src, dst, index = loads[name]
        return pltpu.make_async_copy(src.at[layer], dst, load_sem.at[index])

    def load_h(layer, index):
        slot = lax.rem(index, 2)
        return pltpu.make_async_copy(
            h_hbm.at[layer, :, block_of(index)], h_in.at[slot], h_sem.at[slot]
        )

    low_rows = pl.ds(0, SPLIT)
    high_rows = pl.ds(SPLIT, rows - SPLIT)
    every = pl.ds(0, rows)

    def ya_copy(chunk):
        cols = cols_of(chunk)
        return remote(
            w.at[layer_of(chunk), :, 1 - y, low_rows, cols],
            land_a.at[:, low_rows, cols],
            ya_send.at[chunk],
            ya_recv.at[chunk],
            place.beside,
        )

    def xb_copy(chunk):
        cols = cols_of(chunk)
        return remote(
            w.at[layer_of(chunk), :, 1 - y, high_rows, cols],
            land_b.at[:, :, cols],
            xb_send.at[chunk],
            xb_recv.at[chunk],
            place.across,
        )

    def x_copy(chunk):
        cols = cols_of(chunk)
        return remote(
            w.at[layer_of(chunk), :, y, :, cols],
            land_a.at[:, :, cols],
            x_send.at[chunk],
            x_recv.at[chunk],
            place.across,
        )

    def y_copy(chunk):
        cols = cols_of(chunk)
        return remote(
            w.at[layer_of(chunk), :, 1 - y, :, cols],
            land_y.at[:, :, cols],
            y_send.at[chunk],
            y_recv.at[chunk],
            place.beside,
        )

    def z_copies(chunk):
        cols = cols_of(chunk)
        layer = layer_of(chunk)
        piece = chunk % chunk_count
        copies = []
        for step in range(LINES):
            line = place.line(step)
            copies.append(
                remote(
                    w.at[layer, line, y, :, cols],
                    landed.at[e, :, cols],
                    z_send.at[chunk, step],
                    z_recv.at[piece, e],
                    (layer, place.row_of(line, y), t),
                )
            )
        local = pltpu.make_async_copy(
            w.at[layer, e, y, :, cols], landed.at[e, :, cols], z_recv.at[piece, e]
        )
        return copies, local

    def add_rows(chunk, which, span, lands):
        start, stop = BWD_CHUNKS[chunk % chunk_count]
        layer = layer_of(chunk)
        first, count = span
        piece = 256 if (stop - start) % 256 == 0 else 128

        def body(index, carry):
            cols = pl.ds(pl.multiple_of(start + index * piece, 128), piece)
            for line in range(LINES):
                total = w[layer, line, which, pl.ds(first, count), cols].astype(F32)
                for land, offset in lands:
                    total = total + land[line, pl.ds(offset, count), cols].astype(F32)
                w[layer, line, which, pl.ds(first, count), cols] = total.astype(BF)
            return carry

        lax.fori_loop(0, (stop - start) // piece, body, 0)

    def signal(sem, chunk, device):
        if chunk < chunk_count:
            pl.semaphore_signal(sem.at[chunk], inc=1, device_id=device, device_id_type=MESH)

    def credit(sem, chunk):
        if chunk >= chunk_count:
            pl.semaphore_wait(sem.at[chunk - chunk_count], 1)

    def step_a(chunk):
        @pl.when(secondary)
        def _():
            credit(ya_free, chunk)
            ya_copy(chunk).start()
            credit(xb_free, chunk)
            xb_copy(chunk).start()

    def step_b(chunk):
        cols = cols_of(chunk)

        @pl.when(secondary)
        def _():
            await_bytes(land_a.at[:, low_rows, cols], ya_recv.at[chunk])
            add_rows(chunk, y, (0, SPLIT), [(land_a, 0)])
            signal(ya_free, chunk, place.beside)
            credit(x_free, chunk)
            x_copy(chunk).start()

        @pl.when(primary)
        def _():
            await_bytes(land_b.at[:, :, cols], xb_recv.at[chunk])
            add_rows(chunk, 1 - y, (SPLIT, rows - SPLIT), [(land_b, 0)])
            signal(xb_free, chunk, place.across)
            credit(y_free, chunk)
            y_copy(chunk).start()

    def step_c(chunk):
        cols = cols_of(chunk)

        @pl.when(primary)
        def _():
            await_bytes(land_a.at[:, :, cols], x_recv.at[chunk])
            await_bytes(land_y.at[:, :, cols], y_recv.at[chunk])
            add_rows(chunk, y, (0, rows), [(land_a, 0), (land_y, 0)])
            signal(x_free, chunk, place.across)
            signal(y_free, chunk, place.beside)
            copies, local = z_copies(chunk)

            @pl.when(s == layer_of(chunk))
            def _():
                local.start()

            @pl.when(s != layer_of(chunk))
            def _():
                copies[0].start()

            for copy in copies[1:]:
                copy.start()

    def exchange(kind, index, layer):
        slot = 2 * layer + kind
        return remote(
            send.at[kind, index],
            recv.at[kind, index],
            e_send.at[slot, index],
            e_recv.at[slot, index],
            place.core,
        )

    def joined(kind, index, layer):
        exchange(kind, index, layer).wait()
        return send[kind, index].astype(F32) + recv[kind, index].astype(F32)

    def store_grads(layer, start, count, value):
        w[layer, :, :, :, pl.ds(start, count)] = value.astype(BF).reshape(
            w.shape[1], w.shape[2], rows, count
        )

    def outer(layer, start, left, right, right_rows):
        tiles = right_rows // 256

        def body(index, carry):
            span = pl.ds(pl.multiple_of(index * 256, 256), 256)
            value = mmt(left[...], right[span, :])
            store_grads(layer, pl.multiple_of(start + index * 256, 128), 256, value)
            return carry

        lax.fori_loop(0, tiles, body, 0)
        if right_rows % 256:
            span = slice(tiles * 256, right_rows)
            value = mmt(left[...], right[span, :])
            store_grads(layer, start + tiles * 256, right_rows % 256, value)

    ones = functools.partial(jnp.ones, (frames, 128), BF)

    def mlp_back(layer):
        def body(index, carry):
            cols = block_of(index)
            for part in range(4):
                units = slice(part * 384, (part + 1) * 384)
                steep = slope[units, cols].astype(F32)
                slope[units, cols] = (mm(wt[units, :], low[:, cols]) * steep).astype(BF)
            term = mm(whole(w, layer, UP, 1536), slope[:, cols])
            send[0, index] = term.astype(BF)
            exchange(0, index, layer).start()
            return carry

        lax.fori_loop(0, blocks, body, 0)

    def fold(value):
        return value[:, 0:128] + value[:, 128:256]

    def norm_back(layer, kind, gain_lane, source, finish):
        sums[...] = jnp.zeros_like(sums)

        def body(index, carry):
            cols = block_of(index)
            rows_in = source(index)
            hat, scale = centre(rows_in)
            grad = joined(kind, index, layer)
            sums[0] += fold(grad * hat)
            sums[1] += fold(grad)
            scaled = grad * vecs[:, gain_lane : gain_lane + 1]
            mean = jnp.mean(scaled, 0, keepdims=True)
            slant = jnp.mean(scaled * hat, 0, keepdims=True)
            finish(index, dy[:, cols] + scale * (scaled - mean - hat * slant))
            return carry

        lax.fori_loop(0, blocks, body, 0)

    def row_sums(value):
        return jnp.sum(value, 1, keepdims=True)

    def attend_back(first, last):
        def one_head(head, carry):
            base = head * HEAD
            q_rows = pl.ds(pl.multiple_of(base, HEAD), HEAD)
            k_rows = pl.ds(pl.multiple_of(384 + base, HEAD), HEAD)
            v_rows = pl.ds(pl.multiple_of(768 + base, HEAD), HEAD)
            keys = qkv[k_rows, :].T
            values = qkv[v_rows, :].T
            key_total = jnp.zeros((HEAD, frames), F32)
            value_total = jnp.zeros((HEAD, frames), F32)
            for index in range(blocks):
                cols = slice(index * BLOCK, (index + 1) * BLOCK)
                queries = qkv[q_rows, cols]
                grads = dctx[q_rows, cols]
                soft = jnp.exp(mm(keys, queries) - lse[pl.ds(head, 1), cols])
                soft_grad = mm(values, grads)
                inner = jnp.sum(soft * soft_grad, 0, keepdims=True)
                score_grad = (soft * (soft_grad - inner)).astype(BF)
                step = mm(qkv[k_rows, :], score_grad) * 0.125
                slope[q_rows, cols] = step.astype(BF)
                key_total = key_total + mmt(queries, score_grad)
                value_total = value_total + mmt(grads, soft.astype(BF))
            slope[k_rows, :] = key_total.astype(BF)
            slope[v_rows, :] = value_total.astype(BF)
            return carry

        lax.fori_loop(first, last, one_head, 0)

    def out_copies(layer):
        mine = pl.ds(pl.multiple_of(t * half, half), half)
        theirs = pl.ds(pl.multiple_of((1 - t) * half, half), half)
        local = pltpu.make_async_copy(stage.at[mine, :], out.at[0, t], out_sem.at[0])
        away = remote(
            stage.at[theirs, :], out.at[0, t], out_sem.at[1], out_sem.at[2], place.across
        )
        return local, away

    def emit(layer):
        @pl.when(s == layer)
        def _():
            for copy in out_copies(layer):
                copy.start()

    def collect_biases():
        def body(group, carry):
            source = group * rows
            for kind in range(2):
                for head in range(6):
                    at = pl.ds(pl.multiple_of(kind * 384 + head * HEAD + group * 8, 8), 8)
                    to = pl.ds(pl.multiple_of(source + kind * 48 + head * 8, 8), 8)
                    vec_grads[to, 6:7] = spread[at, 6:7]
            for unit in range(24):
                at = pl.ds(pl.multiple_of(768 + unit * HEAD + group * 8, 8), 8)
                to = pl.ds(pl.multiple_of(source + (unit % 12) * 8, 8), 8)
                lane = 7 if unit < 12 else 8
                vec_grads[to, lane : lane + 1] = spread[at, lane : lane + 1]
            return carry

        lax.fori_loop(0, GROUPS, body, 0)

    cot_mine = pltpu.make_async_copy(
        cot.at[t], stage.at[pl.ds(pl.multiple_of(t * half, half), half), :], out_sem.at[3]
    )
    cot_theirs = pltpu.make_async_copy(
        cot_other, stage.at[pl.ds(pl.multiple_of((1 - t) * half, half), half), :], out_sem.at[4]
    )
    cot_mine.start()
    cot_theirs.start()
    load_weights(0).start()
    load("slope", 1).start()
    load_weights(1).start()
    load_weights(3).start()
    load("act", 1).start()
    for name in ("n2", "ctx", "qkv", "lse"):
        load(name, 1).start()
    for chunk in (2, 4, 5, 6, 7):
        load_weights(chunk).start()
    cot_mine.wait()
    cot_theirs.wait()

    def take(index, carry):
        cols = block_of(index)
        tile = stage[cols, :].T
        low[:, cols] = tile
        dy[:, cols] = tile.astype(F32)
        return carry

    lax.fori_loop(0, blocks, take, 0)

    for layer in (1, 0):
        base = (1 - layer) * chunk_count
        later = layer == 0
        load_weights(base).wait()
        load_weights(base + 3).wait()
        vecs[...] = whole(w, layer, VEC, 128).astype(F32)
        vec_grads[...] = jnp.zeros_like(vec_grads)
        flip_weights(w, wt, layer, DOWN, 1536)
        load_h(layer, 0).start()
        load_weights(base + 1).wait()
        load("slope", layer).wait()
        mlp_back(layer)
        if later:
            step_b(3)
        load("act", layer).wait()
        outer(layer, DOWN, low, act, 1536)
        vec_grads[:, 5:6] = mm(low[...], ones())[:, 0:1]
        step_a(base)
        load("n1", layer).start()
        load("x", layer).start()
        load("n2", layer).wait()
        outer(layer, UP, n2, slope, 1536)
        spread[768:, :] = mm(slope[...], ones())
        step_a(base + 1)
        step_b(base)
        if later:
            step_c(3)
        flip_weights_ready = load_weights(base + 2)
        flip_weights_ready.wait()
        flip_weights(w, wt, layer, OUT, 384)

        def hidden_in(index, layer=layer):
            @pl.when(index + 1 < blocks)
            def _():
                load_h(layer, index + 1).start()

            load_h(layer, index).wait()
            return h_in[lax.rem(index, 2)]

        def hidden_out(index, total):
            cols = block_of(index)
            dy[:, cols] = total
            rounded = total.astype(BF)
            low[:, cols] = rounded
            dctx[:, cols] = mm(wt[0:384, :], rounded).astype(BF)

        norm_back(layer, 0, 1, hidden_in, hidden_out)
        vec_grads[:, 1:2] = row_sums(sums[0])
        vec_grads[:, 4:5] = row_sums(sums[1])
        vec_grads[:, 3:4] = mm(low[...], ones())[:, 0:1]
        load("ctx", layer).wait()
        outer(layer, OUT, low, ctx, 384)
        step_a(base + 2)
        step_b(base + 1)
        step_c(base)
        load("qkv", layer).wait()
        load("lse", layer).wait()
        attend_back(0, 3)
        step_b(base + 2)
        step_c(base + 1)
        attend_back(3, 6)
        step_c(base + 2)

        def first_body(index, carry, layer=layer):
            term = mm(whole(w, layer, QKV, 1152), slope[0:1152, block_of(index)])
            send[1, index] = term.astype(BF)
            exchange(1, index, layer).start()
            return carry

        lax.fori_loop(0, blocks, first_body, 0)
        load("n1", layer).wait()
        load("x", layer).wait()
        outer(layer, QKV, act.at[pl.ds(0, width), :], slope, 1152)
        spread[0:384, :] = mm(slope[0:384, :], ones())
        spread[384:768, :] = mm(slope[768:1152, :], ones())
        if layer == 1:
            for name in ("slope", "n2", "ctx", "qkv", "lse"):
                load(name, 0).start()

        def rows_x(index):
            return act[width : 2 * width, block_of(index)].astype(F32)

        def rows_dx(index, total, layer=layer):
            cols = block_of(index)
            rounded = total.astype(BF)
            if layer == 1:
                low[:, cols] = rounded
                dy[:, cols] = rounded.astype(F32)

            @pl.when(s == layer)
            def _():
                stage[cols, :] = rounded.T

        norm_back(layer, 1, 0, rows_x, rows_dx)
        emit(layer)
        if layer == 1:
            load("act", 0).start()
        vec_grads[:, 0:1] = row_sums(sums[0])
        vec_grads[:, 2:3] = row_sums(sums[1])
        collect_biases()
        store_grads(layer, VEC, 128, vec_grads[...])
        step_a(base + 3)

    step_b(7)
    step_c(7)

    for chunk in range(2 * chunk_count):

        @pl.when(secondary)
        def _():
            ya_copy(chunk).wait_send()
            xb_copy(chunk).wait_send()
            x_copy(chunk).wait_send()

        @pl.when(primary)
        def _():
            y_copy(chunk).wait_send()
            copies, _ = z_copies(chunk)

            @pl.when(s != layer_of(chunk))
            def _():
                copies[0].wait_send()

            for copy in copies[1:]:
                copy.wait_send()

    for piece in range(chunk_count):
        for line in range(LINES):
            await_bytes(landed.at[line, :, cols_of(piece)], z_recv.at[piece, line])
    local, away = out_copies(0)
    local.wait()
    away.wait()


def backward_call(share, clips, cotangent, saved, dims):
    width, frames, hidden_units, heads_width = dims
    rows = width // GROUPS
    sem = pltpu.SemaphoreType.DMA
    free = pltpu.SemaphoreType.REGULAR
    packed = (2, LINES, 2, rows, END)
    blocks = frames // BLOCK
    count = len(BWD_CHUNKS)
    outs = [
        jax.ShapeDtypeStruct((1,) + clips.shape, BF),
        jax.ShapeDtypeStruct((LINES, rows, END), BF),
    ]
    scratch = [
        pltpu.VMEM(packed, BF),
        pltpu.VMEM((width, frames), F32),
        pltpu.VMEM((hidden_units, frames), BF),
        pltpu.VMEM((hidden_units, frames), BF),
        pltpu.VMEM((2, width, BLOCK), F32),
        pltpu.VMEM((width, frames), BF),
        pltpu.VMEM((3 * heads_width, frames), BF),
        pltpu.VMEM((heads_width, frames), BF),
        pltpu.VMEM((heads_width, frames), BF),
        pltpu.VMEM((width, frames), BF),
        pltpu.VMEM((8, frames), F32),
        pltpu.VMEM((hidden_units, width), BF),
        pltpu.VMEM((2, blocks, width, BLOCK), BF),
        pltpu.VMEM((2, blocks, width, BLOCK), BF),
        pltpu.VMEM((width, 128), F32),
        pltpu.VMEM((width, 128), F32),
        pltpu.VMEM((2, width, 128), F32),
        pltpu.VMEM((2 * heads_width + hidden_units, 128), F32),
        pltpu.VMEM((frames, width), BF),
        pltpu.VMEM((LINES, rows, END), BF),
        pltpu.VMEM((LINES, rows - SPLIT, END), BF),
        pltpu.VMEM((LINES, rows, END), BF),
    ]
    scratch += [sem((2 * count,))] * 8
    scratch += [
        sem((2 * count, LINES)),
        sem((count, LINES)),
        sem((4, blocks)),
        sem((4, blocks)),
        sem((2 * count,)),
        sem((8,)),
        sem((2,)),
        sem((5,)),
    ]
    scratch += [free((count,))] * 4
    anywhere = pl.BlockSpec(memory_space=pl.ANY)
    operands = [cotangent, *saved]
    return pl.pallas_call(
        functools.partial(backward_kernel, share),
        out_shape=outs,
        in_specs=[anywhere] * len(operands),
        out_specs=[anywhere] * len(outs),
        scratch_shapes=scratch,
        compiler_params=pltpu.CompilerParams(
            collective_id=1, has_side_effects=True, vmem_limit_bytes=VMEM_LIMIT
        ),
        cost_estimate=pl.CostEstimate(
            flops=40_000_000_000, bytes_accessed=60_000_000, transcendentals=0
        ),
    )(*operands)


def group_piece(value, axis, share):
    if share == 1:
        return value
    size = value.shape[axis] * share
    group = lax.axis_index("dp") // share
    full = lax.all_gather(value, "dp", axis=axis, tiled=True)
    return lax.dynamic_slice_in_dim(full, group * size, size, axis)


def own_part(value, axis, share, parts, index):
    size = value.shape[axis] // parts
    if parts == 1:
        return value
    return lax.dynamic_slice_in_dim(value, index * size, size, axis)


def on_device(share, clips, cotangent, ln_gains, row_biases, w_qkv, b_qv, w_o, w_up, b_ff, w_down):
    width = clips.shape[2]
    rows = width // GROUPS
    dims = (width, 2 * clips.shape[1], w_up.shape[2], w_o.shape[1])
    ln_gains = group_piece(ln_gains, 2, share)
    row_biases = group_piece(row_biases, 2, share)
    w_qkv = group_piece(w_qkv, 2, share)
    b_qv = group_piece(b_qv, 3, share)
    w_o = group_piece(w_o, 2, share)
    w_up = group_piece(w_up, 1, share)
    b_ff = group_piece(b_ff, 2, share)
    w_down = group_piece(w_down, 2, share)
    vectors = jnp.concatenate([ln_gains[0], row_biases[0]], 0).T
    heads = jnp.concatenate([b_qv[0, 0].reshape(-1), b_qv[0, 1].reshape(-1)])[:, None]
    units = b_ff[0].reshape(2, rows).T
    packed = jnp.concatenate([vectors, heads, units], 1)
    packed = jnp.pad(packed, ((0, 0), (0, 128 - packed.shape[1])))
    shard = jnp.concatenate(
        [packed, w_qkv[0, 0], w_qkv[0, 1], w_qkv[0, 2], w_o[0].T, w_up[0], w_down[0].T], 1
    )
    section_out, *saved = forward_call(share, clips, cotangent, shard, dims)
    section_in_grad, landed = backward_call(share, clips, cotangent, saved, dims)
    grads = jnp.sum(landed.astype(F32), 0)
    rest = lax.axis_index("dp") % share
    side = lax.axis_index("tensor")
    if share > 1:
        group = lax.axis_index("dp") // share
        padded = jnp.zeros((width, END), F32)
        padded = lax.dynamic_update_slice_in_dim(padded, grads, group * rows, 0)
        grads = lax.dynamic_slice_in_dim(lax.psum(padded, "dp"), group * rows, rows, 0)
    mine = own_part(grads, 0, share, share, rest)
    vec = own_part(mine, 0, share, 2, side)
    heads_grad = grads[:, 6].reshape(2, -1, HEAD // GROUPS)
    units_grad = grads[:, 7:9].T.reshape(-1, HEAD // GROUPS)
    qkv_grad = mine[:, QKV:OUT].reshape(mine.shape[0], 3, -1)
    return (
        section_out,
        section_in_grad,
        vec[:, 0:2].T[None],
        vec[:, 2:6].T[None],
        jnp.stack([qkv_grad[:, 0], qkv_grad[:, 1], qkv_grad[:, 2]])[None],
        own_part(heads_grad, 2, share, share, rest)[None],
        mine[:, OUT:UP].T[None],
        mine[:, UP:DOWN][None],
        own_part(units_grad, 1, share, share, rest)[None],
        mine[:, DOWN:END].T[None],
    )


def solution(mesh):
    placed = (
        P("dp", "tensor", None),
        P("dp", "tensor", None),
        P("section", None, "dp"),
        P("section", None, "dp"),
        P("section", None, "dp", "tensor"),
        P("section", None, "tensor", "dp"),
        P("section", "tensor", "dp"),
        P("section", "dp", "tensor"),
        P("section", "tensor", "dp"),
        P("section", "tensor", "dp"),
    )
    share = mesh.shape["dp"] // GROUPS
    return jax.shard_map(
        functools.partial(on_device, share),
        mesh=mesh,
        in_specs=placed,
        out_specs=(
            P("section", "dp", "tensor", None),
            P("section", "dp", "tensor", None),
            P("section", None, ("dp", "tensor")),
            P("section", None, ("dp", "tensor")),
            P("section", None, "dp", "tensor"),
            P("section", None, "tensor", "dp"),
            P("section", "tensor", "dp"),
            P("section", "dp", "tensor"),
            P("section", "tensor", "dp"),
            P("section", "tensor", "dp"),
        ),
        check_vma=False,
    )
```

```python
import functools

import jax
import jax.numpy as jnp
from jax import lax
from jax.experimental import pallas as pl
from jax.experimental.pallas import tpu as pltpu
from jax.sharding import PartitionSpec as P

BF = jnp.bfloat16
F32 = jnp.float32
MESH = pl.DeviceIdType.MESH
EPSILON = 1e-05
HEAD = 64
GROUPS = 8
LINES = 4
BLOCK = 256
VMEM_LIMIT = 62 * 1024 * 1024

VEC = 0
QKV = 128
OUT = 1280
UP = 1664
DOWN = 3200
END = 4736
SPLIT = 64
WIDE = 384
CHUNKS = 12


def mm(left, right):
    return jnp.dot(left, right, preferred_element_type=F32)


def mmt(left, right):
    return lax.dot_general(left, right, (((1,), (1,)), ((), ())), preferred_element_type=F32)


class Place:
    def __init__(self, share):
        self.s = lax.axis_index("section")
        self.d = lax.axis_index("dp")
        self.t = lax.axis_index("tensor")
        group = self.d // share
        self.rest = self.d - group * share
        self.share = share
        self.e = group // 2
        self.y = group - self.e * 2
        self.primary = self.s == self.t
        self.core = (1 - self.s, self.d, self.t)
        self.across = (self.s, self.d, 1 - self.t)
        self.beside = (self.s, self.row_of(self.e, 1 - self.y), self.t)

    def row_of(self, line, y):
        return (line * 2 + y) * self.share + self.rest

    def line(self, step):
        return lax.rem(self.e + step, LINES)

    def greet(self):
        barrier = pltpu.get_barrier_semaphore()
        peers = [self.core, self.across, self.beside]
        for step in range(1, LINES):
            for section in range(2):
                peers.append((section, self.row_of(self.line(step), self.y), self.t))
        for peer in peers:
            pl.semaphore_signal(barrier, inc=1, device_id=peer, device_id_type=MESH)
        pl.semaphore_wait(barrier, len(peers))


def remote(src, dst, send_sem, recv_sem, device):
    return pltpu.make_async_remote_copy(
        src_ref=src,
        dst_ref=dst,
        send_sem=send_sem,
        recv_sem=recv_sem,
        device_id=device,
        device_id_type=MESH,
    )


def await_bytes(ref, sem):
    pltpu.make_async_copy(ref, ref, sem).wait()


def centre(rows_in):
    mean = jnp.mean(rows_in, 0, keepdims=True)
    centred = rows_in - mean
    variance = jnp.mean(centred * centred, 0, keepdims=True)
    scale = lax.rsqrt(variance + EPSILON)
    return centred * scale, scale


def gelu_parts(values):
    bell = jnp.exp(-0.5 * values * values)
    reach = jnp.abs(values) * 0.7071067811865476
    inv = 1.0 / (1.0 + 0.3275911 * reach)
    poly = inv * (
        0.254829592
        + inv * (-0.284496736 + inv * (1.421413741 + inv * (-1.453152027 + inv * 1.061405429)))
    )
    tail = 0.5 * poly * bell
    cdf = jnp.where(values >= 0.0, 1.0 - tail, tail)
    return values * cdf, cdf + values * bell * 0.3989422804014327


def block_of(index):
    return pl.ds(pl.multiple_of(index * BLOCK, BLOCK), BLOCK)


def flip_weights(w, wt, layer, start, width, target=0):
    def body(index, carry):
        cols = pl.ds(pl.multiple_of(start + index * 128, 128), 128)
        rows = pl.ds(pl.multiple_of(target + index * 128, 128), 128)
        tile = w[layer, :, :, :, cols]
        wt[rows, :] = tile.reshape(tile.shape[0] * tile.shape[1] * tile.shape[2], 128).T
        return carry

    lax.fori_loop(0, width // 128, body, 0)


def whole(w, layer, start, width):
    tile = w[layer, :, :, :, start : start + width]
    return tile.reshape(tile.shape[0] * tile.shape[1] * tile.shape[2], width)


def spread_biases(vecs, spread, rows):
    def body(group, carry):
        source = group * rows
        for kind in range(2):
            for head in range(6):
                to = pl.ds(pl.multiple_of(kind * 384 + head * HEAD + group * 8, 8), 8)
                at = pl.ds(pl.multiple_of(source + kind * 48 + head * 8, 8), 8)
                spread[to, :] = vecs[at, :]
        for unit in range(24):
            to = pl.ds(pl.multiple_of(768 + unit * HEAD + group * 8, 8), 8)
            at = pl.ds(pl.multiple_of(source + (unit % 12) * 8, 8), 8)
            spread[to, :] = vecs[at, :]
        return carry

    lax.fori_loop(0, GROUPS, body, 0)


def layers_kernel(
    share,
    clips,
    cot,
    shard,
    out,
    in_grad,
    landed,
    cot_other,
    x_hbm,
    h_hbm,
    n1_hbm,
    n2_hbm,
    qkv_hbm,
    ctx_hbm,
    lse_hbm,
    act_hbm,
    slope_hbm,
    w,
    res,
    act,
    slope,
    n1,
    n2,
    low,
    qkv,
    ctx,
    dctx,
    lse,
    h_in,
    wt,
    send,
    recv,
    vecs,
    vec_grads,
    sums,
    spread,
    stage,
    land_a,
    land_b,
    land_y,
    z_send,
    z_recv,
    x_send,
    x_recv,
    xb_send,
    xb_recv,
    y_send,
    y_recv,
    ya_send,
    ya_recv,
    gz_send,
    gz_recv,
    gx_send,
    gx_recv,
    gxb_send,
    gxb_recv,
    gy_send,
    gy_recv,
    gya_send,
    gya_recv,
    e_send,
    e_recv,
    in_sem,
    cot_sem,
    out_sem,
    save_sem,
    load_sem,
    h_sem,
    ya_free,
    xb_free,
    x_free,
    y_free,
):
    place = Place(share)
    s, t, e, y = place.s, place.t, place.e, place.y
    primary, secondary = place.primary, jnp.logical_not(place.primary)
    width, frames = res.shape
    blocks = frames // BLOCK
    half = frames // 2
    quarter = half // 2
    rows = w.shape[3]
    low_rows = pl.ds(0, SPLIT)
    high_rows = pl.ds(SPLIT, rows - SPLIT)
    mine = pl.ds(pl.multiple_of(t * half, half), half)
    theirs = pl.ds(pl.multiple_of((1 - t) * half, half), half)

    place.greet()

    def gather_cols(piece):
        if isinstance(piece, int) and piece == 0:
            return pl.ds(VEC, QKV + WIDE)
        return pl.ds(pl.multiple_of(QKV + piece * WIDE, 128), WIDE)

    def z_copies(piece):
        cols = gather_cols(piece)
        copies = []
        for step in range(LINES):
            copies.append(
                remote(
                    shard.at[:, cols],
                    w.at[s, e, y, :, cols],
                    z_send.at[piece, step],
                    z_recv.at[s, piece, e],
                    (t, place.row_of(place.line(step), y), t),
                )
            )
        local = pltpu.make_async_copy(
            shard.at[:, cols], w.at[s, e, y, :, cols], z_recv.at[s, piece, e]
        )
        return copies, local

    def z_start(layer, piece):
        @pl.when(s == layer)
        def _():
            copies, local = z_copies(piece)

            @pl.when(primary)
            def _():
                local.start()

            @pl.when(secondary)
            def _():
                copies[0].start()

            for copy in copies[1:]:
                copy.start()

    def z_finish(piece):
        copies, _ = z_copies(piece)

        @pl.when(secondary)
        def _():
            copies[0].wait_send()

        for copy in copies[1:]:
            copy.wait_send()

    def x_copy(layer, piece):
        part = w.at[layer, :, y, :, gather_cols(piece)]
        return remote(part, part, x_send.at[layer, piece], x_recv.at[layer, piece], place.across)

    def y_copy(layer, piece):
        part = w.at[layer, :, y, :, gather_cols(piece)]
        return remote(part, part, y_send.at[layer, piece], y_recv.at[layer, piece], place.beside)

    def xb_copy(layer, piece):
        part = w.at[layer, :, 1 - y, high_rows, gather_cols(piece)]
        return remote(part, part, xb_send.at[layer, piece], xb_recv.at[layer, piece], place.across)

    def ya_copy(layer, piece):
        part = w.at[layer, :, y, low_rows, gather_cols(piece)]
        return remote(part, part, ya_send.at[layer, piece], ya_recv.at[layer, piece], place.beside)

    def step_z(layer, piece):
        @pl.when(primary)
        def _():
            for line in range(LINES):
                await_bytes(w.at[layer, line, y, :, gather_cols(piece)], z_recv.at[layer, piece, line])
            x_copy(layer, piece).start()
            y_copy(layer, piece).start()

    def step_plane(layer, piece):
        @pl.when(primary)
        def _():
            await_bytes(w.at[layer, :, 1 - y, :, gather_cols(piece)], y_recv.at[layer, piece])
            xb_copy(layer, piece).start()

        @pl.when(secondary)
        def _():
            await_bytes(w.at[layer, :, y, :, gather_cols(piece)], x_recv.at[layer, piece])
            ya_copy(layer, piece).start()

    def complete(layer, *pieces):
        @pl.when(secondary)
        def _():
            for piece in pieces:
                cols = gather_cols(piece)
                await_bytes(w.at[layer, :, 1 - y, high_rows, cols], xb_recv.at[layer, piece])
                await_bytes(w.at[layer, :, 1 - y, low_rows, cols], ya_recv.at[layer, piece])

    kept = {
        "x": (n2, x_hbm),
        "h": (res, h_hbm),
        "n1": (n1, n1_hbm),
        "n2": (n2, n2_hbm),
        "qkv": (qkv, qkv_hbm),
        "ctx": (ctx, ctx_hbm),
        "lse": (lse, lse_hbm),
        "act": (act, act_hbm),
        "slope": (slope, slope_hbm),
    }
    names = tuple(kept)

    def save(name, layer):
        src, dst = kept[name]
        if name in ("x", "h"):
            dst = dst.at[layer]
        return pltpu.make_async_copy(src, dst, save_sem.at[names.index(name), layer])

    def load(name, layer=0):
        dst, src = kept[name]
        if name == "x":
            dst, src = act.at[pl.ds(0, width), :], src.at[layer]
        return pltpu.make_async_copy(src, dst, load_sem.at[names.index(name)])

    def load_h(layer, index):
        slot = lax.rem(index, 2)
        return pltpu.make_async_copy(
            h_hbm.at[layer, :, block_of(index)], h_in.at[slot], h_sem.at[slot]
        )

    my_quarter = pl.ds(s * quarter, quarter)
    my_rows = pl.ds(pl.multiple_of((1 - t) * half + s * quarter, quarter), quarter)

    def clip_across():
        there = pl.ds(pl.multiple_of(t * half + s * quarter, quarter), quarter)
        return remote(
            clips.at[1 - t, my_quarter, :],
            stage.at[there, :],
            in_sem.at[0],
            in_sem.at[1],
            place.across,
        )

    def clip_core():
        part = stage.at[my_rows, :]
        return remote(part, part, in_sem.at[2], in_sem.at[3], place.core)

    def cot_across():
        return remote(
            cot.at[1 - t, my_quarter, :],
            cot_other.at[my_quarter, :],
            cot_sem.at[0],
            cot_sem.at[1],
            place.across,
        )

    def cot_core():
        part = cot_other.at[my_quarter, :]
        return remote(part, part, cot_sem.at[2], cot_sem.at[3], place.core)

    def exchange(kind, index, slot):
        return remote(
            send.at[kind, index],
            recv.at[kind, index],
            e_send.at[slot, index],
            e_recv.at[slot, index],
            place.core,
        )

    def joined(kind, index, slot):
        exchange(kind, index, slot).wait()
        return send[kind, index].astype(F32) + recv[kind, index].astype(F32)

    def result_copies(ref, first):
        local = pltpu.make_async_copy(stage.at[mine, :], ref.at[0, t], out_sem.at[first])
        away = remote(
            stage.at[theirs, :],
            ref.at[0, t],
            out_sem.at[first + 1],
            out_sem.at[first + 2],
            place.across,
        )
        return local, away

    def emit(layer, ref, first):
        @pl.when(s == layer)
        def _():
            for copy in result_copies(ref, first):
                copy.start()

    for piece in range(5):
        z_start(0, piece)
    own_clip = pltpu.make_async_copy(clips.at[t], stage.at[mine, :], in_sem.at[4])
    own_clip.start()
    clip_across().start()
    cot_across().start()

    def take_clip(first):
        def body(index, carry):
            at = pl.ds(pl.multiple_of(first + index * BLOCK, BLOCK), BLOCK)
            tile = stage[at, :].T
            n2[:, at] = tile
            res[:, at] = tile.astype(F32)
            return carry

        lax.fori_loop(0, half // BLOCK, body, 0)

    own_clip.wait()
    take_clip(t * half)
    clip_across().wait()
    clip_core().start()
    step_z(0, 0)
    z_start(0, 5)
    step_z(0, 1)
    z_start(0, 6)
    clip_core().wait()
    take_clip((1 - t) * half)
    save("x", 0).start()
    step_plane(0, 0)
    step_z(0, 2)
    z_start(0, 7)
    step_plane(0, 1)
    cot_across().wait()
    cot_core().start()
    step_z(0, 3)
    z_start(0, 8)
    step_plane(0, 2)

    def project(index, rows_in):
        normed = centre(rows_in)[0] * vecs[:, 0:1] + vecs[:, 2:3]
        normed = normed.astype(BF)
        cols = block_of(index)
        n1[:, cols] = normed
        for part in range(3):
            value = mm(wt[part * WIDE : (part + 1) * WIDE, :], normed)
            if part == 0:
                value = (value + spread[0:384, 6:7]) * 0.125
            if part == 2:
                value = value + spread[384:768, 6:7]
            qkv[part * WIDE : (part + 1) * WIDE, cols] = value.astype(BF)

    def attend(layer):
        def one_head(head, carry):
            base = head * HEAD
            keys = qkv[pl.ds(pl.multiple_of(384 + base, HEAD), HEAD), :].T
            values = qkv[pl.ds(pl.multiple_of(768 + base, HEAD), HEAD), :]
            queries = pl.ds(pl.multiple_of(base, HEAD), HEAD)
            for index in range(blocks):
                cols = slice(index * BLOCK, (index + 1) * BLOCK)
                scores = mm(keys, qkv[queries, cols])
                top = jnp.max(scores, 0, keepdims=True)
                soft = jnp.exp(scores - top)
                total = jnp.sum(soft, 0, keepdims=True)
                mixed = mm(values, soft.astype(BF)) / total
                ctx[queries, cols] = mixed.astype(BF)
                lse[pl.ds(head, 1), cols] = top + jnp.log(total)
            step_z(layer, 5 + head)
            step_plane(layer, 4 + head)
            return carry

        lax.fori_loop(0, ctx.shape[0] // HEAD, one_head, 0)

    def out_project(layer):
        def body(index, carry):
            part = mm(whole(w, layer, OUT, 384), ctx[:, block_of(index)])
            send[0, index] = part.astype(BF)
            exchange(0, index, 2 * layer).start()
            return carry

        lax.fori_loop(0, blocks, body, 0)

    def middle_norm(layer):
        def body(index, carry):
            cols = block_of(index)
            rows_in = res[:, cols] + joined(0, index, 2 * layer) + vecs[:, 3:4]
            res[:, cols] = rows_in
            n2[:, cols] = (centre(rows_in)[0] * vecs[:, 1:2] + vecs[:, 4:5]).astype(BF)
            return carry

        lax.fori_loop(0, blocks, body, 0)

    def hidden_part(layer, part):
        flip_weights(w, wt, layer, UP + part * WIDE, WIDE, part * WIDE)
        units = slice(part * WIDE, (part + 1) * WIDE)
        lane = 7 if part < 2 else 8

        def body(index, carry):
            cols = block_of(index)
            pre = mm(wt[units, :], n2[:, cols])
            pre = pre + spread[768 + part * WIDE : 768 + (part + 1) * WIDE, lane : lane + 1]
            value, steep = gelu_parts(pre)
            act[units, cols] = value.astype(BF)
            slope[units, cols] = steep.astype(BF)
            return carry

        lax.fori_loop(0, blocks, body, 0)

    def down_project(layer):
        def body(index, carry):
            part = mm(whole(w, layer, DOWN, 1536), act[:, block_of(index)])
            send[1, index] = part.astype(BF)
            exchange(1, index, 2 * layer + 1).start()
            return carry

        lax.fori_loop(0, blocks, body, 0)

    def layer_end(layer, index):
        total = res[:, block_of(index)] + joined(1, index, 2 * layer + 1) + vecs[:, 5:6]
        return total.astype(BF)

    def take_vectors(layer):
        vecs[...] = whole(w, layer, VEC, 128).astype(F32)
        spread_biases(vecs, spread, rows)

    def project_all(layer):
        flip_weights(w, wt, layer, QKV, 1152)

        def body(index, carry):
            project(index, res[:, block_of(index)])
            return carry

        lax.fori_loop(0, blocks, body, 0)
        if layer == 0:
            save("n1", 0).start()
            save("qkv", 0).start()

    complete(0, 0, 1, 2)
    take_vectors(0)
    project_all(0)
    step_z(0, 4)
    step_plane(0, 3)
    for piece in (9, 10, 11):
        z_start(0, piece)
    cot_core().wait()
    load_cot = pltpu.make_async_copy(cot_other, stage.at[theirs, :], cot_sem.at[4])
    load_cot.start()
    own_cot = pltpu.make_async_copy(cot.at[t], stage.at[mine, :], cot_sem.at[5])
    own_cot.start()
    attend(0)
    save("ctx", 0).start()
    save("lse", 0).start()
    complete(0, 3)
    out_project(0)
    step_z(0, 11)
    step_plane(0, 10)
    for piece in (0, 1, 2):
        z_start(1, piece)
    load_cot.wait()
    own_cot.wait()

    def take_cot(index, carry):
        low[:, block_of(index)] = stage[block_of(index), :].T
        return carry

    lax.fori_loop(0, blocks, take_cot, 0)
    save("x", 0).wait()
    middle_norm(0)
    save("h", 0).start()
    save("n2", 0).start()
    for part in range(4):
        complete(0, 4 + part)
        hidden_part(0, part)
        step_z(1, part)
        if part == 0:
            step_plane(0, 11)
        else:
            step_plane(1, part - 1)
        z_start(1, part + 3)
    save("act", 0).start()
    save("slope", 0).start()
    complete(0, 8, 9, 10, 11)
    down_project(0)
    step_z(1, 4)
    step_plane(1, 3)
    z_start(1, 7)
    z_start(1, 8)
    for name in ("n1", "qkv", "h", "n2"):
        save(name, 0).wait()

    def finish_body(index, carry):
        rows_out = layer_end(0, index)
        cols = block_of(index)
        n2[:, cols] = rows_out
        res[:, cols] = rows_out.astype(F32)

        @pl.when(s == 0)
        def _():
            stage[cols, :] = rows_out.T

        return carry

    lax.fori_loop(0, blocks, finish_body, 0)
    emit(0, out, 0)
    save("x", 1).start()
    complete(1, 0, 1, 2)
    take_vectors(1)
    project_all(1)
    for piece in (9, 10, 11):
        z_start(1, piece)
    save("ctx", 0).wait()
    save("lse", 0).wait()
    attend(1)
    complete(1, 3)
    out_project(1)
    step_z(1, 11)
    step_plane(1, 10)
    save("x", 1).wait()
    middle_norm(1)
    save("h", 1).start()
    save("act", 0).wait()
    save("slope", 0).wait()
    for part in range(4):
        complete(1, 4 + part)
        hidden_part(1, part)
        if part == 0:
            step_plane(1, 11)
    complete(1, 8, 9, 10, 11)
    down_project(1)
    flip_weights(w, wt, 1, DOWN, 1536)

    def last_body(index, carry):
        rows_out = layer_end(1, index)

        @pl.when(s == 1)
        def _():
            stage[block_of(index), :] = rows_out.T

        return carry

    lax.fori_loop(0, blocks, last_body, 0)
    emit(1, out, 0)
    save("h", 1).wait()

    VECTORS = CHUNKS

    def grad_cols(piece):
        if isinstance(piece, int) and piece == VECTORS:
            return pl.ds(VEC, QKV)
        return pl.ds(pl.multiple_of(QKV + piece * WIDE, 128), WIDE)

    def gya_copy(layer, piece):
        cols = grad_cols(piece)
        return remote(
            w.at[layer, :, 1 - y, low_rows, cols],
            land_a.at[:, low_rows, cols],
            gya_send.at[layer, piece],
            gya_recv.at[layer, piece],
            place.beside,
        )

    def gxb_copy(layer, piece):
        cols = grad_cols(piece)
        return remote(
            w.at[layer, :, 1 - y, high_rows, cols],
            land_b.at[:, :, cols],
            gxb_send.at[layer, piece],
            gxb_recv.at[layer, piece],
            place.across,
        )

    def gx_copy(layer, piece):
        cols = grad_cols(piece)
        return remote(
            w.at[layer, :, y, :, cols],
            land_a.at[:, :, cols],
            gx_send.at[layer, piece],
            gx_recv.at[layer, piece],
            place.across,
        )

    def gy_copy(layer, piece):
        cols = grad_cols(piece)
        return remote(
            w.at[layer, :, 1 - y, :, cols],
            land_y.at[:, :, cols],
            gy_send.at[layer, piece],
            gy_recv.at[layer, piece],
            place.beside,
        )

    def gz_copies(layer, piece):
        cols = grad_cols(piece)
        copies = []
        for step in range(LINES):
            line = place.line(step)
            copies.append(
                remote(
                    w.at[layer, line, y, :, cols],
                    landed.at[e, :, cols],
                    gz_send.at[layer, piece, step],
                    gz_recv.at[piece, e],
                    (layer, place.row_of(line, y), t),
                )
            )
        local = pltpu.make_async_copy(
            w.at[layer, e, y, :, cols], landed.at[e, :, cols], gz_recv.at[piece, e]
        )
        return copies, local

    def add_rows(layer, piece, which, span, lands):
        cols = grad_cols(piece)
        first, count = span
        for line in range(LINES):
            total = w[layer, line, which, pl.ds(first, count), cols].astype(F32)
            for land, offset in lands:
                total = total + land[line, pl.ds(offset, count), cols].astype(F32)
            w[layer, line, which, pl.ds(first, count), cols] = total.astype(BF)

    def signal(sem, layer, piece, device):
        if layer == 1:
            pl.semaphore_signal(sem.at[piece], inc=1, device_id=device, device_id_type=MESH)

    def credit(sem, layer, piece):
        if layer == 0:
            pl.semaphore_wait(sem.at[piece], 1)

    def step_a(layer, piece):
        @pl.when(secondary)
        def _():
            credit(ya_free, layer, piece)
            gya_copy(layer, piece).start()
            credit(xb_free, layer, piece)
            gxb_copy(layer, piece).start()

    def step_b(layer, piece):
        cols = grad_cols(piece)

        @pl.when(secondary)
        def _():
            await_bytes(land_a.at[:, low_rows, cols], gya_recv.at[layer, piece])
            add_rows(layer, piece, y, (0, SPLIT), [(land_a, 0)])
            signal(ya_free, layer, piece, place.beside)
            credit(x_free, layer, piece)
            gx_copy(layer, piece).start()

        @pl.when(primary)
        def _():
            await_bytes(land_b.at[:, :, cols], gxb_recv.at[layer, piece])
            add_rows(layer, piece, 1 - y, (SPLIT, rows - SPLIT), [(land_b, 0)])
            signal(xb_free, layer, piece, place.across)
            credit(y_free, layer, piece)
            gy_copy(layer, piece).start()

    def step_c(layer, piece):
        cols = grad_cols(piece)

        @pl.when(primary)
        def _():
            await_bytes(land_a.at[:, :, cols], gx_recv.at[layer, piece])
            await_bytes(land_y.at[:, :, cols], gy_recv.at[layer, piece])
            add_rows(layer, piece, y, (0, rows), [(land_a, 0), (land_y, 0)])
            signal(x_free, layer, piece, place.across)
            signal(y_free, layer, piece, place.beside)
            copies, local = gz_copies(layer, piece)

            @pl.when(s == layer)
            def _():
                local.start()

            @pl.when(s != layer)
            def _():
                copies[0].start()

            for copy in copies[1:]:
                copy.start()

    def store_grads(layer, start, count, value):
        w[layer, :, :, :, pl.ds(start, count)] = value.astype(BF).reshape(
            w.shape[1], w.shape[2], rows, count
        )

    ones = functools.partial(jnp.ones, (frames, 128), BF)

    def mlp_back(layer, beside):
        def body(index, carry):
            cols = block_of(index)
            for part in range(4):
                units = slice(part * WIDE, (part + 1) * WIDE)
                steep = slope[units, cols].astype(F32)
                slope[units, cols] = (mm(wt[units, :], low[:, cols]) * steep).astype(BF)
            term = mm(whole(w, layer, UP, 1536), slope[:, cols])
            send[0, index] = term.astype(BF)
            exchange(0, index, 4 + 2 * layer).start()
            beside(index)
            return carry

        lax.fori_loop(0, blocks, body, 0)

    def outer_pair(layer, start, left, right, first, beside):
        def body(index, carry):
            for part in range(3):
                base = index * 768 + part * 256
                span = pl.ds(pl.multiple_of(base, 256), 256)
                value = mmt(left[...], right[span, :])
                store_grads(layer, pl.multiple_of(start + base, 128), 256, value)
            step_a(layer, first + 2 * index)
            step_a(layer, first + 2 * index + 1)
            beside(index)
            return carry

        lax.fori_loop(0, 2, body, 0)

    def fold(value):
        return value[:, 0:128] + value[:, 128:256]

    def norm_back(layer, kind, gain_lane, source, finish, beside):
        sums[...] = jnp.zeros_like(sums)

        def body(index, carry):
            cols = block_of(index)
            rows_in = source(index)
            hat, scale = centre(rows_in)
            grad = joined(kind, index, 4 + 2 * layer + kind)
            sums[0] += fold(grad * hat)
            sums[1] += fold(grad)
            scaled = grad * vecs[:, gain_lane : gain_lane + 1]
            mean = jnp.mean(scaled, 0, keepdims=True)
            slant = jnp.mean(scaled * hat, 0, keepdims=True)
            finish(index, res[:, cols] + scale * (scaled - mean - hat * slant))
            beside(index)
            return carry

        lax.fori_loop(0, blocks, body, 0)

    def row_sums(value):
        return jnp.sum(value, 1, keepdims=True)

    def attend_back(layer):
        def one_head(head, carry):
            base = head * HEAD
            q_rows = pl.ds(pl.multiple_of(base, HEAD), HEAD)
            k_rows = pl.ds(pl.multiple_of(384 + base, HEAD), HEAD)
            v_rows = pl.ds(pl.multiple_of(768 + base, HEAD), HEAD)
            keys = qkv[k_rows, :].T
            values = qkv[v_rows, :].T
            key_total = jnp.zeros((HEAD, frames), F32)
            value_total = jnp.zeros((HEAD, frames), F32)
            for index in range(blocks):
                cols = slice(index * BLOCK, (index + 1) * BLOCK)
                queries = qkv[q_rows, cols]
                grads = dctx[q_rows, cols]
                soft = jnp.exp(mm(keys, queries) - lse[pl.ds(head, 1), cols])
                soft_grad = mm(values, grads)
                inner = jnp.sum(soft * soft_grad, 0, keepdims=True)
                score_grad = (soft * (soft_grad - inner)).astype(BF)
                step = mm(qkv[k_rows, :], score_grad) * 0.125
                slope[q_rows, cols] = step.astype(BF)
                key_total = key_total + mmt(queries, score_grad)
                value_total = value_total + mmt(grads, soft.astype(BF))
            slope[k_rows, :] = key_total.astype(BF)
            slope[v_rows, :] = value_total.astype(BF)
            step_c(layer, 8 + head - 8 * (head // 4))
            return carry

        lax.fori_loop(0, ctx.shape[0] // HEAD, one_head, 0)

    def collect_biases():
        def body(group, carry):
            source = group * rows
            for kind in range(2):
                for head in range(6):
                    at = pl.ds(pl.multiple_of(kind * 384 + head * HEAD + group * 8, 8), 8)
                    to = pl.ds(pl.multiple_of(source + kind * 48 + head * 8, 8), 8)
                    vec_grads[to, 6:7] = spread[at, 6:7]
            for unit in range(24):
                at = pl.ds(pl.multiple_of(768 + unit * HEAD + group * 8, 8), 8)
                to = pl.ds(pl.multiple_of(source + (unit % 12) * 8, 8), 8)
                lane = 7 if unit < 12 else 8
                vec_grads[to, lane : lane + 1] = spread[at, lane : lane + 1]
            return carry

        lax.fori_loop(0, GROUPS, body, 0)

    def nothing(index):
        del index

    def finish_gather(piece):
        z_finish(piece)
        for layer in range(2):

            @pl.when(primary)
            def _():
                x_copy(layer, piece).wait_send()
                y_copy(layer, piece).wait_send()
                xb_copy(layer, piece).wait_send()

            @pl.when(secondary)
            def _():
                ya_copy(layer, piece).wait_send()

    def finish_body_gather(piece, carry):
        finish_gather(piece)
        return carry

    res[...] = low[...].astype(F32)

    for layer in (1, 0):
        later = layer == 0
        load_h(layer, 0).start()
        if later:
            vecs[...] = whole(w, layer, VEC, 128).astype(F32)
            flip_weights(w, wt, layer, DOWN, 1536)
            load("slope").wait()
        vec_grads[...] = jnp.zeros_like(vec_grads)

        def early(index):
            @pl.when(index < 3)
            def _():
                step_c(1, index)

            @pl.when(index == 3)
            def _():
                step_b(1, VECTORS)

        mlp_back(layer, early if later else nothing)
        if not later:
            finish_gather(0)
            lax.fori_loop(1, CHUNKS, finish_body_gather, 0)
        if later:
            load("act").wait()
        outer_pair(layer, DOWN, low, act, 8, nothing)
        load("x", layer).start()
        if later:
            step_c(1, VECTORS)
            load("n2").wait()
        vec_grads[:, 5:6] = mm(low[...], ones())[:, 0:1]

        def drain_down(index, layer=layer):
            step_b(layer, 8 + 2 * index)
            step_b(layer, 9 + 2 * index)

        outer_pair(layer, UP, n2, slope, 4, drain_down)
        spread[768:, :] = mm(slope[...], ones())
        flip_weights(w, wt, layer, OUT, 384)

        def hidden_in(index, layer=layer):
            @pl.when(index + 1 < blocks)
            def _():
                load_h(layer, index + 1).start()

            load_h(layer, index).wait()
            return h_in[lax.rem(index, 2)]

        def hidden_out(index, total):
            cols = block_of(index)
            res[:, cols] = total
            rounded = total.astype(BF)
            low[:, cols] = rounded
            dctx[:, cols] = mm(wt[0:384, :], rounded).astype(BF)

        def drain_up(index, layer=layer):
            step_b(layer, 4 + index)

        norm_back(layer, 0, 1, hidden_in, hidden_out, drain_up)
        vec_grads[:, 1:2] = row_sums(sums[0])
        vec_grads[:, 4:5] = row_sums(sums[1])
        vec_grads[:, 3:4] = mm(low[...], ones())[:, 0:1]
        if later:
            for name in ("ctx", "qkv", "lse"):
                load(name).wait()
        store_grads(layer, OUT, 384, mmt(low[...], ctx[...]))
        step_a(layer, 3)
        attend_back(layer)
        step_b(layer, 3)

        def first_body(index, carry, layer=layer):
            term = mm(whole(w, layer, QKV, 1152), slope[0:1152, block_of(index)])
            send[1, index] = term.astype(BF)
            exchange(1, index, 5 + 2 * layer).start()
            return carry

        lax.fori_loop(0, blocks, first_body, 0)
        step_c(layer, 6)
        if later:
            load("n1").wait()

        def qkv_body(index, carry, layer=layer):
            span = pl.ds(pl.multiple_of(index * WIDE, WIDE), WIDE)
            store_grads(
                layer, pl.multiple_of(QKV + index * WIDE, 128), WIDE, mmt(n1[...], slope[span, :])
            )
            step_a(layer, index)
            return carry

        lax.fori_loop(0, 3, qkv_body, 0)
        spread[0:384, :] = mm(slope[0:384, :], ones())
        spread[384:768, :] = mm(slope[768:1152, :], ones())
        step_c(layer, 7)
        if layer == 1:
            for name in ("slope", "n1", "n2", "ctx", "qkv", "lse"):
                load(name).start()
        load("x", layer).wait()

        @pl.when(s == layer)
        def _():
            local, away = result_copies(out, 0)
            local.wait()
            away.wait_send()

        def rows_x(index):
            return act[0:width, block_of(index)].astype(F32)

        def rows_dx(index, total, layer=layer):
            cols = block_of(index)
            rounded = total.astype(BF)
            if layer == 1:
                low[:, cols] = rounded
                res[:, cols] = rounded.astype(F32)

            @pl.when(s == layer)
            def _():
                stage[cols, :] = rounded.T

        def drain_qkv(index, layer=layer):
            @pl.when(index < 3)
            def _():
                step_b(layer, index)

        norm_back(layer, 1, 0, rows_x, rows_dx, drain_qkv)
        emit(layer, in_grad, 3)
        if layer == 1:
            load("act").start()
        vec_grads[:, 0:1] = row_sums(sums[0])
        vec_grads[:, 2:3] = row_sums(sums[1])
        collect_biases()
        store_grads(layer, VEC, 128, vec_grads[...])
        step_a(layer, VECTORS)
        step_c(layer, 3)

    for piece in range(3):
        step_c(0, piece)
    step_b(0, VECTORS)
    step_c(0, VECTORS)

    def finish_scatter(piece):
        for layer in range(2):

            @pl.when(secondary)
            def _():
                gya_copy(layer, piece).wait_send()
                gxb_copy(layer, piece).wait_send()
                gx_copy(layer, piece).wait_send()

            @pl.when(primary)
            def _():
                gy_copy(layer, piece).wait_send()
                copies, _ = gz_copies(layer, piece)

                @pl.when(s != layer)
                def _():
                    copies[0].wait_send()

                for copy in copies[1:]:
                    copy.wait_send()

    def await_landed(piece):
        for line in range(LINES):
            await_bytes(landed.at[line, :, grad_cols(piece)], gz_recv.at[piece, line])

    def finish_body_all(piece, carry):
        finish_scatter(piece)
        await_landed(piece)
        return carry

    finish_scatter(0)
    await_landed(0)
    lax.fori_loop(1, CHUNKS, finish_body_all, 0)
    finish_scatter(VECTORS)
    await_landed(VECTORS)

    _, away = result_copies(out, 0)
    away.wait_recv()
    local, away = result_copies(in_grad, 3)
    local.wait()
    away.wait()


def layers_call(share, clips, cotangent, shard, dims):
    width, frames, hidden_units, heads_width = dims
    rows = shard.shape[0]
    sem = pltpu.SemaphoreType.DMA
    free = pltpu.SemaphoreType.REGULAR
    packed = (2, LINES, 2, rows, END)
    blocks = frames // BLOCK
    shape = jax.ShapeDtypeStruct
    outs = [
        shape((1,) + clips.shape, BF),
        shape((1,) + clips.shape, BF),
        shape((LINES, rows, END), BF),
        shape(clips.shape[1:], BF),
        shape((2, width, frames), BF),
        shape((2, width, frames), F32),
        shape((width, frames), BF),
        shape((width, frames), BF),
        shape((3 * heads_width, frames), BF),
        shape((heads_width, frames), BF),
        shape((8, frames), F32),
        shape((hidden_units, frames), BF),
        shape((hidden_units, frames), BF),
    ]
    scratch = [
        pltpu.VMEM(packed, BF),
        pltpu.VMEM((width, frames), F32),
        pltpu.VMEM((hidden_units, frames), BF),
        pltpu.VMEM((hidden_units, frames), BF),
        pltpu.VMEM((width, frames), BF),
        pltpu.VMEM((width, frames), BF),
        pltpu.VMEM((width, frames), BF),
        pltpu.VMEM((3 * heads_width, frames), BF),
        pltpu.VMEM((heads_width, frames), BF),
        pltpu.VMEM((heads_width, frames), BF),
        pltpu.VMEM((8, frames), F32),
        pltpu.VMEM((2, width, BLOCK), F32),
        pltpu.VMEM((hidden_units, width), BF),
        pltpu.VMEM((2, blocks, width, BLOCK), BF),
        pltpu.VMEM((2, blocks, width, BLOCK), BF),
        pltpu.VMEM((width, 128), F32),
        pltpu.VMEM((width, 128), F32),
        pltpu.VMEM((2, width, 128), F32),
        pltpu.VMEM((2 * heads_width + hidden_units, 128), F32),
        pltpu.VMEM((frames, width), BF),
        pltpu.VMEM((LINES, rows, END), BF),
        pltpu.VMEM((LINES, rows - SPLIT, END), BF),
        pltpu.VMEM((LINES, rows, END), BF),
    ]
    scratch += [sem((CHUNKS, LINES)), sem((2, CHUNKS, LINES))]
    scratch += [sem((2, CHUNKS))] * 8
    scratch += [sem((2, CHUNKS + 1, LINES)), sem((CHUNKS + 1, LINES))]
    scratch += [sem((2, CHUNKS + 1))] * 8
    scratch += [
        sem((8, blocks)),
        sem((8, blocks)),
        sem((5,)),
        sem((6,)),
        sem((6,)),
        sem((9, 2)),
        sem((9,)),
        sem((2,)),
    ]
    scratch += [free((CHUNKS + 1,))] * 4
    anywhere = pl.BlockSpec(memory_space=pl.ANY)
    return pl.pallas_call(
        functools.partial(layers_kernel, share),
        out_shape=outs,
        in_specs=[anywhere] * 3,
        out_specs=[anywhere] * len(outs),
        scratch_shapes=scratch,
        compiler_params=pltpu.CompilerParams(
            collective_id=0, has_side_effects=True, vmem_limit_bytes=VMEM_LIMIT
        ),
        cost_estimate=pl.CostEstimate(
            flops=60_000_000_000, bytes_accessed=60_000_000, transcendentals=0
        ),
    )(clips, cotangent, shard)


def group_piece(value, axis, share):
    if share == 1:
        return value
    size = value.shape[axis] * share
    group = lax.axis_index("dp") // share
    full = lax.all_gather(value, "dp", axis=axis, tiled=True)
    return lax.dynamic_slice_in_dim(full, group * size, size, axis)


def own_part(value, axis, share, parts, index):
    size = value.shape[axis] // parts
    if parts == 1:
        return value
    return lax.dynamic_slice_in_dim(value, index * size, size, axis)


def on_device(share, clips, cotangent, ln_gains, row_biases, w_qkv, b_qv, w_o, w_up, b_ff, w_down):
    width = clips.shape[2]
    rows = width // GROUPS
    dims = (width, 2 * clips.shape[1], w_up.shape[2], w_o.shape[1])
    ln_gains = group_piece(ln_gains, 2, share)
    row_biases = group_piece(row_biases, 2, share)
    w_qkv = group_piece(w_qkv, 2, share)
    b_qv = group_piece(b_qv, 3, share)
    w_o = group_piece(w_o, 2, share)
    w_up = group_piece(w_up, 1, share)
    b_ff = group_piece(b_ff, 2, share)
    w_down = group_piece(w_down, 2, share)
    vectors = jnp.concatenate([ln_gains[0], row_biases[0]], 0).T
    heads = jnp.concatenate([b_qv[0, 0].reshape(-1), b_qv[0, 1].reshape(-1)])[:, None]
    units = b_ff[0].reshape(2, rows).T
    packed = jnp.concatenate([vectors, heads, units], 1)
    packed = jnp.pad(packed, ((0, 0), (0, 128 - packed.shape[1])))
    shard = jnp.concatenate(
        [packed, w_qkv[0, 0], w_qkv[0, 1], w_qkv[0, 2], w_o[0].T, w_up[0], w_down[0].T], 1
    )
    section_out, section_in_grad, landed, *_ = layers_call(
        share, clips, cotangent, shard, dims
    )
    grads = jnp.sum(landed.astype(F32), 0)
    rest = lax.axis_index("dp") % share
    side = lax.axis_index("tensor")
    if share > 1:
        group = lax.axis_index("dp") // share
        padded = jnp.zeros((width, END), F32)
        padded = lax.dynamic_update_slice_in_dim(padded, grads, group * rows, 0)
        grads = lax.dynamic_slice_in_dim(lax.psum(padded, "dp"), group * rows, rows, 0)
    mine = own_part(grads, 0, share, share, rest)
    vec = own_part(mine, 0, share, 2, side)
    heads_grad = grads[:, 6].reshape(2, -1, HEAD // GROUPS)
    units_grad = grads[:, 7:9].T.reshape(-1, HEAD // GROUPS)
    qkv_grad = mine[:, QKV:OUT].reshape(mine.shape[0], 3, -1)
    return (
        section_out,
        section_in_grad,
        vec[:, 0:2].T[None],
        vec[:, 2:6].T[None],
        jnp.stack([qkv_grad[:, 0], qkv_grad[:, 1], qkv_grad[:, 2]])[None],
        own_part(heads_grad, 2, share, share, rest)[None],
        mine[:, OUT:UP].T[None],
        mine[:, UP:DOWN][None],
        own_part(units_grad, 1, share, share, rest)[None],
        mine[:, DOWN:END].T[None],
    )


def solution(mesh):
    placed = (
        P("dp", "tensor", None),
        P("dp", "tensor", None),
        P("section", None, "dp"),
        P("section", None, "dp"),
        P("section", None, "dp", "tensor"),
        P("section", None, "tensor", "dp"),
        P("section", "tensor", "dp"),
        P("section", "dp", "tensor"),
        P("section", "tensor", "dp"),
        P("section", "tensor", "dp"),
    )
    share = mesh.shape["dp"] // GROUPS
    return jax.shard_map(
        functools.partial(on_device, share),
        mesh=mesh,
        in_specs=placed,
        out_specs=(
            P("section", "dp", "tensor", None),
            P("section", "dp", "tensor", None),
            P("section", None, ("dp", "tensor")),
            P("section", None, ("dp", "tensor")),
            P("section", None, "dp", "tensor"),
            P("section", None, "tensor", "dp"),
            P("section", "tensor", "dp"),
            P("section", "dp", "tensor"),
            P("section", "tensor", "dp"),
            P("section", "tensor", "dp"),
        ),
        check_vma=False,
    )
```

```python
import functools

import jax
import jax.numpy as jnp
from jax import lax
from jax.experimental import pallas as pl
from jax.experimental.pallas import tpu as pltpu
from jax.sharding import PartitionSpec as P

BF = jnp.bfloat16
F32 = jnp.float32
MESH = pl.DeviceIdType.MESH
EPSILON = 1e-05
HEAD = 64
GROUPS = 8
LINES = 4
BLOCK = 256
VMEM_LIMIT = 62 * 1024 * 1024

VEC = 0
QKV = 128
OUT = 1280
UP = 1664
DOWN = 3200
END = 4736
SPLIT = 64
WIDE = 384
CHUNKS = 12


PARTS = (
    (0, 256, "q", 0),
    (256, 256, "k", 0),
    (512, 256, "v", 384),
    (768, 128, "q", 256),
    (896, 128, "k", 256),
    (1024, 128, "v", 640),
)


def mm(left, right):
    return jnp.dot(left, right, preferred_element_type=F32)


def mmt(left, right):
    return lax.dot_general(left, right, (((1,), (1,)), ((), ())), preferred_element_type=F32)


class Place:
    def __init__(self, share):
        self.s = lax.axis_index("section")
        self.d = lax.axis_index("dp")
        self.t = lax.axis_index("tensor")
        group = self.d // share
        self.rest = self.d - group * share
        self.share = share
        self.e = group // 2
        self.y = group - self.e * 2
        self.primary = self.s == self.t
        self.core = (1 - self.s, self.d, self.t)
        self.across = (self.s, self.d, 1 - self.t)
        self.beside = (self.s, self.row_of(self.e, 1 - self.y), self.t)

    def row_of(self, line, y):
        return (line * 2 + y) * self.share + self.rest

    def line(self, step):
        return lax.rem(self.e + step, LINES)

    def greet(self):
        barrier = pltpu.get_barrier_semaphore()
        peers = [self.core, self.across, self.beside]
        for step in range(1, LINES):
            for section in range(2):
                peers.append((section, self.row_of(self.line(step), self.y), self.t))
        for peer in peers:
            pl.semaphore_signal(barrier, inc=1, device_id=peer, device_id_type=MESH)
        pl.semaphore_wait(barrier, len(peers))


def remote(src, dst, send_sem, recv_sem, device):
    return pltpu.make_async_remote_copy(
        src_ref=src,
        dst_ref=dst,
        send_sem=send_sem,
        recv_sem=recv_sem,
        device_id=device,
        device_id_type=MESH,
    )


def await_bytes(ref, sem):
    pltpu.make_async_copy(ref, ref, sem).wait()


def centre(rows_in):
    mean = jnp.mean(rows_in, 0, keepdims=True)
    centred = rows_in - mean
    variance = jnp.mean(centred * centred, 0, keepdims=True)
    scale = lax.rsqrt(variance + EPSILON)
    return centred * scale, scale


def gelu_parts(values):
    bell = jnp.exp(-0.5 * values * values)
    reach = jnp.abs(values) * 0.7071067811865476
    inv = 1.0 / (1.0 + 0.3275911 * reach)
    poly = inv * (
        0.254829592
        + inv * (-0.284496736 + inv * (1.421413741 + inv * (-1.453152027 + inv * 1.061405429)))
    )
    tail = 0.5 * poly * bell
    cdf = jnp.where(values >= 0.0, 1.0 - tail, tail)
    return values * cdf, cdf + values * bell * 0.3989422804014327


def block_of(index):
    return pl.ds(pl.multiple_of(index * BLOCK, BLOCK), BLOCK)


def flip_weights(w, wt, layer, start, width, target=0):
    def body(index, carry):
        cols = pl.ds(pl.multiple_of(start + index * 128, 128), 128)
        rows = pl.ds(pl.multiple_of(target + index * 128, 128), 128)
        tile = w[layer, :, :, :, cols]
        wt[rows, :] = tile.reshape(tile.shape[0] * tile.shape[1] * tile.shape[2], 128).T
        return carry

    lax.fori_loop(0, width // 128, body, 0)


def whole(w, layer, start, width):
    tile = w[layer, :, :, :, start : start + width]
    return tile.reshape(tile.shape[0] * tile.shape[1] * tile.shape[2], width)


def spread_biases(vecs, spread, rows):
    def body(group, carry):
        source = group * rows
        for kind in range(2):
            for head in range(6):
                to = pl.ds(pl.multiple_of(kind * 384 + head * HEAD + group * 8, 8), 8)
                at = pl.ds(pl.multiple_of(source + kind * 48 + head * 8, 8), 8)
                spread[to, :] = vecs[at, :]
        for unit in range(24):
            to = pl.ds(pl.multiple_of(768 + unit * HEAD + group * 8, 8), 8)
            at = pl.ds(pl.multiple_of(source + (unit % 12) * 8, 8), 8)
            spread[to, :] = vecs[at, :]
        return carry

    lax.fori_loop(0, GROUPS, body, 0)


def layers_kernel(
    share,
    clips,
    cot,
    shard,
    out,
    in_grad,
    landed,
    cot_other,
    x_hbm,
    h_hbm,
    n1_hbm,
    n2_hbm,
    qkv_hbm,
    ctx_hbm,
    lse_hbm,
    act_hbm,
    slope_hbm,
    w,
    res,
    act,
    slope,
    n1,
    n2,
    low,
    qkv,
    ctx,
    dctx,
    lse,
    h_in,
    wt,
    send,
    recv,
    vecs,
    vec_grads,
    sums,
    spread,
    stage,
    land_a,
    land_b,
    land_y,
    z_send,
    z_recv,
    x_send,
    x_recv,
    xb_send,
    xb_recv,
    y_send,
    y_recv,
    ya_send,
    ya_recv,
    gz_send,
    gz_recv,
    gx_send,
    gx_recv,
    gxb_send,
    gxb_recv,
    gy_send,
    gy_recv,
    gya_send,
    gya_recv,
    e_send,
    e_recv,
    in_sem,
    cot_sem,
    out_sem,
    save_sem,
    load_sem,
    h_sem,
    ya_free,
    xb_free,
    x_free,
    y_free,
):
    place = Place(share)
    s, t, e, y = place.s, place.t, place.e, place.y
    primary, secondary = place.primary, jnp.logical_not(place.primary)
    width, frames = res.shape
    blocks = frames // BLOCK
    half = frames // 2
    quarter = half // 2
    rows = w.shape[3]
    low_rows = pl.ds(0, SPLIT)
    high_rows = pl.ds(SPLIT, rows - SPLIT)
    mine = pl.ds(pl.multiple_of(t * half, half), half)
    theirs = pl.ds(pl.multiple_of((1 - t) * half, half), half)

    place.greet()

    def gather_cols(piece):
        if isinstance(piece, int) and piece == 0:
            return pl.ds(VEC, QKV + WIDE)
        return pl.ds(pl.multiple_of(QKV + piece * WIDE, 128), WIDE)

    def z_copies(piece):
        cols = gather_cols(piece)
        copies = []
        for step in range(LINES):
            copies.append(
                remote(
                    shard.at[:, cols],
                    w.at[s, e, y, :, cols],
                    z_send.at[piece, step],
                    z_recv.at[s, piece, e],
                    (t, place.row_of(place.line(step), y), t),
                )
            )
        local = pltpu.make_async_copy(
            shard.at[:, cols], w.at[s, e, y, :, cols], z_recv.at[s, piece, e]
        )
        return copies, local

    def z_start(layer, piece):
        @pl.when(s == layer)
        def _():
            copies, local = z_copies(piece)

            @pl.when(primary)
            def _():
                local.start()

            @pl.when(secondary)
            def _():
                copies[0].start()

            for copy in copies[1:]:
                copy.start()

    def z_finish(piece):
        copies, _ = z_copies(piece)

        @pl.when(secondary)
        def _():
            copies[0].wait_send()

        for copy in copies[1:]:
            copy.wait_send()

    def x_copy(layer, piece):
        part = w.at[layer, :, y, :, gather_cols(piece)]
        return remote(part, part, x_send.at[layer, piece], x_recv.at[layer, piece], place.across)

    def y_copy(layer, piece):
        part = w.at[layer, :, y, :, gather_cols(piece)]
        return remote(part, part, y_send.at[layer, piece], y_recv.at[layer, piece], place.beside)

    def xb_copy(layer, piece):
        part = w.at[layer, :, 1 - y, high_rows, gather_cols(piece)]
        return remote(part, part, xb_send.at[layer, piece], xb_recv.at[layer, piece], place.across)

    def ya_copy(layer, piece):
        part = w.at[layer, :, y, low_rows, gather_cols(piece)]
        return remote(part, part, ya_send.at[layer, piece], ya_recv.at[layer, piece], place.beside)

    def step_z(layer, piece):
        @pl.when(primary)
        def _():
            for line in range(LINES):
                await_bytes(w.at[layer, line, y, :, gather_cols(piece)], z_recv.at[layer, piece, line])
            x_copy(layer, piece).start()
            y_copy(layer, piece).start()

    def step_plane(layer, piece):
        @pl.when(primary)
        def _():
            await_bytes(w.at[layer, :, 1 - y, :, gather_cols(piece)], y_recv.at[layer, piece])
            xb_copy(layer, piece).start()

        @pl.when(secondary)
        def _():
            await_bytes(w.at[layer, :, y, :, gather_cols(piece)], x_recv.at[layer, piece])
            ya_copy(layer, piece).start()

    def complete(layer, *pieces):
        @pl.when(secondary)
        def _():
            for piece in pieces:
                cols = gather_cols(piece)
                await_bytes(w.at[layer, :, 1 - y, high_rows, cols], xb_recv.at[layer, piece])
                await_bytes(w.at[layer, :, 1 - y, low_rows, cols], ya_recv.at[layer, piece])

    kept = {
        "x": (n2, x_hbm),
        "h": (res, h_hbm),
        "n1": (n1, n1_hbm),
        "n2": (n2, n2_hbm),
        "qkv": (qkv, qkv_hbm),
        "ctx": (ctx, ctx_hbm),
        "lse": (lse, lse_hbm),
        "act": (act, act_hbm),
        "slope": (slope, slope_hbm),
    }
    names = tuple(kept)

    def save(name, layer):
        src, dst = kept[name]
        if name in ("x", "h"):
            dst = dst.at[layer]
        return pltpu.make_async_copy(src, dst, save_sem.at[names.index(name), layer])

    def load(name, layer=0):
        dst, src = kept[name]
        if name == "x":
            dst, src = act.at[pl.ds(0, width), :], src.at[layer]
        return pltpu.make_async_copy(src, dst, load_sem.at[names.index(name)])

    def load_h(layer, index):
        slot = lax.rem(index, 2)
        return pltpu.make_async_copy(
            h_hbm.at[layer, :, block_of(index)], h_in.at[slot], h_sem.at[slot]
        )

    my_quarter = pl.ds(s * quarter, quarter)
    my_rows = pl.ds(pl.multiple_of((1 - t) * half + s * quarter, quarter), quarter)

    def clip_across():
        there = pl.ds(pl.multiple_of(t * half + s * quarter, quarter), quarter)
        return remote(
            clips.at[1 - t, my_quarter, :],
            stage.at[there, :],
            in_sem.at[0],
            in_sem.at[1],
            place.across,
        )

    def clip_core():
        part = stage.at[my_rows, :]
        return remote(part, part, in_sem.at[2], in_sem.at[3], place.core)

    def cot_across():
        return remote(
            cot.at[1 - t, my_quarter, :],
            cot_other.at[my_quarter, :],
            cot_sem.at[0],
            cot_sem.at[1],
            place.across,
        )

    def cot_core():
        part = cot_other.at[my_quarter, :]
        return remote(part, part, cot_sem.at[2], cot_sem.at[3], place.core)

    def exchange(kind, index, slot):
        return remote(
            send.at[kind, index],
            recv.at[kind, index],
            e_send.at[slot, index],
            e_recv.at[slot, index],
            place.core,
        )

    def joined(kind, index, slot):
        exchange(kind, index, slot).wait()
        return send[kind, index].astype(F32) + recv[kind, index].astype(F32)

    def result_copies(ref, first):
        local = pltpu.make_async_copy(stage.at[mine, :], ref.at[0, t], out_sem.at[first])
        away = remote(
            stage.at[theirs, :],
            ref.at[0, t],
            out_sem.at[first + 1],
            out_sem.at[first + 2],
            place.across,
        )
        return local, away

    def emit(layer, ref, first):
        @pl.when(s == layer)
        def _():
            for copy in result_copies(ref, first):
                copy.start()

    for piece in range(5):
        z_start(0, piece)
    own_clip = pltpu.make_async_copy(clips.at[t], stage.at[mine, :], in_sem.at[4])
    own_clip.start()
    clip_across().start()
    cot_across().start()

    def take_clip(first):
        def body(index, carry):
            at = pl.ds(pl.multiple_of(first + index * BLOCK, BLOCK), BLOCK)
            tile = stage[at, :].T
            n2[:, at] = tile
            res[:, at] = tile.astype(F32)
            return carry

        lax.fori_loop(0, half // BLOCK, body, 0)

    own_clip.wait()
    take_clip(t * half)
    clip_across().wait()
    clip_core().start()
    step_z(0, 0)
    z_start(0, 5)
    step_z(0, 1)
    z_start(0, 6)
    clip_core().wait()
    take_clip((1 - t) * half)
    save("x", 0).start()
    step_plane(0, 0)
    step_z(0, 2)
    z_start(0, 7)
    step_plane(0, 1)
    cot_across().wait()
    cot_core().start()
    step_z(0, 3)
    z_start(0, 8)
    step_plane(0, 2)

    def project(index, rows_in):
        normed = centre(rows_in)[0] * vecs[:, 0:1] + vecs[:, 2:3]
        normed = normed.astype(BF)
        cols = block_of(index)
        n1[:, cols] = normed
        for first, many, kind, bias in PARTS:
            value = mm(wt[first : first + many, :], normed)
            if kind != "k":
                value = value + spread[bias : bias + many, 6:7]
            if kind == "q":
                value = value * 0.125
            qkv[first : first + many, cols] = value.astype(BF)

    def head_rows(head, first):
        return pl.ds(pl.multiple_of(first + head * HEAD, HEAD), HEAD)

    def attend(layer):
        def heads_of(first_head, base, stride):
            def one_head(index_in, carry):
                head = first_head + index_in
                q_rows = head_rows(index_in, base)
                k_rows = head_rows(index_in, base + stride)
                v_rows = head_rows(index_in, base + 2 * stride)
                c_rows = head_rows(head, 0)
                keys = qkv[k_rows, :].T
                for index in range(blocks):
                    cols = slice(index * BLOCK, (index + 1) * BLOCK)
                    queries = qkv[q_rows, cols]
                    tiles = []
                    top = None
                    for tile in range(blocks):
                        scores = mm(keys[tile * BLOCK : (tile + 1) * BLOCK, :], queries)
                        peak = jnp.max(scores, 0, keepdims=True)
                        top = peak if top is None else jnp.maximum(top, peak)
                        tiles.append(scores)
                    total = jnp.zeros_like(top)
                    mixed = jnp.zeros((HEAD, BLOCK), F32)
                    for tile in range(blocks):
                        soft = jnp.exp(tiles[tile] - top)
                        total = total + jnp.sum(soft, 0, keepdims=True)
                        span = slice(tile * BLOCK, (tile + 1) * BLOCK)
                        mixed = mixed + mm(qkv[v_rows, span], soft.astype(BF))
                    ctx[c_rows, cols] = (mixed / total).astype(BF)
                    lse[pl.ds(head, 1), cols] = top + jnp.log(total)
                step_z(layer, 5 + head)
                step_plane(layer, 4 + head)
                return carry

            return one_head

        lax.fori_loop(0, 4, heads_of(0, 0, 256), 0)
        lax.fori_loop(0, 2, heads_of(4, 768, 128), 0)

    def out_project(layer):
        def body(index, carry):
            part = mm(whole(w, layer, OUT, 384), ctx[:, block_of(index)])
            send[0, index] = part.astype(BF)
            exchange(0, index, 2 * layer).start()
            return carry

        lax.fori_loop(0, blocks, body, 0)

    def middle_norm(layer):
        def body(index, carry):
            cols = block_of(index)
            rows_in = res[:, cols] + joined(0, index, 2 * layer) + vecs[:, 3:4]
            res[:, cols] = rows_in
            n2[:, cols] = (centre(rows_in)[0] * vecs[:, 1:2] + vecs[:, 4:5]).astype(BF)
            return carry

        lax.fori_loop(0, blocks, body, 0)

    def hidden_part(layer, part):
        flip_weights(w, wt, layer, UP + part * WIDE, WIDE, part * WIDE)
        units = slice(part * WIDE, (part + 1) * WIDE)
        lane = 7 if part < 2 else 8

        def body(index, carry):
            cols = block_of(index)
            pre = mm(wt[units, :], n2[:, cols])
            pre = pre + spread[768 + part * WIDE : 768 + (part + 1) * WIDE, lane : lane + 1]
            value, steep = gelu_parts(pre)
            act[units, cols] = value.astype(BF)
            slope[units, cols] = steep.astype(BF)
            return carry

        lax.fori_loop(0, blocks, body, 0)

    def down_project(layer):
        def body(index, carry):
            part = mm(whole(w, layer, DOWN, 1536), act[:, block_of(index)])
            send[1, index] = part.astype(BF)
            exchange(1, index, 2 * layer + 1).start()
            return carry

        lax.fori_loop(0, blocks, body, 0)

    def layer_end(layer, index):
        total = res[:, block_of(index)] + joined(1, index, 2 * layer + 1) + vecs[:, 5:6]
        return total.astype(BF)

    def take_vectors(layer):
        vecs[...] = whole(w, layer, VEC, 128).astype(F32)
        spread_biases(vecs, spread, rows)

    def project_all(layer):
        flip_weights(w, wt, layer, QKV, 1152)

        def body(index, carry):
            project(index, res[:, block_of(index)])
            return carry

        lax.fori_loop(0, blocks, body, 0)
        if layer == 0:
            save("n1", 0).start()
            save("qkv", 0).start()

    complete(0, 0, 1, 2)
    take_vectors(0)
    project_all(0)
    step_z(0, 4)
    step_plane(0, 3)
    for piece in (9, 10, 11):
        z_start(0, piece)
    cot_core().wait()
    load_cot = pltpu.make_async_copy(cot_other, stage.at[theirs, :], cot_sem.at[4])
    load_cot.start()
    own_cot = pltpu.make_async_copy(cot.at[t], stage.at[mine, :], cot_sem.at[5])
    own_cot.start()
    attend(0)
    save("ctx", 0).start()
    save("lse", 0).start()
    complete(0, 3)
    out_project(0)
    step_z(0, 11)
    step_plane(0, 10)
    for piece in (0, 1, 2):
        z_start(1, piece)
    load_cot.wait()
    own_cot.wait()

    def take_cot(index, carry):
        low[:, block_of(index)] = stage[block_of(index), :].T
        return carry

    lax.fori_loop(0, blocks, take_cot, 0)
    save("x", 0).wait()
    middle_norm(0)
    save("h", 0).start()
    save("n2", 0).start()
    for part in range(4):
        complete(0, 4 + part)
        hidden_part(0, part)
        step_z(1, part)
        if part == 0:
            step_plane(0, 11)
        else:
            step_plane(1, part - 1)
        z_start(1, part + 3)
    save("act", 0).start()
    save("slope", 0).start()
    complete(0, 8, 9, 10, 11)
    down_project(0)
    step_z(1, 4)
    step_plane(1, 3)
    z_start(1, 7)
    z_start(1, 8)
    for name in ("n1", "qkv", "h", "n2"):
        save(name, 0).wait()

    def finish_body(index, carry):
        rows_out = layer_end(0, index)
        cols = block_of(index)
        n2[:, cols] = rows_out
        res[:, cols] = rows_out.astype(F32)

        @pl.when(s == 0)
        def _():
            stage[cols, :] = rows_out.T

        return carry

    lax.fori_loop(0, blocks, finish_body, 0)
    emit(0, out, 0)
    save("x", 1).start()
    complete(1, 0, 1, 2)
    take_vectors(1)
    project_all(1)
    for piece in (9, 10, 11):
        z_start(1, piece)
    save("ctx", 0).wait()
    save("lse", 0).wait()
    attend(1)
    complete(1, 3)
    out_project(1)
    step_z(1, 11)
    step_plane(1, 10)
    save("x", 1).wait()
    middle_norm(1)
    save("h", 1).start()
    save("act", 0).wait()
    save("slope", 0).wait()
    for part in range(4):
        complete(1, 4 + part)
        hidden_part(1, part)
        if part == 0:
            step_plane(1, 11)
    complete(1, 8, 9, 10, 11)
    down_project(1)
    flip_weights(w, wt, 1, DOWN, 1536)

    def last_body(index, carry):
        rows_out = layer_end(1, index)

        @pl.when(s == 1)
        def _():
            stage[block_of(index), :] = rows_out.T

        return carry

    lax.fori_loop(0, blocks, last_body, 0)
    emit(1, out, 0)
    save("h", 1).wait()

    VECTORS = CHUNKS

    def grad_cols(piece):
        if isinstance(piece, int) and piece == VECTORS:
            return pl.ds(VEC, QKV)
        return pl.ds(pl.multiple_of(QKV + piece * WIDE, 128), WIDE)

    def gya_copy(layer, piece):
        cols = grad_cols(piece)
        return remote(
            w.at[layer, :, 1 - y, low_rows, cols],
            land_a.at[:, low_rows, cols],
            gya_send.at[layer, piece],
            gya_recv.at[layer, piece],
            place.beside,
        )

    def gxb_copy(layer, piece):
        cols = grad_cols(piece)
        return remote(
            w.at[layer, :, 1 - y, high_rows, cols],
            land_b.at[:, :, cols],
            gxb_send.at[layer, piece],
            gxb_recv.at[layer, piece],
            place.across,
        )

    def gx_copy(layer, piece):
        cols = grad_cols(piece)
        return remote(
            w.at[layer, :, y, :, cols],
            land_a.at[:, :, cols],
            gx_send.at[layer, piece],
            gx_recv.at[layer, piece],
            place.across,
        )

    def gy_copy(layer, piece):
        cols = grad_cols(piece)
        return remote(
            w.at[layer, :, 1 - y, :, cols],
            land_y.at[:, :, cols],
            gy_send.at[layer, piece],
            gy_recv.at[layer, piece],
            place.beside,
        )

    def gz_copies(layer, piece):
        cols = grad_cols(piece)
        copies = []
        for step in range(LINES):
            line = place.line(step)
            copies.append(
                remote(
                    w.at[layer, line, y, :, cols],
                    landed.at[e, :, cols],
                    gz_send.at[layer, piece, step],
                    gz_recv.at[piece, e],
                    (layer, place.row_of(line, y), t),
                )
            )
        local = pltpu.make_async_copy(
            w.at[layer, e, y, :, cols], landed.at[e, :, cols], gz_recv.at[piece, e]
        )
        return copies, local

    def add_rows(layer, piece, which, span, lands):
        cols = grad_cols(piece)
        first, count = span
        for line in range(LINES):
            total = w[layer, line, which, pl.ds(first, count), cols].astype(F32)
            for land, offset in lands:
                total = total + land[line, pl.ds(offset, count), cols].astype(F32)
            w[layer, line, which, pl.ds(first, count), cols] = total.astype(BF)

    def signal(sem, layer, piece, device):
        if layer == 1:
            pl.semaphore_signal(sem.at[piece], inc=1, device_id=device, device_id_type=MESH)

    def credit(sem, layer, piece):
        if layer == 0:
            pl.semaphore_wait(sem.at[piece], 1)

    def step_a(layer, piece):
        @pl.when(secondary)
        def _():
            credit(ya_free, layer, piece)
            gya_copy(layer, piece).start()
            credit(xb_free, layer, piece)
            gxb_copy(layer, piece).start()

    def step_b(layer, piece):
        cols = grad_cols(piece)

        @pl.when(secondary)
        def _():
            await_bytes(land_a.at[:, low_rows, cols], gya_recv.at[layer, piece])
            add_rows(layer, piece, y, (0, SPLIT), [(land_a, 0)])
            signal(ya_free, layer, piece, place.beside)
            credit(x_free, layer, piece)
            gx_copy(layer, piece).start()

        @pl.when(primary)
        def _():
            await_bytes(land_b.at[:, :, cols], gxb_recv.at[layer, piece])
            add_rows(layer, piece, 1 - y, (SPLIT, rows - SPLIT), [(land_b, 0)])
            signal(xb_free, layer, piece, place.across)
            credit(y_free, layer, piece)
            gy_copy(layer, piece).start()

    def step_c(layer, piece):
        cols = grad_cols(piece)

        @pl.when(primary)
        def _():
            await_bytes(land_a.at[:, :, cols], gx_recv.at[layer, piece])
            await_bytes(land_y.at[:, :, cols], gy_recv.at[layer, piece])
            add_rows(layer, piece, y, (0, rows), [(land_a, 0), (land_y, 0)])
            signal(x_free, layer, piece, place.across)
            signal(y_free, layer, piece, place.beside)
            copies, local = gz_copies(layer, piece)

            @pl.when(s == layer)
            def _():
                local.start()

            @pl.when(s != layer)
            def _():
                copies[0].start()

            for copy in copies[1:]:
                copy.start()

    def store_grads(layer, start, count, value):
        w[layer, :, :, :, pl.ds(start, count)] = value.astype(BF).reshape(
            w.shape[1], w.shape[2], rows, count
        )

    ones = functools.partial(jnp.ones, (frames, 128), BF)

    def mlp_back(layer, beside):
        def body(index, carry):
            cols = block_of(index)
            for part in range(4):
                units = slice(part * WIDE, (part + 1) * WIDE)
                steep = slope[units, cols].astype(F32)
                slope[units, cols] = (mm(wt[units, :], low[:, cols]) * steep).astype(BF)
            term = mm(whole(w, layer, UP, 1536), slope[:, cols])
            send[0, index] = term.astype(BF)
            exchange(0, index, 4 + 2 * layer).start()
            beside(index)
            return carry

        lax.fori_loop(0, blocks, body, 0)

    def outer_pair(layer, start, left, right, first, beside):
        def body(index, carry):
            for part in range(3):
                base = index * 768 + part * 256
                span = pl.ds(pl.multiple_of(base, 256), 256)
                value = mmt(left[...], right[span, :])
                store_grads(layer, pl.multiple_of(start + base, 128), 256, value)
            step_a(layer, first + 2 * index)
            step_a(layer, first + 2 * index + 1)
            beside(index)
            return carry

        lax.fori_loop(0, 2, body, 0)

    def fold(value):
        return value[:, 0:128] + value[:, 128:256]

    def norm_back(layer, kind, gain_lane, source, finish, beside):
        sums[...] = jnp.zeros_like(sums)

        def body(index, carry):
            cols = block_of(index)
            rows_in = source(index)
            hat, scale = centre(rows_in)
            grad = joined(kind, index, 4 + 2 * layer + kind)
            sums[0] += fold(grad * hat)
            sums[1] += fold(grad)
            scaled = grad * vecs[:, gain_lane : gain_lane + 1]
            mean = jnp.mean(scaled, 0, keepdims=True)
            slant = jnp.mean(scaled * hat, 0, keepdims=True)
            finish(index, res[:, cols] + scale * (scaled - mean - hat * slant))
            beside(index)
            return carry

        lax.fori_loop(0, blocks, body, 0)

    def row_sums(value):
        return jnp.sum(value, 1, keepdims=True)

    def attend_back(first_head, many, base, stride, beside):
        def one_head(index_in, carry):
            head = first_head + index_in
            q_rows = head_rows(index_in, base)
            k_rows = head_rows(index_in, base + stride)
            v_rows = head_rows(index_in, base + 2 * stride)
            c_rows = head_rows(head, 0)
            keys = qkv[k_rows, :].T
            values = qkv[v_rows, :].T
            key_totals = [jnp.zeros((HEAD, BLOCK), F32)] * blocks
            value_totals = [jnp.zeros((HEAD, BLOCK), F32)] * blocks
            for index in range(blocks):
                cols = slice(index * BLOCK, (index + 1) * BLOCK)
                queries = qkv[q_rows, cols]
                grads = dctx[c_rows, cols]
                level = lse[pl.ds(head, 1), cols]
                inner = jnp.sum(
                    grads.astype(F32) * ctx[c_rows, cols].astype(F32), 0, keepdims=True
                )
                step = jnp.zeros((HEAD, BLOCK), F32)
                for tile in range(blocks):
                    span = slice(tile * BLOCK, (tile + 1) * BLOCK)
                    soft = jnp.exp(mm(keys[span, :], queries) - level)
                    soft_grad = mm(values[span, :], grads)
                    score_grad = (soft * (soft_grad - inner)).astype(BF)
                    step = step + mm(qkv[k_rows, span], score_grad)
                    key_totals[tile] = key_totals[tile] + mmt(queries, score_grad)
                    value_totals[tile] = value_totals[tile] + mmt(grads, soft.astype(BF))
                slope[q_rows, cols] = (step * 0.125).astype(BF)
            for tile in range(blocks):
                span = slice(tile * BLOCK, (tile + 1) * BLOCK)
                slope[k_rows, span] = key_totals[tile].astype(BF)
                slope[v_rows, span] = value_totals[tile].astype(BF)
            beside(index_in)
            return carry

        lax.fori_loop(0, many, one_head, 0)

    def collect_biases():
        def body(group, carry):
            source = group * rows
            for kind in range(2):
                for head in range(6):
                    at = pl.ds(pl.multiple_of(kind * 384 + head * HEAD + group * 8, 8), 8)
                    to = pl.ds(pl.multiple_of(source + kind * 48 + head * 8, 8), 8)
                    vec_grads[to, 6:7] = spread[at, 6:7]
            for unit in range(24):
                at = pl.ds(pl.multiple_of(768 + unit * HEAD + group * 8, 8), 8)
                to = pl.ds(pl.multiple_of(source + (unit % 12) * 8, 8), 8)
                lane = 7 if unit < 12 else 8
                vec_grads[to, lane : lane + 1] = spread[at, lane : lane + 1]
            return carry

        lax.fori_loop(0, GROUPS, body, 0)

    def nothing(index):
        del index

    def at_turns(turns):
        def beside(index):
            for turn, steps in turns.items():

                @pl.when(index == turn)
                def _():
                    for step in steps:
                        step()

        return beside

    def finish_gather(piece):
        z_finish(piece)
        for layer in range(2):

            @pl.when(primary)
            def _():
                x_copy(layer, piece).wait_send()
                y_copy(layer, piece).wait_send()
                xb_copy(layer, piece).wait_send()

            @pl.when(secondary)
            def _():
                ya_copy(layer, piece).wait_send()

    def finish_body_gather(piece, carry):
        finish_gather(piece)
        return carry

    res[...] = low[...].astype(F32)

    for layer in (1, 0):
        later = layer == 0
        load_h(layer, 0).start()
        if later:
            vecs[...] = whole(w, layer, VEC, 128).astype(F32)
            flip_weights(w, wt, layer, DOWN, 1536)
            load("slope").wait()
        vec_grads[...] = jnp.zeros_like(vec_grads)

        early = at_turns({0: (lambda: step_b(1, VECTORS),), 1: (lambda: step_c(1, VECTORS),)})
        mlp_back(layer, early if later else nothing)
        if not later:
            finish_gather(0)
            lax.fori_loop(1, CHUNKS, finish_body_gather, 0)
        if later:
            load("act").wait()
        outer_pair(layer, DOWN, low, act, 8, nothing)
        load("x", layer).start()
        if later:
            load("n2").wait()
        vec_grads[:, 5:6] = mm(low[...], ones())[:, 0:1]

        def b(piece, layer=layer):
            return lambda: step_b(layer, piece)

        def c(piece, layer=layer):
            return lambda: step_c(layer, piece)

        outer_pair(layer, UP, n2, slope, 4, at_turns({1: (b(8), b(9))}))
        spread[768:, :] = mm(slope[...], ones())
        flip_weights(w, wt, layer, OUT, 384)

        def hidden_in(index, layer=layer):
            @pl.when(index + 1 < blocks)
            def _():
                load_h(layer, index + 1).start()

            load_h(layer, index).wait()
            return h_in[lax.rem(index, 2)]

        def hidden_out(index, total):
            cols = block_of(index)
            res[:, cols] = total
            rounded = total.astype(BF)
            low[:, cols] = rounded
            dctx[:, cols] = mm(wt[0:384, :], rounded).astype(BF)

        drain = at_turns({0: (b(10),), 1: (b(11),), 2: (b(4), c(8)), 3: (b(5), c(9))})
        norm_back(layer, 0, 1, hidden_in, hidden_out, drain)
        vec_grads[:, 1:2] = row_sums(sums[0])
        vec_grads[:, 4:5] = row_sums(sums[1])
        vec_grads[:, 3:4] = mm(low[...], ones())[:, 0:1]
        if later:
            for name in ("ctx", "qkv", "lse"):
                load(name).wait()
        store_grads(layer, OUT, 384, mmt(low[...], ctx[...]))
        step_a(layer, 3)
        step_b(layer, 6)
        step_c(layer, 10)
        drain = at_turns({0: (b(7), c(11)), 1: (b(3), c(4)), 2: (c(5),), 3: (c(6),)})
        attend_back(0, 4, 0, 256, drain)
        if later:
            load("n1").wait()
        wt[0:768, :] = whole(w, layer, QKV, 768)

        def qkv_body(index, carry, layer=layer):
            span = pl.ds(pl.multiple_of(index * 256, 256), 256)
            value = mmt(n1[...], slope[span, :])
            store_grads(layer, pl.multiple_of(QKV + index * 256, 128), 256, value)
            return carry

        lax.fori_loop(0, 3, qkv_body, 0)
        step_a(layer, 0)
        step_a(layer, 1)
        step_c(layer, 7)
        attend_back(4, 2, 768, 128, at_turns({0: (b(0), c(3)), 1: (b(1),)}))

        def first_body(index, carry, layer=layer):
            cols = block_of(index)
            term = mm(wt[0:768, :], slope[0:768, cols])
            term = term + mm(whole(w, layer, QKV + 768, WIDE), slope[768:1152, cols])
            send[1, index] = term.astype(BF)
            exchange(1, index, 5 + 2 * layer).start()
            return carry

        lax.fori_loop(0, blocks, first_body, 0)
        store_grads(layer, QKV + 768, WIDE, mmt(n1[...], slope[768:1152, :]))
        step_a(layer, 2)
        step_c(layer, 0)
        for first, many, kind, bias in PARTS:
            if kind != "k":
                spread[bias : bias + many, :] = mm(slope[first : first + many, :], ones())
        collect_biases()
        if layer == 1:
            for name in ("slope", "n1", "n2", "ctx", "qkv", "lse"):
                load(name).start()
        load("x", layer).wait()

        @pl.when(s == layer)
        def _():
            local, away = result_copies(out, 0)
            local.wait()
            away.wait_send()

        def rows_x(index):
            return act[0:width, block_of(index)].astype(F32)

        def rows_dx(index, total, layer=layer):
            cols = block_of(index)
            rounded = total.astype(BF)
            if layer == 1:
                low[:, cols] = rounded
                res[:, cols] = rounded.astype(F32)

            @pl.when(s == layer)
            def _():
                stage[cols, :] = rounded.T

        drain = at_turns({0: (c(1),), 1: (b(2),), 3: (c(2),)})
        norm_back(layer, 1, 0, rows_x, rows_dx, drain)
        emit(layer, in_grad, 3)
        if layer == 1:
            load("act").start()
        vec_grads[:, 0:1] = row_sums(sums[0])
        vec_grads[:, 2:3] = row_sums(sums[1])
        store_grads(layer, VEC, 128, vec_grads[...])
        step_a(layer, VECTORS)

    step_b(0, VECTORS)
    step_c(0, VECTORS)

    def finish_scatter(piece):
        for layer in range(2):

            @pl.when(secondary)
            def _():
                gya_copy(layer, piece).wait_send()
                gxb_copy(layer, piece).wait_send()
                gx_copy(layer, piece).wait_send()

            @pl.when(primary)
            def _():
                gy_copy(layer, piece).wait_send()
                copies, _ = gz_copies(layer, piece)

                @pl.when(s != layer)
                def _():
                    copies[0].wait_send()

                for copy in copies[1:]:
                    copy.wait_send()

    def await_landed(piece):
        for line in range(LINES):
            await_bytes(landed.at[line, :, grad_cols(piece)], gz_recv.at[piece, line])

    def finish_body_all(piece, carry):
        finish_scatter(piece)
        await_landed(piece)
        return carry

    finish_scatter(0)
    await_landed(0)
    lax.fori_loop(1, CHUNKS, finish_body_all, 0)
    finish_scatter(VECTORS)
    await_landed(VECTORS)

    _, away = result_copies(out, 0)
    away.wait_recv()
    local, away = result_copies(in_grad, 3)
    local.wait()
    away.wait()


def layers_call(share, clips, cotangent, shard, dims):
    width, frames, hidden_units, heads_width = dims
    rows = shard.shape[0]
    sem = pltpu.SemaphoreType.DMA
    free = pltpu.SemaphoreType.REGULAR
    packed = (2, LINES, 2, rows, END)
    blocks = frames // BLOCK
    shape = jax.ShapeDtypeStruct
    outs = [
        shape((1,) + clips.shape, BF),
        shape((1,) + clips.shape, BF),
        shape((LINES, rows, END), BF),
        shape(clips.shape[1:], BF),
        shape((2, width, frames), BF),
        shape((2, width, frames), F32),
        shape((width, frames), BF),
        shape((width, frames), BF),
        shape((3 * heads_width, frames), BF),
        shape((heads_width, frames), BF),
        shape((8, frames), F32),
        shape((hidden_units, frames), BF),
        shape((hidden_units, frames), BF),
    ]
    scratch = [
        pltpu.VMEM(packed, BF),
        pltpu.VMEM((width, frames), F32),
        pltpu.VMEM((hidden_units, frames), BF),
        pltpu.VMEM((hidden_units, frames), BF),
        pltpu.VMEM((width, frames), BF),
        pltpu.VMEM((width, frames), BF),
        pltpu.VMEM((width, frames), BF),
        pltpu.VMEM((3 * heads_width, frames), BF),
        pltpu.VMEM((heads_width, frames), BF),
        pltpu.VMEM((heads_width, frames), BF),
        pltpu.VMEM((8, frames), F32),
        pltpu.VMEM((2, width, BLOCK), F32),
        pltpu.VMEM((hidden_units, width), BF),
        pltpu.VMEM((2, blocks, width, BLOCK), BF),
        pltpu.VMEM((2, blocks, width, BLOCK), BF),
        pltpu.VMEM((width, 128), F32),
        pltpu.VMEM((width, 128), F32),
        pltpu.VMEM((2, width, 128), F32),
        pltpu.VMEM((2 * heads_width + hidden_units, 128), F32),
        pltpu.VMEM((frames, width), BF),
        pltpu.VMEM((LINES, rows, END), BF),
        pltpu.VMEM((LINES, rows - SPLIT, END), BF),
        pltpu.VMEM((LINES, rows, END), BF),
    ]
    scratch += [sem((CHUNKS, LINES)), sem((2, CHUNKS, LINES))]
    scratch += [sem((2, CHUNKS))] * 8
    scratch += [sem((2, CHUNKS + 1, LINES)), sem((CHUNKS + 1, LINES))]
    scratch += [sem((2, CHUNKS + 1))] * 8
    scratch += [
        sem((8, blocks)),
        sem((8, blocks)),
        sem((5,)),
        sem((6,)),
        sem((6,)),
        sem((9, 2)),
        sem((9,)),
        sem((2,)),
    ]
    scratch += [free((CHUNKS + 1,))] * 4
    anywhere = pl.BlockSpec(memory_space=pl.ANY)
    return pl.pallas_call(
        functools.partial(layers_kernel, share),
        out_shape=outs,
        in_specs=[anywhere] * 3,
        out_specs=[anywhere] * len(outs),
        scratch_shapes=scratch,
        compiler_params=pltpu.CompilerParams(
            collective_id=0, has_side_effects=True, vmem_limit_bytes=VMEM_LIMIT
        ),
        cost_estimate=pl.CostEstimate(
            flops=60_000_000_000, bytes_accessed=60_000_000, transcendentals=0
        ),
    )(clips, cotangent, shard)


def group_piece(value, axis, share):
    if share == 1:
        return value
    size = value.shape[axis] * share
    group = lax.axis_index("dp") // share
    full = lax.all_gather(value, "dp", axis=axis, tiled=True)
    return lax.dynamic_slice_in_dim(full, group * size, size, axis)


def own_part(value, axis, share, parts, index):
    size = value.shape[axis] // parts
    if parts == 1:
        return value
    return lax.dynamic_slice_in_dim(value, index * size, size, axis)


def on_device(share, clips, cotangent, ln_gains, row_biases, w_qkv, b_qv, w_o, w_up, b_ff, w_down):
    width = clips.shape[2]
    rows = width // GROUPS
    dims = (width, 2 * clips.shape[1], w_up.shape[2], w_o.shape[1])
    ln_gains = group_piece(ln_gains, 2, share)
    row_biases = group_piece(row_biases, 2, share)
    w_qkv = group_piece(w_qkv, 2, share)
    b_qv = group_piece(b_qv, 3, share)
    w_o = group_piece(w_o, 2, share)
    w_up = group_piece(w_up, 1, share)
    b_ff = group_piece(b_ff, 2, share)
    w_down = group_piece(w_down, 2, share)
    vectors = jnp.concatenate([ln_gains[0], row_biases[0]], 0).T
    heads = jnp.concatenate([b_qv[0, 0].reshape(-1), b_qv[0, 1].reshape(-1)])[:, None]
    units = b_ff[0].reshape(2, rows).T
    packed = jnp.concatenate([vectors, heads, units], 1)
    packed = jnp.pad(packed, ((0, 0), (0, 128 - packed.shape[1])))
    shard = jnp.concatenate(
        [packed]
        + [w_qkv[0, "qkv".index(kind), :, bias % 384 : bias % 384 + many] for _, many, kind, bias in PARTS]
        + [w_o[0].T, w_up[0], w_down[0].T],
        1,
    )
    section_out, section_in_grad, landed, *_ = layers_call(
        share, clips, cotangent, shard, dims
    )
    grads = jnp.sum(landed.astype(F32), 0)
    rest = lax.axis_index("dp") % share
    side = lax.axis_index("tensor")
    if share > 1:
        group = lax.axis_index("dp") // share
        padded = jnp.zeros((width, END), F32)
        padded = lax.dynamic_update_slice_in_dim(padded, grads, group * rows, 0)
        grads = lax.dynamic_slice_in_dim(lax.psum(padded, "dp"), group * rows, rows, 0)
    mine = own_part(grads, 0, share, share, rest)
    vec = own_part(mine, 0, share, 2, side)
    heads_grad = grads[:, 6].reshape(2, -1, HEAD // GROUPS)
    units_grad = grads[:, 7:9].T.reshape(-1, HEAD // GROUPS)
    qkv_grad = {"q": [], "k": [], "v": []}
    for first, many, kind, _ in PARTS:
        qkv_grad[kind].append(mine[:, QKV + first : QKV + first + many])
    return (
        section_out,
        section_in_grad,
        vec[:, 0:2].T[None],
        vec[:, 2:6].T[None],
        jnp.stack([jnp.concatenate(qkv_grad[kind], 1) for kind in "qkv"])[None],
        own_part(heads_grad, 2, share, share, rest)[None],
        mine[:, OUT:UP].T[None],
        mine[:, UP:DOWN][None],
        own_part(units_grad, 1, share, share, rest)[None],
        mine[:, DOWN:END].T[None],
    )


def solution(mesh):
    placed = (
        P("dp", "tensor", None),
        P("dp", "tensor", None),
        P("section", None, "dp"),
        P("section", None, "dp"),
        P("section", None, "dp", "tensor"),
        P("section", None, "tensor", "dp"),
        P("section", "tensor", "dp"),
        P("section", "dp", "tensor"),
        P("section", "tensor", "dp"),
        P("section", "tensor", "dp"),
    )
    share = mesh.shape["dp"] // GROUPS
    return jax.shard_map(
        functools.partial(on_device, share),
        mesh=mesh,
        in_specs=placed,
        out_specs=(
            P("section", "dp", "tensor", None),
            P("section", "dp", "tensor", None),
            P("section", None, ("dp", "tensor")),
            P("section", None, ("dp", "tensor")),
            P("section", None, "dp", "tensor"),
            P("section", None, "tensor", "dp"),
            P("section", "tensor", "dp"),
            P("section", "dp", "tensor"),
            P("section", "tensor", "dp"),
            P("section", "tensor", "dp"),
        ),
        check_vma=False,
    )
```

```python
import functools

import jax
import jax.numpy as jnp
from jax import lax
from jax.experimental import pallas as pl
from jax.experimental.pallas import tpu as pltpu
from jax.sharding import PartitionSpec as P

BF = jnp.bfloat16
F32 = jnp.float32
MESH = pl.DeviceIdType.MESH
EPSILON = 1e-05
HEAD = 64
GROUPS = 8
LINES = 4
BLOCK = 256
ROWS = 64
VMEM_LIMIT = 62 * 1024 * 1024

VEC = 0
QKV = 128
OUT = 1280
UP = 1664
DOWN = 3200
END = 4736
SPLIT = 64
WIDE = 384
CHUNKS = 12


PARTS = (
    (0, 256, "q", 0),
    (256, 256, "k", 0),
    (512, 256, "v", 384),
    (768, 128, "q", 256),
    (896, 128, "k", 256),
    (1024, 128, "v", 640),
)


def mm(left, right):
    return jnp.dot(left, right, preferred_element_type=F32)


def mmt(left, right):
    return lax.dot_general(left, right, (((1,), (1,)), ((), ())), preferred_element_type=F32)


class Place:
    def __init__(self, share):
        self.s = lax.axis_index("section")
        self.d = lax.axis_index("dp")
        self.t = lax.axis_index("tensor")
        group = self.d // share
        self.rest = self.d - group * share
        self.share = share
        self.e = group // 2
        self.y = group - self.e * 2
        self.primary = self.s == self.t
        self.core = (1 - self.s, self.d, self.t)
        self.across = (self.s, self.d, 1 - self.t)
        self.beside = (self.s, self.row_of(self.e, 1 - self.y), self.t)

    def row_of(self, line, y):
        return (line * 2 + y) * self.share + self.rest

    def line(self, step):
        return lax.rem(self.e + step, LINES)

    def greet(self):
        barrier = pltpu.get_barrier_semaphore()
        peers = [self.core, self.across, self.beside]
        for step in range(1, LINES):
            for section in range(2):
                peers.append((section, self.row_of(self.line(step), self.y), self.t))
        for peer in peers:
            pl.semaphore_signal(barrier, inc=1, device_id=peer, device_id_type=MESH)
        pl.semaphore_wait(barrier, len(peers))


def remote(src, dst, send_sem, recv_sem, device):
    return pltpu.make_async_remote_copy(
        src_ref=src,
        dst_ref=dst,
        send_sem=send_sem,
        recv_sem=recv_sem,
        device_id=device,
        device_id_type=MESH,
    )


def await_bytes(ref, sem):
    pltpu.make_async_copy(ref, ref, sem).wait()


def chunks_of(count, size=ROWS):
    return [slice(first, first + size) for first in range(0, count, size)]


def by_eights(value):
    return value.reshape(value.shape[0] // 8, 8, value.shape[1])


def stack_sum(value):
    return jnp.sum(by_eights(value), 0)


def stack_max(value):
    return jnp.max(by_eights(value), 0)


def mean_of(parts, count):
    return jnp.sum(parts, 0, keepdims=True) / count


def norm_stats(read, count):
    total = jnp.zeros((8, BLOCK), F32)
    for span in chunks_of(count):
        total = total + stack_sum(read(span))
    mean = mean_of(total, count)
    square = jnp.zeros((8, BLOCK), F32)
    for span in chunks_of(count):
        centred = read(span) - mean
        square = square + stack_sum(centred * centred)
    return mean, lax.rsqrt(mean_of(square, count) + EPSILON)


def gelu_parts(values):
    bell = jnp.exp(-0.5 * values * values)
    reach = jnp.abs(values) * 0.7071067811865476
    inv = 1.0 / (1.0 + 0.3275911 * reach)
    poly = inv * (
        0.254829592
        + inv * (-0.284496736 + inv * (1.421413741 + inv * (-1.453152027 + inv * 1.061405429)))
    )
    tail = 0.5 * poly * bell
    cdf = jnp.where(values >= 0.0, 1.0 - tail, tail)
    return values * cdf, cdf + values * bell * 0.3989422804014327


def block_of(index):
    return pl.ds(pl.multiple_of(index * BLOCK, BLOCK), BLOCK)


def flip_weights(w, wt, layer, start, width, target=0):
    def body(index, carry):
        cols = pl.ds(pl.multiple_of(start + index * 128, 128), 128)
        rows = pl.ds(pl.multiple_of(target + index * 128, 128), 128)
        tile = w[layer, :, :, :, cols]
        wt[rows, :] = tile.reshape(tile.shape[0] * tile.shape[1] * tile.shape[2], 128).T
        return carry

    lax.fori_loop(0, width // 128, body, 0)


def whole(w, layer, start, width):
    tile = w[layer, :, :, :, start : start + width]
    return tile.reshape(tile.shape[0] * tile.shape[1] * tile.shape[2], width)


def spread_biases(vecs, spread, rows):
    def body(group, carry):
        source = group * rows
        for kind in range(2):
            for head in range(6):
                to = pl.ds(pl.multiple_of(kind * 384 + head * HEAD + group * 8, 8), 8)
                at = pl.ds(pl.multiple_of(source + kind * 48 + head * 8, 8), 8)
                spread[to, :] = vecs[at, :]
        for unit in range(24):
            to = pl.ds(pl.multiple_of(768 + unit * HEAD + group * 8, 8), 8)
            at = pl.ds(pl.multiple_of(source + (unit % 12) * 8, 8), 8)
            spread[to, :] = vecs[at, :]
        return carry

    lax.fori_loop(0, GROUPS, body, 0)


def layers_kernel(
    share,
    clips,
    cot,
    vec_in,
    qkv_in,
    out_in,
    up_in,
    down_in,
    out,
    in_grad,
    landed_vec,
    landed_qkv,
    landed_out,
    landed_up,
    landed_down,
    cot_other,
    x_hbm,
    h_hbm,
    n1_hbm,
    n2_hbm,
    qkv_hbm,
    ctx_hbm,
    lse_hbm,
    act_hbm,
    slope_hbm,
    w,
    res,
    act,
    slope,
    n1,
    n2,
    low,
    qkv,
    ctx,
    dctx,
    lse,
    h_in,
    wt,
    send,
    recv,
    vecs,
    vec_grads,
    sums,
    spread,
    stage,
    shard,
    flat,
    land_a,
    land_b,
    land_y,
    z_send,
    z_recv,
    x_send,
    x_recv,
    xb_send,
    xb_recv,
    y_send,
    y_recv,
    ya_send,
    ya_recv,
    gz_send,
    gz_recv,
    gx_send,
    gx_recv,
    gxb_send,
    gxb_recv,
    gy_send,
    gy_recv,
    gya_send,
    gya_recv,
    e_send,
    e_recv,
    own_sem,
    in_sem,
    cot_sem,
    out_sem,
    save_sem,
    load_sem,
    h_sem,
    ya_free,
    xb_free,
    x_free,
    y_free,
):
    place = Place(share)
    s, t, e, y = place.s, place.t, place.e, place.y
    primary, secondary = place.primary, jnp.logical_not(place.primary)
    width, frames = res.shape
    blocks = frames // BLOCK
    half = frames // 2
    quarter = half // 2
    rows = w.shape[3]
    low_rows = pl.ds(0, SPLIT)
    high_rows = pl.ds(SPLIT, rows - SPLIT)
    mine = pl.ds(pl.multiple_of(t * half, half), half)
    theirs = pl.ds(pl.multiple_of((1 - t) * half, half), half)

    own_loads = [pltpu.make_async_copy(vec_in, shard.at[:, pl.ds(VEC, QKV)], own_sem.at[0])]
    for number, (first, many, kind, bias) in enumerate(PARTS):
        own_loads.append(
            pltpu.make_async_copy(
                qkv_in.at[0, "qkv".index(kind), :, pl.ds(bias % WIDE, many)],
                shard.at[:, pl.ds(QKV + first, many)],
                own_sem.at[1 + number],
            )
        )
    own_up = pltpu.make_async_copy(up_in.at[0], shard.at[:, pl.ds(UP, DOWN - UP)], own_sem.at[7])
    own_out = pltpu.make_async_copy(out_in.at[0], flat.at[pl.ds(0, WIDE), :], own_sem.at[8])
    own_down = pltpu.make_async_copy(
        down_in.at[0], flat.at[pl.ds(WIDE, END - DOWN), :], own_sem.at[9]
    )
    for copy in own_loads + [own_out, own_up, own_down]:
        copy.start()

    place.greet()

    def gather_cols(piece):
        if isinstance(piece, int) and piece == 0:
            return pl.ds(VEC, QKV + WIDE)
        return pl.ds(pl.multiple_of(QKV + piece * WIDE, 128), WIDE)

    def z_copies(piece):
        cols = gather_cols(piece)
        copies = []
        for step in range(LINES):
            copies.append(
                remote(
                    shard.at[:, cols],
                    w.at[s, e, y, :, cols],
                    z_send.at[piece, step],
                    z_recv.at[s, piece, e],
                    (t, place.row_of(place.line(step), y), t),
                )
            )
        local = pltpu.make_async_copy(
            shard.at[:, cols], w.at[s, e, y, :, cols], z_recv.at[s, piece, e]
        )
        return copies, local

    def z_start(layer, piece):
        @pl.when(s == layer)
        def _():
            copies, local = z_copies(piece)

            @pl.when(primary)
            def _():
                local.start()

            @pl.when(secondary)
            def _():
                copies[0].start()

            for copy in copies[1:]:
                copy.start()

    def z_finish(piece):
        copies, _ = z_copies(piece)

        @pl.when(secondary)
        def _():
            copies[0].wait_send()

        for copy in copies[1:]:
            copy.wait_send()

    def x_copy(layer, piece):
        part = w.at[layer, :, y, :, gather_cols(piece)]
        return remote(part, part, x_send.at[layer, piece], x_recv.at[layer, piece], place.across)

    def y_copy(layer, piece):
        part = w.at[layer, :, y, :, gather_cols(piece)]
        return remote(part, part, y_send.at[layer, piece], y_recv.at[layer, piece], place.beside)

    def xb_copy(layer, piece):
        part = w.at[layer, :, 1 - y, high_rows, gather_cols(piece)]
        return remote(part, part, xb_send.at[layer, piece], xb_recv.at[layer, piece], place.across)

    def ya_copy(layer, piece):
        part = w.at[layer, :, y, low_rows, gather_cols(piece)]
        return remote(part, part, ya_send.at[layer, piece], ya_recv.at[layer, piece], place.beside)

    def step_z(layer, piece):
        @pl.when(primary)
        def _():
            for line in range(LINES):
                await_bytes(w.at[layer, line, y, :, gather_cols(piece)], z_recv.at[layer, piece, line])
            x_copy(layer, piece).start()
            y_copy(layer, piece).start()

    def step_plane(layer, piece):
        @pl.when(primary)
        def _():
            await_bytes(w.at[layer, :, 1 - y, :, gather_cols(piece)], y_recv.at[layer, piece])
            xb_copy(layer, piece).start()

        @pl.when(secondary)
        def _():
            await_bytes(w.at[layer, :, y, :, gather_cols(piece)], x_recv.at[layer, piece])
            ya_copy(layer, piece).start()

    def complete(layer, *pieces):
        @pl.when(secondary)
        def _():
            for piece in pieces:
                cols = gather_cols(piece)
                await_bytes(w.at[layer, :, 1 - y, high_rows, cols], xb_recv.at[layer, piece])
                await_bytes(w.at[layer, :, 1 - y, low_rows, cols], ya_recv.at[layer, piece])

    kept = {
        "x": (n2, x_hbm),
        "h": (res, h_hbm),
        "n1": (n1, n1_hbm),
        "n2": (n2, n2_hbm),
        "qkv": (qkv, qkv_hbm),
        "ctx": (ctx, ctx_hbm),
        "lse": (lse, lse_hbm),
        "act": (act, act_hbm),
        "slope": (slope, slope_hbm),
    }
    names = tuple(kept)

    def save(name, layer):
        src, dst = kept[name]
        if name in ("x", "h"):
            dst = dst.at[layer]
        return pltpu.make_async_copy(src, dst, save_sem.at[names.index(name), layer])

    def load(name, layer=0):
        dst, src = kept[name]
        if name == "x":
            dst, src = act.at[pl.ds(0, width), :], src.at[layer]
        return pltpu.make_async_copy(src, dst, load_sem.at[names.index(name)])

    def load_h(layer, index):
        slot = lax.rem(index, 2)
        return pltpu.make_async_copy(
            h_hbm.at[layer, :, block_of(index)], h_in.at[slot], h_sem.at[slot]
        )

    my_quarter = pl.ds(s * quarter, quarter)
    my_rows = pl.ds(pl.multiple_of((1 - t) * half + s * quarter, quarter), quarter)

    def clip_across():
        there = pl.ds(pl.multiple_of(t * half + s * quarter, quarter), quarter)
        return remote(
            clips.at[1 - t, my_quarter, :],
            stage.at[there, :],
            in_sem.at[0],
            in_sem.at[1],
            place.across,
        )

    def clip_core():
        part = stage.at[my_rows, :]
        return remote(part, part, in_sem.at[2], in_sem.at[3], place.core)

    def cot_across():
        return remote(
            cot.at[1 - t, my_quarter, :],
            cot_other.at[my_quarter, :],
            cot_sem.at[0],
            cot_sem.at[1],
            place.across,
        )

    def cot_core():
        part = cot_other.at[my_quarter, :]
        return remote(part, part, cot_sem.at[2], cot_sem.at[3], place.core)

    def exchange(kind, index, slot):
        return remote(
            send.at[kind, index],
            recv.at[kind, index],
            e_send.at[slot, index],
            e_recv.at[slot, index],
            place.core,
        )

    def result_copies(ref, first):
        local = pltpu.make_async_copy(stage.at[mine, :], ref.at[0, t], out_sem.at[first])
        away = remote(
            stage.at[theirs, :],
            ref.at[0, t],
            out_sem.at[first + 1],
            out_sem.at[first + 2],
            place.across,
        )
        return local, away

    def emit(layer, ref, first):
        @pl.when(s == layer)
        def _():
            for copy in result_copies(ref, first):
                copy.start()

    for copy in own_loads:
        copy.wait()
    for piece in range(3):
        z_start(0, piece)
    own_clip = pltpu.make_async_copy(clips.at[t], stage.at[mine, :], in_sem.at[4])
    own_clip.start()
    clip_across().start()
    cot_across().start()
    own_out.wait()
    shard[:, OUT:UP] = flat[0:WIDE, :].T
    own_up.wait()
    for piece in (3, 4):
        z_start(0, piece)

    def take_clip(first):
        def body(index, carry):
            at = pl.ds(pl.multiple_of(first + index * BLOCK, BLOCK), BLOCK)
            tile = stage[at, :].T
            n2[:, at] = tile
            res[:, at] = tile.astype(F32)
            return carry

        lax.fori_loop(0, half // BLOCK, body, 0)

    own_clip.wait()
    take_clip(t * half)
    own_down.wait()
    for piece in range(4):
        span = slice((1 + piece) * WIDE, (2 + piece) * WIDE)
        shard[:, DOWN + piece * WIDE : DOWN + (piece + 1) * WIDE] = flat[span, :].T
    clip_across().wait()
    clip_core().start()
    step_z(0, 0)
    z_start(0, 5)
    step_z(0, 1)
    z_start(0, 6)
    clip_core().wait()
    take_clip((1 - t) * half)
    save("x", 0).start()
    step_plane(0, 0)
    step_z(0, 2)
    z_start(0, 7)
    step_plane(0, 1)
    cot_across().wait()
    cot_core().start()
    step_z(0, 3)
    z_start(0, 8)
    step_plane(0, 2)

    def project(index):
        cols = block_of(index)
        mean, scale = norm_stats(lambda span: res[span, cols], width)
        for span in chunks_of(width):
            hat = (res[span, cols] - mean) * scale
            n1[span, cols] = (hat * vecs[span, 0:1] + vecs[span, 2:3]).astype(BF)
        for first, many, kind, bias in PARTS:
            value = mm(wt[first : first + many, :], n1[:, cols])
            for span in chunks_of(many):
                part = value[span, :]
                if kind != "k":
                    part = part + spread[bias + span.start : bias + span.stop, 6:7]
                if kind == "q":
                    part = part * 0.125
                qkv[first + span.start : first + span.stop, cols] = part.astype(BF)

    def head_rows(head, first):
        return pl.ds(pl.multiple_of(first + head * HEAD, HEAD), HEAD)

    def attend(layer):
        def heads_of(first_head, base, stride):
            def one_head(index_in, carry):
                head = first_head + index_in
                q_rows = head_rows(index_in, base)
                k_rows = head_rows(index_in, base + stride)
                v_rows = head_rows(index_in, base + 2 * stride)
                c_rows = head_rows(head, 0)
                keys = qkv[k_rows, :].T
                for index in range(blocks):
                    cols = slice(index * BLOCK, (index + 1) * BLOCK)
                    queries = qkv[q_rows, cols]
                    tiles = []
                    top = None
                    for tile in chunks_of(frames, BLOCK):
                        scores = mm(keys[tile, :], queries)
                        for span in chunks_of(BLOCK):
                            peak = stack_max(scores[span, :])
                            top = peak if top is None else jnp.maximum(top, peak)
                        tiles.append(scores)
                    top = jnp.max(top, 0, keepdims=True)
                    total = jnp.zeros((8, BLOCK), F32)
                    mixed = jnp.zeros((HEAD, BLOCK), F32)
                    for tile, scores in zip(chunks_of(frames, BLOCK), tiles):
                        soft = []
                        for span in chunks_of(BLOCK):
                            part = jnp.exp(scores[span, :] - top)
                            total = total + stack_sum(part)
                            soft.append(part.astype(BF))
                        mixed = mixed + mm(qkv[v_rows, tile], jnp.concatenate(soft, 0))
                    total = jnp.sum(total, 0, keepdims=True)
                    ctx[c_rows, cols] = (mixed / total).astype(BF)
                    lse[pl.ds(head, 1), cols] = top + jnp.log(total)
                step_z(layer, 5 + head)
                step_plane(layer, 4 + head)
                return carry

            return one_head

        lax.fori_loop(0, 4, heads_of(0, 0, 256), 0)
        lax.fori_loop(0, 2, heads_of(4, 768, 128), 0)

    def out_project(layer):
        def body(index, carry):
            part = mm(whole(w, layer, OUT, 384), ctx[:, block_of(index)])
            send[0, index] = part.astype(BF)
            exchange(0, index, 2 * layer).start()
            return carry

        lax.fori_loop(0, blocks, body, 0)

    def middle_norm(layer):
        def body(index, carry):
            cols = block_of(index)
            exchange(0, index, 2 * layer).wait()
            for span in chunks_of(width):
                added = send[0, index, span, :].astype(F32) + recv[0, index, span, :].astype(F32)
                res[span, cols] = res[span, cols] + added + vecs[span, 3:4]
            mean, scale = norm_stats(lambda span: res[span, cols], width)
            for span in chunks_of(width):
                hat = (res[span, cols] - mean) * scale
                n2[span, cols] = (hat * vecs[span, 1:2] + vecs[span, 4:5]).astype(BF)
            return carry

        lax.fori_loop(0, blocks, body, 0)

    def hidden_part(layer, part):
        flip_weights(w, wt, layer, UP + part * WIDE, WIDE, part * WIDE)
        units = slice(part * WIDE, (part + 1) * WIDE)
        lane = 7 if part < 2 else 8

        def body(index, carry):
            cols = block_of(index)
            pre = mm(wt[units, :], n2[:, cols])
            for span in chunks_of(WIDE):
                first = part * WIDE + span.start
                bias = spread[768 + first : 768 + first + ROWS, lane : lane + 1]
                value, steep = gelu_parts(pre[span, :] + bias)
                act[first : first + ROWS, cols] = value.astype(BF)
                slope[first : first + ROWS, cols] = steep.astype(BF)
            return carry

        lax.fori_loop(0, blocks, body, 0)

    def down_project(layer):
        def body(index, carry):
            part = mm(whole(w, layer, DOWN, 1536), act[:, block_of(index)])
            send[1, index] = part.astype(BF)
            exchange(1, index, 2 * layer + 1).start()
            return carry

        lax.fori_loop(0, blocks, body, 0)

    def layer_end(layer, index, span):
        added = send[1, index, span, :].astype(F32) + recv[1, index, span, :].astype(F32)
        return (res[span, block_of(index)] + added + vecs[span, 5:6]).astype(BF)

    def take_vectors(layer):
        vecs[...] = whole(w, layer, VEC, 128).astype(F32)
        spread_biases(vecs, spread, rows)

    def project_all(layer):
        flip_weights(w, wt, layer, QKV, 1152)

        def body(index, carry):
            project(index)
            return carry

        lax.fori_loop(0, blocks, body, 0)
        if layer == 0:
            save("n1", 0).start()
            save("qkv", 0).start()

    complete(0, 0, 1, 2)
    take_vectors(0)
    project_all(0)
    step_z(0, 4)
    step_plane(0, 3)
    for piece in (9, 10, 11):
        z_start(0, piece)
    cot_core().wait()
    load_cot = pltpu.make_async_copy(cot_other, stage.at[theirs, :], cot_sem.at[4])
    load_cot.start()
    own_cot = pltpu.make_async_copy(cot.at[t], stage.at[mine, :], cot_sem.at[5])
    own_cot.start()
    attend(0)
    save("ctx", 0).start()
    save("lse", 0).start()
    complete(0, 3)
    out_project(0)
    step_z(0, 11)
    step_plane(0, 10)
    for piece in (0, 1, 2):
        z_start(1, piece)
    load_cot.wait()
    own_cot.wait()

    def take_cot(index, carry):
        low[:, block_of(index)] = stage[block_of(index), :].T
        return carry

    lax.fori_loop(0, blocks, take_cot, 0)
    save("x", 0).wait()
    middle_norm(0)
    save("h", 0).start()
    save("n2", 0).start()
    for part in range(4):
        complete(0, 4 + part)
        hidden_part(0, part)
        step_z(1, part)
        if part == 0:
            step_plane(0, 11)
        else:
            step_plane(1, part - 1)
        z_start(1, part + 3)
    save("act", 0).start()
    save("slope", 0).start()
    complete(0, 8, 9, 10, 11)
    down_project(0)
    step_z(1, 4)
    step_plane(1, 3)
    z_start(1, 7)
    z_start(1, 8)
    for name in ("n1", "qkv", "h", "n2"):
        save(name, 0).wait()

    def finish_body(index, carry):
        exchange(1, index, 1).wait()
        cols = block_of(index)
        for span in chunks_of(width):
            rows_out = layer_end(0, index, span)
            n2[span, cols] = rows_out
            res[span, cols] = rows_out.astype(F32)

        @pl.when(s == 0)
        def _():
            stage[cols, :] = n2[:, cols].T

        return carry

    lax.fori_loop(0, blocks, finish_body, 0)
    emit(0, out, 0)
    save("x", 1).start()
    complete(1, 0, 1, 2)
    take_vectors(1)
    project_all(1)
    for piece in (9, 10, 11):
        z_start(1, piece)
    save("ctx", 0).wait()
    save("lse", 0).wait()
    attend(1)
    complete(1, 3)
    out_project(1)
    step_z(1, 11)
    step_plane(1, 10)
    save("x", 1).wait()
    middle_norm(1)
    save("h", 1).start()
    save("act", 0).wait()
    save("slope", 0).wait()
    for part in range(4):
        complete(1, 4 + part)
        hidden_part(1, part)
        if part == 0:
            step_plane(1, 11)
    complete(1, 8, 9, 10, 11)
    down_project(1)
    flip_weights(w, wt, 1, DOWN, 1536)

    def last_body(index, carry):
        exchange(1, index, 3).wait()

        @pl.when(s == 1)
        def _():
            for span in chunks_of(width, 128):
                stage[block_of(index), span] = layer_end(1, index, span).T

        return carry

    lax.fori_loop(0, blocks, last_body, 0)
    emit(1, out, 0)
    save("h", 1).wait()

    VECTORS = CHUNKS

    def grad_cols(piece):
        if isinstance(piece, int) and piece == VECTORS:
            return pl.ds(VEC, QKV)
        return pl.ds(pl.multiple_of(QKV + piece * WIDE, 128), WIDE)

    def gya_copy(layer, piece):
        cols = grad_cols(piece)
        return remote(
            w.at[layer, :, 1 - y, low_rows, cols],
            land_a.at[:, low_rows, cols],
            gya_send.at[layer, piece],
            gya_recv.at[layer, piece],
            place.beside,
        )

    def gxb_copy(layer, piece):
        cols = grad_cols(piece)
        return remote(
            w.at[layer, :, 1 - y, high_rows, cols],
            land_b.at[:, :, cols],
            gxb_send.at[layer, piece],
            gxb_recv.at[layer, piece],
            place.across,
        )

    def gx_copy(layer, piece):
        cols = grad_cols(piece)
        return remote(
            w.at[layer, :, y, :, cols],
            land_a.at[:, :, cols],
            gx_send.at[layer, piece],
            gx_recv.at[layer, piece],
            place.across,
        )

    def gy_copy(layer, piece):
        cols = grad_cols(piece)
        return remote(
            w.at[layer, :, 1 - y, :, cols],
            land_y.at[:, :, cols],
            gy_send.at[layer, piece],
            gy_recv.at[layer, piece],
            place.beside,
        )

    def landed_part(piece):
        if piece == VECTORS:
            return landed_vec
        ref, first = (
            (landed_qkv, 0)
            if piece < 3
            else (landed_out, 3)
            if piece < 4
            else (landed_up, 4)
            if piece < 8
            else (landed_down, 8)
        )
        return ref.at[:, :, pl.ds((piece - first) * WIDE, WIDE)]

    def gz_copies(layer, piece):
        cols = grad_cols(piece)
        target = landed_part(piece)
        copies = []
        for step in range(LINES):
            line = place.line(step)
            copies.append(
                remote(
                    w.at[layer, line, y, :, cols],
                    target.at[e],
                    gz_send.at[layer, piece, step],
                    gz_recv.at[piece, e],
                    (layer, place.row_of(line, y), t),
                )
            )
        local = pltpu.make_async_copy(
            w.at[layer, e, y, :, cols], target.at[e], gz_recv.at[piece, e]
        )
        return copies, local

    def add_rows(layer, piece, which, span, lands):
        cols = grad_cols(piece)
        first, count = span
        for line in range(LINES):
            total = w[layer, line, which, pl.ds(first, count), cols].astype(F32)
            for land, offset in lands:
                total = total + land[line, pl.ds(offset, count), cols].astype(F32)
            w[layer, line, which, pl.ds(first, count), cols] = total.astype(BF)

    def signal(sem, layer, piece, device):
        if layer == 1:
            pl.semaphore_signal(sem.at[piece], inc=1, device_id=device, device_id_type=MESH)

    def credit(sem, layer, piece):
        if layer == 0:
            pl.semaphore_wait(sem.at[piece], 1)

    def step_a(layer, piece):
        @pl.when(secondary)
        def _():
            credit(ya_free, layer, piece)
            gya_copy(layer, piece).start()
            credit(xb_free, layer, piece)
            gxb_copy(layer, piece).start()

    def step_b(layer, piece):
        cols = grad_cols(piece)

        @pl.when(secondary)
        def _():
            await_bytes(land_a.at[:, low_rows, cols], gya_recv.at[layer, piece])
            add_rows(layer, piece, y, (0, SPLIT), [(land_a, 0)])
            signal(ya_free, layer, piece, place.beside)
            credit(x_free, layer, piece)
            gx_copy(layer, piece).start()

        @pl.when(primary)
        def _():
            await_bytes(land_b.at[:, :, cols], gxb_recv.at[layer, piece])
            add_rows(layer, piece, 1 - y, (SPLIT, rows - SPLIT), [(land_b, 0)])
            signal(xb_free, layer, piece, place.across)
            credit(y_free, layer, piece)
            gy_copy(layer, piece).start()

    def step_c(layer, piece):
        cols = grad_cols(piece)

        @pl.when(primary)
        def _():
            await_bytes(land_a.at[:, :, cols], gx_recv.at[layer, piece])
            await_bytes(land_y.at[:, :, cols], gy_recv.at[layer, piece])
            add_rows(layer, piece, y, (0, rows), [(land_a, 0), (land_y, 0)])
            signal(x_free, layer, piece, place.across)
            signal(y_free, layer, piece, place.beside)
            copies, local = gz_copies(layer, piece)

            @pl.when(s == layer)
            def _():
                local.start()

            @pl.when(s != layer)
            def _():
                copies[0].start()

            for copy in copies[1:]:
                copy.start()

    def store_grads(layer, start, count, value):
        w[layer, :, :, :, pl.ds(start, count)] = value.astype(BF).reshape(
            w.shape[1], w.shape[2], rows, count
        )

    ones = functools.partial(jnp.ones, (frames, 128), BF)

    def mlp_back(layer, beside):
        def body(index, carry):
            cols = block_of(index)
            for part in range(4):
                units = slice(part * WIDE, (part + 1) * WIDE)
                grad = mm(wt[units, :], low[:, cols])
                for span in chunks_of(WIDE):
                    rows_in = slice(units.start + span.start, units.start + span.stop)
                    steep = slope[rows_in, cols].astype(F32)
                    slope[rows_in, cols] = (grad[span, :] * steep).astype(BF)
            term = mm(whole(w, layer, UP, 1536), slope[:, cols])
            send[0, index] = term.astype(BF)
            exchange(0, index, 4 + 2 * layer).start()
            beside(index)
            return carry

        lax.fori_loop(0, blocks, body, 0)

    def outer_pair(layer, start, left, right, first, beside):
        def body(index, carry):
            for part in range(3):
                base = index * 768 + part * 256
                span = pl.ds(pl.multiple_of(base, 256), 256)
                value = mmt(left[...], right[span, :])
                store_grads(layer, pl.multiple_of(start + base, 128), 256, value)
            step_a(layer, first + 2 * index)
            step_a(layer, first + 2 * index + 1)
            beside(index)
            return carry

        lax.fori_loop(0, 2, body, 0)

    def fold(value):
        return value[:, 0:128] + value[:, 128:256]

    def norm_back(layer, kind, gain_lane, source, put, finish, beside):
        sums[...] = jnp.zeros_like(sums)

        def body(index, carry):
            cols = block_of(index)
            read = source(index)
            mean, scale = norm_stats(read, width)
            exchange(kind, index, 4 + 2 * layer + kind).wait()
            first = jnp.zeros((8, BLOCK), F32)
            second = jnp.zeros((8, BLOCK), F32)

            def terms(span):
                hat = (read(span) - mean) * scale
                grad = send[kind, index, span, :].astype(F32)
                grad = grad + recv[kind, index, span, :].astype(F32)
                return hat, grad, grad * vecs[span, gain_lane : gain_lane + 1]

            for span in chunks_of(width):
                hat, grad, scaled = terms(span)
                sums[0, span, :] += fold(grad * hat)
                sums[1, span, :] += fold(grad)
                first = first + stack_sum(scaled)
                second = second + stack_sum(scaled * hat)
            level = mean_of(first, width)
            slant = mean_of(second, width)
            for span in chunks_of(width):
                hat, _, scaled = terms(span)
                put(span, cols, res[span, cols] + scale * (scaled - level - hat * slant))
            finish(cols)
            beside(index)
            return carry

        lax.fori_loop(0, blocks, body, 0)

    def row_sums(value):
        return jnp.sum(value, 1, keepdims=True)

    def attend_back(first_head, many, base, stride, beside):
        def one_head(index_in, carry):
            head = first_head + index_in
            q_rows = head_rows(index_in, base)
            k_rows = head_rows(index_in, base + stride)
            v_rows = head_rows(index_in, base + 2 * stride)
            c_rows = head_rows(head, 0)
            keys = qkv[k_rows, :].T
            values = qkv[v_rows, :].T
            key_totals = [jnp.zeros((HEAD, BLOCK), F32)] * blocks
            value_totals = [jnp.zeros((HEAD, BLOCK), F32)] * blocks
            for index in range(blocks):
                cols = slice(index * BLOCK, (index + 1) * BLOCK)
                queries = qkv[q_rows, cols]
                grads = dctx[c_rows, cols]
                level = lse[pl.ds(head, 1), cols]
                inner = jnp.sum(
                    grads.astype(F32) * ctx[c_rows, cols].astype(F32), 0, keepdims=True
                )
                step = jnp.zeros((HEAD, BLOCK), F32)
                for tile in range(blocks):
                    span = slice(tile * BLOCK, (tile + 1) * BLOCK)
                    scores = mm(keys[span, :], queries)
                    soft_grad = mm(values[span, :], grads)
                    soft = []
                    score_grad = []
                    for part in chunks_of(BLOCK):
                        strength = jnp.exp(scores[part, :] - level)
                        soft.append(strength.astype(BF))
                        score_grad.append((strength * (soft_grad[part, :] - inner)).astype(BF))
                    soft = jnp.concatenate(soft, 0)
                    score_grad = jnp.concatenate(score_grad, 0)
                    step = step + mm(qkv[k_rows, span], score_grad)
                    key_totals[tile] = key_totals[tile] + mmt(queries, score_grad)
                    value_totals[tile] = value_totals[tile] + mmt(grads, soft)
                slope[q_rows, cols] = (step * 0.125).astype(BF)
            for tile in range(blocks):
                span = slice(tile * BLOCK, (tile + 1) * BLOCK)
                slope[k_rows, span] = key_totals[tile].astype(BF)
                slope[v_rows, span] = value_totals[tile].astype(BF)
            beside(index_in)
            return carry

        lax.fori_loop(0, many, one_head, 0)

    def collect_biases():
        def body(group, carry):
            source = group * rows
            for kind in range(2):
                for head in range(6):
                    at = pl.ds(pl.multiple_of(kind * 384 + head * HEAD + group * 8, 8), 8)
                    to = pl.ds(pl.multiple_of(source + kind * 48 + head * 8, 8), 8)
                    vec_grads[to, 6:7] = spread[at, 6:7]
            for unit in range(24):
                at = pl.ds(pl.multiple_of(768 + unit * HEAD + group * 8, 8), 8)
                to = pl.ds(pl.multiple_of(source + (unit % 12) * 8, 8), 8)
                lane = 7 if unit < 12 else 8
                vec_grads[to, lane : lane + 1] = spread[at, lane : lane + 1]
            return carry

        lax.fori_loop(0, GROUPS, body, 0)

    def nothing(index):
        del index

    def at_turns(turns):
        def beside(index):
            for turn, steps in turns.items():

                @pl.when(index == turn)
                def _():
                    for step in steps:
                        step()

        return beside

    def finish_gather(piece):
        z_finish(piece)
        for layer in range(2):

            @pl.when(primary)
            def _():
                x_copy(layer, piece).wait_send()
                y_copy(layer, piece).wait_send()
                xb_copy(layer, piece).wait_send()

            @pl.when(secondary)
            def _():
                ya_copy(layer, piece).wait_send()

    def finish_body_gather(piece, carry):
        finish_gather(piece)
        return carry

    res[...] = low[...].astype(F32)

    for layer in (1, 0):
        later = layer == 0
        load_h(layer, 0).start()
        if later:
            vecs[...] = whole(w, layer, VEC, 128).astype(F32)
            flip_weights(w, wt, layer, DOWN, 1536)
            load("slope").wait()
        vec_grads[...] = jnp.zeros_like(vec_grads)

        early = at_turns({0: (lambda: step_b(1, VECTORS),), 1: (lambda: step_c(1, VECTORS),)})
        mlp_back(layer, early if later else nothing)
        if not later:
            finish_gather(0)
            lax.fori_loop(1, CHUNKS, finish_body_gather, 0)
        if later:
            load("act").wait()
        outer_pair(layer, DOWN, low, act, 8, nothing)
        load("x", layer).start()
        if later:
            load("n2").wait()
        vec_grads[:, 5:6] = mm(low[...], ones())[:, 0:1]

        def b(piece, layer=layer):
            return lambda: step_b(layer, piece)

        def c(piece, layer=layer):
            return lambda: step_c(layer, piece)

        outer_pair(layer, UP, n2, slope, 4, at_turns({1: (b(8), b(9))}))
        spread[768:, :] = mm(slope[...], ones())
        flip_weights(w, wt, layer, OUT, 384)

        def hidden_in(index, layer=layer):
            @pl.when(index + 1 < blocks)
            def _():
                load_h(layer, index + 1).start()

            load_h(layer, index).wait()
            slot = lax.rem(index, 2)
            return lambda span: h_in[slot, span, :]

        def hidden_put(span, cols, total):
            res[span, cols] = total
            low[span, cols] = total.astype(BF)

        def hidden_out(cols):
            dctx[:, cols] = mm(wt[0:384, :], low[:, cols]).astype(BF)

        drain = at_turns({0: (b(10),), 1: (b(11),), 2: (b(4), c(8)), 3: (b(5), c(9))})
        norm_back(layer, 0, 1, hidden_in, hidden_put, hidden_out, drain)
        vec_grads[:, 1:2] = row_sums(sums[0])
        vec_grads[:, 4:5] = row_sums(sums[1])
        vec_grads[:, 3:4] = mm(low[...], ones())[:, 0:1]
        if later:
            for name in ("ctx", "qkv", "lse"):
                load(name).wait()
        store_grads(layer, OUT, 384, mmt(low[...], ctx[...]))
        step_a(layer, 3)
        step_b(layer, 6)
        step_c(layer, 10)
        drain = at_turns({0: (b(7), c(11)), 1: (b(3), c(4)), 2: (c(5),), 3: (c(6),)})
        attend_back(0, 4, 0, 256, drain)
        if later:
            load("n1").wait()
        wt[0:768, :] = whole(w, layer, QKV, 768)

        def qkv_body(index, carry, layer=layer):
            span = pl.ds(pl.multiple_of(index * 256, 256), 256)
            value = mmt(n1[...], slope[span, :])
            store_grads(layer, pl.multiple_of(QKV + index * 256, 128), 256, value)
            return carry

        lax.fori_loop(0, 3, qkv_body, 0)
        step_a(layer, 0)
        step_a(layer, 1)
        step_c(layer, 7)
        attend_back(4, 2, 768, 128, at_turns({0: (b(0), c(3)), 1: (b(1),)}))

        def first_body(index, carry, layer=layer):
            cols = block_of(index)
            term = mm(wt[0:768, :], slope[0:768, cols])
            term = term + mm(whole(w, layer, QKV + 768, WIDE), slope[768:1152, cols])
            send[1, index] = term.astype(BF)
            exchange(1, index, 5 + 2 * layer).start()
            return carry

        lax.fori_loop(0, blocks, first_body, 0)
        store_grads(layer, QKV + 768, WIDE, mmt(n1[...], slope[768:1152, :]))
        step_a(layer, 2)
        step_c(layer, 0)
        for first, many, kind, bias in PARTS:
            if kind != "k":
                spread[bias : bias + many, :] = mm(slope[first : first + many, :], ones())
        collect_biases()
        if layer == 1:
            for name in ("slope", "n1", "n2", "ctx", "qkv", "lse"):
                load(name).start()
        load("x", layer).wait()

        @pl.when(s == layer)
        def _():
            local, away = result_copies(out, 0)
            local.wait()
            away.wait_send()

        def rows_x(index):
            return lambda span: act[span, block_of(index)].astype(F32)

        def rows_put(span, cols, total, layer=layer):
            rounded = total.astype(BF)
            low[span, cols] = rounded
            if layer == 1:
                res[span, cols] = rounded.astype(F32)

        def rows_out(cols, layer=layer):
            @pl.when(s == layer)
            def _():
                stage[cols, :] = low[:, cols].T

        drain = at_turns({0: (c(1),), 1: (b(2),), 3: (c(2),)})
        norm_back(layer, 1, 0, rows_x, rows_put, rows_out, drain)
        emit(layer, in_grad, 3)
        if layer == 1:
            load("act").start()
        vec_grads[:, 0:1] = row_sums(sums[0])
        vec_grads[:, 2:3] = row_sums(sums[1])
        store_grads(layer, VEC, 128, vec_grads[...])
        step_a(layer, VECTORS)

    step_b(0, VECTORS)
    step_c(0, VECTORS)

    def finish_scatter(piece):
        for layer in range(2):

            @pl.when(secondary)
            def _():
                gya_copy(layer, piece).wait_send()
                gxb_copy(layer, piece).wait_send()
                gx_copy(layer, piece).wait_send()

            @pl.when(primary)
            def _():
                gy_copy(layer, piece).wait_send()
                copies, _ = gz_copies(layer, piece)

                @pl.when(s != layer)
                def _():
                    copies[0].wait_send()

                for copy in copies[1:]:
                    copy.wait_send()

    for piece in range(CHUNKS + 1):
        finish_scatter(piece)
        for line in range(LINES):
            await_bytes(landed_part(piece).at[line], gz_recv.at[piece, line])

    _, away = result_copies(out, 0)
    away.wait_recv()
    local, away = result_copies(in_grad, 3)
    local.wait()
    away.wait()


def layers_call(share, clips, cotangent, shards, dims):
    width, frames, hidden_units, heads_width = dims
    rows = width // GROUPS
    sem = pltpu.SemaphoreType.DMA
    free = pltpu.SemaphoreType.REGULAR
    packed = (2, LINES, 2, rows, END)
    blocks = frames // BLOCK
    shape = jax.ShapeDtypeStruct
    outs = [
        shape((1,) + clips.shape, BF),
        shape((1,) + clips.shape, BF),
        shape((LINES, rows, QKV - VEC), BF),
        shape((LINES, rows, OUT - QKV), BF),
        shape((LINES, rows, UP - OUT), BF),
        shape((LINES, rows, DOWN - UP), BF),
        shape((LINES, rows, END - DOWN), BF),
        shape(clips.shape[1:], BF),
        shape((2, width, frames), BF),
        shape((2, width, frames), F32),
        shape((width, frames), BF),
        shape((width, frames), BF),
        shape((3 * heads_width, frames), BF),
        shape((heads_width, frames), BF),
        shape((8, frames), F32),
        shape((hidden_units, frames), BF),
        shape((hidden_units, frames), BF),
    ]
    scratch = [
        pltpu.VMEM(packed, BF),
        pltpu.VMEM((width, frames), F32),
        pltpu.VMEM((hidden_units, frames), BF),
        pltpu.VMEM((hidden_units, frames), BF),
        pltpu.VMEM((width, frames), BF),
        pltpu.VMEM((width, frames), BF),
        pltpu.VMEM((width, frames), BF),
        pltpu.VMEM((3 * heads_width, frames), BF),
        pltpu.VMEM((heads_width, frames), BF),
        pltpu.VMEM((heads_width, frames), BF),
        pltpu.VMEM((8, frames), F32),
        pltpu.VMEM((2, width, BLOCK), F32),
        pltpu.VMEM((hidden_units, width), BF),
        pltpu.VMEM((2, blocks, width, BLOCK), BF),
        pltpu.VMEM((2, blocks, width, BLOCK), BF),
        pltpu.VMEM((width, 128), F32),
        pltpu.VMEM((width, 128), F32),
        pltpu.VMEM((2, width, 128), F32),
        pltpu.VMEM((2 * heads_width + hidden_units, 128), F32),
        pltpu.VMEM((frames, width), BF),
        pltpu.VMEM((rows, END), BF),
        pltpu.VMEM((WIDE + END - DOWN, rows), BF),
        pltpu.VMEM((LINES, rows, END), BF),
        pltpu.VMEM((LINES, rows - SPLIT, END), BF),
        pltpu.VMEM((LINES, rows, END), BF),
    ]
    scratch += [sem((CHUNKS, LINES)), sem((2, CHUNKS, LINES))]
    scratch += [sem((2, CHUNKS))] * 8
    scratch += [sem((2, CHUNKS + 1, LINES)), sem((CHUNKS + 1, LINES))]
    scratch += [sem((2, CHUNKS + 1))] * 8
    scratch += [
        sem((8, blocks)),
        sem((8, blocks)),
        sem((10,)),
        sem((5,)),
        sem((6,)),
        sem((6,)),
        sem((9, 2)),
        sem((9,)),
        sem((2,)),
    ]
    scratch += [free((CHUNKS + 1,))] * 4
    anywhere = pl.BlockSpec(memory_space=pl.ANY)
    return pl.pallas_call(
        functools.partial(layers_kernel, share),
        out_shape=outs,
        in_specs=[anywhere] * (2 + len(shards)),
        out_specs=[anywhere] * len(outs),
        scratch_shapes=scratch,
        compiler_params=pltpu.CompilerParams(
            collective_id=0, has_side_effects=True, vmem_limit_bytes=VMEM_LIMIT
        ),
        cost_estimate=pl.CostEstimate(
            flops=60_000_000_000, bytes_accessed=60_000_000, transcendentals=0
        ),
    )(clips, cotangent, *shards)


def group_piece(value, axis, share):
    if share == 1:
        return value
    size = value.shape[axis] * share
    group = lax.axis_index("dp") // share
    full = lax.all_gather(value, "dp", axis=axis, tiled=True)
    return lax.dynamic_slice_in_dim(full, group * size, size, axis)


def own_part(value, axis, share, parts, index):
    size = value.shape[axis] // parts
    if parts == 1:
        return value
    return lax.dynamic_slice_in_dim(value, index * size, size, axis)


def on_device(share, clips, cotangent, ln_gains, row_biases, w_qkv, b_qv, w_o, w_up, b_ff, w_down):
    width = clips.shape[2]
    rows = width // GROUPS
    dims = (width, 2 * clips.shape[1], w_up.shape[2], w_o.shape[1])
    ln_gains = group_piece(ln_gains, 2, share)
    row_biases = group_piece(row_biases, 2, share)
    w_qkv = group_piece(w_qkv, 2, share)
    b_qv = group_piece(b_qv, 3, share)
    w_o = group_piece(w_o, 2, share)
    w_up = group_piece(w_up, 1, share)
    b_ff = group_piece(b_ff, 2, share)
    w_down = group_piece(w_down, 2, share)
    vectors = jnp.concatenate([ln_gains[0], row_biases[0]], 0).T
    heads = jnp.concatenate([b_qv[0, 0].reshape(-1), b_qv[0, 1].reshape(-1)])[:, None]
    units = b_ff[0].reshape(2, rows).T
    packed = jnp.concatenate([vectors, heads, units], 1)
    packed = jnp.pad(packed, ((0, 0), (0, 128 - packed.shape[1])))
    section_out, section_in_grad, *landed = layers_call(
        share, clips, cotangent, (packed, w_qkv, w_o, w_up, w_down), dims
    )
    rest = lax.axis_index("dp") % share
    side = lax.axis_index("tensor")

    def joined(value):
        total = jnp.sum(value.astype(F32), 0)
        if share == 1:
            return total
        group = lax.axis_index("dp") // share
        padded = jnp.zeros((width, total.shape[1]), F32)
        padded = lax.dynamic_update_slice_in_dim(padded, total, group * rows, 0)
        return lax.dynamic_slice_in_dim(lax.psum(padded, "dp"), group * rows, rows, 0)

    def mine(value):
        return own_part(joined(value), 0, share, share, rest)

    vectors = joined(landed[0])
    vec = own_part(own_part(vectors, 0, share, share, rest), 0, share, 2, side)
    heads_grad = vectors[:, 6].reshape(2, -1, HEAD // GROUPS)
    units_grad = vectors[:, 7:9].T.reshape(-1, HEAD // GROUPS)
    qkv_grad = {"q": [], "k": [], "v": []}
    for first, many, kind, _ in PARTS:
        qkv_grad[kind].append(mine(landed[1][:, :, first : first + many]))
    return (
        section_out,
        section_in_grad,
        vec[:, 0:2].T[None],
        vec[:, 2:6].T[None],
        jnp.stack([jnp.concatenate(qkv_grad[kind], 1) for kind in "qkv"])[None],
        own_part(heads_grad, 2, share, share, rest)[None],
        mine(landed[2]).T[None],
        mine(landed[3])[None],
        own_part(units_grad, 1, share, share, rest)[None],
        mine(landed[4]).T[None],
    )


def solution(mesh):
    placed = (
        P("dp", "tensor", None),
        P("dp", "tensor", None),
        P("section", None, "dp"),
        P("section", None, "dp"),
        P("section", None, "dp", "tensor"),
        P("section", None, "tensor", "dp"),
        P("section", "tensor", "dp"),
        P("section", "dp", "tensor"),
        P("section", "tensor", "dp"),
        P("section", "tensor", "dp"),
    )
    share = mesh.shape["dp"] // GROUPS
    return jax.shard_map(
        functools.partial(on_device, share),
        mesh=mesh,
        in_specs=placed,
        out_specs=(
            P("section", "dp", "tensor", None),
            P("section", "dp", "tensor", None),
            P("section", None, ("dp", "tensor")),
            P("section", None, ("dp", "tensor")),
            P("section", None, "dp", "tensor"),
            P("section", None, "tensor", "dp"),
            P("section", "tensor", "dp"),
            P("section", "dp", "tensor"),
            P("section", "tensor", "dp"),
            P("section", "tensor", "dp"),
        ),
        check_vma=False,
    )
```

```python
import functools

import jax
import jax.numpy as jnp
from jax import lax
from jax.experimental import pallas as pl
from jax.experimental.pallas import tpu as pltpu
from jax.sharding import PartitionSpec as P

BF = jnp.bfloat16
F32 = jnp.float32
MESH = pl.DeviceIdType.MESH
EPSILON = 1e-05
HEAD = 64
GROUPS = 8
LINES = 4
BLOCK = 256
ROWS = 64
VMEM_LIMIT = 62 * 1024 * 1024

VEC = 0
QKV = 128
OUT = 1280
UP = 1664
DOWN = 3200
END = 4736
SPLIT = 48
WIDE = 384
CHUNKS = 12


PARTS = (
    (0, 256, "q", 0),
    (256, 256, "k", 0),
    (512, 256, "v", 384),
    (768, 128, "q", 256),
    (896, 128, "k", 256),
    (1024, 128, "v", 640),
)


def mm(left, right):
    return jnp.dot(left, right, preferred_element_type=F32)


def mmt(left, right):
    return lax.dot_general(left, right, (((1,), (1,)), ((), ())), preferred_element_type=F32)


class Place:
    def __init__(self, share):
        self.s = lax.axis_index("section")
        self.d = lax.axis_index("dp")
        self.t = lax.axis_index("tensor")
        group = self.d // share
        self.rest = self.d - group * share
        self.share = share
        self.e = group // 2
        self.y = group - self.e * 2
        self.primary = self.s == self.t
        self.core = (1 - self.s, self.d, self.t)
        self.across = (self.s, self.d, 1 - self.t)
        self.beside = (self.s, self.row_of(self.e, 1 - self.y), self.t)

    def row_of(self, line, y):
        return (line * 2 + y) * self.share + self.rest

    def line(self, step):
        return lax.rem(self.e + step, LINES)

    def greet(self):
        barrier = pltpu.get_barrier_semaphore()
        peers = [self.core, self.across, self.beside]
        for step in range(1, LINES):
            for section in range(2):
                peers.append((section, self.row_of(self.line(step), self.y), self.t))
        for peer in peers:
            pl.semaphore_signal(barrier, inc=1, device_id=peer, device_id_type=MESH)
        pl.semaphore_wait(barrier, len(peers))


def remote(src, dst, send_sem, recv_sem, device):
    return pltpu.make_async_remote_copy(
        src_ref=src,
        dst_ref=dst,
        send_sem=send_sem,
        recv_sem=recv_sem,
        device_id=device,
        device_id_type=MESH,
    )


def await_bytes(ref, sem):
    pltpu.make_async_copy(ref, ref, sem).wait()


def chunks_of(count, size=ROWS):
    return [slice(first, first + size) for first in range(0, count, size)]


def by_eights(value):
    return value.reshape(value.shape[0] // 8, 8, value.shape[1])


def stack_sum(value):
    return jnp.sum(by_eights(value), 0)


def stack_max(value):
    return jnp.max(by_eights(value), 0)


def mean_of(parts, count):
    return jnp.sum(parts, 0, keepdims=True) / count


def norm_stats(read, count):
    total = jnp.zeros((8, BLOCK), F32)
    for span in chunks_of(count):
        total = total + stack_sum(read(span))
    mean = mean_of(total, count)
    square = jnp.zeros((8, BLOCK), F32)
    for span in chunks_of(count):
        centred = read(span) - mean
        square = square + stack_sum(centred * centred)
    return mean, lax.rsqrt(mean_of(square, count) + EPSILON)


def gelu_parts(values):
    bell = jnp.exp(-0.5 * values * values)
    reach = jnp.abs(values) * 0.7071067811865476
    inv = 1.0 / (1.0 + 0.3275911 * reach)
    poly = inv * (
        0.254829592
        + inv * (-0.284496736 + inv * (1.421413741 + inv * (-1.453152027 + inv * 1.061405429)))
    )
    tail = 0.5 * poly * bell
    cdf = jnp.where(values >= 0.0, 1.0 - tail, tail)
    return values * cdf, cdf + values * bell * 0.3989422804014327


def block_of(index):
    return pl.ds(pl.multiple_of(index * BLOCK, BLOCK), BLOCK)


def flip_weights(w, wt, layer, start, width, target=0):
    def body(index, carry):
        cols = pl.ds(pl.multiple_of(start + index * 128, 128), 128)
        rows = pl.ds(pl.multiple_of(target + index * 128, 128), 128)
        tile = w[layer, :, :, :, cols]
        wt[rows, :] = tile.reshape(tile.shape[0] * tile.shape[1] * tile.shape[2], 128).T
        return carry

    lax.fori_loop(0, width // 128, body, 0)


def whole(w, layer, start, width):
    tile = w[layer, :, :, :, start : start + width]
    return tile.reshape(tile.shape[0] * tile.shape[1] * tile.shape[2], width)


def spread_biases(vecs, spread, rows):
    def body(group, carry):
        source = group * rows
        for kind in range(2):
            for head in range(6):
                to = pl.ds(pl.multiple_of(kind * 384 + head * HEAD + group * 8, 8), 8)
                at = pl.ds(pl.multiple_of(source + kind * 48 + head * 8, 8), 8)
                spread[to, :] = vecs[at, :]
        for unit in range(24):
            to = pl.ds(pl.multiple_of(768 + unit * HEAD + group * 8, 8), 8)
            at = pl.ds(pl.multiple_of(source + (unit % 12) * 8, 8), 8)
            spread[to, :] = vecs[at, :]
        return carry

    lax.fori_loop(0, GROUPS, body, 0)


def layers_kernel(
    share,
    clips,
    cot,
    vec_in,
    qkv_in,
    out_in,
    up_in,
    down_in,
    out,
    in_grad,
    landed_vec,
    landed_qkv,
    landed_out,
    landed_up,
    landed_down,
    cot_other,
    x_hbm,
    h_hbm,
    n1_hbm,
    n2_hbm,
    qkv_hbm,
    ctx_hbm,
    lse_hbm,
    act_hbm,
    slope_hbm,
    w,
    res,
    act,
    slope,
    n1,
    n2,
    low,
    qkv,
    ctx,
    dctx,
    lse,
    h_in,
    wt,
    send,
    recv,
    vecs,
    vec_grads,
    sums,
    spread,
    stage,
    shard,
    flat,
    land_a,
    land_b,
    land_y,
    z_send,
    z_recv,
    x_send,
    x_recv,
    xb_send,
    xb_recv,
    y_send,
    y_recv,
    ya_send,
    ya_recv,
    gz_send,
    gz_recv,
    gx_send,
    gx_recv,
    gxb_send,
    gxb_recv,
    gy_send,
    gy_recv,
    gya_send,
    gya_recv,
    e_send,
    e_recv,
    own_sem,
    in_sem,
    cot_sem,
    out_sem,
    save_sem,
    load_sem,
    h_sem,
    ya_free,
    xb_free,
    x_free,
    y_free,
):
    place = Place(share)
    s, t, e, y = place.s, place.t, place.e, place.y
    primary, secondary = place.primary, jnp.logical_not(place.primary)
    width, frames = res.shape
    blocks = frames // BLOCK
    half = frames // 2
    quarter = half // 2
    rows = w.shape[3]
    low_rows = pl.ds(0, SPLIT)
    high_rows = pl.ds(SPLIT, rows - SPLIT)
    mine = pl.ds(pl.multiple_of(t * half, half), half)
    theirs = pl.ds(pl.multiple_of((1 - t) * half, half), half)

    own_loads = [pltpu.make_async_copy(vec_in, shard.at[:, pl.ds(VEC, QKV)], own_sem.at[0])]
    for number, (first, many, kind, bias) in enumerate(PARTS):
        own_loads.append(
            pltpu.make_async_copy(
                qkv_in.at[0, "qkv".index(kind), :, pl.ds(bias % WIDE, many)],
                shard.at[:, pl.ds(QKV + first, many)],
                own_sem.at[1 + number],
            )
        )
    own_up = pltpu.make_async_copy(up_in.at[0], shard.at[:, pl.ds(UP, DOWN - UP)], own_sem.at[7])
    own_out = pltpu.make_async_copy(out_in.at[0], flat.at[pl.ds(0, WIDE), :], own_sem.at[8])
    own_down = pltpu.make_async_copy(
        down_in.at[0], flat.at[pl.ds(WIDE, END - DOWN), :], own_sem.at[9]
    )
    for copy in own_loads + [own_out, own_up, own_down]:
        copy.start()

    place.greet()

    def gather_cols(piece):
        if isinstance(piece, int) and piece == 0:
            return pl.ds(VEC, QKV + WIDE)
        return pl.ds(pl.multiple_of(QKV + piece * WIDE, 128), WIDE)

    def z_copies(piece):
        cols = gather_cols(piece)
        copies = []
        for step in range(LINES):
            copies.append(
                remote(
                    shard.at[:, cols],
                    w.at[s, e, y, :, cols],
                    z_send.at[piece, step],
                    z_recv.at[s, piece, e],
                    (t, place.row_of(place.line(step), y), t),
                )
            )
        local = pltpu.make_async_copy(
            shard.at[:, cols], w.at[s, e, y, :, cols], z_recv.at[s, piece, e]
        )
        return copies, local

    def z_start(layer, piece):
        @pl.when(s == layer)
        def _():
            copies, local = z_copies(piece)

            @pl.when(primary)
            def _():
                local.start()

            @pl.when(secondary)
            def _():
                copies[0].start()

            for copy in copies[1:]:
                copy.start()

    def z_finish(piece):
        copies, _ = z_copies(piece)

        @pl.when(secondary)
        def _():
            copies[0].wait_send()

        for copy in copies[1:]:
            copy.wait_send()

    def x_copy(layer, piece):
        part = w.at[layer, :, y, :, gather_cols(piece)]
        return remote(part, part, x_send.at[layer, piece], x_recv.at[layer, piece], place.across)

    def y_copy(layer, piece):
        part = w.at[layer, :, y, :, gather_cols(piece)]
        return remote(part, part, y_send.at[layer, piece], y_recv.at[layer, piece], place.beside)

    def xb_copy(layer, piece):
        part = w.at[layer, :, 1 - y, high_rows, gather_cols(piece)]
        return remote(part, part, xb_send.at[layer, piece], xb_recv.at[layer, piece], place.across)

    def ya_copy(layer, piece):
        part = w.at[layer, :, y, low_rows, gather_cols(piece)]
        return remote(part, part, ya_send.at[layer, piece], ya_recv.at[layer, piece], place.beside)

    def step_z(layer, piece):
        @pl.when(primary)
        def _():
            for line in range(LINES):
                await_bytes(w.at[layer, line, y, :, gather_cols(piece)], z_recv.at[layer, piece, line])
            x_copy(layer, piece).start()
            y_copy(layer, piece).start()

    def step_plane(layer, piece):
        @pl.when(primary)
        def _():
            await_bytes(w.at[layer, :, 1 - y, :, gather_cols(piece)], y_recv.at[layer, piece])
            xb_copy(layer, piece).start()

        @pl.when(secondary)
        def _():
            await_bytes(w.at[layer, :, y, :, gather_cols(piece)], x_recv.at[layer, piece])
            ya_copy(layer, piece).start()

    def complete(layer, *pieces):
        @pl.when(secondary)
        def _():
            for piece in pieces:
                cols = gather_cols(piece)
                await_bytes(w.at[layer, :, 1 - y, high_rows, cols], xb_recv.at[layer, piece])
                await_bytes(w.at[layer, :, 1 - y, low_rows, cols], ya_recv.at[layer, piece])

    kept = {
        "x": (n2, x_hbm),
        "h": (res, h_hbm),
        "n1": (n1, n1_hbm),
        "n2": (n2, n2_hbm),
        "qkv": (qkv, qkv_hbm),
        "ctx": (ctx, ctx_hbm),
        "lse": (lse, lse_hbm),
        "act": (act, act_hbm),
        "slope": (slope, slope_hbm),
    }
    names = tuple(kept)

    def save(name, layer):
        src, dst = kept[name]
        if name in ("x", "h"):
            dst = dst.at[layer]
        return pltpu.make_async_copy(src, dst, save_sem.at[names.index(name), layer])

    def load(name, layer=0):
        dst, src = kept[name]
        if name == "x":
            dst, src = act.at[pl.ds(0, width), :], src.at[layer]
        return pltpu.make_async_copy(src, dst, load_sem.at[names.index(name)])

    def load_h(layer, index):
        slot = lax.rem(index, 2)
        return pltpu.make_async_copy(
            h_hbm.at[layer, :, block_of(index)], h_in.at[slot], h_sem.at[slot]
        )

    my_quarter = pl.ds(s * quarter, quarter)
    my_rows = pl.ds(pl.multiple_of((1 - t) * half + s * quarter, quarter), quarter)

    def clip_across():
        there = pl.ds(pl.multiple_of(t * half + s * quarter, quarter), quarter)
        return remote(
            clips.at[1 - t, my_quarter, :],
            stage.at[there, :],
            in_sem.at[0],
            in_sem.at[1],
            place.across,
        )

    def clip_core():
        part = stage.at[my_rows, :]
        return remote(part, part, in_sem.at[2], in_sem.at[3], place.core)

    def cot_across():
        return remote(
            cot.at[1 - t, my_quarter, :],
            cot_other.at[my_quarter, :],
            cot_sem.at[0],
            cot_sem.at[1],
            place.across,
        )

    def cot_core():
        part = cot_other.at[my_quarter, :]
        return remote(part, part, cot_sem.at[2], cot_sem.at[3], place.core)

    def exchange(kind, index, slot):
        return remote(
            send.at[kind, index],
            recv.at[kind, index],
            e_send.at[slot, index],
            e_recv.at[slot, index],
            place.core,
        )

    def result_copies(ref, first):
        local = pltpu.make_async_copy(stage.at[mine, :], ref.at[0, t], out_sem.at[first])
        away = remote(
            stage.at[theirs, :],
            ref.at[0, t],
            out_sem.at[first + 1],
            out_sem.at[first + 2],
            place.across,
        )
        return local, away

    def emit(layer, ref, first):
        @pl.when(s == layer)
        def _():
            for copy in result_copies(ref, first):
                copy.start()

    for copy in own_loads:
        copy.wait()
    for piece in range(3):
        z_start(0, piece)
    own_clip = pltpu.make_async_copy(clips.at[t], stage.at[mine, :], in_sem.at[4])
    own_clip.start()
    clip_across().start()
    cot_across().start()
    own_out.wait()
    shard[:, OUT:UP] = flat[0:WIDE, :].T
    own_up.wait()
    for piece in (3, 4):
        z_start(0, piece)

    def take_clip(first):
        def body(index, carry):
            at = pl.ds(pl.multiple_of(first + index * BLOCK, BLOCK), BLOCK)
            tile = stage[at, :].T
            n2[:, at] = tile
            res[:, at] = tile.astype(F32)
            return carry

        lax.fori_loop(0, half // BLOCK, body, 0)

    own_clip.wait()
    take_clip(t * half)
    own_down.wait()
    for piece in range(4):
        span = slice((1 + piece) * WIDE, (2 + piece) * WIDE)
        shard[:, DOWN + piece * WIDE : DOWN + (piece + 1) * WIDE] = flat[span, :].T
    clip_across().wait()
    clip_core().start()
    step_z(0, 0)
    z_start(0, 5)
    step_z(0, 1)
    z_start(0, 6)
    clip_core().wait()
    take_clip((1 - t) * half)
    save("x", 0).start()
    step_plane(0, 0)
    step_z(0, 2)
    z_start(0, 7)
    step_plane(0, 1)
    cot_across().wait()
    cot_core().start()
    step_z(0, 3)
    z_start(0, 8)
    step_plane(0, 2)

    def project(index):
        cols = block_of(index)
        mean, scale = norm_stats(lambda span: res[span, cols], width)
        for span in chunks_of(width):
            hat = (res[span, cols] - mean) * scale
            n1[span, cols] = (hat * vecs[span, 0:1] + vecs[span, 2:3]).astype(BF)
        for first, many, kind, bias in PARTS:
            value = mm(wt[first : first + many, :], n1[:, cols])
            for span in chunks_of(many):
                part = value[span, :]
                if kind != "k":
                    part = part + spread[bias + span.start : bias + span.stop, 6:7]
                if kind == "q":
                    part = part * 0.125
                qkv[first + span.start : first + span.stop, cols] = part.astype(BF)

    def head_rows(head, first):
        return pl.ds(pl.multiple_of(first + head * HEAD, HEAD), HEAD)

    def attend(layer):
        def heads_of(first_head, base, stride):
            def one_head(index_in, carry):
                head = first_head + index_in
                q_rows = head_rows(index_in, base)
                k_rows = head_rows(index_in, base + stride)
                v_rows = head_rows(index_in, base + 2 * stride)
                c_rows = head_rows(head, 0)
                keys = qkv[k_rows, :].T
                for index in range(blocks):
                    cols = slice(index * BLOCK, (index + 1) * BLOCK)
                    queries = qkv[q_rows, cols]
                    tiles = []
                    top = None
                    for tile in chunks_of(frames, BLOCK):
                        scores = mm(keys[tile, :], queries)
                        for span in chunks_of(BLOCK):
                            peak = stack_max(scores[span, :])
                            top = peak if top is None else jnp.maximum(top, peak)
                        tiles.append(scores)
                    top = jnp.max(top, 0, keepdims=True)
                    total = jnp.zeros((8, BLOCK), F32)
                    mixed = jnp.zeros((HEAD, BLOCK), F32)
                    for tile, scores in zip(chunks_of(frames, BLOCK), tiles):
                        soft = []
                        for span in chunks_of(BLOCK):
                            part = jnp.exp(scores[span, :] - top)
                            total = total + stack_sum(part)
                            soft.append(part.astype(BF))
                        mixed = mixed + mm(qkv[v_rows, tile], jnp.concatenate(soft, 0))
                    total = jnp.sum(total, 0, keepdims=True)
                    ctx[c_rows, cols] = (mixed / total).astype(BF)
                    lse[pl.ds(head, 1), cols] = top + jnp.log(total)
                step_z(layer, 5 + head)
                step_plane(layer, 4 + head)
                return carry

            return one_head

        lax.fori_loop(0, 4, heads_of(0, 0, 256), 0)
        lax.fori_loop(0, 2, heads_of(4, 768, 128), 0)

    def out_project(layer):
        def body(index, carry):
            part = mm(whole(w, layer, OUT, 384), ctx[:, block_of(index)])
            send[0, index] = part.astype(BF)
            exchange(0, index, 2 * layer).start()
            return carry

        lax.fori_loop(0, blocks, body, 0)

    def middle_norm(layer):
        def body(index, carry):
            cols = block_of(index)
            exchange(0, index, 2 * layer).wait()
            for span in chunks_of(width):
                added = send[0, index, span, :].astype(F32) + recv[0, index, span, :].astype(F32)
                res[span, cols] = res[span, cols] + added + vecs[span, 3:4]
            mean, scale = norm_stats(lambda span: res[span, cols], width)
            for span in chunks_of(width):
                hat = (res[span, cols] - mean) * scale
                n2[span, cols] = (hat * vecs[span, 1:2] + vecs[span, 4:5]).astype(BF)
            return carry

        lax.fori_loop(0, blocks, body, 0)

    def hidden_part(layer, part):
        flip_weights(w, wt, layer, UP + part * WIDE, WIDE, part * WIDE)
        units = slice(part * WIDE, (part + 1) * WIDE)
        lane = 7 if part < 2 else 8

        def body(index, carry):
            cols = block_of(index)
            pre = mm(wt[units, :], n2[:, cols])
            for span in chunks_of(WIDE):
                first = part * WIDE + span.start
                bias = spread[768 + first : 768 + first + ROWS, lane : lane + 1]
                value, steep = gelu_parts(pre[span, :] + bias)
                act[first : first + ROWS, cols] = value.astype(BF)
                slope[first : first + ROWS, cols] = steep.astype(BF)
            return carry

        lax.fori_loop(0, blocks, body, 0)

    def down_project(layer):
        def body(index, carry):
            part = mm(whole(w, layer, DOWN, 1536), act[:, block_of(index)])
            send[1, index] = part.astype(BF)
            exchange(1, index, 2 * layer + 1).start()
            return carry

        lax.fori_loop(0, blocks, body, 0)

    def layer_end(layer, index, span):
        added = send[1, index, span, :].astype(F32) + recv[1, index, span, :].astype(F32)
        return (res[span, block_of(index)] + added + vecs[span, 5:6]).astype(BF)

    def take_vectors(layer):
        vecs[...] = whole(w, layer, VEC, 128).astype(F32)
        spread_biases(vecs, spread, rows)

    def project_all(layer):
        flip_weights(w, wt, layer, QKV, 1152)

        def body(index, carry):
            project(index)
            return carry

        lax.fori_loop(0, blocks, body, 0)
        if layer == 0:
            save("n1", 0).start()
            save("qkv", 0).start()

    complete(0, 0, 1, 2)
    take_vectors(0)
    project_all(0)
    step_z(0, 4)
    step_plane(0, 3)
    for piece in (9, 10, 11):
        z_start(0, piece)
    cot_core().wait()
    load_cot = pltpu.make_async_copy(cot_other, stage.at[theirs, :], cot_sem.at[4])
    load_cot.start()
    own_cot = pltpu.make_async_copy(cot.at[t], stage.at[mine, :], cot_sem.at[5])
    own_cot.start()
    attend(0)
    save("ctx", 0).start()
    save("lse", 0).start()
    complete(0, 3)
    out_project(0)
    step_z(0, 11)
    step_plane(0, 10)
    for piece in (0, 1, 2):
        z_start(1, piece)
    load_cot.wait()
    own_cot.wait()

    def take_cot(index, carry):
        low[:, block_of(index)] = stage[block_of(index), :].T
        return carry

    lax.fori_loop(0, blocks, take_cot, 0)
    save("x", 0).wait()
    middle_norm(0)
    save("h", 0).start()
    save("n2", 0).start()
    for part in range(4):
        complete(0, 4 + part)
        hidden_part(0, part)
        step_z(1, part)
        if part == 0:
            step_plane(0, 11)
        else:
            step_plane(1, part - 1)
        z_start(1, part + 3)
    save("act", 0).start()
    save("slope", 0).start()
    complete(0, 8, 9, 10, 11)
    down_project(0)
    step_z(1, 4)
    step_plane(1, 3)
    z_start(1, 7)
    z_start(1, 8)
    for name in ("n1", "qkv", "h", "n2"):
        save(name, 0).wait()

    def finish_body(index, carry):
        exchange(1, index, 1).wait()
        cols = block_of(index)
        for span in chunks_of(width):
            rows_out = layer_end(0, index, span)
            n2[span, cols] = rows_out
            res[span, cols] = rows_out.astype(F32)

        @pl.when(s == 0)
        def _():
            stage[cols, :] = n2[:, cols].T

        return carry

    lax.fori_loop(0, blocks, finish_body, 0)
    emit(0, out, 0)
    save("x", 1).start()
    complete(1, 0, 1, 2)
    take_vectors(1)
    project_all(1)
    for piece in (9, 10, 11):
        z_start(1, piece)
    save("ctx", 0).wait()
    save("lse", 0).wait()
    attend(1)
    complete(1, 3)
    out_project(1)
    step_z(1, 11)
    step_plane(1, 10)
    save("x", 1).wait()
    middle_norm(1)
    save("h", 1).start()
    save("act", 0).wait()
    save("slope", 0).wait()
    for part in range(4):
        complete(1, 4 + part)
        hidden_part(1, part)
        if part == 0:
            step_plane(1, 11)
    complete(1, 8, 9, 10, 11)
    down_project(1)
    flip_weights(w, wt, 1, DOWN, 1536)

    def last_body(index, carry):
        exchange(1, index, 3).wait()

        @pl.when(s == 1)
        def _():
            for span in chunks_of(width, 128):
                stage[block_of(index), span] = layer_end(1, index, span).T

        return carry

    lax.fori_loop(0, blocks, last_body, 0)
    emit(1, out, 0)
    save("h", 1).wait()

    VECTORS = CHUNKS

    def grad_cols(piece):
        if isinstance(piece, int) and piece == VECTORS:
            return pl.ds(VEC, QKV)
        return pl.ds(pl.multiple_of(QKV + piece * WIDE, 128), WIDE)

    def gya_copy(layer, piece):
        cols = grad_cols(piece)
        return remote(
            w.at[layer, :, 1 - y, low_rows, cols],
            land_a.at[:, low_rows, cols],
            gya_send.at[layer, piece],
            gya_recv.at[layer, piece],
            place.beside,
        )

    def gxb_copy(layer, piece):
        cols = grad_cols(piece)
        return remote(
            w.at[layer, :, 1 - y, high_rows, cols],
            land_b.at[:, :, cols],
            gxb_send.at[layer, piece],
            gxb_recv.at[layer, piece],
            place.across,
        )

    def gx_copy(layer, piece):
        cols = grad_cols(piece)
        return remote(
            w.at[layer, :, y, :, cols],
            land_a.at[:, :, cols],
            gx_send.at[layer, piece],
            gx_recv.at[layer, piece],
            place.across,
        )

    def gy_copy(layer, piece):
        cols = grad_cols(piece)
        return remote(
            w.at[layer, :, 1 - y, :, cols],
            land_y.at[:, :, cols],
            gy_send.at[layer, piece],
            gy_recv.at[layer, piece],
            place.beside,
        )

    def landed_part(piece):
        if piece == VECTORS:
            return landed_vec
        ref, first = (
            (landed_qkv, 0)
            if piece < 3
            else (landed_out, 3)
            if piece < 4
            else (landed_up, 4)
            if piece < 8
            else (landed_down, 8)
        )
        return ref.at[:, :, pl.ds((piece - first) * WIDE, WIDE)]

    def gz_copies(layer, piece):
        cols = grad_cols(piece)
        target = landed_part(piece)
        copies = []
        for step in range(LINES):
            line = place.line(step)
            copies.append(
                remote(
                    w.at[layer, line, y, :, cols],
                    target.at[e],
                    gz_send.at[layer, piece, step],
                    gz_recv.at[piece, e],
                    (layer, place.row_of(line, y), t),
                )
            )
        local = pltpu.make_async_copy(
            w.at[layer, e, y, :, cols], target.at[e], gz_recv.at[piece, e]
        )
        return copies, local

    def add_rows(layer, piece, which, span, lands):
        cols = grad_cols(piece)
        first, count = span
        for line in range(LINES):
            total = w[layer, line, which, pl.ds(first, count), cols].astype(F32)
            for land, offset in lands:
                total = total + land[line, pl.ds(offset, count), cols].astype(F32)
            w[layer, line, which, pl.ds(first, count), cols] = total.astype(BF)

    def signal(sem, layer, piece, device):
        if layer == 1:
            pl.semaphore_signal(sem.at[piece], inc=1, device_id=device, device_id_type=MESH)

    def credit(sem, layer, piece):
        if layer == 0:
            pl.semaphore_wait(sem.at[piece], 1)

    def step_a(layer, piece):
        @pl.when(secondary)
        def _():
            credit(ya_free, layer, piece)
            gya_copy(layer, piece).start()
            credit(xb_free, layer, piece)
            gxb_copy(layer, piece).start()

    def step_b(layer, piece):
        cols = grad_cols(piece)

        @pl.when(secondary)
        def _():
            await_bytes(land_a.at[:, low_rows, cols], gya_recv.at[layer, piece])
            add_rows(layer, piece, y, (0, SPLIT), [(land_a, 0)])
            signal(ya_free, layer, piece, place.beside)
            credit(x_free, layer, piece)
            gx_copy(layer, piece).start()

        @pl.when(primary)
        def _():
            await_bytes(land_b.at[:, :, cols], gxb_recv.at[layer, piece])
            add_rows(layer, piece, 1 - y, (SPLIT, rows - SPLIT), [(land_b, 0)])
            signal(xb_free, layer, piece, place.across)
            credit(y_free, layer, piece)
            gy_copy(layer, piece).start()

    def step_c(layer, piece):
        cols = grad_cols(piece)

        @pl.when(primary)
        def _():
            await_bytes(land_a.at[:, :, cols], gx_recv.at[layer, piece])
            await_bytes(land_y.at[:, :, cols], gy_recv.at[layer, piece])
            add_rows(layer, piece, y, (0, rows), [(land_a, 0), (land_y, 0)])
            signal(x_free, layer, piece, place.across)
            signal(y_free, layer, piece, place.beside)
            copies, local = gz_copies(layer, piece)

            @pl.when(s == layer)
            def _():
                local.start()

            @pl.when(s != layer)
            def _():
                copies[0].start()

            for copy in copies[1:]:
                copy.start()

    def store_grads(layer, start, count, value):
        w[layer, :, :, :, pl.ds(start, count)] = value.astype(BF).reshape(
            w.shape[1], w.shape[2], rows, count
        )

    ones = functools.partial(jnp.ones, (frames, 128), BF)

    def mlp_back(layer, beside):
        def body(index, carry):
            cols = block_of(index)
            for part in range(4):
                units = slice(part * WIDE, (part + 1) * WIDE)
                grad = mm(wt[units, :], low[:, cols])
                for span in chunks_of(WIDE):
                    rows_in = slice(units.start + span.start, units.start + span.stop)
                    steep = slope[rows_in, cols].astype(F32)
                    slope[rows_in, cols] = (grad[span, :] * steep).astype(BF)
            term = mm(whole(w, layer, UP, 1536), slope[:, cols])
            send[0, index] = term.astype(BF)
            exchange(0, index, 4 + 2 * layer).start()
            beside(index)
            return carry

        lax.fori_loop(0, blocks, body, 0)

    def outer_pair(layer, start, left, right, first, beside):
        def body(index, carry):
            for part in range(3):
                base = index * 768 + part * 256
                span = pl.ds(pl.multiple_of(base, 256), 256)
                value = mmt(left[...], right[span, :])
                store_grads(layer, pl.multiple_of(start + base, 128), 256, value)
            step_a(layer, first + 2 * index)
            step_a(layer, first + 2 * index + 1)
            beside(index)
            return carry

        lax.fori_loop(0, 2, body, 0)

    def fold(value):
        return value[:, 0:128] + value[:, 128:256]

    def norm_back(layer, kind, gain_lane, source, put, finish, beside):
        sums[...] = jnp.zeros_like(sums)

        def body(index, carry):
            cols = block_of(index)
            read = source(index)
            mean, scale = norm_stats(read, width)
            exchange(kind, index, 4 + 2 * layer + kind).wait()
            first = jnp.zeros((8, BLOCK), F32)
            second = jnp.zeros((8, BLOCK), F32)

            def terms(span):
                hat = (read(span) - mean) * scale
                grad = send[kind, index, span, :].astype(F32)
                grad = grad + recv[kind, index, span, :].astype(F32)
                return hat, grad, grad * vecs[span, gain_lane : gain_lane + 1]

            for span in chunks_of(width):
                hat, grad, scaled = terms(span)
                sums[0, span, :] += fold(grad * hat)
                sums[1, span, :] += fold(grad)
                first = first + stack_sum(scaled)
                second = second + stack_sum(scaled * hat)
            level = mean_of(first, width)
            slant = mean_of(second, width)
            for span in chunks_of(width):
                hat, _, scaled = terms(span)
                put(span, cols, res[span, cols] + scale * (scaled - level - hat * slant))
            finish(cols)
            beside(index)
            return carry

        lax.fori_loop(0, blocks, body, 0)

    def row_sums(value):
        return jnp.sum(value, 1, keepdims=True)

    def attend_back(first_head, many, base, stride, beside):
        def one_head(index_in, carry):
            head = first_head + index_in
            q_rows = head_rows(index_in, base)
            k_rows = head_rows(index_in, base + stride)
            v_rows = head_rows(index_in, base + 2 * stride)
            c_rows = head_rows(head, 0)
            keys = qkv[k_rows, :].T
            values = qkv[v_rows, :].T
            key_totals = [jnp.zeros((HEAD, BLOCK), F32)] * blocks
            value_totals = [jnp.zeros((HEAD, BLOCK), F32)] * blocks
            for index in range(blocks):
                cols = slice(index * BLOCK, (index + 1) * BLOCK)
                queries = qkv[q_rows, cols]
                grads = dctx[c_rows, cols]
                level = lse[pl.ds(head, 1), cols]
                inner = jnp.sum(
                    grads.astype(F32) * ctx[c_rows, cols].astype(F32), 0, keepdims=True
                )
                step = jnp.zeros((HEAD, BLOCK), F32)
                for tile in range(blocks):
                    span = slice(tile * BLOCK, (tile + 1) * BLOCK)
                    scores = mm(keys[span, :], queries)
                    soft_grad = mm(values[span, :], grads)
                    soft = []
                    score_grad = []
                    for part in chunks_of(BLOCK):
                        strength = jnp.exp(scores[part, :] - level)
                        soft.append(strength.astype(BF))
                        score_grad.append((strength * (soft_grad[part, :] - inner)).astype(BF))
                    soft = jnp.concatenate(soft, 0)
                    score_grad = jnp.concatenate(score_grad, 0)
                    step = step + mm(qkv[k_rows, span], score_grad)
                    key_totals[tile] = key_totals[tile] + mmt(queries, score_grad)
                    value_totals[tile] = value_totals[tile] + mmt(grads, soft)
                slope[q_rows, cols] = (step * 0.125).astype(BF)
            for tile in range(blocks):
                span = slice(tile * BLOCK, (tile + 1) * BLOCK)
                slope[k_rows, span] = key_totals[tile].astype(BF)
                slope[v_rows, span] = value_totals[tile].astype(BF)
            beside(index_in)
            return carry

        lax.fori_loop(0, many, one_head, 0)

    def collect_biases():
        def body(group, carry):
            source = group * rows
            for kind in range(2):
                for head in range(6):
                    at = pl.ds(pl.multiple_of(kind * 384 + head * HEAD + group * 8, 8), 8)
                    to = pl.ds(pl.multiple_of(source + kind * 48 + head * 8, 8), 8)
                    vec_grads[to, 6:7] = spread[at, 6:7]
            for unit in range(24):
                at = pl.ds(pl.multiple_of(768 + unit * HEAD + group * 8, 8), 8)
                to = pl.ds(pl.multiple_of(source + (unit % 12) * 8, 8), 8)
                lane = 7 if unit < 12 else 8
                vec_grads[to, lane : lane + 1] = spread[at, lane : lane + 1]
            return carry

        lax.fori_loop(0, GROUPS, body, 0)

    def nothing(index):
        del index

    def at_turns(turns):
        def beside(index):
            for turn, steps in turns.items():

                @pl.when(index == turn)
                def _():
                    for step in steps:
                        step()

        return beside

    def finish_gather(piece):
        z_finish(piece)
        for layer in range(2):

            @pl.when(primary)
            def _():
                x_copy(layer, piece).wait_send()
                y_copy(layer, piece).wait_send()
                xb_copy(layer, piece).wait_send()

            @pl.when(secondary)
            def _():
                ya_copy(layer, piece).wait_send()

    def finish_body_gather(piece, carry):
        finish_gather(piece)
        return carry

    res[...] = low[...].astype(F32)

    for layer in (1, 0):
        later = layer == 0
        load_h(layer, 0).start()
        if later:
            vecs[...] = whole(w, layer, VEC, 128).astype(F32)
            flip_weights(w, wt, layer, DOWN, 1536)
            load("slope").wait()
        vec_grads[...] = jnp.zeros_like(vec_grads)

        early = at_turns({0: (lambda: step_b(1, VECTORS),), 1: (lambda: step_c(1, VECTORS),)})
        mlp_back(layer, early if later else nothing)
        if not later:
            finish_gather(0)
            lax.fori_loop(1, CHUNKS, finish_body_gather, 0)
        if later:
            load("act").wait()
        outer_pair(layer, DOWN, low, act, 8, nothing)
        load("x", layer).start()
        if later:
            load("n2").wait()
        vec_grads[:, 5:6] = mm(low[...], ones())[:, 0:1]

        def b(piece, layer=layer):
            return lambda: step_b(layer, piece)

        def c(piece, layer=layer):
            return lambda: step_c(layer, piece)

        outer_pair(layer, UP, n2, slope, 4, at_turns({1: (b(8), b(9))}))
        spread[768:, :] = mm(slope[...], ones())
        flip_weights(w, wt, layer, OUT, 384)

        def hidden_in(index, layer=layer):
            @pl.when(index + 1 < blocks)
            def _():
                load_h(layer, index + 1).start()

            load_h(layer, index).wait()
            slot = lax.rem(index, 2)
            return lambda span: h_in[slot, span, :]

        def hidden_put(span, cols, total):
            res[span, cols] = total
            low[span, cols] = total.astype(BF)

        def hidden_out(cols):
            dctx[:, cols] = mm(wt[0:384, :], low[:, cols]).astype(BF)

        drain = at_turns({0: (b(10),), 1: (b(11),), 2: (b(4), c(8)), 3: (b(5), c(9))})
        norm_back(layer, 0, 1, hidden_in, hidden_put, hidden_out, drain)
        vec_grads[:, 1:2] = row_sums(sums[0])
        vec_grads[:, 4:5] = row_sums(sums[1])
        vec_grads[:, 3:4] = mm(low[...], ones())[:, 0:1]
        if later:
            for name in ("ctx", "qkv", "lse"):
                load(name).wait()
        store_grads(layer, OUT, 384, mmt(low[...], ctx[...]))
        step_a(layer, 3)
        step_b(layer, 6)
        step_c(layer, 10)
        drain = at_turns({0: (b(7), c(11)), 1: (b(3), c(4)), 2: (c(5),), 3: (c(6),)})
        attend_back(0, 4, 0, 256, drain)
        if later:
            load("n1").wait()
        wt[0:768, :] = whole(w, layer, QKV, 768)

        def qkv_body(index, carry, layer=layer):
            span = pl.ds(pl.multiple_of(index * 256, 256), 256)
            value = mmt(n1[...], slope[span, :])
            store_grads(layer, pl.multiple_of(QKV + index * 256, 128), 256, value)
            return carry

        lax.fori_loop(0, 3, qkv_body, 0)
        step_a(layer, 0)
        step_a(layer, 1)
        step_c(layer, 7)
        attend_back(4, 2, 768, 128, at_turns({0: (b(0), c(3)), 1: (b(1),)}))

        def first_body(index, carry, layer=layer):
            cols = block_of(index)
            term = mm(wt[0:768, :], slope[0:768, cols])
            term = term + mm(whole(w, layer, QKV + 768, WIDE), slope[768:1152, cols])
            send[1, index] = term.astype(BF)
            exchange(1, index, 5 + 2 * layer).start()
            return carry

        lax.fori_loop(0, blocks, first_body, 0)
        store_grads(layer, QKV + 768, WIDE, mmt(n1[...], slope[768:1152, :]))
        step_a(layer, 2)
        step_c(layer, 0)
        for first, many, kind, bias in PARTS:
            if kind != "k":
                spread[bias : bias + many, :] = mm(slope[first : first + many, :], ones())
        collect_biases()
        if layer == 1:
            for name in ("slope", "n1", "n2", "ctx", "qkv", "lse"):
                load(name).start()
        load("x", layer).wait()

        @pl.when(s == layer)
        def _():
            local, away = result_copies(out, 0)
            local.wait()
            away.wait_send()

        def rows_x(index):
            return lambda span: act[span, block_of(index)].astype(F32)

        def rows_put(span, cols, total, layer=layer):
            rounded = total.astype(BF)
            low[span, cols] = rounded
            if layer == 1:
                res[span, cols] = rounded.astype(F32)

        def rows_out(cols, layer=layer):
            @pl.when(s == layer)
            def _():
                stage[cols, :] = low[:, cols].T

        drain = at_turns({0: (c(1),), 1: (b(2),), 3: (c(2),)})
        norm_back(layer, 1, 0, rows_x, rows_put, rows_out, drain)
        emit(layer, in_grad, 3)
        if layer == 1:
            load("act").start()
        vec_grads[:, 0:1] = row_sums(sums[0])
        vec_grads[:, 2:3] = row_sums(sums[1])
        store_grads(layer, VEC, 128, vec_grads[...])
        step_a(layer, VECTORS)

    step_b(0, VECTORS)
    step_c(0, VECTORS)

    def finish_scatter(piece):
        for layer in range(2):

            @pl.when(secondary)
            def _():
                gya_copy(layer, piece).wait_send()
                gxb_copy(layer, piece).wait_send()
                gx_copy(layer, piece).wait_send()

            @pl.when(primary)
            def _():
                gy_copy(layer, piece).wait_send()
                copies, _ = gz_copies(layer, piece)

                @pl.when(s != layer)
                def _():
                    copies[0].wait_send()

                for copy in copies[1:]:
                    copy.wait_send()

    for piece in range(CHUNKS + 1):
        finish_scatter(piece)
        for line in range(LINES):
            await_bytes(landed_part(piece).at[line], gz_recv.at[piece, line])

    _, away = result_copies(out, 0)
    away.wait_recv()
    local, away = result_copies(in_grad, 3)
    local.wait()
    away.wait()


def layers_call(share, clips, cotangent, shards, dims):
    width, frames, hidden_units, heads_width = dims
    rows = width // GROUPS
    sem = pltpu.SemaphoreType.DMA
    free = pltpu.SemaphoreType.REGULAR
    packed = (2, LINES, 2, rows, END)
    blocks = frames // BLOCK
    shape = jax.ShapeDtypeStruct
    outs = [
        shape((1,) + clips.shape, BF),
        shape((1,) + clips.shape, BF),
        shape((LINES, rows, QKV - VEC), BF),
        shape((LINES, rows, OUT - QKV), BF),
        shape((LINES, rows, UP - OUT), BF),
        shape((LINES, rows, DOWN - UP), BF),
        shape((LINES, rows, END - DOWN), BF),
        shape(clips.shape[1:], BF),
        shape((2, width, frames), BF),
        shape((2, width, frames), F32),
        shape((width, frames), BF),
        shape((width, frames), BF),
        shape((3 * heads_width, frames), BF),
        shape((heads_width, frames), BF),
        shape((8, frames), F32),
        shape((hidden_units, frames), BF),
        shape((hidden_units, frames), BF),
    ]
    scratch = [
        pltpu.VMEM(packed, BF),
        pltpu.VMEM((width, frames), F32),
        pltpu.VMEM((hidden_units, frames), BF),
        pltpu.VMEM((hidden_units, frames), BF),
        pltpu.VMEM((width, frames), BF),
        pltpu.VMEM((width, frames), BF),
        pltpu.VMEM((width, frames), BF),
        pltpu.VMEM((3 * heads_width, frames), BF),
        pltpu.VMEM((heads_width, frames), BF),
        pltpu.VMEM((heads_width, frames), BF),
        pltpu.VMEM((8, frames), F32),
        pltpu.VMEM((2, width, BLOCK), F32),
        pltpu.VMEM((hidden_units, width), BF),
        pltpu.VMEM((2, blocks, width, BLOCK), BF),
        pltpu.VMEM((2, blocks, width, BLOCK), BF),
        pltpu.VMEM((width, 128), F32),
        pltpu.VMEM((width, 128), F32),
        pltpu.VMEM((2, width, 128), F32),
        pltpu.VMEM((2 * heads_width + hidden_units, 128), F32),
        pltpu.VMEM((frames, width), BF),
        pltpu.VMEM((rows, END), BF),
        pltpu.VMEM((WIDE + END - DOWN, rows), BF),
        pltpu.VMEM((LINES, rows, END), BF),
        pltpu.VMEM((LINES, rows - SPLIT, END), BF),
        pltpu.VMEM((LINES, rows, END), BF),
    ]
    scratch += [sem((CHUNKS, LINES)), sem((2, CHUNKS, LINES))]
    scratch += [sem((2, CHUNKS))] * 8
    scratch += [sem((2, CHUNKS + 1, LINES)), sem((CHUNKS + 1, LINES))]
    scratch += [sem((2, CHUNKS + 1))] * 8
    scratch += [
        sem((8, blocks)),
        sem((8, blocks)),
        sem((10,)),
        sem((5,)),
        sem((6,)),
        sem((6,)),
        sem((9, 2)),
        sem((9,)),
        sem((2,)),
    ]
    scratch += [free((CHUNKS + 1,))] * 4
    anywhere = pl.BlockSpec(memory_space=pl.ANY)
    return pl.pallas_call(
        functools.partial(layers_kernel, share),
        out_shape=outs,
        in_specs=[anywhere] * (2 + len(shards)),
        out_specs=[anywhere] * len(outs),
        scratch_shapes=scratch,
        compiler_params=pltpu.CompilerParams(
            collective_id=0, has_side_effects=True, vmem_limit_bytes=VMEM_LIMIT
        ),
        cost_estimate=pl.CostEstimate(
            flops=60_000_000_000, bytes_accessed=60_000_000, transcendentals=0
        ),
    )(clips, cotangent, *shards)


def group_piece(value, axis, share):
    if share == 1:
        return value
    size = value.shape[axis] * share
    group = lax.axis_index("dp") // share
    full = lax.all_gather(value, "dp", axis=axis, tiled=True)
    return lax.dynamic_slice_in_dim(full, group * size, size, axis)


def own_part(value, axis, share, parts, index):
    size = value.shape[axis] // parts
    if parts == 1:
        return value
    return lax.dynamic_slice_in_dim(value, index * size, size, axis)


def on_device(share, clips, cotangent, ln_gains, row_biases, w_qkv, b_qv, w_o, w_up, b_ff, w_down):
    width = clips.shape[2]
    rows = width // GROUPS
    dims = (width, 2 * clips.shape[1], w_up.shape[2], w_o.shape[1])
    ln_gains = group_piece(ln_gains, 2, share)
    row_biases = group_piece(row_biases, 2, share)
    w_qkv = group_piece(w_qkv, 2, share)
    b_qv = group_piece(b_qv, 3, share)
    w_o = group_piece(w_o, 2, share)
    w_up = group_piece(w_up, 1, share)
    b_ff = group_piece(b_ff, 2, share)
    w_down = group_piece(w_down, 2, share)
    vectors = jnp.concatenate([ln_gains[0], row_biases[0]], 0).T
    heads = jnp.concatenate([b_qv[0, 0].reshape(-1), b_qv[0, 1].reshape(-1)])[:, None]
    units = b_ff[0].reshape(2, rows).T
    packed = jnp.concatenate([vectors, heads, units], 1)
    packed = jnp.pad(packed, ((0, 0), (0, 128 - packed.shape[1])))
    section_out, section_in_grad, *landed = layers_call(
        share, clips, cotangent, (packed, w_qkv, w_o, w_up, w_down), dims
    )
    rest = lax.axis_index("dp") % share
    side = lax.axis_index("tensor")

    def joined(value):
        total = jnp.sum(value.astype(F32), 0)
        if share == 1:
            return total
        group = lax.axis_index("dp") // share
        padded = jnp.zeros((width, total.shape[1]), F32)
        padded = lax.dynamic_update_slice_in_dim(padded, total, group * rows, 0)
        return lax.dynamic_slice_in_dim(lax.psum(padded, "dp"), group * rows, rows, 0)

    def mine(value):
        return own_part(joined(value), 0, share, share, rest)

    vectors = joined(landed[0])
    vec = own_part(own_part(vectors, 0, share, share, rest), 0, share, 2, side)
    heads_grad = vectors[:, 6].reshape(2, -1, HEAD // GROUPS)
    units_grad = vectors[:, 7:9].T.reshape(-1, HEAD // GROUPS)
    qkv_grad = {"q": [], "k": [], "v": []}
    for first, many, kind, _ in PARTS:
        qkv_grad[kind].append(mine(landed[1][:, :, first : first + many]))
    return (
        section_out,
        section_in_grad,
        vec[:, 0:2].T[None],
        vec[:, 2:6].T[None],
        jnp.stack([jnp.concatenate(qkv_grad[kind], 1) for kind in "qkv"])[None],
        own_part(heads_grad, 2, share, share, rest)[None],
        mine(landed[2]).T[None],
        mine(landed[3])[None],
        own_part(units_grad, 1, share, share, rest)[None],
        mine(landed[4]).T[None],
    )


def solution(mesh):
    placed = (
        P("dp", "tensor", None),
        P("dp", "tensor", None),
        P("section", None, "dp"),
        P("section", None, "dp"),
        P("section", None, "dp", "tensor"),
        P("section", None, "tensor", "dp"),
        P("section", "tensor", "dp"),
        P("section", "dp", "tensor"),
        P("section", "tensor", "dp"),
        P("section", "tensor", "dp"),
    )
    share = mesh.shape["dp"] // GROUPS
    return jax.shard_map(
        functools.partial(on_device, share),
        mesh=mesh,
        in_specs=placed,
        out_specs=(
            P("section", "dp", "tensor", None),
            P("section", "dp", "tensor", None),
            P("section", None, ("dp", "tensor")),
            P("section", None, ("dp", "tensor")),
            P("section", None, "dp", "tensor"),
            P("section", None, "tensor", "dp"),
            P("section", "tensor", "dp"),
            P("section", "dp", "tensor"),
            P("section", "tensor", "dp"),
            P("section", "tensor", "dp"),
        ),
        check_vma=False,
    )
```

```python
import functools

import jax
import jax.numpy as jnp
from jax import lax
from jax.experimental import pallas as pl
from jax.experimental.pallas import tpu as pltpu
from jax.sharding import PartitionSpec as P

BF = jnp.bfloat16
F32 = jnp.float32
MESH = pl.DeviceIdType.MESH
EPSILON = 1e-05
HEAD = 64
GROUPS = 8
LINES = 4
BLOCK = 256
ROWS = 64
VMEM_LIMIT = 62 * 1024 * 1024

VEC = 0
QKV = 128
OUT = 1280
UP = 1664
DOWN = 3200
END = 4736
SPLIT = 48
WIDE = 384
CHUNKS = 12


PARTS = (
    (0, 256, "q", 0),
    (256, 256, "k", 0),
    (512, 256, "v", 384),
    (768, 128, "q", 256),
    (896, 128, "k", 256),
    (1024, 128, "v", 640),
)


def mm(left, right):
    return jnp.dot(left, right, preferred_element_type=F32)


def mmt(left, right):
    return lax.dot_general(left, right, (((1,), (1,)), ((), ())), preferred_element_type=F32)


class Place:
    def __init__(self, share):
        self.s = lax.axis_index("section")
        self.d = lax.axis_index("dp")
        self.t = lax.axis_index("tensor")
        group = self.d // share
        self.rest = self.d - group * share
        self.share = share
        self.e = group // 2
        self.y = group - self.e * 2
        self.primary = self.s == self.t
        self.core = (1 - self.s, self.d, self.t)
        self.across = (self.s, self.d, 1 - self.t)
        self.beside = (self.s, self.row_of(self.e, 1 - self.y), self.t)

    def row_of(self, line, y):
        return (line * 2 + y) * self.share + self.rest

    def line(self, step):
        return lax.rem(self.e + step, LINES)

    def greet(self):
        barrier = pltpu.get_barrier_semaphore()
        peers = [self.core, self.across, self.beside]
        for step in range(1, LINES):
            for section in range(2):
                peers.append((section, self.row_of(self.line(step), self.y), self.t))
        for peer in peers:
            pl.semaphore_signal(barrier, inc=1, device_id=peer, device_id_type=MESH)
        pl.semaphore_wait(barrier, len(peers))


def remote(src, dst, send_sem, recv_sem, device):
    return pltpu.make_async_remote_copy(
        src_ref=src,
        dst_ref=dst,
        send_sem=send_sem,
        recv_sem=recv_sem,
        device_id=device,
        device_id_type=MESH,
    )


def await_bytes(ref, sem):
    pltpu.make_async_copy(ref, ref, sem).wait()


def chunks_of(count, size=ROWS):
    return [slice(first, first + size) for first in range(0, count, size)]


def by_eights(value):
    return value.reshape(value.shape[0] // 8, 8, value.shape[1])


def stack_sum(value):
    return jnp.sum(by_eights(value), 0)


def stack_max(value):
    return jnp.max(by_eights(value), 0)


def mean_of(parts, count):
    return jnp.sum(parts, 0, keepdims=True) / count


def norm_stats(read, count):
    total = jnp.zeros((8, BLOCK), F32)
    for span in chunks_of(count):
        total = total + stack_sum(read(span))
    mean = mean_of(total, count)
    square = jnp.zeros((8, BLOCK), F32)
    for span in chunks_of(count):
        centred = read(span) - mean
        square = square + stack_sum(centred * centred)
    return mean, lax.rsqrt(mean_of(square, count) + EPSILON)


def gelu_parts(values):
    bell = jnp.exp(-0.5 * values * values)
    reach = jnp.abs(values) * 0.7071067811865476
    inv = 1.0 / (1.0 + 0.3275911 * reach)
    poly = inv * (
        0.254829592
        + inv * (-0.284496736 + inv * (1.421413741 + inv * (-1.453152027 + inv * 1.061405429)))
    )
    tail = 0.5 * poly * bell
    cdf = jnp.where(values >= 0.0, 1.0 - tail, tail)
    return values * cdf, cdf + values * bell * 0.3989422804014327


def block_of(index):
    return pl.ds(pl.multiple_of(index * BLOCK, BLOCK), BLOCK)


def flip_weights(w, wt, layer, start, width, target=0):
    def body(index, carry):
        cols = pl.ds(pl.multiple_of(start + index * 128, 128), 128)
        rows = pl.ds(pl.multiple_of(target + index * 128, 128), 128)
        tile = w[layer, :, :, :, cols]
        wt[rows, :] = tile.reshape(tile.shape[0] * tile.shape[1] * tile.shape[2], 128).T
        return carry

    lax.fori_loop(0, width // 128, body, 0)


def whole(w, layer, start, width):
    tile = w[layer, :, :, :, start : start + width]
    return tile.reshape(tile.shape[0] * tile.shape[1] * tile.shape[2], width)


def spread_biases(vecs, spread, rows):
    def body(group, carry):
        source = group * rows
        for kind in range(2):
            for head in range(6):
                to = pl.ds(pl.multiple_of(kind * 384 + head * HEAD + group * 8, 8), 8)
                at = pl.ds(pl.multiple_of(source + kind * 48 + head * 8, 8), 8)
                spread[to, :] = vecs[at, :]
        for unit in range(24):
            to = pl.ds(pl.multiple_of(768 + unit * HEAD + group * 8, 8), 8)
            at = pl.ds(pl.multiple_of(source + (unit % 12) * 8, 8), 8)
            spread[to, :] = vecs[at, :]
        return carry

    lax.fori_loop(0, GROUPS, body, 0)


def layers_kernel(
    share,
    clips,
    cot,
    vec_in,
    qkv_in,
    out_in,
    up_in,
    down_in,
    out,
    in_grad,
    landed_vec,
    landed_qkv,
    landed_out,
    landed_up,
    landed_down,
    cot_other,
    x_hbm,
    h_hbm,
    n1_hbm,
    n2_hbm,
    qkv_hbm,
    ctx_hbm,
    lse_hbm,
    act_hbm,
    slope_hbm,
    w,
    res,
    act,
    slope,
    n1,
    n2,
    low,
    qkv,
    ctx,
    dctx,
    lse,
    h_in,
    wt,
    send,
    recv,
    vecs,
    vec_grads,
    sums,
    spread,
    stage,
    shard,
    flat,
    land_a,
    land_b,
    land_y,
    z_send,
    z_recv,
    x_send,
    x_recv,
    xb_send,
    xb_recv,
    y_send,
    y_recv,
    ya_send,
    ya_recv,
    gz_send,
    gz_recv,
    gx_send,
    gx_recv,
    gxb_send,
    gxb_recv,
    gy_send,
    gy_recv,
    gya_send,
    gya_recv,
    e_send,
    e_recv,
    own_sem,
    in_sem,
    cot_sem,
    out_sem,
    grad_sem,
    save_sem,
    load_sem,
    h_sem,
    ya_free,
    xb_free,
    x_free,
    y_free,
):
    place = Place(share)
    s, t, e, y = place.s, place.t, place.e, place.y
    primary, secondary = place.primary, jnp.logical_not(place.primary)
    width, frames = res.shape
    blocks = frames // BLOCK
    half = frames // 2
    quarter = half // 2
    rows = w.shape[3]
    low_rows = pl.ds(0, SPLIT)
    high_rows = pl.ds(SPLIT, rows - SPLIT)
    mine = pl.ds(pl.multiple_of(t * half, half), half)
    theirs = pl.ds(pl.multiple_of((1 - t) * half, half), half)

    own_loads = [pltpu.make_async_copy(vec_in, shard.at[:, pl.ds(VEC, QKV)], own_sem.at[0])]
    for number, (first, many, kind, bias) in enumerate(PARTS):
        own_loads.append(
            pltpu.make_async_copy(
                qkv_in.at[0, "qkv".index(kind), :, pl.ds(bias % WIDE, many)],
                shard.at[:, pl.ds(QKV + first, many)],
                own_sem.at[1 + number],
            )
        )
    own_up = pltpu.make_async_copy(up_in.at[0], shard.at[:, pl.ds(UP, DOWN - UP)], own_sem.at[7])
    own_out = pltpu.make_async_copy(out_in.at[0], flat.at[pl.ds(0, WIDE), :], own_sem.at[8])
    own_down = pltpu.make_async_copy(
        down_in.at[0], flat.at[pl.ds(WIDE, END - DOWN), :], own_sem.at[9]
    )
    for copy in own_loads + [own_out, own_up, own_down]:
        copy.start()

    place.greet()

    VECTORS = CHUNKS

    def piece_cols(piece):
        if isinstance(piece, int) and piece == VECTORS:
            return pl.ds(VEC, QKV)
        return pl.ds(pl.multiple_of(QKV + piece * WIDE, 128), WIDE)

    def pieces_of(step):
        layer, piece = step // CHUNKS, step % CHUNKS
        return layer, (VECTORS, piece) if piece == 0 else (piece,)

    def z_copies(piece):
        cols = piece_cols(piece)
        copies = []
        for step in range(LINES):
            copies.append(
                remote(
                    shard.at[:, cols],
                    w.at[s, e, y, :, cols],
                    z_send.at[piece, step],
                    z_recv.at[s, piece, e],
                    (t, place.row_of(place.line(step), y), t),
                )
            )
        local = pltpu.make_async_copy(
            shard.at[:, cols], w.at[s, e, y, :, cols], z_recv.at[s, piece, e]
        )
        return copies, local

    def z_start(step):
        layer, pieces = pieces_of(step)

        @pl.when(s == layer)
        def _():
            for piece in pieces:
                copies, local = z_copies(piece)

                @pl.when(primary)
                def _():
                    local.start()

                @pl.when(secondary)
                def _():
                    copies[0].start()

                for copy in copies[1:]:
                    copy.start()

    def z_finish(piece):
        copies, _ = z_copies(piece)

        @pl.when(secondary)
        def _():
            copies[0].wait_send()

        for copy in copies[1:]:
            copy.wait_send()

    def x_copy(layer, piece):
        part = w.at[layer, :, y, :, piece_cols(piece)]
        return remote(part, part, x_send.at[layer, piece], x_recv.at[layer, piece], place.across)

    def y_copy(layer, piece):
        part = w.at[layer, :, y, :, piece_cols(piece)]
        return remote(part, part, y_send.at[layer, piece], y_recv.at[layer, piece], place.beside)

    def xb_copy(layer, piece):
        part = w.at[layer, :, 1 - y, high_rows, piece_cols(piece)]
        return remote(part, part, xb_send.at[layer, piece], xb_recv.at[layer, piece], place.across)

    def ya_copy(layer, piece):
        part = w.at[layer, :, y, low_rows, piece_cols(piece)]
        return remote(part, part, ya_send.at[layer, piece], ya_recv.at[layer, piece], place.beside)

    def step_z(step):
        layer, pieces = pieces_of(step)

        @pl.when(primary)
        def _():
            for piece in pieces:
                cols = piece_cols(piece)
                for line in range(LINES):
                    await_bytes(w.at[layer, line, y, :, cols], z_recv.at[layer, piece, line])
                x_copy(layer, piece).start()
                y_copy(layer, piece).start()

    def step_plane(step):
        layer, pieces = pieces_of(step)

        @pl.when(primary)
        def _():
            for piece in pieces:
                await_bytes(w.at[layer, :, 1 - y, :, piece_cols(piece)], y_recv.at[layer, piece])
                xb_copy(layer, piece).start()

        @pl.when(secondary)
        def _():
            for piece in pieces:
                await_bytes(w.at[layer, :, y, :, piece_cols(piece)], x_recv.at[layer, piece])
                ya_copy(layer, piece).start()

    def tick(step):
        if step + 3 < 2 * CHUNKS:
            step_z(step + 3)
        if step + 8 < 2 * CHUNKS:
            z_start(step + 8)
        step_plane(step)

    def complete(*steps):
        @pl.when(secondary)
        def _():
            for step in steps:
                layer, pieces = pieces_of(step)
                for piece in pieces:
                    cols = piece_cols(piece)
                    await_bytes(w.at[layer, :, 1 - y, high_rows, cols], xb_recv.at[layer, piece])
                    await_bytes(w.at[layer, :, 1 - y, low_rows, cols], ya_recv.at[layer, piece])

    def at_turns(turns):
        def beside(index):
            for turn, steps in turns.items():

                @pl.when(index == turn)
                def _():
                    for step in steps:
                        step()

        return beside

    def ticks(turns):
        return at_turns({turn: (functools.partial(tick, step),) for turn, step in turns.items()})

    kept = {
        "x": (n2, x_hbm),
        "h": (res, h_hbm),
        "n1": (n1, n1_hbm),
        "n2": (n2, n2_hbm),
        "qkv": (qkv, qkv_hbm),
        "ctx": (ctx, ctx_hbm),
        "lse": (lse, lse_hbm),
        "act": (act, act_hbm),
        "slope": (slope, slope_hbm),
    }
    names = tuple(kept)

    def save(name, layer):
        src, dst = kept[name]
        if name in ("x", "h"):
            dst = dst.at[layer]
        return pltpu.make_async_copy(src, dst, save_sem.at[names.index(name), layer])

    def load(name, layer=0):
        dst, src = kept[name]
        if name == "x":
            dst, src = act.at[pl.ds(0, width), :], src.at[layer]
        return pltpu.make_async_copy(src, dst, load_sem.at[names.index(name)])

    def load_h(layer, index):
        slot = lax.rem(index, 2)
        return pltpu.make_async_copy(
            h_hbm.at[layer, :, block_of(index)], h_in.at[slot], h_sem.at[slot]
        )

    my_quarter = pl.ds(s * quarter, quarter)
    my_rows = pl.ds(pl.multiple_of((1 - t) * half + s * quarter, quarter), quarter)

    def clip_across():
        there = pl.ds(pl.multiple_of(t * half + s * quarter, quarter), quarter)
        return remote(
            clips.at[1 - t, my_quarter, :],
            stage.at[there, :],
            in_sem.at[0],
            in_sem.at[1],
            place.across,
        )

    def clip_core():
        part = stage.at[my_rows, :]
        return remote(part, part, in_sem.at[2], in_sem.at[3], place.core)

    def cot_across():
        return remote(
            cot.at[1 - t, my_quarter, :],
            cot_other.at[my_quarter, :],
            cot_sem.at[0],
            cot_sem.at[1],
            place.across,
        )

    def cot_core():
        part = cot_other.at[my_quarter, :]
        return remote(part, part, cot_sem.at[2], cot_sem.at[3], place.core)

    def exchange(kind, index, slot):
        return remote(
            send.at[kind, index],
            recv.at[kind, index],
            e_send.at[slot, index],
            e_recv.at[slot, index],
            place.core,
        )

    def result_copies(ref, first):
        local = pltpu.make_async_copy(stage.at[mine, :], ref.at[0, t], out_sem.at[first])
        away = remote(
            stage.at[theirs, :],
            ref.at[0, t],
            out_sem.at[first + 1],
            out_sem.at[first + 2],
            place.across,
        )
        return local, away

    def grad_copies(index):
        place_in = lax.rem(index, blocks // 2)
        part = in_grad.at[0, t, pl.ds(pl.multiple_of(place_in * BLOCK, BLOCK), BLOCK), :]
        src = stage.at[block_of(index), :]
        local = pltpu.make_async_copy(src, part, grad_sem.at[0, place_in])
        away = remote(
            src, part, grad_sem.at[1, place_in], grad_sem.at[2, place_in], place.across
        )
        return local, away

    def emit(layer, ref, first):
        @pl.when(s == layer)
        def _():
            for copy in result_copies(ref, first):
                copy.start()

    for copy in own_loads:
        copy.wait()
    for step in range(3):
        z_start(step)
    own_clip = pltpu.make_async_copy(clips.at[t], stage.at[mine, :], in_sem.at[4])
    own_clip.start()
    clip_across().start()
    cot_across().start()
    own_out.wait()
    shard[:, OUT:UP] = flat[0:WIDE, :].T
    own_up.wait()
    for step in (3, 4):
        z_start(step)

    def take_clip(first):
        def body(index, carry):
            at = pl.ds(pl.multiple_of(first + index * BLOCK, BLOCK), BLOCK)
            tile = stage[at, :].T
            n2[:, at] = tile
            res[:, at] = tile.astype(F32)
            return carry

        lax.fori_loop(0, half // BLOCK, body, 0)

    own_clip.wait()
    take_clip(t * half)
    own_down.wait()
    for piece in range(4):
        span = slice((1 + piece) * WIDE, (2 + piece) * WIDE)
        shard[:, DOWN + piece * WIDE : DOWN + (piece + 1) * WIDE] = flat[span, :].T
    clip_across().wait()
    clip_core().start()
    step_z(0)
    z_start(5)
    step_z(1)
    z_start(6)
    clip_core().wait()
    take_clip((1 - t) * half)
    save("x", 0).start()
    step_plane(0)
    step_z(2)
    z_start(7)
    step_plane(1)
    cot_across().wait()
    cot_core().start()
    step_z(3)
    z_start(8)
    step_plane(2)
    step_z(4)
    z_start(9)
    step_z(5)
    z_start(10)

    def project(index):
        cols = block_of(index)
        mean, scale = norm_stats(lambda span: res[span, cols], width)
        for span in chunks_of(width):
            hat = (res[span, cols] - mean) * scale
            n1[span, cols] = (hat * vecs[span, 0:1] + vecs[span, 2:3]).astype(BF)
        for first, many, kind, bias in PARTS:
            value = mm(wt[first : first + many, :], n1[:, cols])
            for span in chunks_of(many):
                part = value[span, :]
                if kind != "k":
                    part = part + spread[bias + span.start : bias + span.stop, 6:7]
                if kind == "q":
                    part = part * 0.125
                qkv[first + span.start : first + span.stop, cols] = part.astype(BF)

    def head_rows(head, first):
        return pl.ds(pl.multiple_of(first + head * HEAD, HEAD), HEAD)

    def attend(layer, turns, later_turns):
        def heads_of(first_head, base, stride, beside):
            def one_head(index_in, carry):
                head = first_head + index_in
                q_rows = head_rows(index_in, base)
                k_rows = head_rows(index_in, base + stride)
                v_rows = head_rows(index_in, base + 2 * stride)
                c_rows = head_rows(head, 0)
                keys = qkv[k_rows, :].T
                for index in range(blocks):
                    cols = slice(index * BLOCK, (index + 1) * BLOCK)
                    queries = qkv[q_rows, cols]
                    tiles = []
                    top = None
                    for tile in chunks_of(frames, BLOCK):
                        scores = mm(keys[tile, :], queries)
                        for span in chunks_of(BLOCK):
                            peak = stack_max(scores[span, :])
                            top = peak if top is None else jnp.maximum(top, peak)
                        tiles.append(scores)
                    top = jnp.max(top, 0, keepdims=True)
                    total = jnp.zeros((8, BLOCK), F32)
                    mixed = jnp.zeros((HEAD, BLOCK), F32)
                    for tile, scores in zip(chunks_of(frames, BLOCK), tiles):
                        soft = []
                        for span in chunks_of(BLOCK):
                            part = jnp.exp(scores[span, :] - top)
                            total = total + stack_sum(part)
                            soft.append(part.astype(BF))
                        mixed = mixed + mm(qkv[v_rows, tile], jnp.concatenate(soft, 0))
                    total = jnp.sum(total, 0, keepdims=True)
                    ctx[c_rows, cols] = (mixed / total).astype(BF)
                    lse[pl.ds(head, 1), cols] = top + jnp.log(total)
                beside(index_in)
                return carry

            return one_head

        lax.fori_loop(0, 4, heads_of(0, 0, 256, ticks(turns)), 0)
        lax.fori_loop(0, 2, heads_of(4, 768, 128, ticks(later_turns)), 0)

    def out_project(layer, turns):
        beside = ticks(turns)

        def body(index, carry):
            part = mm(whole(w, layer, OUT, 384), ctx[:, block_of(index)])
            send[0, index] = part.astype(BF)
            exchange(0, index, 2 * layer).start()
            beside(index)
            return carry

        lax.fori_loop(0, blocks, body, 0)

    def middle_norm(layer, turns):
        beside = ticks(turns)

        def body(index, carry):
            cols = block_of(index)
            exchange(0, index, 2 * layer).wait()
            for span in chunks_of(width):
                added = send[0, index, span, :].astype(F32) + recv[0, index, span, :].astype(F32)
                res[span, cols] = res[span, cols] + added + vecs[span, 3:4]
            mean, scale = norm_stats(lambda span: res[span, cols], width)
            for span in chunks_of(width):
                hat = (res[span, cols] - mean) * scale
                n2[span, cols] = (hat * vecs[span, 1:2] + vecs[span, 4:5]).astype(BF)
            beside(index)
            return carry

        lax.fori_loop(0, blocks, body, 0)

    def hidden_part(layer, part):
        flip_weights(w, wt, layer, UP + part * WIDE, WIDE, part * WIDE)
        units = slice(part * WIDE, (part + 1) * WIDE)
        lane = 7 if part < 2 else 8

        def body(index, carry):
            cols = block_of(index)
            pre = mm(wt[units, :], n2[:, cols])
            for span in chunks_of(WIDE):
                first = part * WIDE + span.start
                bias = spread[768 + first : 768 + first + ROWS, lane : lane + 1]
                value, steep = gelu_parts(pre[span, :] + bias)
                act[first : first + ROWS, cols] = value.astype(BF)
                slope[first : first + ROWS, cols] = steep.astype(BF)
            return carry

        lax.fori_loop(0, blocks, body, 0)

    def down_project(layer, turns):
        beside = ticks(turns)

        def body(index, carry):
            part = mm(whole(w, layer, DOWN, 1536), act[:, block_of(index)])
            send[1, index] = part.astype(BF)
            exchange(1, index, 2 * layer + 1).start()
            beside(index)
            return carry

        lax.fori_loop(0, blocks, body, 0)

    def layer_end(layer, index, span):
        added = send[1, index, span, :].astype(F32) + recv[1, index, span, :].astype(F32)
        return (res[span, block_of(index)] + added + vecs[span, 5:6]).astype(BF)

    def take_vectors(layer):
        vecs[...] = whole(w, layer, VEC, 128).astype(F32)
        spread_biases(vecs, spread, rows)

    def project_all(layer, turns):
        beside = ticks(turns)
        flip_weights(w, wt, layer, QKV, 1152)

        def body(index, carry):
            project(index)
            beside(index)
            return carry

        lax.fori_loop(0, blocks, body, 0)
        if layer == 0:
            save("n1", 0).start()
            save("qkv", 0).start()

    complete(0, 1, 2)
    take_vectors(0)
    project_all(0, {1: 3, 3: 4})
    cot_core().wait()
    load_cot = pltpu.make_async_copy(cot_other, stage.at[theirs, :], cot_sem.at[4])
    load_cot.start()
    own_cot = pltpu.make_async_copy(cot.at[t], stage.at[mine, :], cot_sem.at[5])
    own_cot.start()
    attend(0, {0: 5, 2: 6}, {0: 7})
    save("ctx", 0).start()
    save("lse", 0).start()
    complete(3)
    out_project(0, {3: 8})
    load_cot.wait()
    own_cot.wait()

    def take_cot(index, carry):
        low[:, block_of(index)] = stage[block_of(index), :].T
        return carry

    lax.fori_loop(0, blocks, take_cot, 0)
    save("x", 0).wait()
    middle_norm(0, {1: 9})
    save("h", 0).start()
    save("n2", 0).start()
    for part in range(4):
        complete(4 + part)
        hidden_part(0, part)
        tick(10 + part)
    save("act", 0).start()
    save("slope", 0).start()
    complete(8, 9, 10, 11)
    down_project(0, {3: 14})
    for name in ("n1", "qkv", "h", "n2"):
        save(name, 0).wait()

    def finish_body(index, carry):
        exchange(1, index, 1).wait()
        cols = block_of(index)
        for span in chunks_of(width):
            rows_out = layer_end(0, index, span)
            n2[span, cols] = rows_out
            res[span, cols] = rows_out.astype(F32)

        @pl.when(s == 0)
        def _():
            stage[cols, :] = n2[:, cols].T

        return carry

    lax.fori_loop(0, blocks, finish_body, 0)
    emit(0, out, 0)
    save("x", 1).start()
    complete(12, 13, 14)
    take_vectors(1)
    project_all(1, {1: 15, 3: 16})
    save("ctx", 0).wait()
    save("lse", 0).wait()
    attend(1, {0: 17, 2: 18}, {0: 19})
    complete(15)
    out_project(1, {3: 20})
    save("x", 1).wait()
    middle_norm(1, {1: 21})
    save("h", 1).start()
    save("act", 0).wait()
    save("slope", 0).wait()
    for part in range(4):
        complete(16 + part)
        hidden_part(1, part)
        if part < 2:
            tick(22 + part)
    for part in range(4):
        complete(20 + part)
        flip_weights(w, wt, 1, DOWN + part * WIDE, WIDE, part * WIDE)
    down_project(1, {})

    def gya_copy(layer, piece):
        cols = piece_cols(piece)
        return remote(
            w.at[layer, :, 1 - y, low_rows, cols],
            land_a.at[:, low_rows, cols],
            gya_send.at[layer, piece],
            gya_recv.at[layer, piece],
            place.beside,
        )

    def gxb_copy(layer, piece):
        cols = piece_cols(piece)
        return remote(
            w.at[layer, :, 1 - y, high_rows, cols],
            land_b.at[:, :, cols],
            gxb_send.at[layer, piece],
            gxb_recv.at[layer, piece],
            place.across,
        )

    def gx_copy(layer, piece):
        cols = piece_cols(piece)
        return remote(
            w.at[layer, :, y, :, cols],
            land_a.at[:, :, cols],
            gx_send.at[layer, piece],
            gx_recv.at[layer, piece],
            place.across,
        )

    def gy_copy(layer, piece):
        cols = piece_cols(piece)
        return remote(
            w.at[layer, :, 1 - y, :, cols],
            land_y.at[:, :, cols],
            gy_send.at[layer, piece],
            gy_recv.at[layer, piece],
            place.beside,
        )

    def landed_part(piece):
        if piece == VECTORS:
            return landed_vec
        ref, first = (
            (landed_qkv, 0)
            if piece < 3
            else (landed_out, 3)
            if piece < 4
            else (landed_up, 4)
            if piece < 8
            else (landed_down, 8)
        )
        return ref.at[:, :, pl.ds((piece - first) * WIDE, WIDE)]

    def gz_copies(layer, piece):
        cols = piece_cols(piece)
        target = landed_part(piece)
        copies = []
        for step in range(LINES):
            line = place.line(step)
            copies.append(
                remote(
                    w.at[layer, line, y, :, cols],
                    target.at[e],
                    gz_send.at[layer, piece, step],
                    gz_recv.at[piece, e],
                    (layer, place.row_of(line, y), t),
                )
            )
        local = pltpu.make_async_copy(
            w.at[layer, e, y, :, cols], target.at[e], gz_recv.at[piece, e]
        )
        return copies, local

    def add_rows(layer, piece, which, span, lands):
        cols = piece_cols(piece)
        first, count = span
        for line in range(LINES):
            total = w[layer, line, which, pl.ds(first, count), cols].astype(F32)
            for land, offset in lands:
                total = total + land[line, pl.ds(offset, count), cols].astype(F32)
            w[layer, line, which, pl.ds(first, count), cols] = total.astype(BF)

    def signal(sem, layer, piece, device):
        if layer == 1:
            pl.semaphore_signal(sem.at[piece], inc=1, device_id=device, device_id_type=MESH)

    def credit(sem, layer, piece):
        if layer == 0:
            pl.semaphore_wait(sem.at[piece], 1)

    def step_a(layer, piece):
        @pl.when(secondary)
        def _():
            credit(ya_free, layer, piece)
            gya_copy(layer, piece).start()
            credit(xb_free, layer, piece)
            gxb_copy(layer, piece).start()

    def step_b(layer, piece):
        cols = piece_cols(piece)

        @pl.when(secondary)
        def _():
            await_bytes(land_a.at[:, low_rows, cols], gya_recv.at[layer, piece])
            add_rows(layer, piece, y, (0, SPLIT), [(land_a, 0)])
            signal(ya_free, layer, piece, place.beside)
            credit(x_free, layer, piece)
            gx_copy(layer, piece).start()

        @pl.when(primary)
        def _():
            await_bytes(land_b.at[:, :, cols], gxb_recv.at[layer, piece])
            add_rows(layer, piece, 1 - y, (SPLIT, rows - SPLIT), [(land_b, 0)])
            signal(xb_free, layer, piece, place.across)
            credit(y_free, layer, piece)
            gy_copy(layer, piece).start()

    def step_c(layer, piece):
        cols = piece_cols(piece)

        @pl.when(primary)
        def _():
            await_bytes(land_a.at[:, :, cols], gx_recv.at[layer, piece])
            await_bytes(land_y.at[:, :, cols], gy_recv.at[layer, piece])
            add_rows(layer, piece, y, (0, rows), [(land_a, 0), (land_y, 0)])
            signal(x_free, layer, piece, place.across)
            signal(y_free, layer, piece, place.beside)
            copies, local = gz_copies(layer, piece)

            @pl.when(s == layer)
            def _():
                local.start()

            @pl.when(s != layer)
            def _():
                copies[0].start()

            for copy in copies[1:]:
                copy.start()

    def store_grads(layer, start, count, value):
        w[layer, :, :, :, pl.ds(start, count)] = value.astype(BF).reshape(
            w.shape[1], w.shape[2], rows, count
        )

    ones = functools.partial(jnp.ones, (frames, 128), BF)

    def mlp_back(layer, beside):
        def body(index, carry):
            cols = block_of(index)
            for part in range(4):
                units = slice(part * WIDE, (part + 1) * WIDE)
                grad = mm(wt[units, :], low[:, cols])
                for span in chunks_of(WIDE):
                    rows_in = slice(units.start + span.start, units.start + span.stop)
                    steep = slope[rows_in, cols].astype(F32)
                    slope[rows_in, cols] = (grad[span, :] * steep).astype(BF)
            term = mm(whole(w, layer, UP, 1536), slope[:, cols])
            send[0, index] = term.astype(BF)
            exchange(0, index, 4 + 2 * layer).start()
            beside(index)
            return carry

        lax.fori_loop(0, blocks, body, 0)

    def outer_pair(layer, start, left, right, first, before, beside):
        def body(index, carry):
            before(index)
            for part in range(3):
                base = index * 768 + part * 256
                span = pl.ds(pl.multiple_of(base, 256), 256)
                value = mmt(left[...], right[span, :])
                store_grads(layer, pl.multiple_of(start + base, 128), 256, value)
            step_a(layer, first + 2 * index)
            step_a(layer, first + 2 * index + 1)
            beside(index)
            return carry

        lax.fori_loop(0, 2, body, 0)

    def turned(turn):
        return lax.rem(turn + (1 - t) * (blocks // 2), blocks)

    def fold(value):
        return value[:, 0:128] + value[:, 128:256]

    def norm_back(layer, kind, gain_lane, source, put, finish, beside):
        sums[...] = jnp.zeros_like(sums)

        def body(turn, carry):
            index = turned(turn)
            cols = block_of(index)
            read = source(index)
            mean, scale = norm_stats(read, width)
            exchange(kind, index, 4 + 2 * layer + kind).wait()
            first = jnp.zeros((8, BLOCK), F32)
            second = jnp.zeros((8, BLOCK), F32)

            def terms(span):
                hat = (read(span) - mean) * scale
                grad = send[kind, index, span, :].astype(F32)
                grad = grad + recv[kind, index, span, :].astype(F32)
                return hat, grad, grad * vecs[span, gain_lane : gain_lane + 1]

            for span in chunks_of(width):
                hat, grad, scaled = terms(span)
                sums[0, span, :] += fold(grad * hat)
                sums[1, span, :] += fold(grad)
                first = first + stack_sum(scaled)
                second = second + stack_sum(scaled * hat)
            level = mean_of(first, width)
            slant = mean_of(second, width)
            for span in chunks_of(width):
                hat, _, scaled = terms(span)
                put(span, cols, res[span, cols] + scale * (scaled - level - hat * slant))
            finish(index)
            beside(turn)
            return carry

        lax.fori_loop(0, blocks, body, 0)

    def row_sums(value):
        return jnp.sum(value, 1, keepdims=True)

    def attend_back(first_head, many, base, stride, beside):
        def one_head(index_in, carry):
            head = first_head + index_in
            q_rows = head_rows(index_in, base)
            k_rows = head_rows(index_in, base + stride)
            v_rows = head_rows(index_in, base + 2 * stride)
            c_rows = head_rows(head, 0)
            keys = qkv[k_rows, :].T
            values = qkv[v_rows, :].T
            flat_queries = qkv[q_rows, :].T
            flat_grads = dctx[c_rows, :].T
            level = lse[pl.ds(head, 1), :]
            inner = jnp.sum(
                dctx[c_rows, :].astype(F32) * ctx[c_rows, :].astype(F32), 0, keepdims=True
            )
            step = jnp.zeros((HEAD, frames), F32)
            for tile in chunks_of(frames, BLOCK):
                soft = []
                score_grad = []
                for cols in chunks_of(frames, BLOCK):
                    scores = mm(keys[tile, :], qkv[q_rows, cols])
                    soft_grad = mm(values[tile, :], dctx[c_rows, cols])
                    soft_parts = []
                    grad_parts = []
                    for part in chunks_of(BLOCK):
                        strength = jnp.exp(scores[part, :] - level[:, cols])
                        soft_parts.append(strength.astype(BF))
                        strength = strength * (soft_grad[part, :] - inner[:, cols])
                        grad_parts.append(strength.astype(BF))
                    soft.append(jnp.concatenate(soft_parts, 0))
                    score_grad.append(jnp.concatenate(grad_parts, 0))
                soft = jnp.concatenate(soft, 1)
                score_grad = jnp.concatenate(score_grad, 1)
                step = step + mm(qkv[k_rows, tile], score_grad)
                slope[k_rows, tile] = mm(score_grad, flat_queries).astype(BF).T
                slope[v_rows, tile] = mm(soft, flat_grads).astype(BF).T
            slope[q_rows, :] = (step * 0.125).astype(BF)
            beside(index_in)
            return carry

        lax.fori_loop(0, many, one_head, 0)

    def collect_biases():
        def body(group, carry):
            source = group * rows
            for kind in range(2):
                for head in range(6):
                    at = pl.ds(pl.multiple_of(kind * 384 + head * HEAD + group * 8, 8), 8)
                    to = pl.ds(pl.multiple_of(source + kind * 48 + head * 8, 8), 8)
                    vec_grads[to, 6:7] = spread[at, 6:7]
            for unit in range(24):
                at = pl.ds(pl.multiple_of(768 + unit * HEAD + group * 8, 8), 8)
                to = pl.ds(pl.multiple_of(source + (unit % 12) * 8, 8), 8)
                lane = 7 if unit < 12 else 8
                vec_grads[to, lane : lane + 1] = spread[at, lane : lane + 1]
            return carry

        lax.fori_loop(0, GROUPS, body, 0)

    def nothing(index):
        del index

    def finish_gather(layer, piece):
        @pl.when(primary)
        def _():
            x_copy(layer, piece).wait_send()
            y_copy(layer, piece).wait_send()
            xb_copy(layer, piece).wait_send()

        @pl.when(secondary)
        def _():
            ya_copy(layer, piece).wait_send()

    def last_body(index, carry):
        exchange(1, index, 3).wait()

        @pl.when(s == 1)
        def _():
            for span in chunks_of(width, 128):
                stage[block_of(index), span] = layer_end(1, index, span).T

        return carry

    for layer in (1, 0):
        later = layer == 0
        if later:
            load_h(layer, turned(0)).start()
            load("act").wait()
            vecs[...] = whole(w, layer, VEC, 128).astype(F32)
            flip_weights(w, wt, layer, DOWN, 1536)
        vec_grads[...] = jnp.zeros_like(vec_grads)
        if later:
            before = nothing
            early = at_turns({0: (lambda: step_b(1, VECTORS),), 1: (lambda: step_c(1, VECTORS),)})
        else:
            waits = [functools.partial(finish_gather, 1, piece) for piece in (8, 9, 10, 11)]
            before = at_turns({0: waits[:2], 1: waits[2:]})
            early = nothing
        outer_pair(layer, DOWN, low, act, 8, before, early)
        load("x", layer).start()
        vec_grads[:, 5:6] = mm(low[...], ones())[:, 0:1]
        if not later:
            lax.fori_loop(0, blocks, last_body, 0)
            emit(1, out, 0)
            save("h", 1).wait()
            load_h(layer, turned(0)).start()
            res[...] = low[...].astype(F32)
            for piece in range(CHUNKS + 1):
                z_finish(piece)
                finish_gather(0, piece)
                if piece < 8 or piece == VECTORS:
                    finish_gather(1, piece)
        else:
            load("slope").wait()

        def b(piece, layer=layer):
            return lambda: step_b(layer, piece)

        def c(piece, layer=layer):
            return lambda: step_c(layer, piece)

        mlp_back(layer, at_turns({1: (b(8),), 2: (b(9),), 3: (b(10), b(11))}))
        if later:
            load("n2").wait()
        outer_pair(layer, UP, n2, slope, 4, nothing, at_turns({1: (c(8),)}))
        spread[768:, :] = mm(slope[...], ones())
        flip_weights(w, wt, layer, OUT, 384)

        def hidden_in(index, layer=layer):
            turn = lax.rem(index + (1 - t) * (blocks // 2), blocks)

            @pl.when(turn + 1 < blocks)
            def _():
                load_h(layer, turned(turn + 1)).start()

            load_h(layer, index).wait()
            slot = lax.rem(index, 2)
            return lambda span: h_in[slot, span, :]

        def hidden_put(span, cols, total):
            res[span, cols] = total
            low[span, cols] = total.astype(BF)

        def hidden_out(index):
            cols = block_of(index)
            dctx[:, cols] = mm(wt[0:384, :], low[:, cols]).astype(BF)

        drain = at_turns({0: (b(4), c(9)), 1: (b(5), c(10)), 2: (b(6), c(11)), 3: (b(7),)})
        norm_back(layer, 0, 1, hidden_in, hidden_put, hidden_out, drain)
        vec_grads[:, 1:2] = row_sums(sums[0])
        vec_grads[:, 4:5] = row_sums(sums[1])
        vec_grads[:, 3:4] = mm(low[...], ones())[:, 0:1]
        if later:
            for name in ("ctx", "qkv", "lse"):
                load(name).wait()
        store_grads(layer, OUT, 384, mmt(low[...], ctx[...]))
        step_a(layer, 3)
        drain = at_turns({0: (c(4),), 1: (c(5),), 2: (b(3), c(6)), 3: (c(7),)})
        attend_back(0, 4, 0, 256, drain)
        if later:
            load("n1").wait()
        wt[0:768, :] = whole(w, layer, QKV, 768)

        def qkv_body(index, carry, layer=layer):
            span = pl.ds(pl.multiple_of(index * 256, 256), 256)
            value = mmt(n1[...], slope[span, :])
            store_grads(layer, pl.multiple_of(QKV + index * 256, 128), 256, value)
            return carry

        lax.fori_loop(0, 3, qkv_body, 0)
        step_a(layer, 0)
        step_a(layer, 1)
        attend_back(4, 2, 768, 128, at_turns({0: (b(0), c(3)), 1: (b(1),)}))

        def first_body(index, carry, layer=layer):
            cols = block_of(index)
            term = mm(wt[0:768, :], slope[0:768, cols])
            term = term + mm(whole(w, layer, QKV + 768, WIDE), slope[768:1152, cols])
            send[1, index] = term.astype(BF)
            exchange(1, index, 5 + 2 * layer).start()
            return carry

        lax.fori_loop(0, blocks, first_body, 0)
        store_grads(layer, QKV + 768, WIDE, mmt(n1[...], slope[768:1152, :]))
        step_a(layer, 2)
        step_c(layer, 0)
        for first, many, kind, bias in PARTS:
            if kind != "k":
                spread[bias : bias + many, :] = mm(slope[first : first + many, :], ones())
        collect_biases()
        if layer == 1:
            for name in ("slope", "n1", "n2", "ctx", "qkv", "lse"):
                load(name).start()
        load("x", layer).wait()

        @pl.when(s == layer)
        def _():
            local, away = result_copies(out, 0)
            local.wait()
            away.wait_send()

        def rows_x(index):
            return lambda span: act[span, block_of(index)].astype(F32)

        def rows_put(span, cols, total, layer=layer):
            rounded = total.astype(BF)
            low[span, cols] = rounded
            if layer == 1:
                res[span, cols] = rounded.astype(F32)

        def rows_out(index, layer=layer):
            @pl.when(s == layer)
            def _():
                stage[block_of(index), :] = low[:, block_of(index)].T
                local, away = grad_copies(index)

                @pl.when(index // (blocks // 2) == t)
                def _():
                    local.start()

                @pl.when(index // (blocks // 2) != t)
                def _():
                    away.start()

        drain = at_turns({0: (c(1),), 1: (b(2),), 3: (c(2),)})
        norm_back(layer, 1, 0, rows_x, rows_put, rows_out, drain)
        if layer == 1:
            load("act").start()
        vec_grads[:, 0:1] = row_sums(sums[0])
        vec_grads[:, 2:3] = row_sums(sums[1])
        store_grads(layer, VEC, 128, vec_grads[...])
        step_a(layer, VECTORS)

    step_b(0, VECTORS)
    step_c(0, VECTORS)

    def finish_scatter(piece):
        for layer in range(2):

            @pl.when(secondary)
            def _():
                gya_copy(layer, piece).wait_send()
                gxb_copy(layer, piece).wait_send()
                gx_copy(layer, piece).wait_send()

            @pl.when(primary)
            def _():
                gy_copy(layer, piece).wait_send()
                copies, _ = gz_copies(layer, piece)

                @pl.when(s != layer)
                def _():
                    copies[0].wait_send()

                for copy in copies[1:]:
                    copy.wait_send()

    for piece in range(CHUNKS + 1):
        finish_scatter(piece)
        for line in range(LINES):
            await_bytes(landed_part(piece).at[line], gz_recv.at[piece, line])

    _, away = result_copies(out, 0)
    away.wait_recv()
    for index in range(blocks // 2):
        local, away = grad_copies(index)
        local.wait()
        away.wait()


def layers_call(share, clips, cotangent, shards, dims):
    width, frames, hidden_units, heads_width = dims
    rows = width // GROUPS
    sem = pltpu.SemaphoreType.DMA
    free = pltpu.SemaphoreType.REGULAR
    packed = (2, LINES, 2, rows, END)
    blocks = frames // BLOCK
    shape = jax.ShapeDtypeStruct
    outs = [
        shape((1,) + clips.shape, BF),
        shape((1,) + clips.shape, BF),
        shape((LINES, rows, QKV - VEC), BF),
        shape((LINES, rows, OUT - QKV), BF),
        shape((LINES, rows, UP - OUT), BF),
        shape((LINES, rows, DOWN - UP), BF),
        shape((LINES, rows, END - DOWN), BF),
        shape(clips.shape[1:], BF),
        shape((2, width, frames), BF),
        shape((2, width, frames), F32),
        shape((width, frames), BF),
        shape((width, frames), BF),
        shape((3 * heads_width, frames), BF),
        shape((heads_width, frames), BF),
        shape((8, frames), F32),
        shape((hidden_units, frames), BF),
        shape((hidden_units, frames), BF),
    ]
    scratch = [
        pltpu.VMEM(packed, BF),
        pltpu.VMEM((width, frames), F32),
        pltpu.VMEM((hidden_units, frames), BF),
        pltpu.VMEM((hidden_units, frames), BF),
        pltpu.VMEM((width, frames), BF),
        pltpu.VMEM((width, frames), BF),
        pltpu.VMEM((width, frames), BF),
        pltpu.VMEM((3 * heads_width, frames), BF),
        pltpu.VMEM((heads_width, frames), BF),
        pltpu.VMEM((heads_width, frames), BF),
        pltpu.VMEM((8, frames), F32),
        pltpu.VMEM((2, width, BLOCK), F32),
        pltpu.VMEM((hidden_units, width), BF),
        pltpu.VMEM((2, blocks, width, BLOCK), BF),
        pltpu.VMEM((2, blocks, width, BLOCK), BF),
        pltpu.VMEM((width, 128), F32),
        pltpu.VMEM((width, 128), F32),
        pltpu.VMEM((2, width, 128), F32),
        pltpu.VMEM((2 * heads_width + hidden_units, 128), F32),
        pltpu.VMEM((frames, width), BF),
        pltpu.VMEM((rows, END), BF),
        pltpu.VMEM((WIDE + END - DOWN, rows), BF),
        pltpu.VMEM((LINES, rows, END), BF),
        pltpu.VMEM((LINES, rows - SPLIT, END), BF),
        pltpu.VMEM((LINES, rows, END), BF),
    ]
    scratch += [sem((CHUNKS + 1, LINES)), sem((2, CHUNKS + 1, LINES))]
    scratch += [sem((2, CHUNKS + 1))] * 8
    scratch += [sem((2, CHUNKS + 1, LINES)), sem((CHUNKS + 1, LINES))]
    scratch += [sem((2, CHUNKS + 1))] * 8
    scratch += [
        sem((8, blocks)),
        sem((8, blocks)),
        sem((10,)),
        sem((5,)),
        sem((6,)),
        sem((3,)),
        sem((3, blocks // 2)),
        sem((9, 2)),
        sem((9,)),
        sem((2,)),
    ]
    scratch += [free((CHUNKS + 1,))] * 4
    anywhere = pl.BlockSpec(memory_space=pl.ANY)
    return pl.pallas_call(
        functools.partial(layers_kernel, share),
        out_shape=outs,
        in_specs=[anywhere] * (2 + len(shards)),
        out_specs=[anywhere] * len(outs),
        scratch_shapes=scratch,
        compiler_params=pltpu.CompilerParams(
            collective_id=0, has_side_effects=True, vmem_limit_bytes=VMEM_LIMIT
        ),
        cost_estimate=pl.CostEstimate(
            flops=60_000_000_000, bytes_accessed=60_000_000, transcendentals=0
        ),
    )(clips, cotangent, *shards)


def group_piece(value, axis, share):
    if share == 1:
        return value
    size = value.shape[axis] * share
    group = lax.axis_index("dp") // share
    full = lax.all_gather(value, "dp", axis=axis, tiled=True)
    return lax.dynamic_slice_in_dim(full, group * size, size, axis)


def own_part(value, axis, share, parts, index):
    size = value.shape[axis] // parts
    if parts == 1:
        return value
    return lax.dynamic_slice_in_dim(value, index * size, size, axis)


def on_device(share, clips, cotangent, ln_gains, row_biases, w_qkv, b_qv, w_o, w_up, b_ff, w_down):
    width = clips.shape[2]
    rows = width // GROUPS
    dims = (width, 2 * clips.shape[1], w_up.shape[2], w_o.shape[1])
    ln_gains = group_piece(ln_gains, 2, share)
    row_biases = group_piece(row_biases, 2, share)
    w_qkv = group_piece(w_qkv, 2, share)
    b_qv = group_piece(b_qv, 3, share)
    w_o = group_piece(w_o, 2, share)
    w_up = group_piece(w_up, 1, share)
    b_ff = group_piece(b_ff, 2, share)
    w_down = group_piece(w_down, 2, share)
    vectors = jnp.concatenate([ln_gains[0], row_biases[0]], 0).T
    heads = jnp.concatenate([b_qv[0, 0].reshape(-1), b_qv[0, 1].reshape(-1)])[:, None]
    units = b_ff[0].reshape(2, rows).T
    packed = jnp.concatenate([vectors, heads, units], 1)
    packed = jnp.pad(packed, ((0, 0), (0, 128 - packed.shape[1])))
    section_out, section_in_grad, *landed = layers_call(
        share, clips, cotangent, (packed, w_qkv, w_o, w_up, w_down), dims
    )
    rest = lax.axis_index("dp") % share
    side = lax.axis_index("tensor")

    def joined(value):
        total = jnp.sum(value.astype(F32), 0)
        if share == 1:
            return total
        group = lax.axis_index("dp") // share
        padded = jnp.zeros((width, total.shape[1]), F32)
        padded = lax.dynamic_update_slice_in_dim(padded, total, group * rows, 0)
        return lax.dynamic_slice_in_dim(lax.psum(padded, "dp"), group * rows, rows, 0)

    def mine(value):
        return own_part(joined(value), 0, share, share, rest)

    vectors = joined(landed[0])
    vec = own_part(own_part(vectors, 0, share, share, rest), 0, share, 2, side)
    heads_grad = vectors[:, 6].reshape(2, -1, HEAD // GROUPS)
    units_grad = vectors[:, 7:9].T.reshape(-1, HEAD // GROUPS)
    qkv_grad = {"q": [], "k": [], "v": []}
    for first, many, kind, _ in PARTS:
        qkv_grad[kind].append(mine(landed[1][:, :, first : first + many]))
    return (
        section_out,
        section_in_grad,
        vec[:, 0:2].T[None],
        vec[:, 2:6].T[None],
        jnp.stack([jnp.concatenate(qkv_grad[kind], 1) for kind in "qkv"])[None],
        own_part(heads_grad, 2, share, share, rest)[None],
        mine(landed[2]).T[None],
        mine(landed[3])[None],
        own_part(units_grad, 1, share, share, rest)[None],
        mine(landed[4]).T[None],
    )


def solution(mesh):
    placed = (
        P("dp", "tensor", None),
        P("dp", "tensor", None),
        P("section", None, "dp"),
        P("section", None, "dp"),
        P("section", None, "dp", "tensor"),
        P("section", None, "tensor", "dp"),
        P("section", "tensor", "dp"),
        P("section", "dp", "tensor"),
        P("section", "tensor", "dp"),
        P("section", "tensor", "dp"),
    )
    share = mesh.shape["dp"] // GROUPS
    return jax.shard_map(
        functools.partial(on_device, share),
        mesh=mesh,
        in_specs=placed,
        out_specs=(
            P("section", "dp", "tensor", None),
            P("section", "dp", "tensor", None),
            P("section", None, ("dp", "tensor")),
            P("section", None, ("dp", "tensor")),
            P("section", None, "dp", "tensor"),
            P("section", None, "tensor", "dp"),
            P("section", "tensor", "dp"),
            P("section", "dp", "tensor"),
            P("section", "tensor", "dp"),
            P("section", "tensor", "dp"),
        ),
        check_vma=False,
    )
```

```python
import functools

import jax
import jax.numpy as jnp
from jax import lax
from jax.experimental import pallas as pl
from jax.experimental.pallas import tpu as pltpu
from jax.sharding import PartitionSpec as P

BF = jnp.bfloat16
F32 = jnp.float32
MESH = pl.DeviceIdType.MESH
EPSILON = 1e-05
HEAD = 64
GROUPS = 8
LINES = 4
BLOCK = 256
PAIR = 2 * BLOCK
ROWS = 64
ONES = 16
VMEM_LIMIT = 62 * 1024 * 1024

VEC = 0
QKV = 128
OUT = 1280
UP = 1664
DOWN = 3200
END = 4736
SPLIT = 48
WIDE = 384
CHUNKS = 12


PARTS = (
    (0, 256, "q", 0),
    (256, 256, "k", 0),
    (512, 256, "v", 384),
    (768, 128, "q", 256),
    (896, 128, "k", 256),
    (1024, 128, "v", 640),
)


def mm(left, right):
    return jnp.dot(left, right, preferred_element_type=F32)


def mmt(left, right):
    return lax.dot_general(left, right, (((1,), (1,)), ((), ())), preferred_element_type=F32)


class Place:
    def __init__(self, share):
        self.s = lax.axis_index("section")
        self.d = lax.axis_index("dp")
        self.t = lax.axis_index("tensor")
        group = self.d // share
        self.rest = self.d - group * share
        self.share = share
        self.e = group // 2
        self.y = group - self.e * 2
        self.primary = self.s == self.t
        self.core = (1 - self.s, self.d, self.t)
        self.across = (self.s, self.d, 1 - self.t)
        self.beside = (self.s, self.row_of(self.e, 1 - self.y), self.t)

    def row_of(self, line, y):
        return (line * 2 + y) * self.share + self.rest

    def line(self, step):
        return lax.rem(self.e + step, LINES)

    def greet(self):
        barrier = pltpu.get_barrier_semaphore()
        peers = [self.core, self.across, self.beside]
        for step in range(1, LINES):
            for section in range(2):
                peers.append((section, self.row_of(self.line(step), self.y), self.t))
        for peer in peers:
            pl.semaphore_signal(barrier, inc=1, device_id=peer, device_id_type=MESH)
        pl.semaphore_wait(barrier, len(peers))


def remote(src, dst, send_sem, recv_sem, device):
    return pltpu.make_async_remote_copy(
        src_ref=src,
        dst_ref=dst,
        send_sem=send_sem,
        recv_sem=recv_sem,
        device_id=device,
        device_id_type=MESH,
    )


def await_bytes(ref, sem):
    pltpu.make_async_copy(ref, ref, sem).wait()


def chunks_of(count, size=ROWS):
    return [slice(first, first + size) for first in range(0, count, size)]


def by_eights(value):
    return value.reshape(value.shape[0] // 8, 8, value.shape[1])


def stack_sum(value):
    return jnp.sum(by_eights(value), 0)


def stack_max(value):
    return jnp.max(by_eights(value), 0)


def mean_of(parts, count):
    return jnp.sum(parts, 0, keepdims=True) / count


def norm_stats(read, count):
    total = jnp.zeros((8, BLOCK), F32)
    for span in chunks_of(count):
        total = total + stack_sum(read(span))
    mean = mean_of(total, count)
    square = jnp.zeros((8, BLOCK), F32)
    for span in chunks_of(count):
        centred = read(span) - mean
        square = square + stack_sum(centred * centred)
    return mean, lax.rsqrt(mean_of(square, count) + EPSILON)


def gelu_parts(values):
    bell = jnp.exp(-0.5 * values * values)
    reach = jnp.abs(values) * 0.7071067811865476
    inv = 1.0 / (1.0 + 0.3275911 * reach)
    poly = inv * (
        0.254829592
        + inv * (-0.284496736 + inv * (1.421413741 + inv * (-1.453152027 + inv * 1.061405429)))
    )
    tail = 0.5 * poly * bell
    cdf = jnp.where(values >= 0.0, 1.0 - tail, tail)
    return values * cdf, cdf + values * bell * 0.3989422804014327


def fold(value):
    return value[:, 0:128] + value[:, 128:256]


def block_of(index):
    return pl.ds(pl.multiple_of(index * BLOCK, BLOCK), BLOCK)


def pair_of(index):
    return pl.ds(pl.multiple_of(index * PAIR, PAIR), PAIR)


def flip_weights(w, wt, layer, start, width, target=0):
    def body(index, carry):
        cols = pl.ds(pl.multiple_of(start + index * 128, 128), 128)
        rows = pl.ds(pl.multiple_of(target + index * 128, 128), 128)
        tile = w[layer, :, :, :, cols]
        wt[rows, :] = tile.reshape(tile.shape[0] * tile.shape[1] * tile.shape[2], 128).T
        return carry

    lax.fori_loop(0, width // 128, body, 0)


def whole(w, layer, start, width):
    tile = w[layer, :, :, :, start : start + width]
    return tile.reshape(tile.shape[0] * tile.shape[1] * tile.shape[2], width)


def spread_biases(vecs, spread, rows):
    def body(group, carry):
        source = group * rows
        for kind in range(2):
            for head in range(6):
                to = pl.ds(pl.multiple_of(kind * 384 + head * HEAD + group * 8, 8), 8)
                at = pl.ds(pl.multiple_of(source + kind * 48 + head * 8, 8), 8)
                spread[to, :] = vecs[at, :]
        for unit in range(24):
            to = pl.ds(pl.multiple_of(768 + unit * HEAD + group * 8, 8), 8)
            at = pl.ds(pl.multiple_of(source + (unit % 12) * 8, 8), 8)
            spread[to, :] = vecs[at, :]
        return carry

    lax.fori_loop(0, GROUPS, body, 0)


def layers_kernel(
    share,
    clips,
    cot,
    vec_in,
    qkv_in,
    out_in,
    up_in,
    down_in,
    out,
    in_grad,
    landed_vec,
    landed_qkv,
    landed_out,
    landed_up,
    landed_down,
    cot_other,
    x_hbm,
    h_hbm,
    n1_hbm,
    n2_hbm,
    qkv_hbm,
    ctx_hbm,
    lse_hbm,
    act_hbm,
    slope_hbm,
    w,
    res,
    act,
    slope,
    n1,
    n2,
    low,
    qkv,
    ctx,
    dctx,
    lse,
    h_in,
    wt,
    send,
    recv,
    vecs,
    vec_grads,
    sums,
    spread,
    stage,
    shard,
    flat,
    land_a,
    land_b,
    land_y,
    z_send,
    z_recv,
    x_send,
    x_recv,
    xb_send,
    xb_recv,
    y_send,
    y_recv,
    ya_send,
    ya_recv,
    gz_send,
    gz_recv,
    gx_send,
    gx_recv,
    gxb_send,
    gxb_recv,
    gy_send,
    gy_recv,
    gya_send,
    gya_recv,
    e_send,
    e_recv,
    own_sem,
    in_sem,
    cot_sem,
    out_sem,
    grad_sem,
    save_sem,
    load_sem,
    h_sem,
    ya_free,
    xb_free,
    x_free,
    y_free,
):
    place = Place(share)
    s, t, e, y = place.s, place.t, place.e, place.y
    primary, secondary = place.primary, jnp.logical_not(place.primary)
    width, frames = res.shape
    blocks = frames // BLOCK
    half = frames // 2
    quarter = half // 2
    rows = w.shape[3]
    low_rows = pl.ds(0, SPLIT)
    high_rows = pl.ds(SPLIT, rows - SPLIT)
    mine = pl.ds(pl.multiple_of(t * half, half), half)
    theirs = pl.ds(pl.multiple_of((1 - t) * half, half), half)

    own_loads = [pltpu.make_async_copy(vec_in, shard.at[:, pl.ds(VEC, QKV)], own_sem.at[0])]
    for number, (first, many, kind, bias) in enumerate(PARTS):
        own_loads.append(
            pltpu.make_async_copy(
                qkv_in.at[0, "qkv".index(kind), :, pl.ds(bias % WIDE, many)],
                shard.at[:, pl.ds(QKV + first, many)],
                own_sem.at[1 + number],
            )
        )
    own_up = pltpu.make_async_copy(up_in.at[0], shard.at[:, pl.ds(UP, DOWN - UP)], own_sem.at[7])
    own_out = pltpu.make_async_copy(out_in.at[0], flat.at[pl.ds(0, WIDE), :], own_sem.at[8])
    own_down = pltpu.make_async_copy(
        down_in.at[0], flat.at[pl.ds(WIDE, END - DOWN), :], own_sem.at[9]
    )
    for copy in own_loads + [own_out, own_up, own_down]:
        copy.start()

    place.greet()

    VECTORS = CHUNKS

    def piece_cols(piece):
        if isinstance(piece, int) and piece == VECTORS:
            return pl.ds(VEC, QKV)
        return pl.ds(pl.multiple_of(QKV + piece * WIDE, 128), WIDE)

    def pieces_of(step):
        layer, piece = step // CHUNKS, step % CHUNKS
        return layer, (VECTORS, piece) if piece == 0 else (piece,)

    def z_copies(piece):
        cols = piece_cols(piece)
        copies = []
        for step in range(LINES):
            copies.append(
                remote(
                    shard.at[:, cols],
                    w.at[s, e, y, :, cols],
                    z_send.at[piece, step],
                    z_recv.at[s, piece, e],
                    (t, place.row_of(place.line(step), y), t),
                )
            )
        local = pltpu.make_async_copy(
            shard.at[:, cols], w.at[s, e, y, :, cols], z_recv.at[s, piece, e]
        )
        return copies, local

    def z_start(step):
        layer, pieces = pieces_of(step)

        @pl.when(s == layer)
        def _():
            for piece in pieces:
                copies, local = z_copies(piece)

                @pl.when(primary)
                def _():
                    local.start()

                @pl.when(secondary)
                def _():
                    copies[0].start()

                for copy in copies[1:]:
                    copy.start()

    def z_finish(piece):
        copies, _ = z_copies(piece)

        @pl.when(secondary)
        def _():
            copies[0].wait_send()

        for copy in copies[1:]:
            copy.wait_send()

    def x_copy(layer, piece):
        part = w.at[layer, :, y, :, piece_cols(piece)]
        return remote(part, part, x_send.at[layer, piece], x_recv.at[layer, piece], place.across)

    def y_copy(layer, piece):
        part = w.at[layer, :, y, :, piece_cols(piece)]
        return remote(part, part, y_send.at[layer, piece], y_recv.at[layer, piece], place.beside)

    def xb_copy(layer, piece):
        part = w.at[layer, :, 1 - y, high_rows, piece_cols(piece)]
        return remote(part, part, xb_send.at[layer, piece], xb_recv.at[layer, piece], place.across)

    def ya_copy(layer, piece):
        part = w.at[layer, :, y, low_rows, piece_cols(piece)]
        return remote(part, part, ya_send.at[layer, piece], ya_recv.at[layer, piece], place.beside)

    def step_z(step):
        layer, pieces = pieces_of(step)

        @pl.when(primary)
        def _():
            for piece in pieces:
                cols = piece_cols(piece)
                for line in range(LINES):
                    await_bytes(w.at[layer, line, y, :, cols], z_recv.at[layer, piece, line])
                x_copy(layer, piece).start()
                y_copy(layer, piece).start()

    def step_plane(step):
        layer, pieces = pieces_of(step)

        @pl.when(primary)
        def _():
            for piece in pieces:
                await_bytes(w.at[layer, :, 1 - y, :, piece_cols(piece)], y_recv.at[layer, piece])
                xb_copy(layer, piece).start()

        @pl.when(secondary)
        def _():
            for piece in pieces:
                await_bytes(w.at[layer, :, y, :, piece_cols(piece)], x_recv.at[layer, piece])
                ya_copy(layer, piece).start()

    def tick(step):
        if step + 3 < 2 * CHUNKS:
            step_z(step + 3)
        if step + 8 < 2 * CHUNKS:
            z_start(step + 8)
        step_plane(step)

    def complete(*steps):
        @pl.when(secondary)
        def _():
            for step in steps:
                layer, pieces = pieces_of(step)
                for piece in pieces:
                    cols = piece_cols(piece)
                    await_bytes(w.at[layer, :, 1 - y, high_rows, cols], xb_recv.at[layer, piece])
                    await_bytes(w.at[layer, :, 1 - y, low_rows, cols], ya_recv.at[layer, piece])

    def at_turns(turns):
        def beside(index):
            for turn, steps in turns.items():

                @pl.when(index == turn)
                def _():
                    for step in steps:
                        step()

        return beside

    def ticks(turns):
        return at_turns({turn: (functools.partial(tick, step),) for turn, step in turns.items()})

    kept = {
        "x": (n2.at[pl.ds(0, width), :], x_hbm),
        "h": (res, h_hbm),
        "n1": (n1.at[pl.ds(0, width), :], n1_hbm),
        "n2": (n2.at[pl.ds(0, width), :], n2_hbm),
        "qkv": (qkv, qkv_hbm),
        "ctx": (ctx, ctx_hbm),
        "lse": (lse, lse_hbm),
        "act": (act, act_hbm),
        "slope": (slope, slope_hbm),
    }
    names = tuple(kept)

    def save(name, layer):
        src, dst = kept[name]
        if name in ("x", "h"):
            dst = dst.at[layer]
        return pltpu.make_async_copy(src, dst, save_sem.at[names.index(name), layer])

    def load(name, layer=0):
        dst, src = kept[name]
        if name == "x":
            dst, src = act.at[pl.ds(0, width), :], src.at[layer]
        return pltpu.make_async_copy(src, dst, load_sem.at[names.index(name)])

    def load_h(layer, index):
        slot = lax.rem(index, 2)
        return pltpu.make_async_copy(
            h_hbm.at[layer, :, block_of(index)], h_in.at[slot], h_sem.at[slot]
        )

    my_quarter = pl.ds(s * quarter, quarter)
    my_rows = pl.ds(pl.multiple_of((1 - t) * half + s * quarter, quarter), quarter)

    def clip_across():
        there = pl.ds(pl.multiple_of(t * half + s * quarter, quarter), quarter)
        return remote(
            clips.at[1 - t, my_quarter, :],
            stage.at[there, :],
            in_sem.at[0],
            in_sem.at[1],
            place.across,
        )

    def clip_core():
        part = stage.at[my_rows, :]
        return remote(part, part, in_sem.at[2], in_sem.at[3], place.core)

    def cot_across():
        return remote(
            cot.at[1 - t, my_quarter, :],
            cot_other.at[my_quarter, :],
            cot_sem.at[0],
            cot_sem.at[1],
            place.across,
        )

    def cot_core():
        part = cot_other.at[my_quarter, :]
        return remote(part, part, cot_sem.at[2], cot_sem.at[3], place.core)

    def exchange(kind, index, slot):
        return remote(
            send.at[kind, index],
            recv.at[kind, index],
            e_send.at[slot, index],
            e_recv.at[slot, index],
            place.core,
        )

    def result_copies(ref, first):
        local = pltpu.make_async_copy(stage.at[mine, :], ref.at[0, t], out_sem.at[first])
        away = remote(
            stage.at[theirs, :],
            ref.at[0, t],
            out_sem.at[first + 1],
            out_sem.at[first + 2],
            place.across,
        )
        return local, away

    def grad_copies(index):
        place_in = lax.rem(index, blocks // 2)
        part = in_grad.at[0, t, pl.ds(pl.multiple_of(place_in * BLOCK, BLOCK), BLOCK), :]
        src = stage.at[block_of(index), :]
        local = pltpu.make_async_copy(src, part, grad_sem.at[0, place_in])
        away = remote(
            src, part, grad_sem.at[1, place_in], grad_sem.at[2, place_in], place.across
        )
        return local, away

    def emit(layer, ref, first):
        @pl.when(s == layer)
        def _():
            for copy in result_copies(ref, first):
                copy.start()

    for copy in own_loads:
        copy.wait()
    for step in range(3):
        z_start(step)
    n1[width:, :] = jnp.ones((ONES, frames), BF)
    n2[width:, :] = jnp.ones((ONES, frames), BF)
    own_clip = pltpu.make_async_copy(clips.at[t], stage.at[mine, :], in_sem.at[4])
    own_clip.start()
    clip_across().start()
    cot_across().start()
    own_out.wait()
    shard[:, OUT:UP] = flat[0:WIDE, :].T
    own_up.wait()
    for step in (3, 4):
        z_start(step)

    def take_clip(first):
        def body(index, carry):
            at = pl.ds(pl.multiple_of(first + index * BLOCK, BLOCK), BLOCK)
            tile = stage[at, :].T
            n2[0:width, at] = tile
            res[:, at] = tile.astype(F32)
            return carry

        lax.fori_loop(0, half // BLOCK, body, 0)

    own_clip.wait()
    take_clip(t * half)
    own_down.wait()
    for piece in range(4):
        span = slice((1 + piece) * WIDE, (2 + piece) * WIDE)
        shard[:, DOWN + piece * WIDE : DOWN + (piece + 1) * WIDE] = flat[span, :].T
    clip_across().wait()
    clip_core().start()
    step_z(0)
    z_start(5)
    step_z(1)
    z_start(6)
    clip_core().wait()
    take_clip((1 - t) * half)
    save("x", 0).start()
    step_plane(0)
    step_z(2)
    z_start(7)
    step_plane(1)
    cot_across().wait()
    cot_core().start()
    step_z(3)
    z_start(8)
    step_plane(2)
    step_z(4)
    z_start(9)
    step_z(5)
    z_start(10)

    def project(pair):
        for index in (2 * pair, 2 * pair + 1):
            cols = block_of(index)
            mean, scale = norm_stats(lambda span: res[span, cols], width)
            for span in chunks_of(width):
                hat = (res[span, cols] - mean) * scale
                n1[span, cols] = (hat * vecs[span, 0:1] + vecs[span, 2:3]).astype(BF)
        cols = pair_of(pair)
        for first, many, kind, bias in PARTS:
            value = mm(wt[first : first + many, :], n1[0:width, cols])
            for span in chunks_of(many):
                part = value[span, :]
                if kind != "k":
                    part = part + spread[bias + span.start : bias + span.stop, 6:7]
                if kind == "q":
                    part = part * 0.125
                qkv[first + span.start : first + span.stop, cols] = part.astype(BF)

    def send_pair(kind, pair, slot, value):
        for part in range(2):
            index = 2 * pair + part
            send[kind, index] = value[:, part * BLOCK : (part + 1) * BLOCK].astype(BF)
            exchange(kind, index, slot).start()

    def head_rows(head, first):
        return pl.ds(pl.multiple_of(first + head * HEAD, HEAD), HEAD)

    def attend(layer, turns, later_turns):
        def heads_of(first_head, base, stride, beside):
            def one_head(index_in, carry):
                head = first_head + index_in
                q_rows = head_rows(index_in, base)
                k_rows = head_rows(index_in, base + stride)
                v_rows = head_rows(index_in, base + 2 * stride)
                c_rows = head_rows(head, 0)
                keys = qkv[k_rows, :].T
                for index in range(blocks):
                    cols = slice(index * BLOCK, (index + 1) * BLOCK)
                    queries = qkv[q_rows, cols]
                    tiles = []
                    top = None
                    for tile in chunks_of(frames, BLOCK):
                        scores = mm(keys[tile, :], queries)
                        for span in chunks_of(BLOCK):
                            peak = stack_max(scores[span, :])
                            top = peak if top is None else jnp.maximum(top, peak)
                        tiles.append(scores)
                    top = jnp.max(top, 0, keepdims=True)
                    total = jnp.zeros((8, BLOCK), F32)
                    mixed = jnp.zeros((HEAD, BLOCK), F32)
                    for tile, scores in zip(chunks_of(frames, BLOCK), tiles):
                        soft = []
                        for span in chunks_of(BLOCK):
                            part = jnp.exp(scores[span, :] - top)
                            total = total + stack_sum(part)
                            soft.append(part.astype(BF))
                        mixed = mixed + mm(qkv[v_rows, tile], jnp.concatenate(soft, 0))
                    total = jnp.sum(total, 0, keepdims=True)
                    ctx[c_rows, cols] = (mixed / total).astype(BF)
                    lse[pl.ds(head, 1), cols] = top + jnp.log(total)
                beside(index_in)
                return carry

            return one_head

        lax.fori_loop(0, 4, heads_of(0, 0, 256, ticks(turns)), 0)
        lax.fori_loop(0, 2, heads_of(4, 768, 128, ticks(later_turns)), 0)

    def out_project(layer, turns):
        beside = ticks(turns)

        def body(index, carry):
            part = mm(whole(w, layer, OUT, 384), ctx[:, pair_of(index)])
            send_pair(0, index, 2 * layer, part)
            beside(index)
            return carry

        lax.fori_loop(0, blocks // 2, body, 0)

    def middle_norm(layer, turns):
        beside = ticks(turns)

        def body(index, carry):
            cols = block_of(index)
            exchange(0, index, 2 * layer).wait()
            for span in chunks_of(width):
                added = send[0, index, span, :].astype(F32) + recv[0, index, span, :].astype(F32)
                res[span, cols] = res[span, cols] + added + vecs[span, 3:4]
            mean, scale = norm_stats(lambda span: res[span, cols], width)
            for span in chunks_of(width):
                hat = (res[span, cols] - mean) * scale
                n2[span, cols] = (hat * vecs[span, 1:2] + vecs[span, 4:5]).astype(BF)
            beside(index)
            return carry

        lax.fori_loop(0, blocks, body, 0)

    def hidden_part(layer, part):
        flip_weights(w, wt, layer, UP + part * WIDE, WIDE, part * WIDE)
        units = slice(part * WIDE, (part + 1) * WIDE)
        lane = 7 if part < 2 else 8

        def body(index, carry):
            cols = pair_of(index)
            pre = mm(wt[units, :], n2[0:width, cols])
            for span in chunks_of(WIDE):
                first = part * WIDE + span.start
                bias = spread[768 + first : 768 + first + ROWS, lane : lane + 1]
                value, steep = gelu_parts(pre[span, :] + bias)
                act[first : first + ROWS, cols] = value.astype(BF)
                slope[first : first + ROWS, cols] = steep.astype(BF)
            return carry

        lax.fori_loop(0, blocks // 2, body, 0)

    def down_project(layer, turns):
        beside = ticks(turns)

        def body(index, carry):
            part = mm(whole(w, layer, DOWN, 1536), act[:, pair_of(index)])
            send_pair(1, index, 2 * layer + 1, part)
            beside(index)
            return carry

        lax.fori_loop(0, blocks // 2, body, 0)

    def layer_end(layer, index, span):
        added = send[1, index, span, :].astype(F32) + recv[1, index, span, :].astype(F32)
        return (res[span, block_of(index)] + added + vecs[span, 5:6]).astype(BF)

    def take_vectors(layer):
        vecs[...] = whole(w, layer, VEC, 128).astype(F32)
        spread_biases(vecs, spread, rows)

    def project_all(layer, turns):
        beside = ticks(turns)
        flip_weights(w, wt, layer, QKV, 1152)

        def body(index, carry):
            project(index)
            beside(index)
            return carry

        lax.fori_loop(0, blocks // 2, body, 0)
        if layer == 0:
            save("n1", 0).start()
            save("qkv", 0).start()

    complete(0, 1, 2)
    take_vectors(0)
    project_all(0, {0: 3, 1: 4})
    cot_core().wait()
    load_cot = pltpu.make_async_copy(cot_other, stage.at[theirs, :], cot_sem.at[4])
    load_cot.start()
    own_cot = pltpu.make_async_copy(cot.at[t], stage.at[mine, :], cot_sem.at[5])
    own_cot.start()
    attend(0, {0: 5, 2: 6}, {0: 7})
    save("ctx", 0).start()
    save("lse", 0).start()
    complete(3)
    out_project(0, {1: 8})
    load_cot.wait()
    own_cot.wait()

    sums[3] = jnp.zeros_like(sums[3])

    def take_cot(index, carry):
        low[:, block_of(index)] = stage[block_of(index), :].T
        for span in chunks_of(width):
            sums[3, span, :] += fold(low[span, block_of(index)].astype(F32))
        return carry

    lax.fori_loop(0, blocks, take_cot, 0)
    save("x", 0).wait()
    middle_norm(0, {1: 9})
    save("h", 0).start()
    save("n2", 0).start()
    for part in range(4):
        complete(4 + part)
        hidden_part(0, part)
        tick(10 + part)
    save("act", 0).start()
    save("slope", 0).start()
    complete(8, 9, 10, 11)
    down_project(0, {1: 14})
    for name in ("n1", "qkv", "h", "n2"):
        save(name, 0).wait()

    def finish_body(index, carry):
        exchange(1, index, 1).wait()
        cols = block_of(index)
        for span in chunks_of(width):
            rows_out = layer_end(0, index, span)
            n2[span, cols] = rows_out
            res[span, cols] = rows_out.astype(F32)

        @pl.when(s == 0)
        def _():
            stage[cols, :] = n2[0:width, cols].T

        return carry

    lax.fori_loop(0, blocks, finish_body, 0)
    emit(0, out, 0)
    save("x", 1).start()
    complete(12, 13, 14)
    take_vectors(1)
    project_all(1, {0: 15, 1: 16})
    save("ctx", 0).wait()
    save("lse", 0).wait()
    attend(1, {0: 17, 2: 18}, {0: 19})
    complete(15)
    out_project(1, {1: 20})
    save("x", 1).wait()
    middle_norm(1, {1: 21})
    save("h", 1).start()
    save("act", 0).wait()
    save("slope", 0).wait()
    for part in range(4):
        complete(16 + part)
        hidden_part(1, part)
        if part < 2:
            tick(22 + part)
    for part in range(4):
        complete(20 + part)
        flip_weights(w, wt, 1, DOWN + part * WIDE, WIDE, part * WIDE)
    down_project(1, {})

    def gya_copy(layer, piece):
        cols = piece_cols(piece)
        return remote(
            w.at[layer, :, 1 - y, low_rows, cols],
            land_a.at[:, low_rows, cols],
            gya_send.at[layer, piece],
            gya_recv.at[layer, piece],
            place.beside,
        )

    def gxb_copy(layer, piece):
        cols = piece_cols(piece)
        return remote(
            w.at[layer, :, 1 - y, high_rows, cols],
            land_b.at[:, :, cols],
            gxb_send.at[layer, piece],
            gxb_recv.at[layer, piece],
            place.across,
        )

    def gx_copy(layer, piece):
        cols = piece_cols(piece)
        return remote(
            w.at[layer, :, y, :, cols],
            land_a.at[:, :, cols],
            gx_send.at[layer, piece],
            gx_recv.at[layer, piece],
            place.across,
        )

    def gy_copy(layer, piece):
        cols = piece_cols(piece)
        return remote(
            w.at[layer, :, 1 - y, :, cols],
            land_y.at[:, :, cols],
            gy_send.at[layer, piece],
            gy_recv.at[layer, piece],
            place.beside,
        )

    def landed_part(piece):
        if piece == VECTORS:
            return landed_vec
        ref, first = (
            (landed_qkv, 0)
            if piece < 3
            else (landed_out, 3)
            if piece < 4
            else (landed_up, 4)
            if piece < 8
            else (landed_down, 8)
        )
        return ref.at[:, :, pl.ds((piece - first) * WIDE, WIDE)]

    def gz_copies(layer, piece):
        cols = piece_cols(piece)
        target = landed_part(piece)
        copies = []
        for step in range(LINES):
            line = place.line(step)
            copies.append(
                remote(
                    w.at[layer, line, y, :, cols],
                    target.at[e],
                    gz_send.at[layer, piece, step],
                    gz_recv.at[piece, e],
                    (layer, place.row_of(line, y), t),
                )
            )
        local = pltpu.make_async_copy(
            w.at[layer, e, y, :, cols], target.at[e], gz_recv.at[piece, e]
        )
        return copies, local

    def add_rows(layer, piece, which, span, lands):
        cols = piece_cols(piece)
        first, count = span
        for line in range(LINES):
            total = w[layer, line, which, pl.ds(first, count), cols].astype(F32)
            for land, offset in lands:
                total = total + land[line, pl.ds(offset, count), cols].astype(F32)
            w[layer, line, which, pl.ds(first, count), cols] = total.astype(BF)

    def signal(sem, layer, piece, device):
        if layer == 1:
            pl.semaphore_signal(sem.at[piece], inc=1, device_id=device, device_id_type=MESH)

    def credit(sem, layer, piece):
        if layer == 0:
            pl.semaphore_wait(sem.at[piece], 1)

    def step_a(layer, piece):
        @pl.when(secondary)
        def _():
            credit(ya_free, layer, piece)
            gya_copy(layer, piece).start()
            credit(xb_free, layer, piece)
            gxb_copy(layer, piece).start()

    def step_b(layer, piece):
        cols = piece_cols(piece)

        @pl.when(secondary)
        def _():
            await_bytes(land_a.at[:, low_rows, cols], gya_recv.at[layer, piece])
            add_rows(layer, piece, y, (0, SPLIT), [(land_a, 0)])
            signal(ya_free, layer, piece, place.beside)
            credit(x_free, layer, piece)
            gx_copy(layer, piece).start()

        @pl.when(primary)
        def _():
            await_bytes(land_b.at[:, :, cols], gxb_recv.at[layer, piece])
            add_rows(layer, piece, 1 - y, (SPLIT, rows - SPLIT), [(land_b, 0)])
            signal(xb_free, layer, piece, place.across)
            credit(y_free, layer, piece)
            gy_copy(layer, piece).start()

    def step_c(layer, piece):
        cols = piece_cols(piece)

        @pl.when(primary)
        def _():
            await_bytes(land_a.at[:, :, cols], gx_recv.at[layer, piece])
            await_bytes(land_y.at[:, :, cols], gy_recv.at[layer, piece])
            add_rows(layer, piece, y, (0, rows), [(land_a, 0), (land_y, 0)])
            signal(x_free, layer, piece, place.across)
            signal(y_free, layer, piece, place.beside)
            copies, local = gz_copies(layer, piece)

            @pl.when(s == layer)
            def _():
                local.start()

            @pl.when(s != layer)
            def _():
                copies[0].start()

            for copy in copies[1:]:
                copy.start()

    def store_grads(layer, start, count, value):
        w[layer, :, :, :, pl.ds(start, count)] = value.astype(BF).reshape(
            w.shape[1], w.shape[2], rows, count
        )

    def mlp_back(layer, beside):
        def body(index, carry):
            cols = pair_of(index)
            for part in range(4):
                units = slice(part * WIDE, (part + 1) * WIDE)
                grad = mm(wt[units, :], low[:, cols])
                for span in chunks_of(WIDE):
                    rows_in = slice(units.start + span.start, units.start + span.stop)
                    steep = slope[rows_in, cols].astype(F32)
                    slope[rows_in, cols] = (grad[span, :] * steep).astype(BF)
            term = mm(whole(w, layer, UP, 1536), slope[:, cols])
            send_pair(0, index, 4 + 2 * layer, term)
            beside(index)
            return carry

        lax.fori_loop(0, blocks // 2, body, 0)

    def outer(layer, start, left, right, first, many, before, beside):
        def body(index, carry):
            before(index)
            base = index * PAIR
            span = pl.ds(pl.multiple_of(first + base, 128), PAIR)
            value = mmt(left[...], right[span, :])
            store_grads(layer, pl.multiple_of(start + base, 128), PAIR, value[0:width, :])
            if left.shape[0] > width:
                to = pl.ds(pl.multiple_of(768 + base, BLOCK), PAIR)
                spread[to, 0:8] = value[width : width + 8, :].T
            beside(index)
            return carry

        lax.fori_loop(0, many // PAIR, body, 0)

    def turned(turn):
        return lax.rem(turn + (1 - t) * (blocks // 2), blocks)

    def norm_back(layer, kind, gain_lane, source, put, finish, beside):
        sums[0:3] = jnp.zeros((3, width, 128), F32)

        def body(turn, carry):
            index = turned(turn)
            cols = block_of(index)
            read = source(index)
            mean, scale = norm_stats(read, width)
            exchange(kind, index, 4 + 2 * layer + kind).wait()
            first = jnp.zeros((8, BLOCK), F32)
            second = jnp.zeros((8, BLOCK), F32)

            def terms(span):
                hat = (read(span) - mean) * scale
                grad = send[kind, index, span, :].astype(F32)
                grad = grad + recv[kind, index, span, :].astype(F32)
                return hat, grad, grad * vecs[span, gain_lane : gain_lane + 1]

            for span in chunks_of(width):
                hat, grad, scaled = terms(span)
                sums[0, span, :] += fold(grad * hat)
                sums[1, span, :] += fold(grad)
                first = first + stack_sum(scaled)
                second = second + stack_sum(scaled * hat)
            level = mean_of(first, width)
            slant = mean_of(second, width)
            for span in chunks_of(width):
                hat, _, scaled = terms(span)
                put(span, cols, res[span, cols] + scale * (scaled - level - hat * slant))
            finish(index)
            beside(turn)
            return carry

        lax.fori_loop(0, blocks, body, 0)

    def row_sums(value):
        return jnp.sum(value, 1, keepdims=True)

    def attend_back(first_head, many, base, stride, beside):
        def one_head(index_in, carry):
            head = first_head + index_in
            q_rows = head_rows(index_in, base)
            k_rows = head_rows(index_in, base + stride)
            v_rows = head_rows(index_in, base + 2 * stride)
            c_rows = head_rows(head, 0)
            keys = qkv[k_rows, :].T
            values = qkv[v_rows, :].T
            flat_queries = qkv[q_rows, :].T
            flat_grads = dctx[c_rows, :].T
            level = lse[pl.ds(head, 1), :]
            inner = jnp.sum(
                dctx[c_rows, :].astype(F32) * ctx[c_rows, :].astype(F32), 0, keepdims=True
            )
            step = jnp.zeros((HEAD, frames), F32)
            for tile in chunks_of(frames, BLOCK):
                soft = []
                score_grad = []
                for cols in chunks_of(frames, BLOCK):
                    scores = mm(keys[tile, :], qkv[q_rows, cols])
                    soft_grad = mm(values[tile, :], dctx[c_rows, cols])
                    soft_parts = []
                    grad_parts = []
                    for part in chunks_of(BLOCK):
                        strength = jnp.exp(scores[part, :] - level[:, cols])
                        soft_parts.append(strength.astype(BF))
                        strength = strength * (soft_grad[part, :] - inner[:, cols])
                        grad_parts.append(strength.astype(BF))
                    soft.append(jnp.concatenate(soft_parts, 0))
                    score_grad.append(jnp.concatenate(grad_parts, 0))
                soft = jnp.concatenate(soft, 1)
                score_grad = jnp.concatenate(score_grad, 1)
                step = step + mm(qkv[k_rows, tile], score_grad)
                slope[k_rows, tile] = mm(score_grad, flat_queries).astype(BF).T
                slope[v_rows, tile] = mm(soft, flat_grads).astype(BF).T
            slope[q_rows, :] = (step * 0.125).astype(BF)
            beside(index_in)
            return carry

        lax.fori_loop(0, many, one_head, 0)

    def keep_sums(first, value):
        for start, many, kind, bias in PARTS:
            offset = start - first
            if kind != "k" and 0 <= offset < value.shape[1]:
                spread[bias : bias + many, 0:8] = value[
                    width : width + 8, offset : offset + many
                ].T

    def collect_biases():
        def body(group, carry):
            source = group * rows
            for kind in range(2):
                for head in range(6):
                    at = pl.ds(pl.multiple_of(kind * 384 + head * HEAD + group * 8, 8), 8)
                    to = pl.ds(pl.multiple_of(source + kind * 48 + head * 8, 8), 8)
                    vec_grads[to, 6:7] = spread[at, 6:7]
            for unit in range(24):
                at = pl.ds(pl.multiple_of(768 + unit * HEAD + group * 8, 8), 8)
                to = pl.ds(pl.multiple_of(source + (unit % 12) * 8, 8), 8)
                lane = 7 if unit < 12 else 8
                vec_grads[to, lane : lane + 1] = spread[at, 6:7]
            return carry

        lax.fori_loop(0, GROUPS, body, 0)

    def nothing(index):
        del index

    def finish_gather(layer, piece):
        @pl.when(primary)
        def _():
            x_copy(layer, piece).wait_send()
            y_copy(layer, piece).wait_send()
            xb_copy(layer, piece).wait_send()

        @pl.when(secondary)
        def _():
            ya_copy(layer, piece).wait_send()

    def last_body(index, carry):
        exchange(1, index, 3).wait()

        @pl.when(s == 1)
        def _():
            for span in chunks_of(width, 128):
                stage[block_of(index), span] = layer_end(1, index, span).T

        return carry

    for layer in (1, 0):
        later = layer == 0
        if later:
            load_h(layer, turned(0)).start()
            load("act").wait()
            vecs[...] = whole(w, layer, VEC, 128).astype(F32)
            flip_weights(w, wt, layer, DOWN, 1536)
        vec_grads[...] = jnp.zeros_like(vec_grads)

        def a(piece, layer=layer):
            return lambda: step_a(layer, piece)

        def b(piece, layer=layer):
            return lambda: step_b(layer, piece)

        def c(piece, layer=layer):
            return lambda: step_c(layer, piece)

        if later:
            before = nothing
            early = at_turns(
                {
                    0: (a(8), lambda: step_b(1, VECTORS)),
                    1: (a(9), lambda: step_c(1, VECTORS)),
                    2: (a(10), a(11)),
                }
            )
        else:
            waits = [functools.partial(finish_gather, 1, piece) for piece in (8, 9, 10, 11)]
            before = at_turns({0: waits[:2], 1: waits[2:3], 2: waits[3:]})
            early = at_turns({0: (a(8),), 1: (a(9),), 2: (a(10), a(11))})
        outer(layer, DOWN, low, act, 0, 1536, before, early)
        load("x", layer).start()
        vec_grads[:, 5:6] = row_sums(sums[3])
        if not later:
            lax.fori_loop(0, blocks, last_body, 0)
            emit(1, out, 0)
            save("h", 1).wait()
            load_h(layer, turned(0)).start()
            res[...] = low[...].astype(F32)
            for piece in range(CHUNKS + 1):
                z_finish(piece)
                finish_gather(0, piece)
                if piece < 8 or piece == VECTORS:
                    finish_gather(1, piece)
        else:
            load("slope").wait()

        mlp_back(layer, at_turns({0: (b(8),), 1: (b(9), b(10), b(11))}))
        if later:
            load("n2").wait()
        drain = at_turns({0: (a(4),), 1: (a(5),), 2: (a(6), a(7), c(8))})
        outer(layer, UP, n2, slope, 0, 1536, nothing, drain)
        flip_weights(w, wt, layer, OUT, 384)

        def hidden_in(index, layer=layer):
            turn = lax.rem(index + (1 - t) * (blocks // 2), blocks)

            @pl.when(turn + 1 < blocks)
            def _():
                load_h(layer, turned(turn + 1)).start()

            load_h(layer, index).wait()
            slot = lax.rem(index, 2)
            return lambda span: h_in[slot, span, :]

        def hidden_put(span, cols, total):
            res[span, cols] = total
            rounded = total.astype(BF)
            low[span, cols] = rounded
            sums[2, span, :] += fold(rounded.astype(F32))

        drain = at_turns({0: (b(4), c(9)), 1: (b(5), c(10)), 2: (b(6), c(11)), 3: (b(7),)})
        norm_back(layer, 0, 1, hidden_in, hidden_put, nothing, drain)

        def context_back(index, carry):
            cols = pair_of(index)
            dctx[:, cols] = mm(wt[0:384, :], low[:, cols]).astype(BF)
            return carry

        lax.fori_loop(0, blocks // 2, context_back, 0)
        vec_grads[:, 1:2] = row_sums(sums[0])
        vec_grads[:, 4:5] = row_sums(sums[1])
        vec_grads[:, 3:4] = row_sums(sums[2])
        if later:
            for name in ("ctx", "qkv", "lse"):
                load(name).wait()
        store_grads(layer, OUT, 384, mmt(low[...], ctx[...]))
        step_a(layer, 3)
        drain = at_turns({0: (c(4),), 1: (c(5),), 2: (b(3), c(6)), 3: (c(7),)})
        attend_back(0, 4, 0, 256, drain)
        if later:
            load("n1").wait()
        wt[0:768, :] = whole(w, layer, QKV, 768)

        for first, many in ((0, 512), (512, 256)):
            value = mmt(n1[...], slope[first : first + many, :])
            store_grads(layer, QKV + first, many, value[0:width, :])
            keep_sums(first, value)
        step_a(layer, 0)
        step_a(layer, 1)
        attend_back(4, 2, 768, 128, at_turns({0: (b(0), c(3)), 1: (b(1),)}))

        def first_body(index, carry, layer=layer):
            cols = pair_of(index)
            term = mm(wt[0:768, :], slope[0:768, cols])
            term = term + mm(whole(w, layer, QKV + 768, WIDE), slope[768:1152, cols])
            send_pair(1, index, 5 + 2 * layer, term)
            return carry

        lax.fori_loop(0, blocks // 2, first_body, 0)
        value = mmt(n1[...], slope[768:1152, :])
        store_grads(layer, QKV + 768, WIDE, value[0:width, :])
        keep_sums(768, value)
        step_a(layer, 2)
        step_c(layer, 0)
        collect_biases()
        if layer == 1:
            for name in ("slope", "n1", "n2", "ctx", "qkv", "lse"):
                load(name).start()
        load("x", layer).wait()

        @pl.when(s == layer)
        def _():
            local, away = result_copies(out, 0)
            local.wait()
            away.wait_send()

        def rows_x(index):
            return lambda span: act[span, block_of(index)].astype(F32)

        def rows_put(span, cols, total, layer=layer):
            rounded = total.astype(BF)
            low[span, cols] = rounded
            if layer == 1:
                res[span, cols] = rounded.astype(F32)
                sums[2, span, :] += fold(rounded.astype(F32))

        def rows_out(index, layer=layer):
            @pl.when(s == layer)
            def _():
                stage[block_of(index), :] = low[:, block_of(index)].T
                local, away = grad_copies(index)

                @pl.when(index // (blocks // 2) == t)
                def _():
                    local.start()

                @pl.when(index // (blocks // 2) != t)
                def _():
                    away.start()

        drain = at_turns({0: (c(1),), 1: (b(2),), 3: (c(2),)})
        norm_back(layer, 1, 0, rows_x, rows_put, rows_out, drain)
        if layer == 1:
            load("act").start()
        vec_grads[:, 0:1] = row_sums(sums[0])
        vec_grads[:, 2:3] = row_sums(sums[1])
        sums[3] = sums[2]
        store_grads(layer, VEC, 128, vec_grads[...])
        step_a(layer, VECTORS)

    step_b(0, VECTORS)
    step_c(0, VECTORS)

    def finish_scatter(piece):
        for layer in range(2):

            @pl.when(secondary)
            def _():
                gya_copy(layer, piece).wait_send()
                gxb_copy(layer, piece).wait_send()
                gx_copy(layer, piece).wait_send()

            @pl.when(primary)
            def _():
                gy_copy(layer, piece).wait_send()
                copies, _ = gz_copies(layer, piece)

                @pl.when(s != layer)
                def _():
                    copies[0].wait_send()

                for copy in copies[1:]:
                    copy.wait_send()

    for piece in range(CHUNKS + 1):
        finish_scatter(piece)
        for line in range(LINES):
            await_bytes(landed_part(piece).at[line], gz_recv.at[piece, line])

    _, away = result_copies(out, 0)
    away.wait_recv()
    for index in range(blocks // 2):
        local, away = grad_copies(index)
        local.wait()
        away.wait()


def layers_call(share, clips, cotangent, shards, dims):
    width, frames, hidden_units, heads_width = dims
    rows = width // GROUPS
    sem = pltpu.SemaphoreType.DMA
    free = pltpu.SemaphoreType.REGULAR
    packed = (2, LINES, 2, rows, END)
    blocks = frames // BLOCK
    shape = jax.ShapeDtypeStruct
    outs = [
        shape((1,) + clips.shape, BF),
        shape((1,) + clips.shape, BF),
        shape((LINES, rows, QKV - VEC), BF),
        shape((LINES, rows, OUT - QKV), BF),
        shape((LINES, rows, UP - OUT), BF),
        shape((LINES, rows, DOWN - UP), BF),
        shape((LINES, rows, END - DOWN), BF),
        shape(clips.shape[1:], BF),
        shape((2, width, frames), BF),
        shape((2, width, frames), F32),
        shape((width, frames), BF),
        shape((width, frames), BF),
        shape((3 * heads_width, frames), BF),
        shape((heads_width, frames), BF),
        shape((8, frames), F32),
        shape((hidden_units, frames), BF),
        shape((hidden_units, frames), BF),
    ]
    scratch = [
        pltpu.VMEM(packed, BF),
        pltpu.VMEM((width, frames), F32),
        pltpu.VMEM((hidden_units, frames), BF),
        pltpu.VMEM((hidden_units, frames), BF),
        pltpu.VMEM((width + ONES, frames), BF),
        pltpu.VMEM((width + ONES, frames), BF),
        pltpu.VMEM((width, frames), BF),
        pltpu.VMEM((3 * heads_width, frames), BF),
        pltpu.VMEM((heads_width, frames), BF),
        pltpu.VMEM((heads_width, frames), BF),
        pltpu.VMEM((8, frames), F32),
        pltpu.VMEM((2, width, BLOCK), F32),
        pltpu.VMEM((hidden_units, width), BF),
        pltpu.VMEM((2, blocks, width, BLOCK), BF),
        pltpu.VMEM((2, blocks, width, BLOCK), BF),
        pltpu.VMEM((width, 128), F32),
        pltpu.VMEM((width, 128), F32),
        pltpu.VMEM((4, width, 128), F32),
        pltpu.VMEM((2 * heads_width + hidden_units, 128), F32),
        pltpu.VMEM((frames, width), BF),
        pltpu.VMEM((rows, END), BF),
        pltpu.VMEM((WIDE + END - DOWN, rows), BF),
        pltpu.VMEM((LINES, rows, END), BF),
        pltpu.VMEM((LINES, rows - SPLIT, END), BF),
        pltpu.VMEM((LINES, rows, END), BF),
    ]
    scratch += [sem((CHUNKS + 1, LINES)), sem((2, CHUNKS + 1, LINES))]
    scratch += [sem((2, CHUNKS + 1))] * 8
    scratch += [sem((2, CHUNKS + 1, LINES)), sem((CHUNKS + 1, LINES))]
    scratch += [sem((2, CHUNKS + 1))] * 8
    scratch += [
        sem((8, blocks)),
        sem((8, blocks)),
        sem((10,)),
        sem((5,)),
        sem((6,)),
        sem((3,)),
        sem((3, blocks // 2)),
        sem((9, 2)),
        sem((9,)),
        sem((2,)),
    ]
    scratch += [free((CHUNKS + 1,))] * 4
    anywhere = pl.BlockSpec(memory_space=pl.ANY)
    return pl.pallas_call(
        functools.partial(layers_kernel, share),
        out_shape=outs,
        in_specs=[anywhere] * (2 + len(shards)),
        out_specs=[anywhere] * len(outs),
        scratch_shapes=scratch,
        compiler_params=pltpu.CompilerParams(
            collective_id=0, has_side_effects=True, vmem_limit_bytes=VMEM_LIMIT
        ),
        cost_estimate=pl.CostEstimate(
            flops=60_000_000_000, bytes_accessed=60_000_000, transcendentals=0
        ),
    )(clips, cotangent, *shards)


def group_piece(value, axis, share):
    if share == 1:
        return value
    size = value.shape[axis] * share
    group = lax.axis_index("dp") // share
    full = lax.all_gather(value, "dp", axis=axis, tiled=True)
    return lax.dynamic_slice_in_dim(full, group * size, size, axis)


def own_part(value, axis, share, parts, index):
    size = value.shape[axis] // parts
    if parts == 1:
        return value
    return lax.dynamic_slice_in_dim(value, index * size, size, axis)


def on_device(share, clips, cotangent, ln_gains, row_biases, w_qkv, b_qv, w_o, w_up, b_ff, w_down):
    width = clips.shape[2]
    rows = width // GROUPS
    dims = (width, 2 * clips.shape[1], w_up.shape[2], w_o.shape[1])
    ln_gains = group_piece(ln_gains, 2, share)
    row_biases = group_piece(row_biases, 2, share)
    w_qkv = group_piece(w_qkv, 2, share)
    b_qv = group_piece(b_qv, 3, share)
    w_o = group_piece(w_o, 2, share)
    w_up = group_piece(w_up, 1, share)
    b_ff = group_piece(b_ff, 2, share)
    w_down = group_piece(w_down, 2, share)
    vectors = jnp.concatenate([ln_gains[0], row_biases[0]], 0).T
    heads = jnp.concatenate([b_qv[0, 0].reshape(-1), b_qv[0, 1].reshape(-1)])[:, None]
    units = b_ff[0].reshape(2, rows).T
    packed = jnp.concatenate([vectors, heads, units], 1)
    packed = jnp.pad(packed, ((0, 0), (0, 128 - packed.shape[1])))
    section_out, section_in_grad, *landed = layers_call(
        share, clips, cotangent, (packed, w_qkv, w_o, w_up, w_down), dims
    )
    rest = lax.axis_index("dp") % share
    side = lax.axis_index("tensor")

    def joined(value):
        total = jnp.sum(value.astype(F32), 0)
        if share == 1:
            return total
        group = lax.axis_index("dp") // share
        padded = jnp.zeros((width, total.shape[1]), F32)
        padded = lax.dynamic_update_slice_in_dim(padded, total, group * rows, 0)
        return lax.dynamic_slice_in_dim(lax.psum(padded, "dp"), group * rows, rows, 0)

    def mine(value):
        return own_part(joined(value), 0, share, share, rest)

    vectors = joined(landed[0])
    vec = own_part(own_part(vectors, 0, share, share, rest), 0, share, 2, side)
    heads_grad = vectors[:, 6].reshape(2, -1, HEAD // GROUPS)
    units_grad = vectors[:, 7:9].T.reshape(-1, HEAD // GROUPS)
    qkv_grad = {"q": [], "k": [], "v": []}
    for first, many, kind, _ in PARTS:
        qkv_grad[kind].append(mine(landed[1][:, :, first : first + many]))
    return (
        section_out,
        section_in_grad,
        vec[:, 0:2].T[None],
        vec[:, 2:6].T[None],
        jnp.stack([jnp.concatenate(qkv_grad[kind], 1) for kind in "qkv"])[None],
        own_part(heads_grad, 2, share, share, rest)[None],
        mine(landed[2]).T[None],
        mine(landed[3])[None],
        own_part(units_grad, 1, share, share, rest)[None],
        mine(landed[4]).T[None],
    )


def solution(mesh):
    placed = (
        P("dp", "tensor", None),
        P("dp", "tensor", None),
        P("section", None, "dp"),
        P("section", None, "dp"),
        P("section", None, "dp", "tensor"),
        P("section", None, "tensor", "dp"),
        P("section", "tensor", "dp"),
        P("section", "dp", "tensor"),
        P("section", "tensor", "dp"),
        P("section", "tensor", "dp"),
    )
    share = mesh.shape["dp"] // GROUPS
    return jax.shard_map(
        functools.partial(on_device, share),
        mesh=mesh,
        in_specs=placed,
        out_specs=(
            P("section", "dp", "tensor", None),
            P("section", "dp", "tensor", None),
            P("section", None, ("dp", "tensor")),
            P("section", None, ("dp", "tensor")),
            P("section", None, "dp", "tensor"),
            P("section", None, "tensor", "dp"),
            P("section", "tensor", "dp"),
            P("section", "dp", "tensor"),
            P("section", "tensor", "dp"),
            P("section", "tensor", "dp"),
        ),
        check_vma=False,
    )
```

```python
import functools

import jax
import jax.numpy as jnp
from jax import lax
from jax.experimental import pallas as pl
from jax.experimental.pallas import tpu as pltpu
from jax.sharding import PartitionSpec as P

BF = jnp.bfloat16
F32 = jnp.float32
MESH = pl.DeviceIdType.MESH
EPSILON = 1e-05
HEAD = 64
GROUPS = 8
LINES = 4
BLOCK = 256
PAIR = 2 * BLOCK
ROWS = 64
ONES = 16
VMEM_LIMIT = 62 * 1024 * 1024

VEC = 0
QKV = 128
OUT = 1280
UP = 1664
DOWN = 3200
END = 4736
SPLIT = 32
WIDE = 384
CHUNKS = 12


PARTS = (
    (0, 256, "q", 0),
    (256, 256, "k", 0),
    (512, 256, "v", 384),
    (768, 128, "q", 256),
    (896, 128, "k", 256),
    (1024, 128, "v", 640),
)


def mm(left, right):
    return jnp.dot(left, right, preferred_element_type=F32)


def mmt(left, right):
    return lax.dot_general(left, right, (((1,), (1,)), ((), ())), preferred_element_type=F32)


class Place:
    def __init__(self, share):
        self.s = lax.axis_index("section")
        self.d = lax.axis_index("dp")
        self.t = lax.axis_index("tensor")
        group = self.d // share
        self.rest = self.d - group * share
        self.share = share
        self.e = group // 2
        self.y = group - self.e * 2
        self.primary = self.s == self.t
        self.core = (1 - self.s, self.d, self.t)
        self.across = (self.s, self.d, 1 - self.t)
        self.beside = (self.s, self.row_of(self.e, 1 - self.y), self.t)

    def row_of(self, line, y):
        return (line * 2 + y) * self.share + self.rest

    def line(self, step):
        return lax.rem(self.e + step, LINES)

    def greet(self):
        barrier = pltpu.get_barrier_semaphore()
        peers = [self.core, self.across, self.beside]
        for step in range(1, LINES):
            for section in range(2):
                peers.append((section, self.row_of(self.line(step), self.y), self.t))
        for peer in peers:
            pl.semaphore_signal(barrier, inc=1, device_id=peer, device_id_type=MESH)
        pl.semaphore_wait(barrier, len(peers))


def remote(src, dst, send_sem, recv_sem, device):
    return pltpu.make_async_remote_copy(
        src_ref=src,
        dst_ref=dst,
        send_sem=send_sem,
        recv_sem=recv_sem,
        device_id=device,
        device_id_type=MESH,
    )


def await_bytes(ref, sem):
    pltpu.make_async_copy(ref, ref, sem).wait()


def chunks_of(count, size=ROWS):
    return [slice(first, first + size) for first in range(0, count, size)]


def by_eights(value):
    return value.reshape(value.shape[0] // 8, 8, value.shape[1])


def stack_sum(value):
    return jnp.sum(by_eights(value), 0)


def stack_max(value):
    return jnp.max(by_eights(value), 0)


def mean_of(parts, count):
    return jnp.sum(parts, 0, keepdims=True) / count


def norm_stats(read, count):
    total = jnp.zeros((8, BLOCK), F32)
    for span in chunks_of(count):
        total = total + stack_sum(read(span))
    mean = mean_of(total, count)
    square = jnp.zeros((8, BLOCK), F32)
    for span in chunks_of(count):
        centred = read(span) - mean
        square = square + stack_sum(centred * centred)
    return mean, lax.rsqrt(mean_of(square, count) + EPSILON)


def gelu_parts(values):
    bell = jnp.exp(-0.5 * values * values)
    reach = jnp.abs(values) * 0.7071067811865476
    inv = 1.0 / (1.0 + 0.3275911 * reach)
    poly = inv * (
        0.254829592
        + inv * (-0.284496736 + inv * (1.421413741 + inv * (-1.453152027 + inv * 1.061405429)))
    )
    tail = 0.5 * poly * bell
    cdf = jnp.where(values >= 0.0, 1.0 - tail, tail)
    return values * cdf, cdf + values * bell * 0.3989422804014327


def fold(value):
    return value[:, 0:128] + value[:, 128:256]


def block_of(index):
    return pl.ds(pl.multiple_of(index * BLOCK, BLOCK), BLOCK)


def pair_of(index):
    return pl.ds(pl.multiple_of(index * PAIR, PAIR), PAIR)


def flip_weights(w, wt, layer, start, width, target=0):
    def body(index, carry):
        cols = pl.ds(pl.multiple_of(start + index * 128, 128), 128)
        rows = pl.ds(pl.multiple_of(target + index * 128, 128), 128)
        tile = w[layer, :, :, :, cols]
        wt[rows, :] = tile.reshape(tile.shape[0] * tile.shape[1] * tile.shape[2], 128).T
        return carry

    lax.fori_loop(0, width // 128, body, 0)


def whole(w, layer, start, width):
    tile = w[layer, :, :, :, start : start + width]
    return tile.reshape(tile.shape[0] * tile.shape[1] * tile.shape[2], width)


def spread_biases(vecs, spread, rows):
    def body(group, carry):
        source = group * rows
        for kind in range(2):
            for head in range(6):
                to = pl.ds(pl.multiple_of(kind * 384 + head * HEAD + group * 8, 8), 8)
                at = pl.ds(pl.multiple_of(source + kind * 48 + head * 8, 8), 8)
                spread[to, :] = vecs[at, :]
        for unit in range(24):
            to = pl.ds(pl.multiple_of(768 + unit * HEAD + group * 8, 8), 8)
            at = pl.ds(pl.multiple_of(source + (unit % 12) * 8, 8), 8)
            spread[to, :] = vecs[at, :]
        return carry

    lax.fori_loop(0, GROUPS, body, 0)


def layers_kernel(
    share,
    clips,
    cot,
    vec_in,
    qkv_in,
    out_in,
    up_in,
    down_in,
    out,
    in_grad,
    landed_vec,
    landed_qkv,
    landed_out,
    landed_up,
    landed_down,
    cot_other,
    x_hbm,
    h_hbm,
    n1_hbm,
    n2_hbm,
    qkv_hbm,
    ctx_hbm,
    lse_hbm,
    act_hbm,
    slope_hbm,
    w,
    res,
    act,
    slope,
    n1,
    n2,
    low,
    qkv,
    ctx,
    dctx,
    lse,
    h_in,
    wt,
    send,
    recv,
    vecs,
    vec_grads,
    sums,
    spread,
    stage,
    shard,
    flat,
    land_a,
    land_b,
    land_y,
    z_send,
    z_recv,
    x_send,
    x_recv,
    xb_send,
    xb_recv,
    y_send,
    y_recv,
    ya_send,
    ya_recv,
    gz_send,
    gz_recv,
    gx_send,
    gx_recv,
    gxb_send,
    gxb_recv,
    gy_send,
    gy_recv,
    gya_send,
    gya_recv,
    e_send,
    e_recv,
    own_sem,
    in_sem,
    cot_sem,
    out_sem,
    grad_sem,
    save_sem,
    load_sem,
    h_sem,
    ya_free,
    xb_free,
    x_free,
    y_free,
):
    place = Place(share)
    s, t, e, y = place.s, place.t, place.e, place.y
    primary, secondary = place.primary, jnp.logical_not(place.primary)
    width, frames = res.shape
    blocks = frames // BLOCK
    half = frames // 2
    quarter = half // 2
    rows = w.shape[3]
    low_rows = pl.ds(0, SPLIT)
    high_rows = pl.ds(SPLIT, rows - SPLIT)
    mine = pl.ds(pl.multiple_of(t * half, half), half)
    theirs = pl.ds(pl.multiple_of((1 - t) * half, half), half)

    own_loads = [pltpu.make_async_copy(vec_in, shard.at[:, pl.ds(VEC, QKV)], own_sem.at[0])]
    for number, (first, many, kind, bias) in enumerate(PARTS):
        own_loads.append(
            pltpu.make_async_copy(
                qkv_in.at[0, "qkv".index(kind), :, pl.ds(bias % WIDE, many)],
                shard.at[:, pl.ds(QKV + first, many)],
                own_sem.at[1 + number],
            )
        )
    own_up = pltpu.make_async_copy(up_in.at[0], shard.at[:, pl.ds(UP, DOWN - UP)], own_sem.at[7])
    own_out = pltpu.make_async_copy(out_in.at[0], flat.at[pl.ds(0, WIDE), :], own_sem.at[8])
    own_down = pltpu.make_async_copy(
        down_in.at[0], flat.at[pl.ds(WIDE, END - DOWN), :], own_sem.at[9]
    )
    for copy in own_loads + [own_out, own_up, own_down]:
        copy.start()

    place.greet()

    VECTORS = CHUNKS

    def piece_cols(piece):
        if isinstance(piece, int) and piece == VECTORS:
            return pl.ds(VEC, QKV)
        return pl.ds(pl.multiple_of(QKV + piece * WIDE, 128), WIDE)

    def pieces_of(step):
        layer, piece = step // CHUNKS, step % CHUNKS
        return layer, (VECTORS, piece) if piece == 0 else (piece,)

    def z_copies(piece):
        cols = piece_cols(piece)
        copies = []
        for step in range(LINES):
            copies.append(
                remote(
                    shard.at[:, cols],
                    w.at[s, e, y, :, cols],
                    z_send.at[piece, step],
                    z_recv.at[s, piece, e],
                    (t, place.row_of(place.line(step), y), t),
                )
            )
        local = pltpu.make_async_copy(
            shard.at[:, cols], w.at[s, e, y, :, cols], z_recv.at[s, piece, e]
        )
        return copies, local

    def z_start(step):
        layer, pieces = pieces_of(step)

        @pl.when(s == layer)
        def _():
            for piece in pieces:
                copies, local = z_copies(piece)

                @pl.when(primary)
                def _():
                    local.start()

                @pl.when(secondary)
                def _():
                    copies[0].start()

                for copy in copies[1:]:
                    copy.start()

    def z_finish(piece):
        copies, _ = z_copies(piece)

        @pl.when(secondary)
        def _():
            copies[0].wait_send()

        for copy in copies[1:]:
            copy.wait_send()

    def x_copy(layer, piece):
        part = w.at[layer, :, y, :, piece_cols(piece)]
        return remote(part, part, x_send.at[layer, piece], x_recv.at[layer, piece], place.across)

    def y_copy(layer, piece):
        part = w.at[layer, :, y, :, piece_cols(piece)]
        return remote(part, part, y_send.at[layer, piece], y_recv.at[layer, piece], place.beside)

    def xb_copy(layer, piece):
        part = w.at[layer, :, 1 - y, high_rows, piece_cols(piece)]
        return remote(part, part, xb_send.at[layer, piece], xb_recv.at[layer, piece], place.across)

    def ya_copy(layer, piece):
        part = w.at[layer, :, y, low_rows, piece_cols(piece)]
        return remote(part, part, ya_send.at[layer, piece], ya_recv.at[layer, piece], place.beside)

    def step_z(step):
        layer, pieces = pieces_of(step)

        @pl.when(primary)
        def _():
            for piece in pieces:
                cols = piece_cols(piece)
                for line in range(LINES):
                    await_bytes(w.at[layer, line, y, :, cols], z_recv.at[layer, piece, line])
                x_copy(layer, piece).start()
                y_copy(layer, piece).start()

    def step_plane(step):
        layer, pieces = pieces_of(step)

        @pl.when(primary)
        def _():
            for piece in pieces:
                await_bytes(w.at[layer, :, 1 - y, :, piece_cols(piece)], y_recv.at[layer, piece])
                xb_copy(layer, piece).start()

        @pl.when(secondary)
        def _():
            for piece in pieces:
                await_bytes(w.at[layer, :, y, :, piece_cols(piece)], x_recv.at[layer, piece])
                ya_copy(layer, piece).start()

    def tick(step):
        if step + 3 < 2 * CHUNKS:
            step_z(step + 3)
        if step + 8 < 2 * CHUNKS:
            z_start(step + 8)
        step_plane(step)

    def complete(*steps):
        @pl.when(secondary)
        def _():
            for step in steps:
                layer, pieces = pieces_of(step)
                for piece in pieces:
                    cols = piece_cols(piece)
                    await_bytes(w.at[layer, :, 1 - y, high_rows, cols], xb_recv.at[layer, piece])
                    await_bytes(w.at[layer, :, 1 - y, low_rows, cols], ya_recv.at[layer, piece])

    def at_turns(turns):
        def beside(index):
            for turn, steps in turns.items():

                @pl.when(index == turn)
                def _():
                    for step in steps:
                        step()

        return beside

    def ticks(turns):
        return at_turns({turn: (functools.partial(tick, step),) for turn, step in turns.items()})

    kept = {
        "x": (n2.at[pl.ds(0, width), :], x_hbm),
        "h": (res, h_hbm),
        "n1": (n1.at[pl.ds(0, width), :], n1_hbm),
        "n2": (n2.at[pl.ds(0, width), :], n2_hbm),
        "qkv": (qkv, qkv_hbm),
        "ctx": (ctx, ctx_hbm),
        "lse": (lse, lse_hbm),
        "act": (act, act_hbm),
        "slope": (slope, slope_hbm),
    }
    names = tuple(kept)

    def save(name, layer):
        src, dst = kept[name]
        if name in ("x", "h"):
            dst = dst.at[layer]
        return pltpu.make_async_copy(src, dst, save_sem.at[names.index(name), layer])

    def load(name, layer=0):
        dst, src = kept[name]
        if name == "x":
            dst, src = act.at[pl.ds(0, width), :], src.at[layer]
        return pltpu.make_async_copy(src, dst, load_sem.at[names.index(name)])

    def load_h(layer, index):
        slot = lax.rem(index, 2)
        return pltpu.make_async_copy(
            h_hbm.at[layer, :, block_of(index)], h_in.at[slot], h_sem.at[slot]
        )

    my_quarter = pl.ds(s * quarter, quarter)
    my_rows = pl.ds(pl.multiple_of((1 - t) * half + s * quarter, quarter), quarter)

    def clip_across():
        there = pl.ds(pl.multiple_of(t * half + s * quarter, quarter), quarter)
        return remote(
            clips.at[1 - t, my_quarter, :],
            stage.at[there, :],
            in_sem.at[0],
            in_sem.at[1],
            place.across,
        )

    def clip_core():
        part = stage.at[my_rows, :]
        return remote(part, part, in_sem.at[2], in_sem.at[3], place.core)

    def cot_across():
        return remote(
            cot.at[1 - t, my_quarter, :],
            cot_other.at[my_quarter, :],
            cot_sem.at[0],
            cot_sem.at[1],
            place.across,
        )

    def cot_core():
        part = cot_other.at[my_quarter, :]
        return remote(part, part, cot_sem.at[2], cot_sem.at[3], place.core)

    def exchange(kind, index, slot):
        return remote(
            send.at[kind, index],
            recv.at[kind, index],
            e_send.at[slot, index],
            e_recv.at[slot, index],
            place.core,
        )

    def result_copies(ref, first):
        local = pltpu.make_async_copy(stage.at[mine, :], ref.at[0, t], out_sem.at[first])
        away = remote(
            stage.at[theirs, :],
            ref.at[0, t],
            out_sem.at[first + 1],
            out_sem.at[first + 2],
            place.across,
        )
        return local, away

    def grad_copies(index):
        place_in = lax.rem(index, blocks // 2)
        part = in_grad.at[0, t, pl.ds(pl.multiple_of(place_in * BLOCK, BLOCK), BLOCK), :]
        src = stage.at[block_of(index), :]
        local = pltpu.make_async_copy(src, part, grad_sem.at[0, place_in])
        away = remote(
            src, part, grad_sem.at[1, place_in], grad_sem.at[2, place_in], place.across
        )
        return local, away

    def emit(layer, ref, first):
        @pl.when(s == layer)
        def _():
            for copy in result_copies(ref, first):
                copy.start()

    for copy in own_loads:
        copy.wait()
    for step in range(3):
        z_start(step)
    n1[width:, :] = jnp.ones((ONES, frames), BF)
    n2[width:, :] = jnp.ones((ONES, frames), BF)
    own_clip = pltpu.make_async_copy(clips.at[t], stage.at[mine, :], in_sem.at[4])
    own_clip.start()
    clip_across().start()
    cot_across().start()
    own_out.wait()
    shard[:, OUT:UP] = flat[0:WIDE, :].T
    own_up.wait()
    for step in (3, 4):
        z_start(step)

    def take_clip(first):
        def body(index, carry):
            at = pl.ds(pl.multiple_of(first + index * BLOCK, BLOCK), BLOCK)
            tile = stage[at, :].T
            n2[0:width, at] = tile
            res[:, at] = tile.astype(F32)
            return carry

        lax.fori_loop(0, half // BLOCK, body, 0)

    own_clip.wait()
    take_clip(t * half)
    own_down.wait()
    for piece in range(4):
        span = slice((1 + piece) * WIDE, (2 + piece) * WIDE)
        shard[:, DOWN + piece * WIDE : DOWN + (piece + 1) * WIDE] = flat[span, :].T
    clip_across().wait()
    clip_core().start()
    step_z(0)
    z_start(5)
    step_z(1)
    z_start(6)
    clip_core().wait()
    take_clip((1 - t) * half)
    save("x", 0).start()
    step_plane(0)
    step_z(2)
    z_start(7)
    step_plane(1)
    cot_across().wait()
    cot_core().start()
    step_z(3)
    z_start(8)
    step_plane(2)
    step_z(4)
    z_start(9)
    step_z(5)
    z_start(10)

    def project(pair):
        for index in (2 * pair, 2 * pair + 1):
            cols = block_of(index)
            mean, scale = norm_stats(lambda span: res[span, cols], width)
            for span in chunks_of(width):
                hat = (res[span, cols] - mean) * scale
                n1[span, cols] = (hat * vecs[span, 0:1] + vecs[span, 2:3]).astype(BF)
        cols = pair_of(pair)
        for first, many, kind, bias in PARTS:
            value = mm(wt[first : first + many, :], n1[0:width, cols])
            for span in chunks_of(many):
                part = value[span, :]
                if kind != "k":
                    part = part + spread[bias + span.start : bias + span.stop, 6:7]
                if kind == "q":
                    part = part * 0.125
                qkv[first + span.start : first + span.stop, cols] = part.astype(BF)

    def send_pair(kind, pair, slot, value):
        for part in range(2):
            index = 2 * pair + part
            send[kind, index] = value[:, part * BLOCK : (part + 1) * BLOCK].astype(BF)
            exchange(kind, index, slot).start()

    def head_rows(head, first):
        return pl.ds(pl.multiple_of(first + head * HEAD, HEAD), HEAD)

    def attend(layer, turns, later_turns):
        def heads_of(first_head, base, stride, beside):
            def one_head(index_in, carry):
                head = first_head + index_in
                q_rows = head_rows(index_in, base)
                k_rows = head_rows(index_in, base + stride)
                v_rows = head_rows(index_in, base + 2 * stride)
                c_rows = head_rows(head, 0)
                keys = qkv[k_rows, :].T
                for index in range(blocks):
                    cols = slice(index * BLOCK, (index + 1) * BLOCK)
                    queries = qkv[q_rows, cols]
                    tiles = []
                    top = None
                    for tile in chunks_of(frames, BLOCK):
                        scores = mm(keys[tile, :], queries)
                        for span in chunks_of(BLOCK):
                            peak = stack_max(scores[span, :])
                            top = peak if top is None else jnp.maximum(top, peak)
                        tiles.append(scores)
                    top = jnp.max(top, 0, keepdims=True)
                    total = jnp.zeros((8, BLOCK), F32)
                    mixed = jnp.zeros((HEAD, BLOCK), F32)
                    for tile, scores in zip(chunks_of(frames, BLOCK), tiles):
                        soft = []
                        for span in chunks_of(BLOCK):
                            part = jnp.exp(scores[span, :] - top)
                            total = total + stack_sum(part)
                            soft.append(part.astype(BF))
                        mixed = mixed + mm(qkv[v_rows, tile], jnp.concatenate(soft, 0))
                    total = jnp.sum(total, 0, keepdims=True)
                    ctx[c_rows, cols] = (mixed / total).astype(BF)
                    lse[pl.ds(head, 1), cols] = top + jnp.log(total)
                beside(index_in)
                return carry

            return one_head

        lax.fori_loop(0, 4, heads_of(0, 0, 256, ticks(turns)), 0)
        lax.fori_loop(0, 2, heads_of(4, 768, 128, ticks(later_turns)), 0)

    def out_project(layer, turns):
        beside = ticks(turns)

        def body(index, carry):
            part = mm(whole(w, layer, OUT, 384), ctx[:, pair_of(index)])
            send_pair(0, index, 2 * layer, part)
            beside(index)
            return carry

        lax.fori_loop(0, blocks // 2, body, 0)

    def middle_norm(layer, turns):
        beside = ticks(turns)

        def body(index, carry):
            cols = block_of(index)
            exchange(0, index, 2 * layer).wait()
            for span in chunks_of(width):
                added = send[0, index, span, :].astype(F32) + recv[0, index, span, :].astype(F32)
                res[span, cols] = res[span, cols] + added + vecs[span, 3:4]
            mean, scale = norm_stats(lambda span: res[span, cols], width)
            for span in chunks_of(width):
                hat = (res[span, cols] - mean) * scale
                n2[span, cols] = (hat * vecs[span, 1:2] + vecs[span, 4:5]).astype(BF)
            beside(index)
            return carry

        lax.fori_loop(0, blocks, body, 0)

    def hidden_part(layer, part):
        flip_weights(w, wt, layer, UP + part * WIDE, WIDE, part * WIDE)
        units = slice(part * WIDE, (part + 1) * WIDE)
        lane = 7 if part < 2 else 8

        def body(index, carry):
            cols = pair_of(index)
            pre = mm(wt[units, :], n2[0:width, cols])
            for span in chunks_of(WIDE):
                first = part * WIDE + span.start
                bias = spread[768 + first : 768 + first + ROWS, lane : lane + 1]
                value, steep = gelu_parts(pre[span, :] + bias)
                act[first : first + ROWS, cols] = value.astype(BF)
                slope[first : first + ROWS, cols] = steep.astype(BF)
            return carry

        lax.fori_loop(0, blocks // 2, body, 0)

    def down_project(layer, turns):
        beside = ticks(turns)

        def body(index, carry):
            part = mm(whole(w, layer, DOWN, 1536), act[:, pair_of(index)])
            send_pair(1, index, 2 * layer + 1, part)
            beside(index)
            return carry

        lax.fori_loop(0, blocks // 2, body, 0)

    def layer_end(layer, index, span):
        added = send[1, index, span, :].astype(F32) + recv[1, index, span, :].astype(F32)
        return (res[span, block_of(index)] + added + vecs[span, 5:6]).astype(BF)

    def take_vectors(layer):
        vecs[...] = whole(w, layer, VEC, 128).astype(F32)
        spread_biases(vecs, spread, rows)

    def project_all(layer, turns):
        beside = ticks(turns)
        flip_weights(w, wt, layer, QKV, 1152)

        def body(index, carry):
            project(index)
            beside(index)
            return carry

        lax.fori_loop(0, blocks // 2, body, 0)
        if layer == 0:
            save("n1", 0).start()
            save("qkv", 0).start()

    complete(0, 1, 2)
    take_vectors(0)
    project_all(0, {0: 3, 1: 4})
    cot_core().wait()
    load_cot = pltpu.make_async_copy(cot_other, stage.at[theirs, :], cot_sem.at[4])
    load_cot.start()
    own_cot = pltpu.make_async_copy(cot.at[t], stage.at[mine, :], cot_sem.at[5])
    own_cot.start()
    attend(0, {0: 5, 2: 6}, {0: 7})
    save("ctx", 0).start()
    save("lse", 0).start()
    complete(3)
    out_project(0, {1: 8})
    load_cot.wait()
    own_cot.wait()

    sums[3] = jnp.zeros_like(sums[3])

    def take_cot(index, carry):
        low[:, block_of(index)] = stage[block_of(index), :].T
        for span in chunks_of(width):
            sums[3, span, :] += fold(low[span, block_of(index)].astype(F32))
        return carry

    lax.fori_loop(0, blocks, take_cot, 0)
    save("x", 0).wait()
    middle_norm(0, {1: 9})
    save("h", 0).start()
    save("n2", 0).start()
    for part in range(4):
        complete(4 + part)
        hidden_part(0, part)
        tick(10 + part)
    save("act", 0).start()
    save("slope", 0).start()
    complete(8, 9, 10, 11)
    down_project(0, {1: 14})
    for name in ("n1", "qkv", "h", "n2"):
        save(name, 0).wait()

    def finish_body(index, carry):
        exchange(1, index, 1).wait()
        cols = block_of(index)
        for span in chunks_of(width):
            rows_out = layer_end(0, index, span)
            n2[span, cols] = rows_out
            res[span, cols] = rows_out.astype(F32)

        @pl.when(s == 0)
        def _():
            stage[cols, :] = n2[0:width, cols].T

        return carry

    lax.fori_loop(0, blocks, finish_body, 0)
    emit(0, out, 0)
    save("x", 1).start()
    complete(12, 13, 14)
    take_vectors(1)
    project_all(1, {0: 15, 1: 16})
    save("ctx", 0).wait()
    save("lse", 0).wait()
    attend(1, {0: 17, 2: 18}, {0: 19})
    complete(15)
    out_project(1, {1: 20})
    save("x", 1).wait()
    middle_norm(1, {1: 21})
    save("h", 1).start()
    save("act", 0).wait()
    save("slope", 0).wait()
    for part in range(4):
        complete(16 + part)
        hidden_part(1, part)
        if part < 2:
            tick(22 + part)
    for part in range(4):
        complete(20 + part)
        flip_weights(w, wt, 1, DOWN + part * WIDE, WIDE, part * WIDE)
    down_project(1, {})

    def gya_copy(layer, piece):
        cols = piece_cols(piece)
        return remote(
            w.at[layer, :, 1 - y, low_rows, cols],
            land_a.at[:, low_rows, cols],
            gya_send.at[layer, piece],
            gya_recv.at[layer, piece],
            place.beside,
        )

    def gxb_copy(layer, piece):
        cols = piece_cols(piece)
        return remote(
            w.at[layer, :, 1 - y, high_rows, cols],
            land_b.at[:, :, cols],
            gxb_send.at[layer, piece],
            gxb_recv.at[layer, piece],
            place.across,
        )

    def gx_copy(layer, piece):
        cols = piece_cols(piece)
        return remote(
            w.at[layer, :, y, :, cols],
            land_a.at[:, :, cols],
            gx_send.at[layer, piece],
            gx_recv.at[layer, piece],
            place.across,
        )

    def gy_copy(layer, piece):
        cols = piece_cols(piece)
        return remote(
            w.at[layer, :, 1 - y, :, cols],
            land_y.at[:, :, cols],
            gy_send.at[layer, piece],
            gy_recv.at[layer, piece],
            place.beside,
        )

    def landed_part(piece):
        if piece == VECTORS:
            return landed_vec
        ref, first = (
            (landed_qkv, 0)
            if piece < 3
            else (landed_out, 3)
            if piece < 4
            else (landed_up, 4)
            if piece < 8
            else (landed_down, 8)
        )
        return ref.at[:, :, pl.ds((piece - first) * WIDE, WIDE)]

    def gz_copies(layer, piece):
        cols = piece_cols(piece)
        target = landed_part(piece)
        copies = []
        for step in range(LINES):
            line = place.line(step)
            copies.append(
                remote(
                    w.at[layer, line, y, :, cols],
                    target.at[e],
                    gz_send.at[layer, piece, step],
                    gz_recv.at[piece, e],
                    (layer, place.row_of(line, y), t),
                )
            )
        local = pltpu.make_async_copy(
            w.at[layer, e, y, :, cols], target.at[e], gz_recv.at[piece, e]
        )
        return copies, local

    def add_rows(layer, piece, which, span, lands):
        cols = piece_cols(piece)
        first, count = span
        for line in range(LINES):
            total = w[layer, line, which, pl.ds(first, count), cols].astype(F32)
            for land, offset in lands:
                total = total + land[line, pl.ds(offset, count), cols].astype(F32)
            w[layer, line, which, pl.ds(first, count), cols] = total.astype(BF)

    def signal(sem, layer, piece, device):
        if layer == 1:
            pl.semaphore_signal(sem.at[piece], inc=1, device_id=device, device_id_type=MESH)

    def credit(sem, layer, piece):
        if layer == 0:
            pl.semaphore_wait(sem.at[piece], 1)

    def step_a(layer, piece):
        @pl.when(secondary)
        def _():
            credit(ya_free, layer, piece)
            gya_copy(layer, piece).start()
            credit(xb_free, layer, piece)
            gxb_copy(layer, piece).start()

    def step_b(layer, piece):
        cols = piece_cols(piece)

        @pl.when(secondary)
        def _():
            await_bytes(land_a.at[:, low_rows, cols], gya_recv.at[layer, piece])
            add_rows(layer, piece, y, (0, SPLIT), [(land_a, 0)])
            signal(ya_free, layer, piece, place.beside)
            credit(x_free, layer, piece)
            gx_copy(layer, piece).start()

        @pl.when(primary)
        def _():
            await_bytes(land_b.at[:, :, cols], gxb_recv.at[layer, piece])
            add_rows(layer, piece, 1 - y, (SPLIT, rows - SPLIT), [(land_b, 0)])
            signal(xb_free, layer, piece, place.across)
            credit(y_free, layer, piece)
            gy_copy(layer, piece).start()

    def step_c(layer, piece):
        cols = piece_cols(piece)

        @pl.when(primary)
        def _():
            await_bytes(land_a.at[:, :, cols], gx_recv.at[layer, piece])
            await_bytes(land_y.at[:, :, cols], gy_recv.at[layer, piece])
            add_rows(layer, piece, y, (0, rows), [(land_a, 0), (land_y, 0)])
            signal(x_free, layer, piece, place.across)
            signal(y_free, layer, piece, place.beside)
            copies, local = gz_copies(layer, piece)

            @pl.when(s == layer)
            def _():
                local.start()

            @pl.when(s != layer)
            def _():
                copies[0].start()

            for copy in copies[1:]:
                copy.start()

    def store_grads(layer, start, count, value):
        w[layer, :, :, :, pl.ds(start, count)] = value.astype(BF).reshape(
            w.shape[1], w.shape[2], rows, count
        )

    def mlp_back(layer, beside):
        def body(index, carry):
            cols = pair_of(index)
            for part in range(4):
                units = slice(part * WIDE, (part + 1) * WIDE)
                grad = mm(wt[units, :], low[:, cols])
                for span in chunks_of(WIDE):
                    rows_in = slice(units.start + span.start, units.start + span.stop)
                    steep = slope[rows_in, cols].astype(F32)
                    slope[rows_in, cols] = (grad[span, :] * steep).astype(BF)
            term = mm(whole(w, layer, UP, 1536), slope[:, cols])
            send_pair(0, index, 4 + 2 * layer, term)
            beside(index)
            return carry

        lax.fori_loop(0, blocks // 2, body, 0)

    def outer(layer, start, left, right, first, many, before, beside):
        def body(index, carry):
            before(index)
            base = index * PAIR
            span = pl.ds(pl.multiple_of(first + base, 128), PAIR)
            value = mmt(left[...], right[span, :])
            store_grads(layer, pl.multiple_of(start + base, 128), PAIR, value[0:width, :])
            if left.shape[0] > width:
                to = pl.ds(pl.multiple_of(768 + base, BLOCK), PAIR)
                spread[to, 0:8] = value[width : width + 8, :].T
            beside(index)
            return carry

        lax.fori_loop(0, many // PAIR, body, 0)

    def turned(turn):
        return lax.rem(turn + (1 - t) * (blocks // 2), blocks)

    def norm_back(layer, kind, gain_lane, source, put, finish, beside):
        sums[0:3] = jnp.zeros((3, width, 128), F32)

        def body(turn, carry):
            index = turned(turn)
            cols = block_of(index)
            read = source(index)
            mean, scale = norm_stats(read, width)
            exchange(kind, index, 4 + 2 * layer + kind).wait()
            first = jnp.zeros((8, BLOCK), F32)
            second = jnp.zeros((8, BLOCK), F32)

            def terms(span):
                hat = (read(span) - mean) * scale
                grad = send[kind, index, span, :].astype(F32)
                grad = grad + recv[kind, index, span, :].astype(F32)
                return hat, grad, grad * vecs[span, gain_lane : gain_lane + 1]

            for span in chunks_of(width):
                hat, grad, scaled = terms(span)
                sums[0, span, :] += fold(grad * hat)
                sums[1, span, :] += fold(grad)
                first = first + stack_sum(scaled)
                second = second + stack_sum(scaled * hat)
            level = mean_of(first, width)
            slant = mean_of(second, width)
            for span in chunks_of(width):
                hat, _, scaled = terms(span)
                put(span, cols, res[span, cols] + scale * (scaled - level - hat * slant))
            finish(index)
            beside(turn)
            return carry

        lax.fori_loop(0, blocks, body, 0)

    def row_sums(value):
        return jnp.sum(value, 1, keepdims=True)

    def attend_back(first_head, many, base, stride, beside):
        def one_head(index_in, carry):
            head = first_head + index_in
            q_rows = head_rows(index_in, base)
            k_rows = head_rows(index_in, base + stride)
            v_rows = head_rows(index_in, base + 2 * stride)
            c_rows = head_rows(head, 0)
            keys = qkv[k_rows, :].T
            values = qkv[v_rows, :].T
            flat_queries = qkv[q_rows, :].T
            flat_grads = dctx[c_rows, :].T
            level = lse[pl.ds(head, 1), :]
            inner = jnp.sum(
                dctx[c_rows, :].astype(F32) * ctx[c_rows, :].astype(F32), 0, keepdims=True
            )
            step = jnp.zeros((HEAD, frames), F32)
            for tile in chunks_of(frames, BLOCK):
                soft = []
                score_grad = []
                for cols in chunks_of(frames, BLOCK):
                    scores = mm(keys[tile, :], qkv[q_rows, cols])
                    soft_grad = mm(values[tile, :], dctx[c_rows, cols])
                    soft_parts = []
                    grad_parts = []
                    for part in chunks_of(BLOCK):
                        strength = jnp.exp(scores[part, :] - level[:, cols])
                        soft_parts.append(strength.astype(BF))
                        strength = strength * (soft_grad[part, :] - inner[:, cols])
                        grad_parts.append(strength.astype(BF))
                    soft.append(jnp.concatenate(soft_parts, 0))
                    score_grad.append(jnp.concatenate(grad_parts, 0))
                soft = jnp.concatenate(soft, 1)
                score_grad = jnp.concatenate(score_grad, 1)
                step = step + mm(qkv[k_rows, tile], score_grad)
                slope[k_rows, tile] = mm(score_grad, flat_queries).astype(BF).T
                slope[v_rows, tile] = mm(soft, flat_grads).astype(BF).T
            slope[q_rows, :] = (step * 0.125).astype(BF)
            beside(index_in)
            return carry

        lax.fori_loop(0, many, one_head, 0)

    def keep_sums(first, value):
        for start, many, kind, bias in PARTS:
            offset = start - first
            if kind != "k" and 0 <= offset < value.shape[1]:
                spread[bias : bias + many, 0:8] = value[
                    width : width + 8, offset : offset + many
                ].T

    def collect_biases():
        def body(group, carry):
            source = group * rows
            for kind in range(2):
                for head in range(6):
                    at = pl.ds(pl.multiple_of(kind * 384 + head * HEAD + group * 8, 8), 8)
                    to = pl.ds(pl.multiple_of(source + kind * 48 + head * 8, 8), 8)
                    vec_grads[to, 6:7] = spread[at, 6:7]
            for unit in range(24):
                at = pl.ds(pl.multiple_of(768 + unit * HEAD + group * 8, 8), 8)
                to = pl.ds(pl.multiple_of(source + (unit % 12) * 8, 8), 8)
                lane = 7 if unit < 12 else 8
                vec_grads[to, lane : lane + 1] = spread[at, 6:7]
            return carry

        lax.fori_loop(0, GROUPS, body, 0)

    def nothing(index):
        del index

    def finish_gather(layer, piece):
        @pl.when(primary)
        def _():
            x_copy(layer, piece).wait_send()
            y_copy(layer, piece).wait_send()
            xb_copy(layer, piece).wait_send()

        @pl.when(secondary)
        def _():
            ya_copy(layer, piece).wait_send()

    def last_body(index, carry):
        exchange(1, index, 3).wait()

        @pl.when(s == 1)
        def _():
            for span in chunks_of(width, 128):
                stage[block_of(index), span] = layer_end(1, index, span).T

        return carry

    for layer in (1, 0):
        later = layer == 0
        if later:
            load_h(layer, turned(0)).start()
            load("act").wait()
            vecs[...] = whole(w, layer, VEC, 128).astype(F32)
            flip_weights(w, wt, layer, DOWN, 1536)
        vec_grads[...] = jnp.zeros_like(vec_grads)

        def a(piece, layer=layer):
            return lambda: step_a(layer, piece)

        def b(piece, layer=layer):
            return lambda: step_b(layer, piece)

        def c(piece, layer=layer):
            return lambda: step_c(layer, piece)

        if later:
            before = nothing
            early = at_turns(
                {
                    0: (a(8), lambda: step_b(1, VECTORS)),
                    1: (a(9), lambda: step_c(1, VECTORS)),
                    2: (a(10), a(11)),
                }
            )
        else:
            waits = [functools.partial(finish_gather, 1, piece) for piece in (8, 9, 10, 11)]
            before = at_turns({0: waits[:2], 1: waits[2:3], 2: waits[3:]})
            early = at_turns({0: (a(8),), 1: (a(9),), 2: (a(10), a(11))})
        outer(layer, DOWN, low, act, 0, 1536, before, early)
        load("x", layer).start()
        vec_grads[:, 5:6] = row_sums(sums[3])
        if not later:
            lax.fori_loop(0, blocks, last_body, 0)
            emit(1, out, 0)
            save("h", 1).wait()
            load_h(layer, turned(0)).start()
            res[...] = low[...].astype(F32)
            for piece in range(CHUNKS + 1):
                z_finish(piece)
                finish_gather(0, piece)
                if piece < 8 or piece == VECTORS:
                    finish_gather(1, piece)
        else:
            load("slope").wait()

        mlp_back(layer, at_turns({0: (b(8),), 1: (b(9), b(10), b(11))}))
        if later:
            load("n2").wait()
        drain = at_turns({0: (a(4),), 1: (a(5),), 2: (a(6), a(7), c(8))})
        outer(layer, UP, n2, slope, 0, 1536, nothing, drain)
        flip_weights(w, wt, layer, OUT, 384)

        def hidden_in(index, layer=layer):
            turn = lax.rem(index + (1 - t) * (blocks // 2), blocks)

            @pl.when(turn + 1 < blocks)
            def _():
                load_h(layer, turned(turn + 1)).start()

            load_h(layer, index).wait()
            slot = lax.rem(index, 2)
            return lambda span: h_in[slot, span, :]

        def hidden_put(span, cols, total):
            res[span, cols] = total
            rounded = total.astype(BF)
            low[span, cols] = rounded
            sums[2, span, :] += fold(rounded.astype(F32))

        drain = at_turns({0: (b(4), c(9)), 1: (b(5), c(10)), 2: (b(6), c(11)), 3: (b(7),)})
        norm_back(layer, 0, 1, hidden_in, hidden_put, nothing, drain)

        def context_back(index, carry):
            cols = pair_of(index)
            dctx[:, cols] = mm(wt[0:384, :], low[:, cols]).astype(BF)
            return carry

        lax.fori_loop(0, blocks // 2, context_back, 0)
        vec_grads[:, 1:2] = row_sums(sums[0])
        vec_grads[:, 4:5] = row_sums(sums[1])
        vec_grads[:, 3:4] = row_sums(sums[2])
        if later:
            for name in ("ctx", "qkv", "lse"):
                load(name).wait()
        store_grads(layer, OUT, 384, mmt(low[...], ctx[...]))
        step_a(layer, 3)
        drain = at_turns({0: (c(4),), 1: (c(5),), 2: (b(3), c(6)), 3: (c(7),)})
        attend_back(0, 4, 0, 256, drain)
        if later:
            load("n1").wait()
        wt[0:768, :] = whole(w, layer, QKV, 768)

        for first, many in ((0, 512), (512, 256)):
            value = mmt(n1[...], slope[first : first + many, :])
            store_grads(layer, QKV + first, many, value[0:width, :])
            keep_sums(first, value)
        step_a(layer, 0)
        step_a(layer, 1)
        attend_back(4, 2, 768, 128, at_turns({0: (b(0), c(3)), 1: (b(1),)}))

        def first_body(index, carry, layer=layer):
            cols = pair_of(index)
            term = mm(wt[0:768, :], slope[0:768, cols])
            term = term + mm(whole(w, layer, QKV + 768, WIDE), slope[768:1152, cols])
            send_pair(1, index, 5 + 2 * layer, term)
            return carry

        lax.fori_loop(0, blocks // 2, first_body, 0)
        value = mmt(n1[...], slope[768:1152, :])
        store_grads(layer, QKV + 768, WIDE, value[0:width, :])
        keep_sums(768, value)
        step_a(layer, 2)
        step_c(layer, 0)
        collect_biases()
        if layer == 1:
            for name in ("slope", "n1", "n2", "ctx", "qkv", "lse"):
                load(name).start()
        load("x", layer).wait()

        @pl.when(s == layer)
        def _():
            local, away = result_copies(out, 0)
            local.wait()
            away.wait_send()

        def rows_x(index):
            return lambda span: act[span, block_of(index)].astype(F32)

        def rows_put(span, cols, total, layer=layer):
            rounded = total.astype(BF)
            low[span, cols] = rounded
            if layer == 1:
                res[span, cols] = rounded.astype(F32)
                sums[2, span, :] += fold(rounded.astype(F32))

        def rows_out(index, layer=layer):
            @pl.when(s == layer)
            def _():
                stage[block_of(index), :] = low[:, block_of(index)].T
                local, away = grad_copies(index)

                @pl.when(index // (blocks // 2) == t)
                def _():
                    local.start()

                @pl.when(index // (blocks // 2) != t)
                def _():
                    away.start()

        drain = at_turns({0: (c(1),), 1: (b(2),), 3: (c(2),)})
        norm_back(layer, 1, 0, rows_x, rows_put, rows_out, drain)
        if layer == 1:
            load("act").start()
        vec_grads[:, 0:1] = row_sums(sums[0])
        vec_grads[:, 2:3] = row_sums(sums[1])
        sums[3] = sums[2]
        store_grads(layer, VEC, 128, vec_grads[...])
        step_a(layer, VECTORS)

    step_b(0, VECTORS)
    step_c(0, VECTORS)

    def finish_scatter(piece):
        for layer in range(2):

            @pl.when(secondary)
            def _():
                gya_copy(layer, piece).wait_send()
                gxb_copy(layer, piece).wait_send()
                gx_copy(layer, piece).wait_send()

            @pl.when(primary)
            def _():
                gy_copy(layer, piece).wait_send()
                copies, _ = gz_copies(layer, piece)

                @pl.when(s != layer)
                def _():
                    copies[0].wait_send()

                for copy in copies[1:]:
                    copy.wait_send()

    for piece in range(CHUNKS + 1):
        finish_scatter(piece)
        for line in range(LINES):
            await_bytes(landed_part(piece).at[line], gz_recv.at[piece, line])

    _, away = result_copies(out, 0)
    away.wait_recv()
    for index in range(blocks // 2):
        local, away = grad_copies(index)
        local.wait()
        away.wait()


def layers_call(share, clips, cotangent, shards, dims):
    width, frames, hidden_units, heads_width = dims
    rows = width // GROUPS
    sem = pltpu.SemaphoreType.DMA
    free = pltpu.SemaphoreType.REGULAR
    packed = (2, LINES, 2, rows, END)
    blocks = frames // BLOCK
    shape = jax.ShapeDtypeStruct
    outs = [
        shape((1,) + clips.shape, BF),
        shape((1,) + clips.shape, BF),
        shape((LINES, rows, QKV - VEC), BF),
        shape((LINES, rows, OUT - QKV), BF),
        shape((LINES, rows, UP - OUT), BF),
        shape((LINES, rows, DOWN - UP), BF),
        shape((LINES, rows, END - DOWN), BF),
        shape(clips.shape[1:], BF),
        shape((2, width, frames), BF),
        shape((2, width, frames), F32),
        shape((width, frames), BF),
        shape((width, frames), BF),
        shape((3 * heads_width, frames), BF),
        shape((heads_width, frames), BF),
        shape((8, frames), F32),
        shape((hidden_units, frames), BF),
        shape((hidden_units, frames), BF),
    ]
    scratch = [
        pltpu.VMEM(packed, BF),
        pltpu.VMEM((width, frames), F32),
        pltpu.VMEM((hidden_units, frames), BF),
        pltpu.VMEM((hidden_units, frames), BF),
        pltpu.VMEM((width + ONES, frames), BF),
        pltpu.VMEM((width + ONES, frames), BF),
        pltpu.VMEM((width, frames), BF),
        pltpu.VMEM((3 * heads_width, frames), BF),
        pltpu.VMEM((heads_width, frames), BF),
        pltpu.VMEM((heads_width, frames), BF),
        pltpu.VMEM((8, frames), F32),
        pltpu.VMEM((2, width, BLOCK), F32),
        pltpu.VMEM((hidden_units, width), BF),
        pltpu.VMEM((2, blocks, width, BLOCK), BF),
        pltpu.VMEM((2, blocks, width, BLOCK), BF),
        pltpu.VMEM((width, 128), F32),
        pltpu.VMEM((width, 128), F32),
        pltpu.VMEM((4, width, 128), F32),
        pltpu.VMEM((2 * heads_width + hidden_units, 128), F32),
        pltpu.VMEM((frames, width), BF),
        pltpu.VMEM((rows, END), BF),
        pltpu.VMEM((WIDE + END - DOWN, rows), BF),
        pltpu.VMEM((LINES, rows, END), BF),
        pltpu.VMEM((LINES, rows - SPLIT, END), BF),
        pltpu.VMEM((LINES, rows, END), BF),
    ]
    scratch += [sem((CHUNKS + 1, LINES)), sem((2, CHUNKS + 1, LINES))]
    scratch += [sem((2, CHUNKS + 1))] * 8
    scratch += [sem((2, CHUNKS + 1, LINES)), sem((CHUNKS + 1, LINES))]
    scratch += [sem((2, CHUNKS + 1))] * 8
    scratch += [
        sem((8, blocks)),
        sem((8, blocks)),
        sem((10,)),
        sem((5,)),
        sem((6,)),
        sem((3,)),
        sem((3, blocks // 2)),
        sem((9, 2)),
        sem((9,)),
        sem((2,)),
    ]
    scratch += [free((CHUNKS + 1,))] * 4
    anywhere = pl.BlockSpec(memory_space=pl.ANY)
    return pl.pallas_call(
        functools.partial(layers_kernel, share),
        out_shape=outs,
        in_specs=[anywhere] * (2 + len(shards)),
        out_specs=[anywhere] * len(outs),
        scratch_shapes=scratch,
        compiler_params=pltpu.CompilerParams(
            collective_id=0, has_side_effects=True, vmem_limit_bytes=VMEM_LIMIT
        ),
        cost_estimate=pl.CostEstimate(
            flops=60_000_000_000, bytes_accessed=60_000_000, transcendentals=0
        ),
    )(clips, cotangent, *shards)


def group_piece(value, axis, share):
    if share == 1:
        return value
    size = value.shape[axis] * share
    group = lax.axis_index("dp") // share
    full = lax.all_gather(value, "dp", axis=axis, tiled=True)
    return lax.dynamic_slice_in_dim(full, group * size, size, axis)


def own_part(value, axis, share, parts, index):
    size = value.shape[axis] // parts
    if parts == 1:
        return value
    return lax.dynamic_slice_in_dim(value, index * size, size, axis)


def on_device(share, clips, cotangent, ln_gains, row_biases, w_qkv, b_qv, w_o, w_up, b_ff, w_down):
    width = clips.shape[2]
    rows = width // GROUPS
    dims = (width, 2 * clips.shape[1], w_up.shape[2], w_o.shape[1])
    ln_gains = group_piece(ln_gains, 2, share)
    row_biases = group_piece(row_biases, 2, share)
    w_qkv = group_piece(w_qkv, 2, share)
    b_qv = group_piece(b_qv, 3, share)
    w_o = group_piece(w_o, 2, share)
    w_up = group_piece(w_up, 1, share)
    b_ff = group_piece(b_ff, 2, share)
    w_down = group_piece(w_down, 2, share)
    vectors = jnp.concatenate([ln_gains[0], row_biases[0]], 0).T
    heads = jnp.concatenate([b_qv[0, 0].reshape(-1), b_qv[0, 1].reshape(-1)])[:, None]
    units = b_ff[0].reshape(2, rows).T
    packed = jnp.concatenate([vectors, heads, units], 1)
    packed = jnp.pad(packed, ((0, 0), (0, 128 - packed.shape[1])))
    section_out, section_in_grad, *landed = layers_call(
        share, clips, cotangent, (packed, w_qkv, w_o, w_up, w_down), dims
    )
    rest = lax.axis_index("dp") % share
    side = lax.axis_index("tensor")

    def joined(value):
        total = jnp.sum(value.astype(F32), 0)
        if share == 1:
            return total
        group = lax.axis_index("dp") // share
        padded = jnp.zeros((width, total.shape[1]), F32)
        padded = lax.dynamic_update_slice_in_dim(padded, total, group * rows, 0)
        return lax.dynamic_slice_in_dim(lax.psum(padded, "dp"), group * rows, rows, 0)

    def mine(value):
        return own_part(joined(value), 0, share, share, rest)

    vectors = joined(landed[0])
    vec = own_part(own_part(vectors, 0, share, share, rest), 0, share, 2, side)
    heads_grad = vectors[:, 6].reshape(2, -1, HEAD // GROUPS)
    units_grad = vectors[:, 7:9].T.reshape(-1, HEAD // GROUPS)
    qkv_grad = {"q": [], "k": [], "v": []}
    for first, many, kind, _ in PARTS:
        qkv_grad[kind].append(mine(landed[1][:, :, first : first + many]))
    return (
        section_out,
        section_in_grad,
        vec[:, 0:2].T[None],
        vec[:, 2:6].T[None],
        jnp.stack([jnp.concatenate(qkv_grad[kind], 1) for kind in "qkv"])[None],
        own_part(heads_grad, 2, share, share, rest)[None],
        mine(landed[2]).T[None],
        mine(landed[3])[None],
        own_part(units_grad, 1, share, share, rest)[None],
        mine(landed[4]).T[None],
    )


def solution(mesh):
    placed = (
        P("dp", "tensor", None),
        P("dp", "tensor", None),
        P("section", None, "dp"),
        P("section", None, "dp"),
        P("section", None, "dp", "tensor"),
        P("section", None, "tensor", "dp"),
        P("section", "tensor", "dp"),
        P("section", "dp", "tensor"),
        P("section", "tensor", "dp"),
        P("section", "tensor", "dp"),
    )
    share = mesh.shape["dp"] // GROUPS
    return jax.shard_map(
        functools.partial(on_device, share),
        mesh=mesh,
        in_specs=placed,
        out_specs=(
            P("section", "dp", "tensor", None),
            P("section", "dp", "tensor", None),
            P("section", None, ("dp", "tensor")),
            P("section", None, ("dp", "tensor")),
            P("section", None, "dp", "tensor"),
            P("section", None, "tensor", "dp"),
            P("section", "tensor", "dp"),
            P("section", "dp", "tensor"),
            P("section", "tensor", "dp"),
            P("section", "tensor", "dp"),
        ),
        check_vma=False,
    )
```

```python
import functools

import jax
import jax.numpy as jnp
from jax import lax
from jax.experimental import pallas as pl
from jax.experimental.pallas import tpu as pltpu
from jax.sharding import PartitionSpec as P

BF = jnp.bfloat16
F32 = jnp.float32
MESH = pl.DeviceIdType.MESH
EPSILON = 1e-05
HEAD = 64
GROUPS = 8
LINES = 4
BLOCK = 256
PAIR = 2 * BLOCK
ROWS = 64
ONES = 16
VMEM_LIMIT = 62 * 1024 * 1024

VEC = 0
QKV = 128
OUT = 1280
UP = 1664
DOWN = 3200
END = 4736
SPLIT = 64
WIDE = 384
CHUNKS = 12


PARTS = (
    (0, 256, "q", 0),
    (256, 256, "k", 0),
    (512, 256, "v", 384),
    (768, 128, "q", 256),
    (896, 128, "k", 256),
    (1024, 128, "v", 640),
)


def mm(left, right):
    return jnp.dot(left, right, preferred_element_type=F32)


def mmt(left, right):
    return lax.dot_general(left, right, (((1,), (1,)), ((), ())), preferred_element_type=F32)


class Place:
    def __init__(self, share):
        self.s = lax.axis_index("section")
        self.d = lax.axis_index("dp")
        self.t = lax.axis_index("tensor")
        group = self.d // share
        self.rest = self.d - group * share
        self.share = share
        self.e = group // 2
        self.y = group - self.e * 2
        self.primary = self.s == self.t
        self.core = (1 - self.s, self.d, self.t)
        self.across = (self.s, self.d, 1 - self.t)
        self.beside = (self.s, self.row_of(self.e, 1 - self.y), self.t)

    def row_of(self, line, y):
        return (line * 2 + y) * self.share + self.rest

    def line(self, step):
        return lax.rem(self.e + step, LINES)

    def greet(self):
        barrier = pltpu.get_barrier_semaphore()
        peers = [self.core, self.across, self.beside]
        for step in range(1, LINES):
            for section in range(2):
                peers.append((section, self.row_of(self.line(step), self.y), self.t))
        for peer in peers:
            pl.semaphore_signal(barrier, inc=1, device_id=peer, device_id_type=MESH)
        pl.semaphore_wait(barrier, len(peers))


def remote(src, dst, send_sem, recv_sem, device):
    return pltpu.make_async_remote_copy(
        src_ref=src,
        dst_ref=dst,
        send_sem=send_sem,
        recv_sem=recv_sem,
        device_id=device,
        device_id_type=MESH,
    )


def await_bytes(ref, sem):
    pltpu.make_async_copy(ref, ref, sem).wait()


def chunks_of(count, size=ROWS):
    return [slice(first, first + size) for first in range(0, count, size)]


def by_eights(value):
    return value.reshape(value.shape[0] // 8, 8, value.shape[1])


def stack_sum(value):
    return jnp.sum(by_eights(value), 0)


def stack_max(value):
    return jnp.max(by_eights(value), 0)


def mean_of(parts, count):
    return jnp.sum(parts, 0, keepdims=True) / count


def norm_stats(read, count):
    total = jnp.zeros((8, BLOCK), F32)
    for span in chunks_of(count):
        total = total + stack_sum(read(span))
    mean = mean_of(total, count)
    square = jnp.zeros((8, BLOCK), F32)
    for span in chunks_of(count):
        centred = read(span) - mean
        square = square + stack_sum(centred * centred)
    return mean, lax.rsqrt(mean_of(square, count) + EPSILON)


def gelu_parts(values):
    bell = jnp.exp(-0.5 * values * values)
    reach = jnp.abs(values) * 0.7071067811865476
    inv = 1.0 / (1.0 + 0.3275911 * reach)
    poly = inv * (
        0.254829592
        + inv * (-0.284496736 + inv * (1.421413741 + inv * (-1.453152027 + inv * 1.061405429)))
    )
    tail = 0.5 * poly * bell
    cdf = jnp.where(values >= 0.0, 1.0 - tail, tail)
    return values * cdf, cdf + values * bell * 0.3989422804014327


def fold(value):
    return value[:, 0:128] + value[:, 128:256]


def block_of(index):
    return pl.ds(pl.multiple_of(index * BLOCK, BLOCK), BLOCK)


def pair_of(index):
    return pl.ds(pl.multiple_of(index * PAIR, PAIR), PAIR)


def flip_weights(w, wt, layer, start, width, target=0):
    def body(index, carry):
        cols = pl.ds(pl.multiple_of(start + index * 128, 128), 128)
        rows = pl.ds(pl.multiple_of(target + index * 128, 128), 128)
        tile = w[layer, :, :, :, cols]
        wt[rows, :] = tile.reshape(tile.shape[0] * tile.shape[1] * tile.shape[2], 128).T
        return carry

    lax.fori_loop(0, width // 128, body, 0)


def whole(w, layer, start, width):
    tile = w[layer, :, :, :, start : start + width]
    return tile.reshape(tile.shape[0] * tile.shape[1] * tile.shape[2], width)


def spread_biases(vecs, spread, rows):
    def body(group, carry):
        source = group * rows
        for kind in range(2):
            for head in range(6):
                to = pl.ds(pl.multiple_of(kind * 384 + head * HEAD + group * 8, 8), 8)
                at = pl.ds(pl.multiple_of(source + kind * 48 + head * 8, 8), 8)
                spread[to, :] = vecs[at, :]
        for unit in range(24):
            to = pl.ds(pl.multiple_of(768 + unit * HEAD + group * 8, 8), 8)
            at = pl.ds(pl.multiple_of(source + (unit % 12) * 8, 8), 8)
            spread[to, :] = vecs[at, :]
        return carry

    lax.fori_loop(0, GROUPS, body, 0)


def layers_kernel(
    share,
    clips,
    cot,
    vec_in,
    qkv_in,
    out_in,
    up_in,
    down_in,
    out,
    in_grad,
    landed_vec,
    landed_qkv,
    landed_out,
    landed_up,
    landed_down,
    cot_other,
    x_hbm,
    h_hbm,
    n1_hbm,
    n2_hbm,
    qkv_hbm,
    ctx_hbm,
    lse_hbm,
    act_hbm,
    slope_hbm,
    w,
    res,
    act,
    slope,
    n1,
    n2,
    low,
    qkv,
    ctx,
    dctx,
    lse,
    h_in,
    wt,
    send,
    recv,
    vecs,
    vec_grads,
    sums,
    spread,
    stage,
    shard,
    flat,
    land_a,
    land_b,
    land_y,
    z_send,
    z_recv,
    x_send,
    x_recv,
    xb_send,
    xb_recv,
    y_send,
    y_recv,
    ya_send,
    ya_recv,
    gz_send,
    gz_recv,
    gx_send,
    gx_recv,
    gxb_send,
    gxb_recv,
    gy_send,
    gy_recv,
    gya_send,
    gya_recv,
    e_send,
    e_recv,
    own_sem,
    in_sem,
    cot_sem,
    out_sem,
    grad_sem,
    save_sem,
    load_sem,
    h_sem,
    ya_free,
    xb_free,
    x_free,
    y_free,
):
    place = Place(share)
    s, t, e, y = place.s, place.t, place.e, place.y
    primary, secondary = place.primary, jnp.logical_not(place.primary)
    width, frames = res.shape
    blocks = frames // BLOCK
    half = frames // 2
    quarter = half // 2
    rows = w.shape[3]
    low_rows = pl.ds(0, SPLIT)
    high_rows = pl.ds(SPLIT, rows - SPLIT)
    mine = pl.ds(pl.multiple_of(t * half, half), half)
    theirs = pl.ds(pl.multiple_of((1 - t) * half, half), half)

    own_loads = [pltpu.make_async_copy(vec_in, shard.at[:, pl.ds(VEC, QKV)], own_sem.at[0])]
    for number, (first, many, kind, bias) in enumerate(PARTS):
        own_loads.append(
            pltpu.make_async_copy(
                qkv_in.at[0, "qkv".index(kind), :, pl.ds(bias % WIDE, many)],
                shard.at[:, pl.ds(QKV + first, many)],
                own_sem.at[1 + number],
            )
        )
    own_up = pltpu.make_async_copy(up_in.at[0], shard.at[:, pl.ds(UP, DOWN - UP)], own_sem.at[7])
    own_out = pltpu.make_async_copy(out_in.at[0], flat.at[pl.ds(0, WIDE), :], own_sem.at[8])
    own_down = pltpu.make_async_copy(
        down_in.at[0], flat.at[pl.ds(WIDE, END - DOWN), :], own_sem.at[9]
    )
    for copy in own_loads + [own_out, own_up, own_down]:
        copy.start()

    place.greet()

    VECTORS = CHUNKS

    def piece_cols(piece):
        if isinstance(piece, int) and piece == VECTORS:
            return pl.ds(VEC, QKV)
        return pl.ds(pl.multiple_of(QKV + piece * WIDE, 128), WIDE)

    def pieces_of(step):
        layer, piece = step // CHUNKS, step % CHUNKS
        return layer, (VECTORS, piece) if piece == 0 else (piece,)

    def z_copies(piece):
        cols = piece_cols(piece)
        copies = []
        for step in range(LINES):
            copies.append(
                remote(
                    shard.at[:, cols],
                    w.at[s, e, y, :, cols],
                    z_send.at[piece, step],
                    z_recv.at[s, piece, e],
                    (t, place.row_of(place.line(step), y), t),
                )
            )
        local = pltpu.make_async_copy(
            shard.at[:, cols], w.at[s, e, y, :, cols], z_recv.at[s, piece, e]
        )
        return copies, local

    def z_start(step):
        layer, pieces = pieces_of(step)

        @pl.when(s == layer)
        def _():
            for piece in pieces:
                copies, local = z_copies(piece)

                @pl.when(primary)
                def _():
                    local.start()

                @pl.when(secondary)
                def _():
                    copies[0].start()

                for copy in copies[1:]:
                    copy.start()

    def z_finish(piece):
        copies, _ = z_copies(piece)

        @pl.when(secondary)
        def _():
            copies[0].wait_send()

        for copy in copies[1:]:
            copy.wait_send()

    def x_copy(layer, piece):
        part = w.at[layer, :, y, :, piece_cols(piece)]
        return remote(part, part, x_send.at[layer, piece], x_recv.at[layer, piece], place.across)

    def y_copy(layer, piece):
        part = w.at[layer, :, y, :, piece_cols(piece)]
        return remote(part, part, y_send.at[layer, piece], y_recv.at[layer, piece], place.beside)

    def xb_copy(layer, piece):
        part = w.at[layer, :, 1 - y, high_rows, piece_cols(piece)]
        return remote(part, part, xb_send.at[layer, piece], xb_recv.at[layer, piece], place.across)

    def ya_copy(layer, piece):
        part = w.at[layer, :, y, low_rows, piece_cols(piece)]
        return remote(part, part, ya_send.at[layer, piece], ya_recv.at[layer, piece], place.beside)

    def step_z(step):
        layer, pieces = pieces_of(step)

        @pl.when(primary)
        def _():
            for piece in pieces:
                cols = piece_cols(piece)
                for line in range(LINES):
                    await_bytes(w.at[layer, line, y, :, cols], z_recv.at[layer, piece, line])
                x_copy(layer, piece).start()
                y_copy(layer, piece).start()

    def step_plane(step):
        layer, pieces = pieces_of(step)

        @pl.when(primary)
        def _():
            for piece in pieces:
                await_bytes(w.at[layer, :, 1 - y, :, piece_cols(piece)], y_recv.at[layer, piece])
                xb_copy(layer, piece).start()

        @pl.when(secondary)
        def _():
            for piece in pieces:
                await_bytes(w.at[layer, :, y, :, piece_cols(piece)], x_recv.at[layer, piece])
                ya_copy(layer, piece).start()

    def tick(step):
        if step + 3 < 2 * CHUNKS:
            step_z(step + 3)
        if step + 8 < 2 * CHUNKS:
            z_start(step + 8)
        step_plane(step)

    def complete(*steps):
        @pl.when(secondary)
        def _():
            for step in steps:
                layer, pieces = pieces_of(step)
                for piece in pieces:
                    cols = piece_cols(piece)
                    await_bytes(w.at[layer, :, 1 - y, high_rows, cols], xb_recv.at[layer, piece])
                    await_bytes(w.at[layer, :, 1 - y, low_rows, cols], ya_recv.at[layer, piece])

    def at_turns(turns):
        def beside(index):
            for turn, steps in turns.items():

                @pl.when(index == turn)
                def _():
                    for step in steps:
                        step()

        return beside

    def ticks(turns):
        return at_turns({turn: (functools.partial(tick, step),) for turn, step in turns.items()})

    kept = {
        "x": (n2.at[pl.ds(0, width), :], x_hbm),
        "h": (res, h_hbm),
        "n1": (n1.at[pl.ds(0, width), :], n1_hbm),
        "n2": (n2.at[pl.ds(0, width), :], n2_hbm),
        "qkv": (qkv, qkv_hbm),
        "ctx": (ctx, ctx_hbm),
        "lse": (lse, lse_hbm),
        "act": (act, act_hbm),
        "slope": (slope, slope_hbm),
    }
    names = tuple(kept)

    def save(name, layer):
        src, dst = kept[name]
        if name in ("x", "h"):
            dst = dst.at[layer]
        return pltpu.make_async_copy(src, dst, save_sem.at[names.index(name), layer])

    def load(name, layer=0):
        dst, src = kept[name]
        if name == "x":
            dst, src = act.at[pl.ds(0, width), :], src.at[layer]
        return pltpu.make_async_copy(src, dst, load_sem.at[names.index(name)])

    def load_h(layer, index):
        slot = lax.rem(index, 2)
        return pltpu.make_async_copy(
            h_hbm.at[layer, :, block_of(index)], h_in.at[slot], h_sem.at[slot]
        )

    my_quarter = pl.ds(s * quarter, quarter)
    my_rows = pl.ds(pl.multiple_of((1 - t) * half + s * quarter, quarter), quarter)

    def clip_across():
        there = pl.ds(pl.multiple_of(t * half + s * quarter, quarter), quarter)
        return remote(
            clips.at[1 - t, my_quarter, :],
            stage.at[there, :],
            in_sem.at[0],
            in_sem.at[1],
            place.across,
        )

    def clip_core():
        part = stage.at[my_rows, :]
        return remote(part, part, in_sem.at[2], in_sem.at[3], place.core)

    def cot_across():
        return remote(
            cot.at[1 - t, my_quarter, :],
            cot_other.at[my_quarter, :],
            cot_sem.at[0],
            cot_sem.at[1],
            place.across,
        )

    def cot_core():
        part = cot_other.at[my_quarter, :]
        return remote(part, part, cot_sem.at[2], cot_sem.at[3], place.core)

    def exchange(kind, index, slot):
        return remote(
            send.at[kind, index],
            recv.at[kind, index],
            e_send.at[slot, index],
            e_recv.at[slot, index],
            place.core,
        )

    def result_copies(ref, first):
        local = pltpu.make_async_copy(stage.at[mine, :], ref.at[0, t], out_sem.at[first])
        away = remote(
            stage.at[theirs, :],
            ref.at[0, t],
            out_sem.at[first + 1],
            out_sem.at[first + 2],
            place.across,
        )
        return local, away

    def grad_copies(index):
        place_in = lax.rem(index, blocks // 2)
        part = in_grad.at[0, t, pl.ds(pl.multiple_of(place_in * BLOCK, BLOCK), BLOCK), :]
        src = stage.at[block_of(index), :]
        local = pltpu.make_async_copy(src, part, grad_sem.at[0, place_in])
        away = remote(
            src, part, grad_sem.at[1, place_in], grad_sem.at[2, place_in], place.across
        )
        return local, away

    def emit(layer, ref, first):
        @pl.when(s == layer)
        def _():
            for copy in result_copies(ref, first):
                copy.start()

    for copy in own_loads:
        copy.wait()
    for step in range(3):
        z_start(step)
    n1[width:, :] = jnp.ones((ONES, frames), BF)
    n2[width:, :] = jnp.ones((ONES, frames), BF)
    own_clip = pltpu.make_async_copy(clips.at[t], stage.at[mine, :], in_sem.at[4])
    own_clip.start()
    clip_across().start()
    cot_across().start()
    own_out.wait()
    shard[:, OUT:UP] = flat[0:WIDE, :].T
    own_up.wait()
    for step in (3, 4):
        z_start(step)

    def take_clip(first):
        def body(index, carry):
            at = pl.ds(pl.multiple_of(first + index * BLOCK, BLOCK), BLOCK)
            tile = stage[at, :].T
            n2[0:width, at] = tile
            res[:, at] = tile.astype(F32)
            return carry

        lax.fori_loop(0, half // BLOCK, body, 0)

    own_clip.wait()
    take_clip(t * half)
    own_down.wait()
    for piece in range(4):
        span = slice((1 + piece) * WIDE, (2 + piece) * WIDE)
        shard[:, DOWN + piece * WIDE : DOWN + (piece + 1) * WIDE] = flat[span, :].T
    clip_across().wait()
    clip_core().start()
    step_z(0)
    z_start(5)
    step_z(1)
    z_start(6)
    clip_core().wait()
    take_clip((1 - t) * half)
    save("x", 0).start()
    step_plane(0)
    step_z(2)
    z_start(7)
    step_plane(1)
    cot_across().wait()
    cot_core().start()
    step_z(3)
    z_start(8)
    step_plane(2)
    step_z(4)
    z_start(9)
    step_z(5)
    z_start(10)

    def project(pair):
        for index in (2 * pair, 2 * pair + 1):
            cols = block_of(index)
            mean, scale = norm_stats(lambda span: res[span, cols], width)
            for span in chunks_of(width):
                hat = (res[span, cols] - mean) * scale
                n1[span, cols] = (hat * vecs[span, 0:1] + vecs[span, 2:3]).astype(BF)
        cols = pair_of(pair)
        for first, many, kind, bias in PARTS:
            value = mm(wt[first : first + many, :], n1[0:width, cols])
            for span in chunks_of(many):
                part = value[span, :]
                if kind != "k":
                    part = part + spread[bias + span.start : bias + span.stop, 6:7]
                if kind == "q":
                    part = part * 0.125
                qkv[first + span.start : first + span.stop, cols] = part.astype(BF)

    def send_pair(kind, pair, slot, value):
        for part in range(2):
            index = 2 * pair + part
            send[kind, index] = value[:, part * BLOCK : (part + 1) * BLOCK].astype(BF)
            exchange(kind, index, slot).start()

    def head_rows(head, first):
        return pl.ds(pl.multiple_of(first + head * HEAD, HEAD), HEAD)

    def attend(layer, turns, later_turns):
        def heads_of(first_head, base, stride, beside):
            def one_head(index_in, carry):
                head = first_head + index_in
                q_rows = head_rows(index_in, base)
                k_rows = head_rows(index_in, base + stride)
                v_rows = head_rows(index_in, base + 2 * stride)
                c_rows = head_rows(head, 0)
                keys = qkv[k_rows, :].T
                for index in range(blocks):
                    cols = slice(index * BLOCK, (index + 1) * BLOCK)
                    queries = qkv[q_rows, cols]
                    tiles = []
                    top = None
                    for tile in chunks_of(frames, BLOCK):
                        scores = mm(keys[tile, :], queries)
                        for span in chunks_of(BLOCK):
                            peak = stack_max(scores[span, :])
                            top = peak if top is None else jnp.maximum(top, peak)
                        tiles.append(scores)
                    top = jnp.max(top, 0, keepdims=True)
                    total = jnp.zeros((8, BLOCK), F32)
                    mixed = jnp.zeros((HEAD, BLOCK), F32)
                    for tile, scores in zip(chunks_of(frames, BLOCK), tiles):
                        soft = []
                        for span in chunks_of(BLOCK):
                            part = jnp.exp(scores[span, :] - top)
                            total = total + stack_sum(part)
                            soft.append(part.astype(BF))
                        mixed = mixed + mm(qkv[v_rows, tile], jnp.concatenate(soft, 0))
                    total = jnp.sum(total, 0, keepdims=True)
                    ctx[c_rows, cols] = (mixed / total).astype(BF)
                    lse[pl.ds(head, 1), cols] = top + jnp.log(total)
                beside(index_in)
                return carry

            return one_head

        lax.fori_loop(0, 4, heads_of(0, 0, 256, ticks(turns)), 0)
        lax.fori_loop(0, 2, heads_of(4, 768, 128, ticks(later_turns)), 0)

    def out_project(layer, turns):
        beside = ticks(turns)

        def body(index, carry):
            part = mm(whole(w, layer, OUT, 384), ctx[:, pair_of(index)])
            send_pair(0, index, 2 * layer, part)
            beside(index)
            return carry

        lax.fori_loop(0, blocks // 2, body, 0)

    def middle_norm(layer, turns):
        beside = ticks(turns)

        def body(index, carry):
            cols = block_of(index)
            exchange(0, index, 2 * layer).wait()
            for span in chunks_of(width):
                added = send[0, index, span, :].astype(F32) + recv[0, index, span, :].astype(F32)
                res[span, cols] = res[span, cols] + added + vecs[span, 3:4]
            mean, scale = norm_stats(lambda span: res[span, cols], width)
            for span in chunks_of(width):
                hat = (res[span, cols] - mean) * scale
                n2[span, cols] = (hat * vecs[span, 1:2] + vecs[span, 4:5]).astype(BF)
            beside(index)
            return carry

        lax.fori_loop(0, blocks, body, 0)

    def hidden_part(layer, part):
        flip_weights(w, wt, layer, UP + part * WIDE, WIDE, part * WIDE)
        units = slice(part * WIDE, (part + 1) * WIDE)
        lane = 7 if part < 2 else 8

        def body(index, carry):
            cols = pair_of(index)
            pre = mm(wt[units, :], n2[0:width, cols])
            for span in chunks_of(WIDE):
                first = part * WIDE + span.start
                bias = spread[768 + first : 768 + first + ROWS, lane : lane + 1]
                value, steep = gelu_parts(pre[span, :] + bias)
                act[first : first + ROWS, cols] = value.astype(BF)
                slope[first : first + ROWS, cols] = steep.astype(BF)
            return carry

        lax.fori_loop(0, blocks // 2, body, 0)

    def down_project(layer, turns):
        beside = ticks(turns)

        def body(index, carry):
            part = mm(whole(w, layer, DOWN, 1536), act[:, pair_of(index)])
            send_pair(1, index, 2 * layer + 1, part)
            beside(index)
            return carry

        lax.fori_loop(0, blocks // 2, body, 0)

    def layer_end(layer, index, span):
        added = send[1, index, span, :].astype(F32) + recv[1, index, span, :].astype(F32)
        return (res[span, block_of(index)] + added + vecs[span, 5:6]).astype(BF)

    def take_vectors(layer):
        vecs[...] = whole(w, layer, VEC, 128).astype(F32)
        spread_biases(vecs, spread, rows)

    def project_all(layer, turns):
        beside = ticks(turns)
        flip_weights(w, wt, layer, QKV, 1152)

        def body(index, carry):
            project(index)
            beside(index)
            return carry

        lax.fori_loop(0, blocks // 2, body, 0)
        if layer == 0:
            save("n1", 0).start()
            save("qkv", 0).start()

    complete(0, 1, 2)
    take_vectors(0)
    project_all(0, {0: 3, 1: 4})
    cot_core().wait()
    load_cot = pltpu.make_async_copy(cot_other, stage.at[theirs, :], cot_sem.at[4])
    load_cot.start()
    own_cot = pltpu.make_async_copy(cot.at[t], stage.at[mine, :], cot_sem.at[5])
    own_cot.start()
    attend(0, {0: 5, 2: 6}, {0: 7})
    save("ctx", 0).start()
    save("lse", 0).start()
    complete(3)
    out_project(0, {1: 8})
    load_cot.wait()
    own_cot.wait()

    sums[3] = jnp.zeros_like(sums[3])

    def take_cot(index, carry):
        low[:, block_of(index)] = stage[block_of(index), :].T
        for span in chunks_of(width):
            sums[3, span, :] += fold(low[span, block_of(index)].astype(F32))
        return carry

    lax.fori_loop(0, blocks, take_cot, 0)
    save("x", 0).wait()
    middle_norm(0, {1: 9})
    save("h", 0).start()
    save("n2", 0).start()
    for part in range(4):
        complete(4 + part)
        hidden_part(0, part)
        tick(10 + part)
    save("act", 0).start()
    save("slope", 0).start()
    complete(8, 9, 10, 11)
    down_project(0, {1: 14})
    for name in ("n1", "qkv", "h", "n2"):
        save(name, 0).wait()

    def finish_body(index, carry):
        exchange(1, index, 1).wait()
        cols = block_of(index)
        for span in chunks_of(width):
            rows_out = layer_end(0, index, span)
            n2[span, cols] = rows_out
            res[span, cols] = rows_out.astype(F32)

        @pl.when(s == 0)
        def _():
            stage[cols, :] = n2[0:width, cols].T

        return carry

    lax.fori_loop(0, blocks, finish_body, 0)
    emit(0, out, 0)
    save("x", 1).start()
    complete(12, 13, 14)
    take_vectors(1)
    project_all(1, {0: 15, 1: 16})
    save("ctx", 0).wait()
    save("lse", 0).wait()
    attend(1, {0: 17, 2: 18}, {0: 19})
    complete(15)
    out_project(1, {1: 20})
    save("x", 1).wait()
    middle_norm(1, {1: 21})
    save("h", 1).start()
    save("act", 0).wait()
    save("slope", 0).wait()
    for part in range(4):
        complete(16 + part)
        hidden_part(1, part)
        if part < 2:
            tick(22 + part)
    for part in range(4):
        complete(20 + part)
        flip_weights(w, wt, 1, DOWN + part * WIDE, WIDE, part * WIDE)
    down_project(1, {})

    def gya_copy(layer, piece):
        cols = piece_cols(piece)
        return remote(
            w.at[layer, :, 1 - y, low_rows, cols],
            land_a.at[:, low_rows, cols],
            gya_send.at[layer, piece],
            gya_recv.at[layer, piece],
            place.beside,
        )

    def gxb_copy(layer, piece):
        cols = piece_cols(piece)
        return remote(
            w.at[layer, :, 1 - y, high_rows, cols],
            land_b.at[:, :, cols],
            gxb_send.at[layer, piece],
            gxb_recv.at[layer, piece],
            place.across,
        )

    def gx_copy(layer, piece):
        cols = piece_cols(piece)
        return remote(
            w.at[layer, :, y, :, cols],
            land_a.at[:, :, cols],
            gx_send.at[layer, piece],
            gx_recv.at[layer, piece],
            place.across,
        )

    def gy_copy(layer, piece):
        cols = piece_cols(piece)
        return remote(
            w.at[layer, :, 1 - y, :, cols],
            land_y.at[:, :, cols],
            gy_send.at[layer, piece],
            gy_recv.at[layer, piece],
            place.beside,
        )

    def landed_part(piece):
        if piece == VECTORS:
            return landed_vec
        ref, first = (
            (landed_qkv, 0)
            if piece < 3
            else (landed_out, 3)
            if piece < 4
            else (landed_up, 4)
            if piece < 8
            else (landed_down, 8)
        )
        return ref.at[:, :, pl.ds((piece - first) * WIDE, WIDE)]

    def gz_copies(layer, piece):
        cols = piece_cols(piece)
        target = landed_part(piece)
        copies = []
        for step in range(LINES):
            line = place.line(step)
            copies.append(
                remote(
                    w.at[layer, line, y, :, cols],
                    target.at[e],
                    gz_send.at[layer, piece, step],
                    gz_recv.at[piece, e],
                    (layer, place.row_of(line, y), t),
                )
            )
        local = pltpu.make_async_copy(
            w.at[layer, e, y, :, cols], target.at[e], gz_recv.at[piece, e]
        )
        return copies, local

    def add_rows(layer, piece, which, span, lands):
        cols = piece_cols(piece)
        first, count = span
        for line in range(LINES):
            total = w[layer, line, which, pl.ds(first, count), cols].astype(F32)
            for land, offset in lands:
                total = total + land[line, pl.ds(offset, count), cols].astype(F32)
            w[layer, line, which, pl.ds(first, count), cols] = total.astype(BF)

    def signal(sem, layer, piece, device):
        if layer == 1:
            pl.semaphore_signal(sem.at[piece], inc=1, device_id=device, device_id_type=MESH)

    def credit(sem, layer, piece):
        if layer == 0:
            pl.semaphore_wait(sem.at[piece], 1)

    def step_a(layer, piece):
        @pl.when(secondary)
        def _():
            credit(ya_free, layer, piece)
            gya_copy(layer, piece).start()
            credit(xb_free, layer, piece)
            gxb_copy(layer, piece).start()

    def step_b(layer, piece):
        cols = piece_cols(piece)

        @pl.when(secondary)
        def _():
            await_bytes(land_a.at[:, low_rows, cols], gya_recv.at[layer, piece])
            add_rows(layer, piece, y, (0, SPLIT), [(land_a, 0)])
            signal(ya_free, layer, piece, place.beside)
            credit(x_free, layer, piece)
            gx_copy(layer, piece).start()

        @pl.when(primary)
        def _():
            await_bytes(land_b.at[:, :, cols], gxb_recv.at[layer, piece])
            add_rows(layer, piece, 1 - y, (SPLIT, rows - SPLIT), [(land_b, 0)])
            signal(xb_free, layer, piece, place.across)
            credit(y_free, layer, piece)
            gy_copy(layer, piece).start()

    def step_c(layer, piece):
        cols = piece_cols(piece)

        @pl.when(primary)
        def _():
            await_bytes(land_a.at[:, :, cols], gx_recv.at[layer, piece])
            await_bytes(land_y.at[:, :, cols], gy_recv.at[layer, piece])
            add_rows(layer, piece, y, (0, rows), [(land_a, 0), (land_y, 0)])
            signal(x_free, layer, piece, place.across)
            signal(y_free, layer, piece, place.beside)
            copies, local = gz_copies(layer, piece)

            @pl.when(s == layer)
            def _():
                local.start()

            @pl.when(s != layer)
            def _():
                copies[0].start()

            for copy in copies[1:]:
                copy.start()

    def store_grads(layer, start, count, value):
        w[layer, :, :, :, pl.ds(start, count)] = value.astype(BF).reshape(
            w.shape[1], w.shape[2], rows, count
        )

    def mlp_back(layer, beside):
        def body(index, carry):
            cols = pair_of(index)
            for part in range(4):
                units = slice(part * WIDE, (part + 1) * WIDE)
                grad = mm(wt[units, :], low[:, cols])
                for span in chunks_of(WIDE):
                    rows_in = slice(units.start + span.start, units.start + span.stop)
                    steep = slope[rows_in, cols].astype(F32)
                    slope[rows_in, cols] = (grad[span, :] * steep).astype(BF)
            term = mm(whole(w, layer, UP, 1536), slope[:, cols])
            send_pair(0, index, 4 + 2 * layer, term)
            beside(index)
            return carry

        lax.fori_loop(0, blocks // 2, body, 0)

    def outer(layer, start, left, right, first, many, before, beside):
        def body(index, carry):
            before(index)
            base = index * PAIR
            span = pl.ds(pl.multiple_of(first + base, 128), PAIR)
            value = mmt(left[...], right[span, :])
            store_grads(layer, pl.multiple_of(start + base, 128), PAIR, value[0:width, :])
            if left.shape[0] > width:
                to = pl.ds(pl.multiple_of(768 + base, BLOCK), PAIR)
                spread[to, 0:8] = value[width : width + 8, :].T
            beside(index)
            return carry

        lax.fori_loop(0, many // PAIR, body, 0)

    def turned(turn):
        return lax.rem(turn + (1 - t) * (blocks // 2), blocks)

    def norm_back(layer, kind, gain_lane, source, put, finish, beside):
        sums[0:3] = jnp.zeros((3, width, 128), F32)

        def body(turn, carry):
            index = turned(turn)
            cols = block_of(index)
            read = source(index)
            mean, scale = norm_stats(read, width)
            exchange(kind, index, 4 + 2 * layer + kind).wait()
            first = jnp.zeros((8, BLOCK), F32)
            second = jnp.zeros((8, BLOCK), F32)

            def terms(span):
                hat = (read(span) - mean) * scale
                grad = send[kind, index, span, :].astype(F32)
                grad = grad + recv[kind, index, span, :].astype(F32)
                return hat, grad, grad * vecs[span, gain_lane : gain_lane + 1]

            for span in chunks_of(width):
                hat, grad, scaled = terms(span)
                sums[0, span, :] += fold(grad * hat)
                sums[1, span, :] += fold(grad)
                first = first + stack_sum(scaled)
                second = second + stack_sum(scaled * hat)
            level = mean_of(first, width)
            slant = mean_of(second, width)
            for span in chunks_of(width):
                hat, _, scaled = terms(span)
                put(span, cols, res[span, cols] + scale * (scaled - level - hat * slant))
            finish(index)
            beside(turn)
            return carry

        lax.fori_loop(0, blocks, body, 0)

    def row_sums(value):
        return jnp.sum(value, 1, keepdims=True)

    def attend_back(first_head, many, base, stride, beside):
        def one_head(index_in, carry):
            head = first_head + index_in
            q_rows = head_rows(index_in, base)
            k_rows = head_rows(index_in, base + stride)
            v_rows = head_rows(index_in, base + 2 * stride)
            c_rows = head_rows(head, 0)
            keys = qkv[k_rows, :].T
            values = qkv[v_rows, :].T
            flat_queries = qkv[q_rows, :].T
            flat_grads = dctx[c_rows, :].T
            level = lse[pl.ds(head, 1), :]
            inner = jnp.sum(
                dctx[c_rows, :].astype(F32) * ctx[c_rows, :].astype(F32), 0, keepdims=True
            )
            step = jnp.zeros((HEAD, frames), F32)
            for tile in chunks_of(frames, BLOCK):
                soft = []
                score_grad = []
                for cols in chunks_of(frames, BLOCK):
                    scores = mm(keys[tile, :], qkv[q_rows, cols])
                    soft_grad = mm(values[tile, :], dctx[c_rows, cols])
                    soft_parts = []
                    grad_parts = []
                    for part in chunks_of(BLOCK):
                        strength = jnp.exp(scores[part, :] - level[:, cols])
                        soft_parts.append(strength.astype(BF))
                        strength = strength * (soft_grad[part, :] - inner[:, cols])
                        grad_parts.append(strength.astype(BF))
                    soft.append(jnp.concatenate(soft_parts, 0))
                    score_grad.append(jnp.concatenate(grad_parts, 0))
                soft = jnp.concatenate(soft, 1)
                score_grad = jnp.concatenate(score_grad, 1)
                step = step + mm(qkv[k_rows, tile], score_grad)
                slope[k_rows, tile] = mm(score_grad, flat_queries).astype(BF).T
                slope[v_rows, tile] = mm(soft, flat_grads).astype(BF).T
            slope[q_rows, :] = (step * 0.125).astype(BF)
            beside(index_in)
            return carry

        lax.fori_loop(0, many, one_head, 0)

    def keep_sums(first, value):
        for start, many, kind, bias in PARTS:
            offset = start - first
            if kind != "k" and 0 <= offset < value.shape[1]:
                spread[bias : bias + many, 0:8] = value[
                    width : width + 8, offset : offset + many
                ].T

    def collect_biases():
        def body(group, carry):
            source = group * rows
            for kind in range(2):
                for head in range(6):
                    at = pl.ds(pl.multiple_of(kind * 384 + head * HEAD + group * 8, 8), 8)
                    to = pl.ds(pl.multiple_of(source + kind * 48 + head * 8, 8), 8)
                    vec_grads[to, 6:7] = spread[at, 6:7]
            for unit in range(24):
                at = pl.ds(pl.multiple_of(768 + unit * HEAD + group * 8, 8), 8)
                to = pl.ds(pl.multiple_of(source + (unit % 12) * 8, 8), 8)
                lane = 7 if unit < 12 else 8
                vec_grads[to, lane : lane + 1] = spread[at, 6:7]
            return carry

        lax.fori_loop(0, GROUPS, body, 0)

    def nothing(index):
        del index

    def finish_gather(layer, piece):
        @pl.when(primary)
        def _():
            x_copy(layer, piece).wait_send()
            y_copy(layer, piece).wait_send()
            xb_copy(layer, piece).wait_send()

        @pl.when(secondary)
        def _():
            ya_copy(layer, piece).wait_send()

    def last_body(index, carry):
        exchange(1, index, 3).wait()

        @pl.when(s == 1)
        def _():
            for span in chunks_of(width, 128):
                stage[block_of(index), span] = layer_end(1, index, span).T

        return carry

    for layer in (1, 0):
        later = layer == 0
        if later:
            load_h(layer, turned(0)).start()
            load("act").wait()
            vecs[...] = whole(w, layer, VEC, 128).astype(F32)
            flip_weights(w, wt, layer, DOWN, 1536)
        vec_grads[...] = jnp.zeros_like(vec_grads)

        def a(piece, layer=layer):
            return lambda: step_a(layer, piece)

        def b(piece, layer=layer):
            return lambda: step_b(layer, piece)

        def c(piece, layer=layer):
            return lambda: step_c(layer, piece)

        if later:
            before = nothing
            early = at_turns(
                {
                    0: (a(8), lambda: step_b(1, VECTORS)),
                    1: (a(9), lambda: step_c(1, VECTORS)),
                    2: (a(10), a(11)),
                }
            )
        else:
            waits = [functools.partial(finish_gather, 1, piece) for piece in (8, 9, 10, 11)]
            before = at_turns({0: waits[:2], 1: waits[2:3], 2: waits[3:]})
            early = at_turns({0: (a(8),), 1: (a(9),), 2: (a(10), a(11))})
        outer(layer, DOWN, low, act, 0, 1536, before, early)
        load("x", layer).start()
        vec_grads[:, 5:6] = row_sums(sums[3])
        if not later:
            lax.fori_loop(0, blocks, last_body, 0)
            emit(1, out, 0)
            save("h", 1).wait()
            load_h(layer, turned(0)).start()
            res[...] = low[...].astype(F32)
            for piece in range(CHUNKS + 1):
                z_finish(piece)
                finish_gather(0, piece)
                if piece < 8 or piece == VECTORS:
                    finish_gather(1, piece)
        else:
            load("slope").wait()

        mlp_back(layer, at_turns({0: (b(8),), 1: (b(9), b(10), b(11))}))
        if later:
            load("n2").wait()
        drain = at_turns({0: (a(4),), 1: (a(5),), 2: (a(6), a(7), c(8))})
        outer(layer, UP, n2, slope, 0, 1536, nothing, drain)
        flip_weights(w, wt, layer, OUT, 384)

        def hidden_in(index, layer=layer):
            turn = lax.rem(index + (1 - t) * (blocks // 2), blocks)

            @pl.when(turn + 1 < blocks)
            def _():
                load_h(layer, turned(turn + 1)).start()

            load_h(layer, index).wait()
            slot = lax.rem(index, 2)
            return lambda span: h_in[slot, span, :]

        def hidden_put(span, cols, total):
            res[span, cols] = total
            rounded = total.astype(BF)
            low[span, cols] = rounded
            sums[2, span, :] += fold(rounded.astype(F32))

        drain = at_turns({0: (b(4), c(9)), 1: (b(5), c(10)), 2: (b(6), c(11)), 3: (b(7),)})
        norm_back(layer, 0, 1, hidden_in, hidden_put, nothing, drain)

        def context_back(index, carry):
            cols = pair_of(index)
            dctx[:, cols] = mm(wt[0:384, :], low[:, cols]).astype(BF)
            return carry

        lax.fori_loop(0, blocks // 2, context_back, 0)
        vec_grads[:, 1:2] = row_sums(sums[0])
        vec_grads[:, 4:5] = row_sums(sums[1])
        vec_grads[:, 3:4] = row_sums(sums[2])
        if later:
            for name in ("ctx", "qkv", "lse"):
                load(name).wait()
        store_grads(layer, OUT, 384, mmt(low[...], ctx[...]))
        step_a(layer, 3)
        drain = at_turns({0: (c(4),), 1: (c(5),), 2: (b(3), c(6)), 3: (c(7),)})
        attend_back(0, 4, 0, 256, drain)
        if later:
            load("n1").wait()
        wt[0:768, :] = whole(w, layer, QKV, 768)

        for first, many in ((0, 512), (512, 256)):
            value = mmt(n1[...], slope[first : first + many, :])
            store_grads(layer, QKV + first, many, value[0:width, :])
            keep_sums(first, value)
        step_a(layer, 0)
        step_a(layer, 1)
        attend_back(4, 2, 768, 128, at_turns({0: (b(0), c(3)), 1: (b(1),)}))

        def first_body(index, carry, layer=layer):
            cols = pair_of(index)
            term = mm(wt[0:768, :], slope[0:768, cols])
            term = term + mm(whole(w, layer, QKV + 768, WIDE), slope[768:1152, cols])
            send_pair(1, index, 5 + 2 * layer, term)
            return carry

        lax.fori_loop(0, blocks // 2, first_body, 0)
        value = mmt(n1[...], slope[768:1152, :])
        store_grads(layer, QKV + 768, WIDE, value[0:width, :])
        keep_sums(768, value)
        step_a(layer, 2)
        step_c(layer, 0)
        collect_biases()
        if layer == 1:
            for name in ("slope", "n1", "n2", "ctx", "qkv", "lse"):
                load(name).start()
        load("x", layer).wait()

        @pl.when(s == layer)
        def _():
            local, away = result_copies(out, 0)
            local.wait()
            away.wait_send()

        def rows_x(index):
            return lambda span: act[span, block_of(index)].astype(F32)

        def rows_put(span, cols, total, layer=layer):
            rounded = total.astype(BF)
            low[span, cols] = rounded
            if layer == 1:
                res[span, cols] = rounded.astype(F32)
                sums[2, span, :] += fold(rounded.astype(F32))

        def rows_out(index, layer=layer):
            @pl.when(s == layer)
            def _():
                stage[block_of(index), :] = low[:, block_of(index)].T
                local, away = grad_copies(index)

                @pl.when(index // (blocks // 2) == t)
                def _():
                    local.start()

                @pl.when(index // (blocks // 2) != t)
                def _():
                    away.start()

        drain = at_turns({0: (c(1),), 1: (b(2),), 3: (c(2),)})
        norm_back(layer, 1, 0, rows_x, rows_put, rows_out, drain)
        if layer == 1:
            load("act").start()
        vec_grads[:, 0:1] = row_sums(sums[0])
        vec_grads[:, 2:3] = row_sums(sums[1])
        sums[3] = sums[2]
        store_grads(layer, VEC, 128, vec_grads[...])
        step_a(layer, VECTORS)

    step_b(0, VECTORS)
    step_c(0, VECTORS)

    def finish_scatter(piece):
        for layer in range(2):

            @pl.when(secondary)
            def _():
                gya_copy(layer, piece).wait_send()
                gxb_copy(layer, piece).wait_send()
                gx_copy(layer, piece).wait_send()

            @pl.when(primary)
            def _():
                gy_copy(layer, piece).wait_send()
                copies, _ = gz_copies(layer, piece)

                @pl.when(s != layer)
                def _():
                    copies[0].wait_send()

                for copy in copies[1:]:
                    copy.wait_send()

    for piece in range(CHUNKS + 1):
        finish_scatter(piece)
        for line in range(LINES):
            await_bytes(landed_part(piece).at[line], gz_recv.at[piece, line])

    _, away = result_copies(out, 0)
    away.wait_recv()
    for index in range(blocks // 2):
        local, away = grad_copies(index)
        local.wait()
        away.wait()


def layers_call(share, clips, cotangent, shards, dims):
    width, frames, hidden_units, heads_width = dims
    rows = width // GROUPS
    sem = pltpu.SemaphoreType.DMA
    free = pltpu.SemaphoreType.REGULAR
    packed = (2, LINES, 2, rows, END)
    blocks = frames // BLOCK
    shape = jax.ShapeDtypeStruct
    outs = [
        shape((1,) + clips.shape, BF),
        shape((1,) + clips.shape, BF),
        shape((LINES, rows, QKV - VEC), BF),
        shape((LINES, rows, OUT - QKV), BF),
        shape((LINES, rows, UP - OUT), BF),
        shape((LINES, rows, DOWN - UP), BF),
        shape((LINES, rows, END - DOWN), BF),
        shape(clips.shape[1:], BF),
        shape((2, width, frames), BF),
        shape((2, width, frames), F32),
        shape((width, frames), BF),
        shape((width, frames), BF),
        shape((3 * heads_width, frames), BF),
        shape((heads_width, frames), BF),
        shape((8, frames), F32),
        shape((hidden_units, frames), BF),
        shape((hidden_units, frames), BF),
    ]
    scratch = [
        pltpu.VMEM(packed, BF),
        pltpu.VMEM((width, frames), F32),
        pltpu.VMEM((hidden_units, frames), BF),
        pltpu.VMEM((hidden_units, frames), BF),
        pltpu.VMEM((width + ONES, frames), BF),
        pltpu.VMEM((width + ONES, frames), BF),
        pltpu.VMEM((width, frames), BF),
        pltpu.VMEM((3 * heads_width, frames), BF),
        pltpu.VMEM((heads_width, frames), BF),
        pltpu.VMEM((heads_width, frames), BF),
        pltpu.VMEM((8, frames), F32),
        pltpu.VMEM((2, width, BLOCK), F32),
        pltpu.VMEM((hidden_units, width), BF),
        pltpu.VMEM((2, blocks, width, BLOCK), BF),
        pltpu.VMEM((2, blocks, width, BLOCK), BF),
        pltpu.VMEM((width, 128), F32),
        pltpu.VMEM((width, 128), F32),
        pltpu.VMEM((4, width, 128), F32),
        pltpu.VMEM((2 * heads_width + hidden_units, 128), F32),
        pltpu.VMEM((frames, width), BF),
        pltpu.VMEM((rows, END), BF),
        pltpu.VMEM((WIDE + END - DOWN, rows), BF),
        pltpu.VMEM((LINES, rows, END), BF),
        pltpu.VMEM((LINES, rows - SPLIT, END), BF),
        pltpu.VMEM((LINES, rows, END), BF),
    ]
    scratch += [sem((CHUNKS + 1, LINES)), sem((2, CHUNKS + 1, LINES))]
    scratch += [sem((2, CHUNKS + 1))] * 8
    scratch += [sem((2, CHUNKS + 1, LINES)), sem((CHUNKS + 1, LINES))]
    scratch += [sem((2, CHUNKS + 1))] * 8
    scratch += [
        sem((8, blocks)),
        sem((8, blocks)),
        sem((10,)),
        sem((5,)),
        sem((6,)),
        sem((3,)),
        sem((3, blocks // 2)),
        sem((9, 2)),
        sem((9,)),
        sem((2,)),
    ]
    scratch += [free((CHUNKS + 1,))] * 4
    anywhere = pl.BlockSpec(memory_space=pl.ANY)
    return pl.pallas_call(
        functools.partial(layers_kernel, share),
        out_shape=outs,
        in_specs=[anywhere] * (2 + len(shards)),
        out_specs=[anywhere] * len(outs),
        scratch_shapes=scratch,
        compiler_params=pltpu.CompilerParams(
            collective_id=0, has_side_effects=True, vmem_limit_bytes=VMEM_LIMIT
        ),
        cost_estimate=pl.CostEstimate(
            flops=60_000_000_000, bytes_accessed=60_000_000, transcendentals=0
        ),
    )(clips, cotangent, *shards)


def group_piece(value, axis, share):
    if share == 1:
        return value
    size = value.shape[axis] * share
    group = lax.axis_index("dp") // share
    full = lax.all_gather(value, "dp", axis=axis, tiled=True)
    return lax.dynamic_slice_in_dim(full, group * size, size, axis)


def own_part(value, axis, share, parts, index):
    size = value.shape[axis] // parts
    if parts == 1:
        return value
    return lax.dynamic_slice_in_dim(value, index * size, size, axis)


def on_device(share, clips, cotangent, ln_gains, row_biases, w_qkv, b_qv, w_o, w_up, b_ff, w_down):
    width = clips.shape[2]
    rows = width // GROUPS
    dims = (width, 2 * clips.shape[1], w_up.shape[2], w_o.shape[1])
    ln_gains = group_piece(ln_gains, 2, share)
    row_biases = group_piece(row_biases, 2, share)
    w_qkv = group_piece(w_qkv, 2, share)
    b_qv = group_piece(b_qv, 3, share)
    w_o = group_piece(w_o, 2, share)
    w_up = group_piece(w_up, 1, share)
    b_ff = group_piece(b_ff, 2, share)
    w_down = group_piece(w_down, 2, share)
    vectors = jnp.concatenate([ln_gains[0], row_biases[0]], 0).T
    heads = jnp.concatenate([b_qv[0, 0].reshape(-1), b_qv[0, 1].reshape(-1)])[:, None]
    units = b_ff[0].reshape(2, rows).T
    packed = jnp.concatenate([vectors, heads, units], 1)
    packed = jnp.pad(packed, ((0, 0), (0, 128 - packed.shape[1])))
    section_out, section_in_grad, *landed = layers_call(
        share, clips, cotangent, (packed, w_qkv, w_o, w_up, w_down), dims
    )
    rest = lax.axis_index("dp") % share
    side = lax.axis_index("tensor")

    def joined(value):
        total = jnp.sum(value.astype(F32), 0)
        if share == 1:
            return total
        group = lax.axis_index("dp") // share
        padded = jnp.zeros((width, total.shape[1]), F32)
        padded = lax.dynamic_update_slice_in_dim(padded, total, group * rows, 0)
        return lax.dynamic_slice_in_dim(lax.psum(padded, "dp"), group * rows, rows, 0)

    def mine(value):
        return own_part(joined(value), 0, share, share, rest)

    vectors = joined(landed[0])
    vec = own_part(own_part(vectors, 0, share, share, rest), 0, share, 2, side)
    heads_grad = vectors[:, 6].reshape(2, -1, HEAD // GROUPS)
    units_grad = vectors[:, 7:9].T.reshape(-1, HEAD // GROUPS)
    qkv_grad = {"q": [], "k": [], "v": []}
    for first, many, kind, _ in PARTS:
        qkv_grad[kind].append(mine(landed[1][:, :, first : first + many]))
    return (
        section_out,
        section_in_grad,
        vec[:, 0:2].T[None],
        vec[:, 2:6].T[None],
        jnp.stack([jnp.concatenate(qkv_grad[kind], 1) for kind in "qkv"])[None],
        own_part(heads_grad, 2, share, share, rest)[None],
        mine(landed[2]).T[None],
        mine(landed[3])[None],
        own_part(units_grad, 1, share, share, rest)[None],
        mine(landed[4]).T[None],
    )


def solution(mesh):
    placed = (
        P("dp", "tensor", None),
        P("dp", "tensor", None),
        P("section", None, "dp"),
        P("section", None, "dp"),
        P("section", None, "dp", "tensor"),
        P("section", None, "tensor", "dp"),
        P("section", "tensor", "dp"),
        P("section", "dp", "tensor"),
        P("section", "tensor", "dp"),
        P("section", "tensor", "dp"),
    )
    share = mesh.shape["dp"] // GROUPS
    return jax.shard_map(
        functools.partial(on_device, share),
        mesh=mesh,
        in_specs=placed,
        out_specs=(
            P("section", "dp", "tensor", None),
            P("section", "dp", "tensor", None),
            P("section", None, ("dp", "tensor")),
            P("section", None, ("dp", "tensor")),
            P("section", None, "dp", "tensor"),
            P("section", None, "tensor", "dp"),
            P("section", "tensor", "dp"),
            P("section", "dp", "tensor"),
            P("section", "tensor", "dp"),
            P("section", "tensor", "dp"),
        ),
        check_vma=False,
    )
```

```python
import functools

import jax
import jax.numpy as jnp
from jax import lax
from jax.experimental import pallas as pl
from jax.experimental.pallas import tpu as pltpu
from jax.sharding import PartitionSpec as P

BF = jnp.bfloat16
F32 = jnp.float32
MESH = pl.DeviceIdType.MESH
EPSILON = 1e-05
HEAD = 64
GROUPS = 8
LINES = 4
BLOCK = 256
PAIR = 2 * BLOCK
ROWS = 64
ONES = 16
VMEM_LIMIT = 62 * 1024 * 1024

VEC = 0
QKV = 128
OUT = 1280
UP = 1664
DOWN = 3200
END = 4736
SPLIT = 48
EDGE = 80
GATHER_EDGES = ((VEC, OUT), (OUT, UP), (UP, DOWN), (DOWN, END))
SCATTER_EDGES = ((DOWN, END), (UP, DOWN), (OUT, UP), (QKV, QKV + 768), (QKV + 768, OUT), (VEC, QKV))
WIDE = 384
CHUNKS = 12


PARTS = (
    (0, 256, "q", 0),
    (256, 256, "k", 0),
    (512, 256, "v", 384),
    (768, 128, "q", 256),
    (896, 128, "k", 256),
    (1024, 128, "v", 640),
)


def mm(left, right):
    return jnp.dot(left, right, preferred_element_type=F32)


def mmt(left, right):
    return lax.dot_general(left, right, (((1,), (1,)), ((), ())), preferred_element_type=F32)


class Place:
    def __init__(self, share):
        self.s = lax.axis_index("section")
        self.d = lax.axis_index("dp")
        self.t = lax.axis_index("tensor")
        group = self.d // share
        self.rest = self.d - group * share
        self.share = share
        self.e = group // 2
        self.y = group - self.e * 2
        self.primary = self.s == self.t
        self.core = (1 - self.s, self.d, self.t)
        self.across = (self.s, self.d, 1 - self.t)
        self.corner = (1 - self.s, self.d, 1 - self.t)
        self.beside = (self.s, self.row_of(self.e, 1 - self.y), self.t)

    def row_of(self, line, y):
        return (line * 2 + y) * self.share + self.rest

    def line(self, step):
        return lax.rem(self.e + step, LINES)

    def greet(self):
        barrier = pltpu.get_barrier_semaphore()
        peers = [self.core, self.across, self.corner, self.beside]
        for step in range(1, LINES):
            for section in range(2):
                peers.append((section, self.row_of(self.line(step), self.y), self.t))
        for peer in peers:
            pl.semaphore_signal(barrier, inc=1, device_id=peer, device_id_type=MESH)
        pl.semaphore_wait(barrier, len(peers))


def remote(src, dst, send_sem, recv_sem, device):
    return pltpu.make_async_remote_copy(
        src_ref=src,
        dst_ref=dst,
        send_sem=send_sem,
        recv_sem=recv_sem,
        device_id=device,
        device_id_type=MESH,
    )


def await_bytes(ref, sem):
    pltpu.make_async_copy(ref, ref, sem).wait()


def chunks_of(count, size=ROWS):
    return [slice(first, first + size) for first in range(0, count, size)]


def by_eights(value):
    return value.reshape(value.shape[0] // 8, 8, value.shape[1])


def stack_sum(value):
    return jnp.sum(by_eights(value), 0)


def stack_max(value):
    return jnp.max(by_eights(value), 0)


def mean_of(parts, count):
    return jnp.sum(parts, 0, keepdims=True) / count


def norm_stats(read, count):
    total = jnp.zeros((8, BLOCK), F32)
    for span in chunks_of(count):
        total = total + stack_sum(read(span))
    mean = mean_of(total, count)
    square = jnp.zeros((8, BLOCK), F32)
    for span in chunks_of(count):
        centred = read(span) - mean
        square = square + stack_sum(centred * centred)
    return mean, lax.rsqrt(mean_of(square, count) + EPSILON)


def gelu_parts(values):
    bell = jnp.exp(-0.5 * values * values)
    reach = jnp.abs(values) * 0.7071067811865476
    inv = 1.0 / (1.0 + 0.3275911 * reach)
    poly = inv * (
        0.254829592
        + inv * (-0.284496736 + inv * (1.421413741 + inv * (-1.453152027 + inv * 1.061405429)))
    )
    tail = 0.5 * poly * bell
    cdf = jnp.where(values >= 0.0, 1.0 - tail, tail)
    return values * cdf, cdf + values * bell * 0.3989422804014327


def fold(value):
    return value[:, 0:128] + value[:, 128:256]


def block_of(index):
    return pl.ds(pl.multiple_of(index * BLOCK, BLOCK), BLOCK)


def pair_of(index):
    return pl.ds(pl.multiple_of(index * PAIR, PAIR), PAIR)


def flip_weights(w, wt, layer, start, width, target=0):
    def body(index, carry):
        cols = pl.ds(pl.multiple_of(start + index * 128, 128), 128)
        rows = pl.ds(pl.multiple_of(target + index * 128, 128), 128)
        tile = w[layer, :, :, :, cols]
        wt[rows, :] = tile.reshape(tile.shape[0] * tile.shape[1] * tile.shape[2], 128).T
        return carry

    lax.fori_loop(0, width // 128, body, 0)


def whole(w, layer, start, width):
    tile = w[layer, :, :, :, start : start + width]
    return tile.reshape(tile.shape[0] * tile.shape[1] * tile.shape[2], width)


def spread_biases(vecs, spread, rows):
    def body(group, carry):
        source = group * rows
        for kind in range(2):
            for head in range(6):
                to = pl.ds(pl.multiple_of(kind * 384 + head * HEAD + group * 8, 8), 8)
                at = pl.ds(pl.multiple_of(source + kind * 48 + head * 8, 8), 8)
                spread[to, :] = vecs[at, :]
        for unit in range(24):
            to = pl.ds(pl.multiple_of(768 + unit * HEAD + group * 8, 8), 8)
            at = pl.ds(pl.multiple_of(source + (unit % 12) * 8, 8), 8)
            spread[to, :] = vecs[at, :]
        return carry

    lax.fori_loop(0, GROUPS, body, 0)


def layers_kernel(
    share,
    clips,
    cot,
    vec_in,
    qkv_in,
    out_in,
    up_in,
    down_in,
    out,
    in_grad,
    landed_vec,
    landed_qkv,
    landed_out,
    landed_up,
    landed_down,
    edge_vec,
    edge_qkv,
    edge_out,
    edge_up,
    edge_down,
    cot_other,
    x_hbm,
    h_hbm,
    n1_hbm,
    n2_hbm,
    qkv_hbm,
    ctx_hbm,
    lse_hbm,
    act_hbm,
    slope_hbm,
    w,
    res,
    act,
    slope,
    n1,
    n2,
    low,
    qkv,
    ctx,
    dctx,
    lse,
    h_in,
    wt,
    send,
    recv,
    vecs,
    vec_grads,
    sums,
    spread,
    stage,
    shard,
    flat,
    land_a,
    land_b,
    land_y,
    land_e,
    land_f,
    z_send,
    z_recv,
    x_send,
    x_recv,
    xb_send,
    xb_recv,
    y_send,
    y_recv,
    ya_send,
    ya_recv,
    gz_send,
    gz_recv,
    gx_send,
    gx_recv,
    gxb_send,
    gxb_recv,
    gy_send,
    gy_recv,
    gya_send,
    gya_recv,
    e1_send,
    e1_recv,
    e2_send,
    e2_recv,
    e3_send,
    e3_recv,
    g3_send,
    g3_recv,
    g2_send,
    g2_recv,
    g1_send,
    g1_recv,
    e_send,
    e_recv,
    own_sem,
    in_sem,
    cot_sem,
    out_sem,
    grad_sem,
    save_sem,
    load_sem,
    h_sem,
    ya_free,
    xb_free,
    x_free,
    y_free,
    g3_free,
    g2_free,
):
    place = Place(share)
    s, t, e, y = place.s, place.t, place.e, place.y
    primary, secondary = place.primary, jnp.logical_not(place.primary)
    width, frames = res.shape
    blocks = frames // BLOCK
    half = frames // 2
    quarter = half // 2
    rows = w.shape[3]
    low_rows = pl.ds(0, SPLIT)
    high_rows = pl.ds(SPLIT, EDGE - SPLIT)
    main_rows = pl.ds(0, EDGE)
    edge_rows = pl.ds(EDGE, rows - EDGE)
    mine = pl.ds(pl.multiple_of(t * half, half), half)
    theirs = pl.ds(pl.multiple_of((1 - t) * half, half), half)

    own_loads = [pltpu.make_async_copy(vec_in, shard.at[:, pl.ds(VEC, QKV)], own_sem.at[0])]
    for number, (first, many, kind, bias) in enumerate(PARTS):
        own_loads.append(
            pltpu.make_async_copy(
                qkv_in.at[0, "qkv".index(kind), :, pl.ds(bias % WIDE, many)],
                shard.at[:, pl.ds(QKV + first, many)],
                own_sem.at[1 + number],
            )
        )
    own_up = pltpu.make_async_copy(up_in.at[0], shard.at[:, pl.ds(UP, DOWN - UP)], own_sem.at[7])
    own_out = pltpu.make_async_copy(out_in.at[0], flat.at[pl.ds(0, WIDE), :], own_sem.at[8])
    own_down = pltpu.make_async_copy(
        down_in.at[0], flat.at[pl.ds(WIDE, END - DOWN), :], own_sem.at[9]
    )
    for copy in own_loads + [own_out, own_up, own_down]:
        copy.start()

    place.greet()

    VECTORS = CHUNKS

    def piece_cols(piece):
        if isinstance(piece, int) and piece == VECTORS:
            return pl.ds(VEC, QKV)
        return pl.ds(pl.multiple_of(QKV + piece * WIDE, 128), WIDE)

    def pieces_of(step):
        layer, piece = step // CHUNKS, step % CHUNKS
        return layer, (VECTORS, piece) if piece == 0 else (piece,)

    def z_copies(piece):
        cols = piece_cols(piece)
        src = shard.at[main_rows, cols]
        dst = w.at[s, e, y, main_rows, cols]
        copies = []
        for step in range(LINES):
            copies.append(
                remote(
                    src,
                    dst,
                    z_send.at[piece, step],
                    z_recv.at[s, piece, e],
                    (t, place.row_of(place.line(step), y), t),
                )
            )
        return copies, pltpu.make_async_copy(src, dst, z_recv.at[s, piece, e])

    def z_start(step):
        layer, pieces = pieces_of(step)

        @pl.when(s == layer)
        def _():
            for piece in pieces:
                copies, local = z_copies(piece)

                @pl.when(primary)
                def _():
                    local.start()

                @pl.when(secondary)
                def _():
                    copies[0].start()

                for copy in copies[1:]:
                    copy.start()

    def z_finish(piece):
        copies, _ = z_copies(piece)

        @pl.when(secondary)
        def _():
            copies[0].wait_send()

        for copy in copies[1:]:
            copy.wait_send()

    def x_copy(layer, piece):
        part = w.at[layer, :, y, main_rows, piece_cols(piece)]
        return remote(part, part, x_send.at[layer, piece], x_recv.at[layer, piece], place.across)

    def y_copy(layer, piece):
        part = w.at[layer, :, y, main_rows, piece_cols(piece)]
        return remote(part, part, y_send.at[layer, piece], y_recv.at[layer, piece], place.beside)

    def xb_copy(layer, piece):
        part = w.at[layer, :, 1 - y, high_rows, piece_cols(piece)]
        return remote(part, part, xb_send.at[layer, piece], xb_recv.at[layer, piece], place.across)

    def ya_copy(layer, piece):
        part = w.at[layer, :, y, low_rows, piece_cols(piece)]
        return remote(part, part, ya_send.at[layer, piece], ya_recv.at[layer, piece], place.beside)

    def step_z(step):
        layer, pieces = pieces_of(step)

        @pl.when(primary)
        def _():
            for piece in pieces:
                cols = piece_cols(piece)
                for line in range(LINES):
                    await_bytes(
                        w.at[layer, line, y, main_rows, cols], z_recv.at[layer, piece, line]
                    )
                x_copy(layer, piece).start()
                y_copy(layer, piece).start()

    def step_plane(step):
        layer, pieces = pieces_of(step)

        @pl.when(primary)
        def _():
            for piece in pieces:
                cols = piece_cols(piece)
                await_bytes(w.at[layer, :, 1 - y, main_rows, cols], y_recv.at[layer, piece])
                xb_copy(layer, piece).start()

        @pl.when(secondary)
        def _():
            for piece in pieces:
                cols = piece_cols(piece)
                await_bytes(w.at[layer, :, y, main_rows, cols], x_recv.at[layer, piece])
                ya_copy(layer, piece).start()

    def edge_cols(group, edges):
        start, stop = edges[group]
        return pl.ds(start, stop - start)

    def edge_first(group):
        cols = edge_cols(group, GATHER_EDGES)
        src = shard.at[edge_rows, cols]
        dst = w.at[s, e, y, edge_rows, cols]
        recv_sem = e1_recv.at[s, group]
        near = remote(src, dst, e1_send.at[group, 0], recv_sem, (t, place.d, t))
        far = remote(src, dst, e1_send.at[group, 1], recv_sem, (t, place.d, 1 - t))
        return near, far, pltpu.make_async_copy(src, dst, recv_sem)

    def edge_start(group):
        near, far, local = edge_first(group)
        far.start()

        @pl.when(primary)
        def _():
            local.start()

        @pl.when(secondary)
        def _():
            near.start()

    def edge_second(layer, group):
        part = w.at[layer, e, y, edge_rows, edge_cols(group, GATHER_EDGES)]
        return remote(part, part, e2_send.at[layer, group], e2_recv.at[layer, group], place.beside)

    def edge_third(layer, group):
        part = w.at[layer, e, :, edge_rows, edge_cols(group, GATHER_EDGES)]
        return [
            remote(
                part,
                part,
                e3_send.at[layer, group, step - 1],
                e3_recv.at[layer, group, e],
                (s, place.row_of(place.line(step), y), t),
            )
            for step in range(1, LINES)
        ]

    def edge_beside(layer, group):
        part = w.at[layer, e, y, edge_rows, edge_cols(group, GATHER_EDGES)]
        await_bytes(part, e1_recv.at[layer, group])
        edge_second(layer, group).start()

    def edge_along(layer, group):
        part = w.at[layer, e, 1 - y, edge_rows, edge_cols(group, GATHER_EDGES)]
        await_bytes(part, e2_recv.at[layer, group])
        for copy in edge_third(layer, group):
            copy.start()

    def edge_complete(layer, group):
        cols = edge_cols(group, GATHER_EDGES)
        for step in range(1, LINES):
            line = place.line(step)
            await_bytes(w.at[layer, line, :, edge_rows, cols], e3_recv.at[layer, group, line])

    def edge_finish(layer, group):
        edge_second(layer, group).wait_send()
        for copy in edge_third(layer, group):
            copy.wait_send()

    edge_ticks = {
        3: ((edge_along, 0, 1),),
        4: ((edge_along, 0, 2), (edge_beside, 0, 3)),
        5: ((edge_along, 0, 3),),
        8: ((edge_beside, 1, 0),),
        9: ((edge_along, 1, 0), (edge_beside, 1, 1)),
        11: ((edge_along, 1, 1), (edge_beside, 1, 2)),
        13: ((edge_along, 1, 2), (edge_beside, 1, 3)),
        15: ((edge_along, 1, 3),),
    }

    def tick(step):
        if step + 3 < 2 * CHUNKS:
            step_z(step + 3)
        if step + 8 < 2 * CHUNKS:
            z_start(step + 8)
        step_plane(step)
        for action, layer, group in edge_ticks.get(step, ()):
            action(layer, group)

    def complete(*steps):
        @pl.when(secondary)
        def _():
            for step in steps:
                layer, pieces = pieces_of(step)
                for piece in pieces:
                    cols = piece_cols(piece)
                    await_bytes(w.at[layer, :, 1 - y, high_rows, cols], xb_recv.at[layer, piece])
                    await_bytes(w.at[layer, :, 1 - y, low_rows, cols], ya_recv.at[layer, piece])

    def at_turns(turns):
        def beside(index):
            for turn, steps in turns.items():

                @pl.when(index == turn)
                def _():
                    for step in steps:
                        step()

        return beside

    def ticks(turns):
        return at_turns({turn: (functools.partial(tick, step),) for turn, step in turns.items()})

    kept = {
        "x": (n2.at[pl.ds(0, width), :], x_hbm),
        "h": (res, h_hbm),
        "n1": (n1.at[pl.ds(0, width), :], n1_hbm),
        "n2": (n2.at[pl.ds(0, width), :], n2_hbm),
        "qkv": (qkv, qkv_hbm),
        "ctx": (ctx, ctx_hbm),
        "lse": (lse, lse_hbm),
        "act": (act, act_hbm),
        "slope": (slope, slope_hbm),
    }
    names = tuple(kept)

    def save(name, layer):
        src, dst = kept[name]
        if name in ("x", "h"):
            dst = dst.at[layer]
        return pltpu.make_async_copy(src, dst, save_sem.at[names.index(name), layer])

    def load(name, layer=0):
        dst, src = kept[name]
        if name == "x":
            dst, src = act.at[pl.ds(0, width), :], src.at[layer]
        return pltpu.make_async_copy(src, dst, load_sem.at[names.index(name)])

    def load_h(layer, index):
        slot = lax.rem(index, 2)
        return pltpu.make_async_copy(
            h_hbm.at[layer, :, block_of(index)], h_in.at[slot], h_sem.at[slot]
        )

    my_quarter = pl.ds(s * quarter, quarter)
    my_rows = pl.ds(pl.multiple_of((1 - t) * half + s * quarter, quarter), quarter)

    def clip_across():
        there = pl.ds(pl.multiple_of(t * half + s * quarter, quarter), quarter)
        return remote(
            clips.at[1 - t, my_quarter, :],
            stage.at[there, :],
            in_sem.at[0],
            in_sem.at[1],
            place.across,
        )

    def clip_core():
        part = stage.at[my_rows, :]
        return remote(part, part, in_sem.at[2], in_sem.at[3], place.core)

    def cot_across():
        return remote(
            cot.at[1 - t, my_quarter, :],
            cot_other.at[my_quarter, :],
            cot_sem.at[0],
            cot_sem.at[1],
            place.across,
        )

    def cot_core():
        part = cot_other.at[my_quarter, :]
        return remote(part, part, cot_sem.at[2], cot_sem.at[3], place.core)

    def exchange(kind, index, slot):
        return remote(
            send.at[kind, index],
            recv.at[kind, index],
            e_send.at[slot, index],
            e_recv.at[slot, index],
            place.core,
        )

    def result_copies(ref, first):
        local = pltpu.make_async_copy(stage.at[mine, :], ref.at[0, t], out_sem.at[first])
        away = remote(
            stage.at[theirs, :],
            ref.at[0, t],
            out_sem.at[first + 1],
            out_sem.at[first + 2],
            place.across,
        )
        return local, away

    def grad_copies(index):
        place_in = lax.rem(index, blocks // 2)
        part = in_grad.at[0, t, pl.ds(pl.multiple_of(place_in * BLOCK, BLOCK), BLOCK), :]
        src = stage.at[block_of(index), :]
        local = pltpu.make_async_copy(src, part, grad_sem.at[0, place_in])
        away = remote(
            src, part, grad_sem.at[1, place_in], grad_sem.at[2, place_in], place.across
        )
        return local, away

    def emit(layer, ref, first):
        @pl.when(s == layer)
        def _():
            for copy in result_copies(ref, first):
                copy.start()

    for copy in own_loads:
        copy.wait()
    for step in range(3):
        z_start(step)
    edge_start(0)
    n1[width:, :] = jnp.ones((ONES, frames), BF)
    n2[width:, :] = jnp.ones((ONES, frames), BF)
    own_clip = pltpu.make_async_copy(clips.at[t], stage.at[mine, :], in_sem.at[4])
    own_clip.start()
    clip_across().start()
    cot_across().start()
    own_out.wait()
    shard[:, OUT:UP] = flat[0:WIDE, :].T
    own_up.wait()
    for step in (3, 4):
        z_start(step)
    edge_start(1)
    edge_start(2)

    def take_clip(first):
        def body(index, carry):
            at = pl.ds(pl.multiple_of(first + index * BLOCK, BLOCK), BLOCK)
            tile = stage[at, :].T
            n2[0:width, at] = tile
            res[:, at] = tile.astype(F32)
            return carry

        lax.fori_loop(0, half // BLOCK, body, 0)

    own_clip.wait()
    take_clip(t * half)
    own_down.wait()
    for piece in range(4):
        span = slice((1 + piece) * WIDE, (2 + piece) * WIDE)
        shard[:, DOWN + piece * WIDE : DOWN + (piece + 1) * WIDE] = flat[span, :].T
    edge_start(3)
    edge_beside(0, 0)
    clip_across().wait()
    clip_core().start()
    step_z(0)
    z_start(5)
    step_z(1)
    z_start(6)
    clip_core().wait()
    take_clip((1 - t) * half)
    save("x", 0).start()
    step_plane(0)
    edge_along(0, 0)
    step_z(2)
    z_start(7)
    edge_beside(0, 1)
    step_plane(1)
    cot_across().wait()
    cot_core().start()
    step_z(3)
    z_start(8)
    step_plane(2)
    step_z(4)
    z_start(9)
    step_z(5)
    z_start(10)
    edge_beside(0, 2)

    def project(pair):
        for index in (2 * pair, 2 * pair + 1):
            cols = block_of(index)
            mean, scale = norm_stats(lambda span: res[span, cols], width)
            for span in chunks_of(width):
                hat = (res[span, cols] - mean) * scale
                n1[span, cols] = (hat * vecs[span, 0:1] + vecs[span, 2:3]).astype(BF)
        cols = pair_of(pair)
        for first, many, kind, bias in PARTS:
            value = mm(wt[first : first + many, :], n1[0:width, cols])
            for span in chunks_of(many):
                part = value[span, :]
                if kind != "k":
                    part = part + spread[bias + span.start : bias + span.stop, 6:7]
                if kind == "q":
                    part = part * 0.125
                qkv[first + span.start : first + span.stop, cols] = part.astype(BF)

    def send_pair(kind, pair, slot, value):
        for part in range(2):
            index = 2 * pair + part
            send[kind, index] = value[:, part * BLOCK : (part + 1) * BLOCK].astype(BF)
            exchange(kind, index, slot).start()

    def head_rows(head, first):
        return pl.ds(pl.multiple_of(first + head * HEAD, HEAD), HEAD)

    def attend(layer, turns, later_turns):
        def heads_of(first_head, base, stride, beside):
            def one_head(index_in, carry):
                head = first_head + index_in
                q_rows = head_rows(index_in, base)
                k_rows = head_rows(index_in, base + stride)
                v_rows = head_rows(index_in, base + 2 * stride)
                c_rows = head_rows(head, 0)
                keys = qkv[k_rows, :].T
                for index in range(blocks):
                    cols = slice(index * BLOCK, (index + 1) * BLOCK)
                    queries = qkv[q_rows, cols]
                    tiles = []
                    top = None
                    for tile in chunks_of(frames, BLOCK):
                        scores = mm(keys[tile, :], queries)
                        for span in chunks_of(BLOCK):
                            peak = stack_max(scores[span, :])
                            top = peak if top is None else jnp.maximum(top, peak)
                        tiles.append(scores)
                    top = jnp.max(top, 0, keepdims=True)
                    total = jnp.zeros((8, BLOCK), F32)
                    mixed = jnp.zeros((HEAD, BLOCK), F32)
                    for tile, scores in zip(chunks_of(frames, BLOCK), tiles):
                        soft = []
                        for span in chunks_of(BLOCK):
                            part = jnp.exp(scores[span, :] - top)
                            total = total + stack_sum(part)
                            soft.append(part.astype(BF))
                        mixed = mixed + mm(qkv[v_rows, tile], jnp.concatenate(soft, 0))
                    total = jnp.sum(total, 0, keepdims=True)
                    ctx[c_rows, cols] = (mixed / total).astype(BF)
                    lse[pl.ds(head, 1), cols] = top + jnp.log(total)
                beside(index_in)
                return carry

            return one_head

        lax.fori_loop(0, 4, heads_of(0, 0, 256, ticks(turns)), 0)
        lax.fori_loop(0, 2, heads_of(4, 768, 128, ticks(later_turns)), 0)

    def out_project(layer, turns):
        beside = ticks(turns)

        def body(index, carry):
            part = mm(whole(w, layer, OUT, 384), ctx[:, pair_of(index)])
            send_pair(0, index, 2 * layer, part)
            beside(index)
            return carry

        lax.fori_loop(0, blocks // 2, body, 0)

    def middle_norm(layer, turns):
        beside = ticks(turns)

        def body(index, carry):
            cols = block_of(index)
            exchange(0, index, 2 * layer).wait()
            for span in chunks_of(width):
                added = send[0, index, span, :].astype(F32) + recv[0, index, span, :].astype(F32)
                res[span, cols] = res[span, cols] + added + vecs[span, 3:4]
            mean, scale = norm_stats(lambda span: res[span, cols], width)
            for span in chunks_of(width):
                hat = (res[span, cols] - mean) * scale
                n2[span, cols] = (hat * vecs[span, 1:2] + vecs[span, 4:5]).astype(BF)
            beside(index)
            return carry

        lax.fori_loop(0, blocks, body, 0)

    def hidden_part(layer, part):
        flip_weights(w, wt, layer, UP + part * WIDE, WIDE, part * WIDE)
        units = slice(part * WIDE, (part + 1) * WIDE)
        lane = 7 if part < 2 else 8

        def body(index, carry):
            cols = pair_of(index)
            pre = mm(wt[units, :], n2[0:width, cols])
            for span in chunks_of(WIDE):
                first = part * WIDE + span.start
                bias = spread[768 + first : 768 + first + ROWS, lane : lane + 1]
                value, steep = gelu_parts(pre[span, :] + bias)
                act[first : first + ROWS, cols] = value.astype(BF)
                slope[first : first + ROWS, cols] = steep.astype(BF)
            return carry

        lax.fori_loop(0, blocks // 2, body, 0)

    def down_project(layer, turns):
        beside = ticks(turns)

        def body(index, carry):
            part = mm(whole(w, layer, DOWN, 1536), act[:, pair_of(index)])
            send_pair(1, index, 2 * layer + 1, part)
            beside(index)
            return carry

        lax.fori_loop(0, blocks // 2, body, 0)

    def layer_end(layer, index, span):
        added = send[1, index, span, :].astype(F32) + recv[1, index, span, :].astype(F32)
        return (res[span, block_of(index)] + added + vecs[span, 5:6]).astype(BF)

    def take_vectors(layer):
        vecs[...] = whole(w, layer, VEC, 128).astype(F32)
        spread_biases(vecs, spread, rows)

    def project_all(layer, turns):
        beside = ticks(turns)
        flip_weights(w, wt, layer, QKV, 1152)

        def body(index, carry):
            project(index)
            beside(index)
            return carry

        lax.fori_loop(0, blocks // 2, body, 0)
        if layer == 0:
            save("n1", 0).start()
            save("qkv", 0).start()

    complete(0, 1, 2)
    edge_complete(0, 0)
    take_vectors(0)
    project_all(0, {0: 3, 1: 4})
    cot_core().wait()
    load_cot = pltpu.make_async_copy(cot_other, stage.at[theirs, :], cot_sem.at[4])
    load_cot.start()
    own_cot = pltpu.make_async_copy(cot.at[t], stage.at[mine, :], cot_sem.at[5])
    own_cot.start()
    attend(0, {0: 5, 2: 6}, {0: 7})
    save("ctx", 0).start()
    save("lse", 0).start()
    complete(3)
    edge_complete(0, 1)
    out_project(0, {1: 8})
    load_cot.wait()
    own_cot.wait()

    sums[3] = jnp.zeros_like(sums[3])

    def take_cot(index, carry):
        low[:, block_of(index)] = stage[block_of(index), :].T
        for span in chunks_of(width):
            sums[3, span, :] += fold(low[span, block_of(index)].astype(F32))
        return carry

    lax.fori_loop(0, blocks, take_cot, 0)
    save("x", 0).wait()
    middle_norm(0, {1: 9})
    save("h", 0).start()
    save("n2", 0).start()
    edge_complete(0, 2)
    for part in range(4):
        complete(4 + part)
        hidden_part(0, part)
        tick(10 + part)
    save("act", 0).start()
    save("slope", 0).start()
    complete(8, 9, 10, 11)
    edge_complete(0, 3)
    down_project(0, {1: 14})
    for name in ("n1", "qkv", "h", "n2"):
        save(name, 0).wait()

    def finish_body(index, carry):
        exchange(1, index, 1).wait()
        cols = block_of(index)
        for span in chunks_of(width):
            rows_out = layer_end(0, index, span)
            n2[span, cols] = rows_out
            res[span, cols] = rows_out.astype(F32)

        @pl.when(s == 0)
        def _():
            stage[cols, :] = n2[0:width, cols].T

        return carry

    lax.fori_loop(0, blocks, finish_body, 0)
    emit(0, out, 0)
    save("x", 1).start()
    complete(12, 13, 14)
    edge_complete(1, 0)
    take_vectors(1)
    project_all(1, {0: 15, 1: 16})
    save("ctx", 0).wait()
    save("lse", 0).wait()
    attend(1, {0: 17, 2: 18}, {0: 19})
    complete(15)
    edge_complete(1, 1)
    out_project(1, {1: 20})
    save("x", 1).wait()
    middle_norm(1, {1: 21})
    save("h", 1).start()
    save("act", 0).wait()
    save("slope", 0).wait()
    edge_complete(1, 2)
    for part in range(4):
        complete(16 + part)
        hidden_part(1, part)
        if part < 2:
            tick(22 + part)
    edge_complete(1, 3)
    for part in range(4):
        complete(20 + part)
        flip_weights(w, wt, 1, DOWN + part * WIDE, WIDE, part * WIDE)
    down_project(1, {})

    def gya_copy(layer, piece):
        cols = piece_cols(piece)
        return remote(
            w.at[layer, :, 1 - y, low_rows, cols],
            land_a.at[:, low_rows, cols],
            gya_send.at[layer, piece],
            gya_recv.at[layer, piece],
            place.beside,
        )

    def gxb_copy(layer, piece):
        cols = piece_cols(piece)
        return remote(
            w.at[layer, :, 1 - y, high_rows, cols],
            land_b.at[:, :, cols],
            gxb_send.at[layer, piece],
            gxb_recv.at[layer, piece],
            place.across,
        )

    def gx_copy(layer, piece):
        cols = piece_cols(piece)
        return remote(
            w.at[layer, :, y, main_rows, cols],
            land_a.at[:, :, cols],
            gx_send.at[layer, piece],
            gx_recv.at[layer, piece],
            place.across,
        )

    def gy_copy(layer, piece):
        cols = piece_cols(piece)
        return remote(
            w.at[layer, :, 1 - y, main_rows, cols],
            land_y.at[:, :, cols],
            gy_send.at[layer, piece],
            gy_recv.at[layer, piece],
            place.beside,
        )

    def landed_part(piece):
        if piece == VECTORS:
            return landed_vec
        ref, first = (
            (landed_qkv, 0)
            if piece < 3
            else (landed_out, 3)
            if piece < 4
            else (landed_up, 4)
            if piece < 8
            else (landed_down, 8)
        )
        return ref.at[:, :, pl.ds((piece - first) * WIDE, WIDE)]

    def gz_copies(layer, piece):
        cols = piece_cols(piece)
        target = landed_part(piece)
        copies = []
        for step in range(LINES):
            line = place.line(step)
            copies.append(
                remote(
                    w.at[layer, line, y, main_rows, cols],
                    target.at[e],
                    gz_send.at[layer, piece, step],
                    gz_recv.at[piece, e],
                    (layer, place.row_of(line, y), t),
                )
            )
        local = pltpu.make_async_copy(
            w.at[layer, e, y, main_rows, cols], target.at[e], gz_recv.at[piece, e]
        )
        return copies, local

    def add_rows(layer, piece, which, span, lands):
        cols = piece_cols(piece)
        first, count = span
        for line in range(LINES):
            total = w[layer, line, which, pl.ds(first, count), cols].astype(F32)
            for land, offset in lands:
                total = total + land[line, pl.ds(offset, count), cols].astype(F32)
            w[layer, line, which, pl.ds(first, count), cols] = total.astype(BF)

    def signal(sem, layer, piece, device):
        if layer == 1:
            pl.semaphore_signal(sem.at[piece], inc=1, device_id=device, device_id_type=MESH)

    def credit(sem, layer, piece):
        if layer == 0:
            pl.semaphore_wait(sem.at[piece], 1)

    def step_a(layer, piece):
        @pl.when(secondary)
        def _():
            credit(ya_free, layer, piece)
            gya_copy(layer, piece).start()
            credit(xb_free, layer, piece)
            gxb_copy(layer, piece).start()

    def step_b(layer, piece):
        cols = piece_cols(piece)

        @pl.when(secondary)
        def _():
            await_bytes(land_a.at[:, low_rows, cols], gya_recv.at[layer, piece])
            add_rows(layer, piece, y, (0, SPLIT), [(land_a, 0)])
            signal(ya_free, layer, piece, place.beside)
            credit(x_free, layer, piece)
            gx_copy(layer, piece).start()

        @pl.when(primary)
        def _():
            await_bytes(land_b.at[:, :, cols], gxb_recv.at[layer, piece])
            add_rows(layer, piece, 1 - y, (SPLIT, EDGE - SPLIT), [(land_b, 0)])
            signal(xb_free, layer, piece, place.across)
            credit(y_free, layer, piece)
            gy_copy(layer, piece).start()

    def step_c(layer, piece):
        cols = piece_cols(piece)

        @pl.when(primary)
        def _():
            await_bytes(land_a.at[:, :, cols], gx_recv.at[layer, piece])
            await_bytes(land_y.at[:, :, cols], gy_recv.at[layer, piece])
            add_rows(layer, piece, y, (0, EDGE), [(land_a, 0), (land_y, 0)])
            signal(x_free, layer, piece, place.across)
            signal(y_free, layer, piece, place.beside)
            copies, local = gz_copies(layer, piece)

            @pl.when(s == layer)
            def _():
                local.start()

            @pl.when(s != layer)
            def _():
                copies[0].start()

            for copy in copies[1:]:
                copy.start()

    edge_targets = {0: edge_down, 1: edge_up, 2: edge_out, 5: edge_vec}

    def edge_target(group):
        if group in edge_targets:
            return edge_targets[group]
        start, stop = SCATTER_EDGES[group]
        return edge_qkv.at[:, :, pl.ds(start - QKV, stop - start)]

    def sum_third(layer, group):
        cols = edge_cols(group, SCATTER_EDGES)
        return [
            remote(
                w.at[layer, place.line(step), :, edge_rows, cols],
                land_e.at[e, :, :, cols],
                g3_send.at[layer, group, step - 1],
                g3_recv.at[layer, group, e],
                (s, place.row_of(place.line(step), y), t),
            )
            for step in range(1, LINES)
        ]

    def sum_second(layer, group):
        cols = edge_cols(group, SCATTER_EDGES)
        return remote(
            w.at[layer, e, 1 - y, edge_rows, cols],
            land_f.at[:, cols],
            g2_send.at[layer, group],
            g2_recv.at[layer, group],
            place.beside,
        )

    def sum_first(layer, group):
        cols = edge_cols(group, SCATTER_EDGES)
        src = w.at[layer, e, y, edge_rows, cols]
        dst = edge_target(group)
        near = remote(
            src, dst.at[0], g1_send.at[layer, group], g1_recv.at[group, 0], (layer, place.d, t)
        )
        far = remote(
            src, dst.at[1], g1_send.at[layer, group], g1_recv.at[group, 1], (layer, place.d, 1 - t)
        )
        return near, far, pltpu.make_async_copy(src, dst.at[0], g1_recv.at[group, 0])

    def edge_a(layer, group):
        if layer == 0:
            pl.semaphore_wait(g3_free.at[group], LINES - 1)
        for copy in sum_third(layer, group):
            copy.start()

    def edge_b(layer, group):
        start, stop = SCATTER_EDGES[group]
        cols = edge_cols(group, SCATTER_EDGES)
        for step in range(1, LINES):
            line = place.line(step)
            await_bytes(land_e.at[line, :, :, cols], g3_recv.at[layer, group, line])
        piece = 384 if (stop - start) % 384 == 0 else 128

        def body(index, carry):
            part = pl.ds(pl.multiple_of(start + index * piece, 128), piece)
            for which in range(2):
                total = w[layer, e, which, edge_rows, part].astype(F32)
                for step in range(1, LINES):
                    total = total + land_e[place.line(step), which, :, part].astype(F32)
                w[layer, e, which, edge_rows, part] = total.astype(BF)
            return carry

        lax.fori_loop(0, (stop - start) // piece, body, 0)
        if layer == 1:
            for step in range(1, LINES):
                pl.semaphore_signal(
                    g3_free.at[group],
                    inc=1,
                    device_id=(s, place.row_of(place.line(step), y), t),
                    device_id_type=MESH,
                )
        else:
            pl.semaphore_wait(g2_free.at[group], 1)
        sum_second(layer, group).start()

    def edge_c(layer, group):
        start, stop = SCATTER_EDGES[group]
        cols = edge_cols(group, SCATTER_EDGES)
        await_bytes(land_f.at[:, cols], g2_recv.at[layer, group])
        total = w[layer, e, y, edge_rows, cols].astype(F32) + land_f[:, cols].astype(F32)
        w[layer, e, y, edge_rows, cols] = total.astype(BF)
        if layer == 1:
            pl.semaphore_signal(
                g2_free.at[group], inc=1, device_id=place.beside, device_id_type=MESH
            )
        near, far, local = sum_first(layer, group)

        @pl.when(secondary)
        def _():
            far.start()

        @pl.when(jnp.logical_and(primary, s == layer))
        def _():
            local.start()

        @pl.when(jnp.logical_and(primary, s != layer))
        def _():
            near.start()

    def sums_finish(layer, group):
        for copy in sum_third(layer, group):
            copy.wait_send()
        sum_second(layer, group).wait_send()
        near, far, _ = sum_first(layer, group)

        @pl.when(secondary)
        def _():
            far.wait_send()

        @pl.when(jnp.logical_and(primary, s != layer))
        def _():
            near.wait_send()

    def store_grads(layer, start, count, value):
        w[layer, :, :, :, pl.ds(start, count)] = value.astype(BF).reshape(
            w.shape[1], w.shape[2], rows, count
        )

    def mlp_back(layer, beside):
        def body(index, carry):
            cols = pair_of(index)
            for part in range(4):
                units = slice(part * WIDE, (part + 1) * WIDE)
                grad = mm(wt[units, :], low[:, cols])
                for span in chunks_of(WIDE):
                    rows_in = slice(units.start + span.start, units.start + span.stop)
                    steep = slope[rows_in, cols].astype(F32)
                    slope[rows_in, cols] = (grad[span, :] * steep).astype(BF)
            term = mm(whole(w, layer, UP, 1536), slope[:, cols])
            send_pair(0, index, 4 + 2 * layer, term)
            beside(index)
            return carry

        lax.fori_loop(0, blocks // 2, body, 0)

    def outer(layer, start, left, right, first, many, before, beside):
        def body(index, carry):
            before(index)
            base = index * PAIR
            span = pl.ds(pl.multiple_of(first + base, 128), PAIR)
            value = mmt(left[...], right[span, :])
            store_grads(layer, pl.multiple_of(start + base, 128), PAIR, value[0:width, :])
            if left.shape[0] > width:
                to = pl.ds(pl.multiple_of(768 + base, BLOCK), PAIR)
                spread[to, 0:8] = value[width : width + 8, :].T
            beside(index)
            return carry

        lax.fori_loop(0, many // PAIR, body, 0)

    def turned(turn):
        return lax.rem(turn + (1 - t) * (blocks // 2), blocks)

    def norm_back(layer, kind, gain_lane, source, put, finish, beside):
        sums[0:3] = jnp.zeros((3, width, 128), F32)

        def body(turn, carry):
            index = turned(turn)
            cols = block_of(index)
            read = source(index)
            mean, scale = norm_stats(read, width)
            exchange(kind, index, 4 + 2 * layer + kind).wait()
            first = jnp.zeros((8, BLOCK), F32)
            second = jnp.zeros((8, BLOCK), F32)

            def terms(span):
                hat = (read(span) - mean) * scale
                grad = send[kind, index, span, :].astype(F32)
                grad = grad + recv[kind, index, span, :].astype(F32)
                return hat, grad, grad * vecs[span, gain_lane : gain_lane + 1]

            for span in chunks_of(width):
                hat, grad, scaled = terms(span)
                sums[0, span, :] += fold(grad * hat)
                sums[1, span, :] += fold(grad)
                first = first + stack_sum(scaled)
                second = second + stack_sum(scaled * hat)
            level = mean_of(first, width)
            slant = mean_of(second, width)
            for span in chunks_of(width):
                hat, _, scaled = terms(span)
                put(span, cols, res[span, cols] + scale * (scaled - level - hat * slant))
            finish(index)
            beside(turn)
            return carry

        lax.fori_loop(0, blocks, body, 0)

    def row_sums(value):
        return jnp.sum(value, 1, keepdims=True)

    def attend_back(first_head, many, base, stride, beside):
        def one_head(index_in, carry):
            head = first_head + index_in
            q_rows = head_rows(index_in, base)
            k_rows = head_rows(index_in, base + stride)
            v_rows = head_rows(index_in, base + 2 * stride)
            c_rows = head_rows(head, 0)
            keys = qkv[k_rows, :].T
            values = qkv[v_rows, :].T
            flat_queries = qkv[q_rows, :].T
            flat_grads = dctx[c_rows, :].T
            level = lse[pl.ds(head, 1), :]
            inner = jnp.sum(
                dctx[c_rows, :].astype(F32) * ctx[c_rows, :].astype(F32), 0, keepdims=True
            )
            step = jnp.zeros((HEAD, frames), F32)
            for tile in chunks_of(frames, BLOCK):
                soft = []
                score_grad = []
                for cols in chunks_of(frames, BLOCK):
                    scores = mm(keys[tile, :], qkv[q_rows, cols])
                    soft_grad = mm(values[tile, :], dctx[c_rows, cols])
                    soft_parts = []
                    grad_parts = []
                    for part in chunks_of(BLOCK):
                        strength = jnp.exp(scores[part, :] - level[:, cols])
                        soft_parts.append(strength.astype(BF))
                        strength = strength * (soft_grad[part, :] - inner[:, cols])
                        grad_parts.append(strength.astype(BF))
                    soft.append(jnp.concatenate(soft_parts, 0))
                    score_grad.append(jnp.concatenate(grad_parts, 0))
                soft = jnp.concatenate(soft, 1)
                score_grad = jnp.concatenate(score_grad, 1)
                step = step + mm(qkv[k_rows, tile], score_grad)
                slope[k_rows, tile] = mm(score_grad, flat_queries).astype(BF).T
                slope[v_rows, tile] = mm(soft, flat_grads).astype(BF).T
            slope[q_rows, :] = (step * 0.125).astype(BF)
            beside(index_in)
            return carry

        lax.fori_loop(0, many, one_head, 0)

    def keep_sums(first, value):
        for start, many, kind, bias in PARTS:
            offset = start - first
            if kind != "k" and 0 <= offset < value.shape[1]:
                spread[bias : bias + many, 0:8] = value[
                    width : width + 8, offset : offset + many
                ].T

    def collect_biases():
        def body(group, carry):
            source = group * rows
            for kind in range(2):
                for head in range(6):
                    at = pl.ds(pl.multiple_of(kind * 384 + head * HEAD + group * 8, 8), 8)
                    to = pl.ds(pl.multiple_of(source + kind * 48 + head * 8, 8), 8)
                    vec_grads[to, 6:7] = spread[at, 6:7]
            for unit in range(24):
                at = pl.ds(pl.multiple_of(768 + unit * HEAD + group * 8, 8), 8)
                to = pl.ds(pl.multiple_of(source + (unit % 12) * 8, 8), 8)
                lane = 7 if unit < 12 else 8
                vec_grads[to, lane : lane + 1] = spread[at, 6:7]
            return carry

        lax.fori_loop(0, GROUPS, body, 0)

    def nothing(index):
        del index

    def finish_gather(layer, piece):
        @pl.when(primary)
        def _():
            x_copy(layer, piece).wait_send()
            y_copy(layer, piece).wait_send()
            xb_copy(layer, piece).wait_send()

        @pl.when(secondary)
        def _():
            ya_copy(layer, piece).wait_send()

    def last_body(index, carry):
        exchange(1, index, 3).wait()

        @pl.when(s == 1)
        def _():
            for span in chunks_of(width, 128):
                stage[block_of(index), span] = layer_end(1, index, span).T

        return carry

    for layer in (1, 0):
        later = layer == 0
        if later:
            load_h(layer, turned(0)).start()
            load("act").wait()
            vecs[...] = whole(w, layer, VEC, 128).astype(F32)
            flip_weights(w, wt, layer, DOWN, 1536)
        vec_grads[...] = jnp.zeros_like(vec_grads)

        def a(piece, layer=layer):
            return lambda: step_a(layer, piece)

        def b(piece, layer=layer):
            return lambda: step_b(layer, piece)

        def c(piece, layer=layer):
            return lambda: step_c(layer, piece)

        def ea(group, layer=layer):
            return lambda: edge_a(layer, group)

        def eb(group, layer=layer):
            return lambda: edge_b(layer, group)

        def ec(group, layer=layer):
            return lambda: edge_c(layer, group)

        if later:
            before = nothing
            early = at_turns(
                {
                    0: (a(8), lambda: step_b(1, VECTORS), lambda: edge_b(1, 5)),
                    1: (a(9), lambda: step_c(1, VECTORS), lambda: edge_c(1, 5)),
                    2: (a(10), a(11), ea(0)),
                }
            )
        else:
            waits = [functools.partial(finish_gather, 1, piece) for piece in (8, 9, 10, 11)]
            waits.append(functools.partial(edge_finish, 1, 3))
            before = at_turns({0: waits[:2] + waits[4:], 1: waits[2:3], 2: waits[3:4]})
            early = at_turns({0: (a(8),), 1: (a(9),), 2: (a(10), a(11), ea(0))})
        outer(layer, DOWN, low, act, 0, 1536, before, early)
        load("x", layer).start()
        vec_grads[:, 5:6] = row_sums(sums[3])
        if not later:
            lax.fori_loop(0, blocks, last_body, 0)
            emit(1, out, 0)
            save("h", 1).wait()
            load_h(layer, turned(0)).start()
            res[...] = low[...].astype(F32)
            for piece in range(CHUNKS + 1):
                z_finish(piece)
                finish_gather(0, piece)
                if piece < 8 or piece == VECTORS:
                    finish_gather(1, piece)
            for group in range(len(GATHER_EDGES)):
                near, far, _ = edge_first(group)
                far.wait_send()

                @pl.when(secondary)
                def _():
                    near.wait_send()

                edge_finish(0, group)
                if group < 3:
                    edge_finish(1, group)
        else:
            load("slope").wait()

        mlp_back(layer, at_turns({0: (b(8),), 1: (b(9), b(10), b(11), eb(0))}))
        if later:
            load("n2").wait()
        drain = at_turns({0: (a(4),), 1: (a(5),), 2: (a(6), a(7), ea(1), c(8), ec(0))})
        outer(layer, UP, n2, slope, 0, 1536, nothing, drain)
        flip_weights(w, wt, layer, OUT, 384)

        def hidden_in(index, layer=layer):
            turn = lax.rem(index + (1 - t) * (blocks // 2), blocks)

            @pl.when(turn + 1 < blocks)
            def _():
                load_h(layer, turned(turn + 1)).start()

            load_h(layer, index).wait()
            slot = lax.rem(index, 2)
            return lambda span: h_in[slot, span, :]

        def hidden_put(span, cols, total):
            res[span, cols] = total
            rounded = total.astype(BF)
            low[span, cols] = rounded
            sums[2, span, :] += fold(rounded.astype(F32))

        drain = at_turns(
            {0: (b(4), c(9)), 1: (b(5), c(10)), 2: (b(6), c(11)), 3: (b(7), eb(1))}
        )
        norm_back(layer, 0, 1, hidden_in, hidden_put, nothing, drain)

        def context_back(index, carry):
            cols = pair_of(index)
            dctx[:, cols] = mm(wt[0:384, :], low[:, cols]).astype(BF)
            return carry

        lax.fori_loop(0, blocks // 2, context_back, 0)
        vec_grads[:, 1:2] = row_sums(sums[0])
        vec_grads[:, 4:5] = row_sums(sums[1])
        vec_grads[:, 3:4] = row_sums(sums[2])
        if later:
            for name in ("ctx", "qkv", "lse"):
                load(name).wait()
        store_grads(layer, OUT, 384, mmt(low[...], ctx[...]))
        step_a(layer, 3)
        edge_a(layer, 2)
        drain = at_turns(
            {0: (c(4), ec(1)), 1: (c(5), eb(2)), 2: (b(3), c(6)), 3: (c(7), ec(2))}
        )
        attend_back(0, 4, 0, 256, drain)
        if later:
            load("n1").wait()
        wt[0:768, :] = whole(w, layer, QKV, 768)

        for first, many in ((0, 512), (512, 256)):
            value = mmt(n1[...], slope[first : first + many, :])
            store_grads(layer, QKV + first, many, value[0:width, :])
            keep_sums(first, value)
        step_a(layer, 0)
        step_a(layer, 1)
        edge_a(layer, 3)
        attend_back(4, 2, 768, 128, at_turns({0: (b(0), c(3), eb(3)), 1: (b(1), ec(3))}))

        def first_body(index, carry, layer=layer):
            cols = pair_of(index)
            term = mm(wt[0:768, :], slope[0:768, cols])
            term = term + mm(whole(w, layer, QKV + 768, WIDE), slope[768:1152, cols])
            send_pair(1, index, 5 + 2 * layer, term)
            return carry

        lax.fori_loop(0, blocks // 2, first_body, 0)
        value = mmt(n1[...], slope[768:1152, :])
        store_grads(layer, QKV + 768, WIDE, value[0:width, :])
        keep_sums(768, value)
        step_a(layer, 2)
        edge_a(layer, 4)
        step_c(layer, 0)
        collect_biases()
        if layer == 1:
            for name in ("slope", "n1", "n2", "ctx", "qkv", "lse"):
                load(name).start()
        load("x", layer).wait()

        @pl.when(s == layer)
        def _():
            local, away = result_copies(out, 0)
            local.wait()
            away.wait_send()

        def rows_x(index):
            return lambda span: act[span, block_of(index)].astype(F32)

        def rows_put(span, cols, total, layer=layer):
            rounded = total.astype(BF)
            low[span, cols] = rounded
            if layer == 1:
                res[span, cols] = rounded.astype(F32)
                sums[2, span, :] += fold(rounded.astype(F32))

        def rows_out(index, layer=layer):
            @pl.when(s == layer)
            def _():
                stage[block_of(index), :] = low[:, block_of(index)].T
                local, away = grad_copies(index)

                @pl.when(index // (blocks // 2) == t)
                def _():
                    local.start()

                @pl.when(index // (blocks // 2) != t)
                def _():
                    away.start()

        drain = at_turns({0: (c(1),), 1: (b(2), eb(4)), 3: (c(2), ec(4))})
        norm_back(layer, 1, 0, rows_x, rows_put, rows_out, drain)
        if layer == 1:
            load("act").start()
        vec_grads[:, 0:1] = row_sums(sums[0])
        vec_grads[:, 2:3] = row_sums(sums[1])
        sums[3] = sums[2]
        store_grads(layer, VEC, 128, vec_grads[...])
        step_a(layer, VECTORS)
        edge_a(layer, 5)

    step_b(0, VECTORS)
    edge_b(0, 5)
    step_c(0, VECTORS)
    edge_c(0, 5)

    def finish_scatter(piece):
        for layer in range(2):

            @pl.when(secondary)
            def _():
                gya_copy(layer, piece).wait_send()
                gxb_copy(layer, piece).wait_send()
                gx_copy(layer, piece).wait_send()

            @pl.when(primary)
            def _():
                gy_copy(layer, piece).wait_send()
                copies, _ = gz_copies(layer, piece)

                @pl.when(s != layer)
                def _():
                    copies[0].wait_send()

                for copy in copies[1:]:
                    copy.wait_send()

    for group in range(len(SCATTER_EDGES)):
        sums_finish(0, group)
        sums_finish(1, group)
        for slot in range(2):
            await_bytes(edge_target(group).at[slot], g1_recv.at[group, slot])
    for piece in range(CHUNKS + 1):
        finish_scatter(piece)
        for line in range(LINES):
            await_bytes(landed_part(piece).at[line], gz_recv.at[piece, line])

    _, away = result_copies(out, 0)
    away.wait_recv()
    for index in range(blocks // 2):
        local, away = grad_copies(index)
        local.wait()
        away.wait()


def layers_call(share, clips, cotangent, shards, dims):
    width, frames, hidden_units, heads_width = dims
    rows = width // GROUPS
    sem = pltpu.SemaphoreType.DMA
    free = pltpu.SemaphoreType.REGULAR
    packed = (2, LINES, 2, rows, END)
    blocks = frames // BLOCK
    shape = jax.ShapeDtypeStruct
    outs = [
        shape((1,) + clips.shape, BF),
        shape((1,) + clips.shape, BF),
        shape((LINES, EDGE, QKV - VEC), BF),
        shape((LINES, EDGE, OUT - QKV), BF),
        shape((LINES, EDGE, UP - OUT), BF),
        shape((LINES, EDGE, DOWN - UP), BF),
        shape((LINES, EDGE, END - DOWN), BF),
        shape((2, rows - EDGE, QKV - VEC), BF),
        shape((2, rows - EDGE, OUT - QKV), BF),
        shape((2, rows - EDGE, UP - OUT), BF),
        shape((2, rows - EDGE, DOWN - UP), BF),
        shape((2, rows - EDGE, END - DOWN), BF),
        shape(clips.shape[1:], BF),
        shape((2, width, frames), BF),
        shape((2, width, frames), F32),
        shape((width, frames), BF),
        shape((width, frames), BF),
        shape((3 * heads_width, frames), BF),
        shape((heads_width, frames), BF),
        shape((8, frames), F32),
        shape((hidden_units, frames), BF),
        shape((hidden_units, frames), BF),
    ]
    scratch = [
        pltpu.VMEM(packed, BF),
        pltpu.VMEM((width, frames), F32),
        pltpu.VMEM((hidden_units, frames), BF),
        pltpu.VMEM((hidden_units, frames), BF),
        pltpu.VMEM((width + ONES, frames), BF),
        pltpu.VMEM((width + ONES, frames), BF),
        pltpu.VMEM((width, frames), BF),
        pltpu.VMEM((3 * heads_width, frames), BF),
        pltpu.VMEM((heads_width, frames), BF),
        pltpu.VMEM((heads_width, frames), BF),
        pltpu.VMEM((8, frames), F32),
        pltpu.VMEM((2, width, BLOCK), F32),
        pltpu.VMEM((hidden_units, width), BF),
        pltpu.VMEM((2, blocks, width, BLOCK), BF),
        pltpu.VMEM((2, blocks, width, BLOCK), BF),
        pltpu.VMEM((width, 128), F32),
        pltpu.VMEM((width, 128), F32),
        pltpu.VMEM((4, width, 128), F32),
        pltpu.VMEM((2 * heads_width + hidden_units, 128), F32),
        pltpu.VMEM((frames, width), BF),
        pltpu.VMEM((rows, END), BF),
        pltpu.VMEM((WIDE + END - DOWN, rows), BF),
        pltpu.VMEM((LINES, EDGE, END), BF),
        pltpu.VMEM((LINES, EDGE - SPLIT, END), BF),
        pltpu.VMEM((LINES, EDGE, END), BF),
        pltpu.VMEM((LINES, 2, rows - EDGE, END), BF),
        pltpu.VMEM((rows - EDGE, END), BF),
    ]
    scratch += [sem((CHUNKS + 1, LINES)), sem((2, CHUNKS + 1, LINES))]
    scratch += [sem((2, CHUNKS + 1))] * 8
    scratch += [sem((2, CHUNKS + 1, LINES)), sem((CHUNKS + 1, LINES))]
    scratch += [sem((2, CHUNKS + 1))] * 8
    gathers, scatters = len(GATHER_EDGES), len(SCATTER_EDGES)
    scratch += [sem((gathers, 2))] + [sem((2, gathers))] * 3
    scratch += [sem((2, gathers, LINES - 1)), sem((2, gathers, LINES))]
    scratch += [sem((2, scatters, LINES - 1)), sem((2, scatters, LINES))]
    scratch += [sem((2, scatters))] * 3 + [sem((scatters, 2))]
    scratch += [
        sem((8, blocks)),
        sem((8, blocks)),
        sem((10,)),
        sem((5,)),
        sem((6,)),
        sem((3,)),
        sem((3, blocks // 2)),
        sem((9, 2)),
        sem((9,)),
        sem((2,)),
    ]
    scratch += [free((CHUNKS + 1,))] * 4 + [free((scatters,))] * 2
    anywhere = pl.BlockSpec(memory_space=pl.ANY)
    return pl.pallas_call(
        functools.partial(layers_kernel, share),
        out_shape=outs,
        in_specs=[anywhere] * (2 + len(shards)),
        out_specs=[anywhere] * len(outs),
        scratch_shapes=scratch,
        compiler_params=pltpu.CompilerParams(
            collective_id=0, has_side_effects=True, vmem_limit_bytes=VMEM_LIMIT
        ),
        cost_estimate=pl.CostEstimate(
            flops=60_000_000_000, bytes_accessed=60_000_000, transcendentals=0
        ),
    )(clips, cotangent, *shards)


def group_piece(value, axis, share):
    if share == 1:
        return value
    size = value.shape[axis] * share
    group = lax.axis_index("dp") // share
    full = lax.all_gather(value, "dp", axis=axis, tiled=True)
    return lax.dynamic_slice_in_dim(full, group * size, size, axis)


def own_part(value, axis, share, parts, index):
    size = value.shape[axis] // parts
    if parts == 1:
        return value
    return lax.dynamic_slice_in_dim(value, index * size, size, axis)


def on_device(share, clips, cotangent, ln_gains, row_biases, w_qkv, b_qv, w_o, w_up, b_ff, w_down):
    width = clips.shape[2]
    rows = width // GROUPS
    dims = (width, 2 * clips.shape[1], w_up.shape[2], w_o.shape[1])
    ln_gains = group_piece(ln_gains, 2, share)
    row_biases = group_piece(row_biases, 2, share)
    w_qkv = group_piece(w_qkv, 2, share)
    b_qv = group_piece(b_qv, 3, share)
    w_o = group_piece(w_o, 2, share)
    w_up = group_piece(w_up, 1, share)
    b_ff = group_piece(b_ff, 2, share)
    w_down = group_piece(w_down, 2, share)
    vectors = jnp.concatenate([ln_gains[0], row_biases[0]], 0).T
    heads = jnp.concatenate([b_qv[0, 0].reshape(-1), b_qv[0, 1].reshape(-1)])[:, None]
    units = b_ff[0].reshape(2, rows).T
    packed = jnp.concatenate([vectors, heads, units], 1)
    packed = jnp.pad(packed, ((0, 0), (0, 128 - packed.shape[1])))
    section_out, section_in_grad, *rest_out = layers_call(
        share, clips, cotangent, (packed, w_qkv, w_o, w_up, w_down), dims
    )
    landed, edges = rest_out[:5], rest_out[5:10]
    rest = lax.axis_index("dp") % share
    side = lax.axis_index("tensor")

    def joined(value, edge):
        total = jnp.concatenate([jnp.sum(value.astype(F32), 0), jnp.sum(edge.astype(F32), 0)], 0)
        if share == 1:
            return total
        group = lax.axis_index("dp") // share
        padded = jnp.zeros((width, total.shape[1]), F32)
        padded = lax.dynamic_update_slice_in_dim(padded, total, group * rows, 0)
        return lax.dynamic_slice_in_dim(lax.psum(padded, "dp"), group * rows, rows, 0)

    def mine(value, edge):
        return own_part(joined(value, edge), 0, share, share, rest)

    vectors = joined(landed[0], edges[0])
    vec = own_part(own_part(vectors, 0, share, share, rest), 0, share, 2, side)
    heads_grad = vectors[:, 6].reshape(2, -1, HEAD // GROUPS)
    units_grad = vectors[:, 7:9].T.reshape(-1, HEAD // GROUPS)
    qkv_grad = {"q": [], "k": [], "v": []}
    for first, many, kind, _ in PARTS:
        span = slice(first, first + many)
        qkv_grad[kind].append(mine(landed[1][:, :, span], edges[1][:, :, span]))
    return (
        section_out,
        section_in_grad,
        vec[:, 0:2].T[None],
        vec[:, 2:6].T[None],
        jnp.stack([jnp.concatenate(qkv_grad[kind], 1) for kind in "qkv"])[None],
        own_part(heads_grad, 2, share, share, rest)[None],
        mine(landed[2], edges[2]).T[None],
        mine(landed[3], edges[3])[None],
        own_part(units_grad, 1, share, share, rest)[None],
        mine(landed[4], edges[4]).T[None],
    )


def solution(mesh):
    placed = (
        P("dp", "tensor", None),
        P("dp", "tensor", None),
        P("section", None, "dp"),
        P("section", None, "dp"),
        P("section", None, "dp", "tensor"),
        P("section", None, "tensor", "dp"),
        P("section", "tensor", "dp"),
        P("section", "dp", "tensor"),
        P("section", "tensor", "dp"),
        P("section", "tensor", "dp"),
    )
    share = mesh.shape["dp"] // GROUPS
    return jax.shard_map(
        functools.partial(on_device, share),
        mesh=mesh,
        in_specs=placed,
        out_specs=(
            P("section", "dp", "tensor", None),
            P("section", "dp", "tensor", None),
            P("section", None, ("dp", "tensor")),
            P("section", None, ("dp", "tensor")),
            P("section", None, "dp", "tensor"),
            P("section", None, "tensor", "dp"),
            P("section", "tensor", "dp"),
            P("section", "dp", "tensor"),
            P("section", "tensor", "dp"),
            P("section", "tensor", "dp"),
        ),
        check_vma=False,
    )
```

```python
import functools

import jax
import jax.numpy as jnp
from jax import lax
from jax.experimental import pallas as pl
from jax.experimental.pallas import tpu as pltpu
from jax.sharding import PartitionSpec as P

BF = jnp.bfloat16
F32 = jnp.float32
MESH = pl.DeviceIdType.MESH
EPSILON = 1e-05
HEAD = 64
GROUPS = 8
LINES = 4
BLOCK = 256
PAIR = 2 * BLOCK
ROWS = 64
ONES = 16
VMEM_LIMIT = 62 * 1024 * 1024

VEC = 0
QKV = 128
OUT = 1280
UP = 1664
DOWN = 3200
END = 4736
SPLIT = 48
WIDE = 384
CHUNKS = 12


PARTS = (
    (0, 256, "q", 0),
    (256, 256, "k", 0),
    (512, 256, "v", 384),
    (768, 128, "q", 256),
    (896, 128, "k", 256),
    (1024, 128, "v", 640),
)


HEAD_LANE = 8
UNIT_LANE = 20


def head_lane(kind, head):
    return HEAD_LANE + 2 * head + kind


def mm(left, right):
    return jnp.dot(left, right, preferred_element_type=F32)


def mmt(left, right):
    return lax.dot_general(left, right, (((1,), (1,)), ((), ())), preferred_element_type=F32)


class Place:
    def __init__(self, share):
        self.s = lax.axis_index("section")
        self.d = lax.axis_index("dp")
        self.t = lax.axis_index("tensor")
        group = self.d // share
        self.rest = self.d - group * share
        self.share = share
        self.e = group // 2
        self.y = group - self.e * 2
        self.primary = self.s == self.t
        self.core = (1 - self.s, self.d, self.t)
        self.across = (self.s, self.d, 1 - self.t)
        self.beside = (self.s, self.row_of(self.e, 1 - self.y), self.t)

    def row_of(self, line, y):
        return (line * 2 + y) * self.share + self.rest

    def line(self, step):
        return lax.rem(self.e + step, LINES)

    def greet(self):
        barrier = pltpu.get_barrier_semaphore()
        peers = [self.core, self.across, self.beside]
        for step in range(1, LINES):
            for section in range(2):
                peers.append((section, self.row_of(self.line(step), self.y), self.t))
        for peer in peers:
            pl.semaphore_signal(barrier, inc=1, device_id=peer, device_id_type=MESH)
        pl.semaphore_wait(barrier, len(peers))


def remote(src, dst, send_sem, recv_sem, device):
    return pltpu.make_async_remote_copy(
        src_ref=src,
        dst_ref=dst,
        send_sem=send_sem,
        recv_sem=recv_sem,
        device_id=device,
        device_id_type=MESH,
    )


def await_bytes(ref, sem):
    pltpu.make_async_copy(ref, ref, sem).wait()


def chunks_of(count, size=ROWS):
    return [slice(first, first + size) for first in range(0, count, size)]


def by_eights(value):
    return value.reshape(value.shape[0] // 8, 8, value.shape[1])


def stack_sum(value):
    return jnp.sum(by_eights(value), 0)


def stack_max(value):
    return jnp.max(by_eights(value), 0)


def mean_of(parts, count):
    return jnp.sum(parts, 0, keepdims=True) / count


def norm_stats(read, count):
    total = jnp.zeros((8, BLOCK), F32)
    for span in chunks_of(count):
        total = total + stack_sum(read(span))
    mean = mean_of(total, count)
    square = jnp.zeros((8, BLOCK), F32)
    for span in chunks_of(count):
        centred = read(span) - mean
        square = square + stack_sum(centred * centred)
    return mean, lax.rsqrt(mean_of(square, count) + EPSILON)


def gelu_parts(values):
    bell = jnp.exp(-0.5 * values * values)
    reach = jnp.abs(values) * 0.7071067811865476
    inv = 1.0 / (1.0 + 0.3275911 * reach)
    poly = inv * (
        0.254829592
        + inv * (-0.284496736 + inv * (1.421413741 + inv * (-1.453152027 + inv * 1.061405429)))
    )
    tail = 0.5 * poly * bell
    cdf = jnp.where(values >= 0.0, 1.0 - tail, tail)
    return values * cdf, cdf + values * bell * 0.3989422804014327


def fold(value):
    return value[:, 0:128] + value[:, 128:256]


def block_of(index):
    return pl.ds(pl.multiple_of(index * BLOCK, BLOCK), BLOCK)


def pair_of(index):
    return pl.ds(pl.multiple_of(index * PAIR, PAIR), PAIR)


def flip_weights(w, wt, layer, start, width, target=0):
    def body(index, carry):
        cols = pl.ds(pl.multiple_of(start + index * 128, 128), 128)
        rows = pl.ds(pl.multiple_of(target + index * 128, 128), 128)
        tile = w[layer, :, :, :, cols]
        wt[rows, :] = tile.reshape(tile.shape[0] * tile.shape[1] * tile.shape[2], 128).T
        return carry

    lax.fori_loop(0, width // 128, body, 0)


def whole(w, layer, start, width):
    tile = w[layer, :, :, :, start : start + width]
    return tile.reshape(tile.shape[0] * tile.shape[1] * tile.shape[2], width)


def spread_biases(vecs, spread, rows):
    def body(group, carry):
        at = pl.ds(pl.multiple_of(group * rows, 8), 8)
        for kind in range(2):
            for head in range(6):
                to = pl.ds(pl.multiple_of(kind * 384 + head * HEAD + group * 8, 8), 8)
                lane = head_lane(kind, head)
                spread[to, 6:7] = vecs[at, lane : lane + 1]
        for unit in range(24):
            to = pl.ds(pl.multiple_of(768 + unit * HEAD + group * 8, 8), 8)
            lane = UNIT_LANE + unit
            spread[to, 6:7] = vecs[at, lane : lane + 1]
        return carry

    lax.fori_loop(0, GROUPS, body, 0)


def layers_kernel(
    share,
    clips,
    cot,
    gains_in,
    biases_in,
    heads_in,
    units_in,
    qkv_in,
    out_in,
    up_in,
    down_in,
    out,
    in_grad,
    landed_vec,
    landed_qkv,
    landed_out,
    landed_up,
    landed_down,
    cot_other,
    x_hbm,
    h_hbm,
    n1_hbm,
    n2_hbm,
    qkv_hbm,
    ctx_hbm,
    lse_hbm,
    act_hbm,
    slope_hbm,
    w,
    res,
    act,
    slope,
    n1,
    n2,
    low,
    qkv,
    ctx,
    dctx,
    lse,
    h_in,
    wt,
    send,
    recv,
    vecs,
    vec_grads,
    sums,
    spread,
    stage,
    shard,
    land_a,
    land_b,
    land_y,
    z_send,
    z_recv,
    x_send,
    x_recv,
    xb_send,
    xb_recv,
    y_send,
    y_recv,
    ya_send,
    ya_recv,
    gz_send,
    gz_recv,
    gx_send,
    gx_recv,
    gxb_send,
    gxb_recv,
    gy_send,
    gy_recv,
    gya_send,
    gya_recv,
    e_send,
    e_recv,
    own_sem,
    in_sem,
    cot_sem,
    out_sem,
    grad_sem,
    save_sem,
    load_sem,
    h_sem,
    ya_free,
    xb_free,
    x_free,
    y_free,
):
    place = Place(share)
    s, t, e, y = place.s, place.t, place.e, place.y
    primary, secondary = place.primary, jnp.logical_not(place.primary)
    width, frames = res.shape
    blocks = frames // BLOCK
    half = frames // 2
    quarter = half // 2
    rows = w.shape[3]
    low_rows = pl.ds(0, SPLIT)
    high_rows = pl.ds(SPLIT, rows - SPLIT)
    mine = pl.ds(pl.multiple_of(t * half, half), half)
    theirs = pl.ds(pl.multiple_of((1 - t) * half, half), half)

    own_loads = []
    for number, (first, many, kind, bias) in enumerate(PARTS):
        own_loads.append(
            pltpu.make_async_copy(
                qkv_in.at[0, "qkv".index(kind), :, pl.ds(bias % WIDE, many)],
                shard.at[:, pl.ds(QKV + first, many)],
                own_sem.at[1 + number],
            )
        )
    own_up = pltpu.make_async_copy(up_in.at[0], shard.at[:, pl.ds(UP, DOWN - UP)], own_sem.at[7])
    own_out = pltpu.make_async_copy(out_in.at[0], shard.at[:, pl.ds(OUT, UP - OUT)], own_sem.at[8])
    own_down = pltpu.make_async_copy(
        down_in.at[0], shard.at[:, pl.ds(DOWN, END - DOWN)], own_sem.at[9]
    )
    for copy in own_loads + [own_out, own_up, own_down]:
        copy.start()
    spread[0:32, :] = jnp.zeros((32, 128), F32)
    vec_grads[0:rows, :] = jnp.zeros((rows, 128), F32)
    spread[0:2, 0:rows] = gains_in[0].astype(F32)
    spread[2:6, 0:rows] = biases_in[0].astype(F32)
    for head in range(6):
        spread[8 + 2 * head : 10 + 2 * head, 0:8] = heads_in[0, head].astype(F32)
    vec_grads[0:rows, 0:8] = spread[0:8, :].T[0:rows, :]
    vec_grads[0:8, HEAD_LANE : HEAD_LANE + 12] = spread[8:24, :].T[0:8, 0:12]
    vec_grads[0:8, UNIT_LANE : UNIT_LANE + 24] = units_in[0].astype(F32)
    shard[:, VEC:QKV] = vec_grads[0:rows, :].astype(BF)

    place.greet()

    VECTORS = CHUNKS

    def piece_cols(piece):
        if isinstance(piece, int) and piece == VECTORS:
            return pl.ds(VEC, QKV)
        return pl.ds(pl.multiple_of(QKV + piece * WIDE, 128), WIDE)

    def pieces_of(step):
        layer, piece = step // CHUNKS, step % CHUNKS
        return layer, (VECTORS, piece) if piece == 0 else (piece,)

    def z_copies(piece):
        cols = piece_cols(piece)
        copies = []
        for step in range(LINES):
            copies.append(
                remote(
                    shard.at[:, cols],
                    w.at[s, e, y, :, cols],
                    z_send.at[piece, step],
                    z_recv.at[s, piece, e],
                    (t, place.row_of(place.line(step), y), t),
                )
            )
        local = pltpu.make_async_copy(
            shard.at[:, cols], w.at[s, e, y, :, cols], z_recv.at[s, piece, e]
        )
        return copies, local

    def z_start(step):
        layer, pieces = pieces_of(step)

        @pl.when(s == layer)
        def _():
            for piece in pieces:
                copies, local = z_copies(piece)

                @pl.when(primary)
                def _():
                    local.start()

                @pl.when(secondary)
                def _():
                    copies[0].start()

                for copy in copies[1:]:
                    copy.start()

    def z_finish(piece):
        copies, _ = z_copies(piece)

        @pl.when(secondary)
        def _():
            copies[0].wait_send()

        for copy in copies[1:]:
            copy.wait_send()

    def x_copy(layer, piece):
        part = w.at[layer, :, y, :, piece_cols(piece)]
        return remote(part, part, x_send.at[layer, piece], x_recv.at[layer, piece], place.across)

    def y_copy(layer, piece):
        part = w.at[layer, :, y, :, piece_cols(piece)]
        return remote(part, part, y_send.at[layer, piece], y_recv.at[layer, piece], place.beside)

    def xb_copy(layer, piece):
        part = w.at[layer, :, 1 - y, high_rows, piece_cols(piece)]
        return remote(part, part, xb_send.at[layer, piece], xb_recv.at[layer, piece], place.across)

    def ya_copy(layer, piece):
        part = w.at[layer, :, y, low_rows, piece_cols(piece)]
        return remote(part, part, ya_send.at[layer, piece], ya_recv.at[layer, piece], place.beside)

    def step_z(step):
        layer, pieces = pieces_of(step)

        @pl.when(primary)
        def _():
            for piece in pieces:
                cols = piece_cols(piece)
                for line in range(LINES):
                    await_bytes(w.at[layer, line, y, :, cols], z_recv.at[layer, piece, line])
                x_copy(layer, piece).start()
                y_copy(layer, piece).start()

    def step_plane(step):
        layer, pieces = pieces_of(step)

        @pl.when(primary)
        def _():
            for piece in pieces:
                await_bytes(w.at[layer, :, 1 - y, :, piece_cols(piece)], y_recv.at[layer, piece])
                xb_copy(layer, piece).start()

        @pl.when(secondary)
        def _():
            for piece in pieces:
                await_bytes(w.at[layer, :, y, :, piece_cols(piece)], x_recv.at[layer, piece])
                ya_copy(layer, piece).start()

    def tick(step):
        if step + 3 < 2 * CHUNKS:
            step_z(step + 3)
        if step + 8 < 2 * CHUNKS:
            z_start(step + 8)
        step_plane(step)

    def complete(*steps):
        @pl.when(secondary)
        def _():
            for step in steps:
                layer, pieces = pieces_of(step)
                for piece in pieces:
                    cols = piece_cols(piece)
                    await_bytes(w.at[layer, :, 1 - y, high_rows, cols], xb_recv.at[layer, piece])
                    await_bytes(w.at[layer, :, 1 - y, low_rows, cols], ya_recv.at[layer, piece])

    def at_turns(turns):
        def beside(index):
            for turn, steps in turns.items():

                @pl.when(index == turn)
                def _():
                    for step in steps:
                        step()

        return beside

    def ticks(turns):
        return at_turns({turn: (functools.partial(tick, step),) for turn, step in turns.items()})

    kept = {
        "x": (n2.at[pl.ds(0, width), :], x_hbm),
        "h": (res, h_hbm),
        "n1": (n1.at[pl.ds(0, width), :], n1_hbm),
        "n2": (n2.at[pl.ds(0, width), :], n2_hbm),
        "qkv": (qkv, qkv_hbm),
        "ctx": (ctx, ctx_hbm),
        "lse": (lse, lse_hbm),
        "act": (act, act_hbm),
        "slope": (slope, slope_hbm),
    }
    names = tuple(kept)

    def save(name, layer):
        src, dst = kept[name]
        if name in ("x", "h"):
            dst = dst.at[layer]
        return pltpu.make_async_copy(src, dst, save_sem.at[names.index(name), layer])

    def load(name, layer=0):
        dst, src = kept[name]
        if name == "x":
            dst, src = act.at[pl.ds(0, width), :], src.at[layer]
        return pltpu.make_async_copy(src, dst, load_sem.at[names.index(name)])

    def load_h(layer, index):
        slot = lax.rem(index, 2)
        return pltpu.make_async_copy(
            h_hbm.at[layer, :, block_of(index)], h_in.at[slot], h_sem.at[slot]
        )

    my_quarter = pl.ds(s * quarter, quarter)
    my_rows = pl.ds(pl.multiple_of((1 - t) * half + s * quarter, quarter), quarter)

    def clip_across():
        there = pl.ds(pl.multiple_of(t * half + s * quarter, quarter), quarter)
        return remote(
            clips.at[1 - t, my_quarter, :],
            stage.at[there, :],
            in_sem.at[0],
            in_sem.at[1],
            place.across,
        )

    def clip_core():
        part = stage.at[my_rows, :]
        return remote(part, part, in_sem.at[2], in_sem.at[3], place.core)

    def cot_across():
        return remote(
            cot.at[1 - t, my_quarter, :],
            cot_other.at[my_quarter, :],
            cot_sem.at[0],
            cot_sem.at[1],
            place.across,
        )

    def cot_core():
        part = cot_other.at[my_quarter, :]
        return remote(part, part, cot_sem.at[2], cot_sem.at[3], place.core)

    def exchange(kind, index, slot):
        return remote(
            send.at[kind, index],
            recv.at[kind, index],
            e_send.at[slot, index],
            e_recv.at[slot, index],
            place.core,
        )

    def result_copies(ref, first):
        local = pltpu.make_async_copy(stage.at[mine, :], ref.at[0, t], out_sem.at[first])
        away = remote(
            stage.at[theirs, :],
            ref.at[0, t],
            out_sem.at[first + 1],
            out_sem.at[first + 2],
            place.across,
        )
        return local, away

    def grad_copies(index):
        place_in = lax.rem(index, blocks // 2)
        part = in_grad.at[0, t, pl.ds(pl.multiple_of(place_in * BLOCK, BLOCK), BLOCK), :]
        src = stage.at[block_of(index), :]
        local = pltpu.make_async_copy(src, part, grad_sem.at[0, place_in])
        away = remote(
            src, part, grad_sem.at[1, place_in], grad_sem.at[2, place_in], place.across
        )
        return local, away

    def emit(layer, ref, first):
        @pl.when(s == layer)
        def _():
            for copy in result_copies(ref, first):
                copy.start()

    for copy in own_loads:
        copy.wait()
    for step in range(3):
        z_start(step)
    n1[width:, :] = jnp.ones((ONES, frames), BF)
    n2[width:, :] = jnp.ones((ONES, frames), BF)
    own_clip = pltpu.make_async_copy(clips.at[t], stage.at[mine, :], in_sem.at[4])
    own_clip.start()
    clip_across().start()
    cot_across().start()
    own_out.wait()
    own_up.wait()
    own_down.wait()
    for step in (3, 4):
        z_start(step)

    def take_clip(first):
        def body(index, carry):
            at = pl.ds(pl.multiple_of(first + index * BLOCK, BLOCK), BLOCK)
            tile = stage[at, :].T
            n2[0:width, at] = tile
            res[:, at] = tile.astype(F32)
            return carry

        lax.fori_loop(0, half // BLOCK, body, 0)

    own_clip.wait()
    take_clip(t * half)
    clip_across().wait()
    clip_core().start()
    step_z(0)
    z_start(5)
    step_z(1)
    z_start(6)
    clip_core().wait()
    take_clip((1 - t) * half)
    save("x", 0).start()
    step_plane(0)
    step_z(2)
    z_start(7)
    step_plane(1)
    cot_across().wait()
    cot_core().start()
    step_z(3)
    z_start(8)
    step_plane(2)
    step_z(4)
    z_start(9)
    step_z(5)
    z_start(10)

    def project(pair):
        for index in (2 * pair, 2 * pair + 1):
            cols = block_of(index)
            mean, scale = norm_stats(lambda span: res[span, cols], width)
            for span in chunks_of(width):
                hat = (res[span, cols] - mean) * scale
                n1[span, cols] = (hat * vecs[span, 0:1] + vecs[span, 2:3]).astype(BF)
        cols = pair_of(pair)
        for first, many, kind, bias in PARTS:
            value = mm(wt[first : first + many, :], n1[0:width, cols])
            for span in chunks_of(many):
                part = value[span, :]
                if kind != "k":
                    part = part + spread[bias + span.start : bias + span.stop, 6:7]
                if kind == "q":
                    part = part * 0.125
                qkv[first + span.start : first + span.stop, cols] = part.astype(BF)

    def send_pair(kind, pair, slot, value):
        for part in range(2):
            index = 2 * pair + part
            send[kind, index] = value[:, part * BLOCK : (part + 1) * BLOCK].astype(BF)
            exchange(kind, index, slot).start()

    def head_rows(head, first):
        return pl.ds(pl.multiple_of(first + head * HEAD, HEAD), HEAD)

    def attend(layer, turns, later_turns):
        def heads_of(first_head, base, stride, beside):
            def one_head(index_in, carry):
                head = first_head + index_in
                q_rows = head_rows(index_in, base)
                k_rows = head_rows(index_in, base + stride)
                v_rows = head_rows(index_in, base + 2 * stride)
                c_rows = head_rows(head, 0)
                keys = qkv[k_rows, :].T
                for index in range(blocks):
                    cols = slice(index * BLOCK, (index + 1) * BLOCK)
                    queries = qkv[q_rows, cols]
                    tiles = []
                    top = None
                    for tile in chunks_of(frames, BLOCK):
                        scores = mm(keys[tile, :], queries)
                        for span in chunks_of(BLOCK):
                            peak = stack_max(scores[span, :])
                            top = peak if top is None else jnp.maximum(top, peak)
                        tiles.append(scores)
                    top = jnp.max(top, 0, keepdims=True)
                    total = jnp.zeros((8, BLOCK), F32)
                    mixed = jnp.zeros((HEAD, BLOCK), F32)
                    for tile, scores in zip(chunks_of(frames, BLOCK), tiles):
                        soft = []
                        for span in chunks_of(BLOCK):
                            part = jnp.exp(scores[span, :] - top)
                            total = total + stack_sum(part)
                            soft.append(part.astype(BF))
                        mixed = mixed + mm(qkv[v_rows, tile], jnp.concatenate(soft, 0))
                    total = jnp.sum(total, 0, keepdims=True)
                    ctx[c_rows, cols] = (mixed / total).astype(BF)
                    lse[pl.ds(head, 1), cols] = top + jnp.log(total)
                beside(index_in)
                return carry

            return one_head

        lax.fori_loop(0, 4, heads_of(0, 0, 256, ticks(turns)), 0)
        lax.fori_loop(0, 2, heads_of(4, 768, 128, ticks(later_turns)), 0)

    def out_project(layer, turns):
        beside = ticks(turns)

        def body(index, carry):
            part = mm(whole(w, layer, OUT, 384), ctx[:, pair_of(index)])
            send_pair(0, index, 2 * layer, part)
            beside(index)
            return carry

        lax.fori_loop(0, blocks // 2, body, 0)

    def middle_norm(layer, turns):
        beside = ticks(turns)

        def body(index, carry):
            cols = block_of(index)
            exchange(0, index, 2 * layer).wait()
            for span in chunks_of(width):
                added = send[0, index, span, :].astype(F32) + recv[0, index, span, :].astype(F32)
                res[span, cols] = res[span, cols] + added + vecs[span, 3:4]
            mean, scale = norm_stats(lambda span: res[span, cols], width)
            for span in chunks_of(width):
                hat = (res[span, cols] - mean) * scale
                n2[span, cols] = (hat * vecs[span, 1:2] + vecs[span, 4:5]).astype(BF)
            beside(index)
            return carry

        lax.fori_loop(0, blocks, body, 0)

    def hidden_part(layer, part):
        flip_weights(w, wt, layer, UP + part * WIDE, WIDE, part * WIDE)
        units = slice(part * WIDE, (part + 1) * WIDE)

        def body(index, carry):
            cols = pair_of(index)
            pre = mm(wt[units, :], n2[0:width, cols])
            for span in chunks_of(WIDE):
                first = part * WIDE + span.start
                bias = spread[768 + first : 768 + first + ROWS, 6:7]
                value, steep = gelu_parts(pre[span, :] + bias)
                act[first : first + ROWS, cols] = value.astype(BF)
                slope[first : first + ROWS, cols] = steep.astype(BF)
            return carry

        lax.fori_loop(0, blocks // 2, body, 0)

    def down_project(layer, turns):
        beside = ticks(turns)

        def body(index, carry):
            part = mm(whole(w, layer, DOWN, 1536), act[:, pair_of(index)])
            send_pair(1, index, 2 * layer + 1, part)
            beside(index)
            return carry

        lax.fori_loop(0, blocks // 2, body, 0)

    def layer_end(layer, index, span):
        added = send[1, index, span, :].astype(F32) + recv[1, index, span, :].astype(F32)
        return (res[span, block_of(index)] + added + vecs[span, 5:6]).astype(BF)

    def take_vectors(layer):
        vecs[...] = whole(w, layer, VEC, 128).astype(F32)
        spread_biases(vecs, spread, rows)

    def project_all(layer, turns):
        beside = ticks(turns)
        flip_weights(w, wt, layer, QKV, 1152)

        def body(index, carry):
            project(index)
            beside(index)
            return carry

        lax.fori_loop(0, blocks // 2, body, 0)
        if layer == 0:
            save("n1", 0).start()
            save("qkv", 0).start()

    complete(0, 1, 2)
    take_vectors(0)
    project_all(0, {0: 3, 1: 4})
    cot_core().wait()
    load_cot = pltpu.make_async_copy(cot_other, stage.at[theirs, :], cot_sem.at[4])
    load_cot.start()
    own_cot = pltpu.make_async_copy(cot.at[t], stage.at[mine, :], cot_sem.at[5])
    own_cot.start()
    attend(0, {0: 5, 2: 6}, {0: 7})
    save("ctx", 0).start()
    save("lse", 0).start()
    complete(3)
    out_project(0, {1: 8})
    load_cot.wait()
    own_cot.wait()

    sums[3] = jnp.zeros_like(sums[3])

    def take_cot(index, carry):
        low[:, block_of(index)] = stage[block_of(index), :].T
        for span in chunks_of(width):
            sums[3, span, :] += fold(low[span, block_of(index)].astype(F32))
        return carry

    lax.fori_loop(0, blocks, take_cot, 0)
    save("x", 0).wait()
    middle_norm(0, {1: 9})
    save("h", 0).start()
    save("n2", 0).start()
    for part in range(4):
        complete(4 + part)
        hidden_part(0, part)
        tick(10 + part)
    save("act", 0).start()
    save("slope", 0).start()
    complete(8, 9, 10, 11)
    down_project(0, {1: 14})
    for name in ("n1", "qkv", "h", "n2"):
        save(name, 0).wait()

    def finish_body(index, carry):
        exchange(1, index, 1).wait()
        cols = block_of(index)
        for span in chunks_of(width):
            rows_out = layer_end(0, index, span)
            n2[span, cols] = rows_out
            res[span, cols] = rows_out.astype(F32)

        @pl.when(s == 0)
        def _():
            stage[cols, :] = n2[0:width, cols].T

        return carry

    lax.fori_loop(0, blocks, finish_body, 0)
    save("x", 1).start()
    complete(12, 13, 14)
    take_vectors(1)
    project_all(1, {0: 15, 1: 16})
    save("ctx", 0).wait()
    save("lse", 0).wait()
    attend(1, {0: 17, 2: 18}, {0: 19})
    complete(15)
    out_project(1, {1: 20})
    save("x", 1).wait()
    middle_norm(1, {1: 21})
    save("h", 1).start()
    save("act", 0).wait()
    save("slope", 0).wait()
    for part in range(4):
        complete(16 + part)
        hidden_part(1, part)
        if part < 2:
            tick(22 + part)
    for part in range(4):
        complete(20 + part)
        flip_weights(w, wt, 1, DOWN + part * WIDE, WIDE, part * WIDE)
    emit(0, out, 0)
    down_project(1, {})

    def gya_copy(layer, piece):
        cols = piece_cols(piece)
        return remote(
            w.at[layer, :, 1 - y, low_rows, cols],
            land_a.at[:, low_rows, cols],
            gya_send.at[layer, piece],
            gya_recv.at[layer, piece],
            place.beside,
        )

    def gxb_copy(layer, piece):
        cols = piece_cols(piece)
        return remote(
            w.at[layer, :, 1 - y, high_rows, cols],
            land_b.at[:, :, cols],
            gxb_send.at[layer, piece],
            gxb_recv.at[layer, piece],
            place.across,
        )

    def gx_copy(layer, piece):
        cols = piece_cols(piece)
        return remote(
            w.at[layer, :, y, :, cols],
            land_a.at[:, :, cols],
            gx_send.at[layer, piece],
            gx_recv.at[layer, piece],
            place.across,
        )

    def gy_copy(layer, piece):
        cols = piece_cols(piece)
        return remote(
            w.at[layer, :, 1 - y, :, cols],
            land_y.at[:, :, cols],
            gy_send.at[layer, piece],
            gy_recv.at[layer, piece],
            place.beside,
        )

    def landed_part(piece):
        if piece == VECTORS:
            return landed_vec
        ref, first = (
            (landed_qkv, 0)
            if piece < 3
            else (landed_out, 3)
            if piece < 4
            else (landed_up, 4)
            if piece < 8
            else (landed_down, 8)
        )
        return ref.at[:, :, pl.ds((piece - first) * WIDE, WIDE)]

    def gz_copies(layer, piece):
        cols = piece_cols(piece)
        target = landed_part(piece)
        copies = []
        for step in range(LINES):
            line = place.line(step)
            copies.append(
                remote(
                    w.at[layer, line, y, :, cols],
                    target.at[e],
                    gz_send.at[layer, piece, step],
                    gz_recv.at[piece, e],
                    (layer, place.row_of(line, y), t),
                )
            )
        local = pltpu.make_async_copy(
            w.at[layer, e, y, :, cols], target.at[e], gz_recv.at[piece, e]
        )
        return copies, local

    def add_rows(layer, piece, which, span, lands):
        cols = piece_cols(piece)
        first, count = span
        for line in range(LINES):
            total = w[layer, line, which, pl.ds(first, count), cols].astype(F32)
            for land, offset in lands:
                total = total + land[line, pl.ds(offset, count), cols].astype(F32)
            w[layer, line, which, pl.ds(first, count), cols] = total.astype(BF)

    def signal(sem, layer, piece, device):
        if layer == 1:
            pl.semaphore_signal(sem.at[piece], inc=1, device_id=device, device_id_type=MESH)

    def credit(sem, layer, piece):
        if layer == 0:
            pl.semaphore_wait(sem.at[piece], 1)

    def step_a(layer, piece):
        @pl.when(secondary)
        def _():
            credit(ya_free, layer, piece)
            gya_copy(layer, piece).start()
            credit(xb_free, layer, piece)
            gxb_copy(layer, piece).start()

    def step_b(layer, piece):
        cols = piece_cols(piece)

        @pl.when(secondary)
        def _():
            await_bytes(land_a.at[:, low_rows, cols], gya_recv.at[layer, piece])
            add_rows(layer, piece, y, (0, SPLIT), [(land_a, 0)])
            signal(ya_free, layer, piece, place.beside)
            credit(x_free, layer, piece)
            gx_copy(layer, piece).start()

        @pl.when(primary)
        def _():
            await_bytes(land_b.at[:, :, cols], gxb_recv.at[layer, piece])
            add_rows(layer, piece, 1 - y, (SPLIT, rows - SPLIT), [(land_b, 0)])
            signal(xb_free, layer, piece, place.across)
            credit(y_free, layer, piece)
            gy_copy(layer, piece).start()

    def step_c(layer, piece):
        cols = piece_cols(piece)

        @pl.when(primary)
        def _():
            await_bytes(land_a.at[:, :, cols], gx_recv.at[layer, piece])
            await_bytes(land_y.at[:, :, cols], gy_recv.at[layer, piece])
            add_rows(layer, piece, y, (0, rows), [(land_a, 0), (land_y, 0)])
            signal(x_free, layer, piece, place.across)
            signal(y_free, layer, piece, place.beside)
            copies, local = gz_copies(layer, piece)

            @pl.when(s == layer)
            def _():
                local.start()

            @pl.when(s != layer)
            def _():
                copies[0].start()

            for copy in copies[1:]:
                copy.start()

    def store_grads(layer, start, count, value):
        w[layer, :, :, :, pl.ds(start, count)] = value.astype(BF).reshape(
            w.shape[1], w.shape[2], rows, count
        )

    def mlp_back(layer, beside):
        def body(index, carry):
            cols = pair_of(index)
            for part in range(4):
                units = slice(part * WIDE, (part + 1) * WIDE)
                grad = mm(wt[units, :], low[:, cols])
                for span in chunks_of(WIDE):
                    rows_in = slice(units.start + span.start, units.start + span.stop)
                    steep = slope[rows_in, cols].astype(F32)
                    slope[rows_in, cols] = (grad[span, :] * steep).astype(BF)
            term = mm(whole(w, layer, UP, 1536), slope[:, cols])
            send_pair(0, index, 4 + 2 * layer, term)
            beside(index)
            return carry

        lax.fori_loop(0, blocks // 2, body, 0)

    def outer(layer, start, left, right, first, many, before, beside):
        def body(index, carry):
            before(index)
            base = index * PAIR
            span = pl.ds(pl.multiple_of(first + base, 128), PAIR)
            value = mmt(left[...], right[span, :])
            store_grads(layer, pl.multiple_of(start + base, 128), PAIR, value[0:width, :])
            if left.shape[0] > width:
                to = pl.ds(pl.multiple_of(768 + base, BLOCK), PAIR)
                spread[to, 0:8] = value[width : width + 8, :].T
            beside(index)
            return carry

        lax.fori_loop(0, many // PAIR, body, 0)

    def turned(turn):
        return lax.rem(turn + (1 - t) * (blocks // 2), blocks)

    def norm_back(layer, kind, gain_lane, source, put, finish, beside):
        sums[0:3] = jnp.zeros((3, width, 128), F32)

        def body(turn, carry):
            index = turned(turn)
            cols = block_of(index)
            read = source(index)
            mean, scale = norm_stats(read, width)
            exchange(kind, index, 4 + 2 * layer + kind).wait()
            first = jnp.zeros((8, BLOCK), F32)
            second = jnp.zeros((8, BLOCK), F32)

            def terms(span):
                hat = (read(span) - mean) * scale
                grad = send[kind, index, span, :].astype(F32)
                grad = grad + recv[kind, index, span, :].astype(F32)
                return hat, grad, grad * vecs[span, gain_lane : gain_lane + 1]

            for span in chunks_of(width):
                hat, grad, scaled = terms(span)
                sums[0, span, :] += fold(grad * hat)
                sums[1, span, :] += fold(grad)
                first = first + stack_sum(scaled)
                second = second + stack_sum(scaled * hat)
            level = mean_of(first, width)
            slant = mean_of(second, width)
            for span in chunks_of(width):
                hat, _, scaled = terms(span)
                put(span, cols, res[span, cols] + scale * (scaled - level - hat * slant))
            finish(index)
            beside(turn)
            return carry

        lax.fori_loop(0, blocks, body, 0)

    def row_sums(value):
        return jnp.sum(value, 1, keepdims=True)

    def attend_back(first_head, many, base, stride, beside):
        def one_head(index_in, carry):
            head = first_head + index_in
            q_rows = head_rows(index_in, base)
            k_rows = head_rows(index_in, base + stride)
            v_rows = head_rows(index_in, base + 2 * stride)
            c_rows = head_rows(head, 0)
            keys = qkv[k_rows, :].T
            values = qkv[v_rows, :].T
            flat_queries = qkv[q_rows, :].T
            flat_grads = dctx[c_rows, :].T
            level = lse[pl.ds(head, 1), :]
            inner = jnp.sum(
                dctx[c_rows, :].astype(F32) * ctx[c_rows, :].astype(F32), 0, keepdims=True
            )
            step = jnp.zeros((HEAD, frames), F32)
            for tile in chunks_of(frames, BLOCK):
                soft = []
                score_grad = []
                for cols in chunks_of(frames, BLOCK):
                    scores = mm(keys[tile, :], qkv[q_rows, cols])
                    soft_grad = mm(values[tile, :], dctx[c_rows, cols])
                    soft_parts = []
                    grad_parts = []
                    for part in chunks_of(BLOCK):
                        strength = jnp.exp(scores[part, :] - level[:, cols])
                        soft_parts.append(strength.astype(BF))
                        strength = strength * (soft_grad[part, :] - inner[:, cols])
                        grad_parts.append(strength.astype(BF))
                    soft.append(jnp.concatenate(soft_parts, 0))
                    score_grad.append(jnp.concatenate(grad_parts, 0))
                soft = jnp.concatenate(soft, 1)
                score_grad = jnp.concatenate(score_grad, 1)
                step = step + mm(qkv[k_rows, tile], score_grad)
                slope[k_rows, tile] = mm(score_grad, flat_queries).astype(BF).T
                slope[v_rows, tile] = mm(soft, flat_grads).astype(BF).T
            slope[q_rows, :] = (step * 0.125).astype(BF)
            beside(index_in)
            return carry

        lax.fori_loop(0, many, one_head, 0)

    def keep_sums(first, value):
        for start, many, kind, bias in PARTS:
            offset = start - first
            if kind != "k" and 0 <= offset < value.shape[1]:
                spread[bias : bias + many, 0:8] = value[
                    width : width + 8, offset : offset + many
                ].T

    def collect_biases():
        def body(group, carry):
            to = pl.ds(pl.multiple_of(group * rows, 8), 8)
            for kind in range(2):
                for head in range(6):
                    at = pl.ds(pl.multiple_of(kind * 384 + head * HEAD + group * 8, 8), 8)
                    lane = head_lane(kind, head)
                    vec_grads[to, lane : lane + 1] = spread[at, 6:7]
            for unit in range(24):
                at = pl.ds(pl.multiple_of(768 + unit * HEAD + group * 8, 8), 8)
                lane = UNIT_LANE + unit
                vec_grads[to, lane : lane + 1] = spread[at, 6:7]
            return carry

        lax.fori_loop(0, GROUPS, body, 0)

    def nothing(index):
        del index

    def finish_gather(layer, piece):
        @pl.when(primary)
        def _():
            x_copy(layer, piece).wait_send()
            y_copy(layer, piece).wait_send()
            xb_copy(layer, piece).wait_send()

        @pl.when(secondary)
        def _():
            ya_copy(layer, piece).wait_send()

    def last_body(index, carry):
        exchange(1, index, 3).wait()

        @pl.when(s == 1)
        def _():
            for span in chunks_of(width, 128):
                stage[block_of(index), span] = layer_end(1, index, span).T

        return carry

    for layer in (1, 0):
        later = layer == 0
        if later:
            load_h(layer, turned(0)).start()
            load("act").wait()
            vecs[...] = whole(w, layer, VEC, 128).astype(F32)
            flip_weights(w, wt, layer, DOWN, 1536)
        vec_grads[...] = jnp.zeros_like(vec_grads)

        def a(piece, layer=layer):
            return lambda: step_a(layer, piece)

        def b(piece, layer=layer):
            return lambda: step_b(layer, piece)

        def c(piece, layer=layer):
            return lambda: step_c(layer, piece)

        if later:
            before = nothing
            early = at_turns(
                {
                    0: (a(8), lambda: step_b(1, VECTORS)),
                    1: (a(9), lambda: step_c(1, VECTORS)),
                    2: (a(10), a(11)),
                }
            )
        else:
            waits = [functools.partial(finish_gather, 1, piece) for piece in (8, 9, 10, 11)]
            before = at_turns({0: waits[:2], 1: waits[2:3], 2: waits[3:]})
            early = at_turns({0: (a(8),), 1: (a(9),), 2: (a(10), a(11))})
        outer(layer, DOWN, low, act, 0, 1536, before, early)
        load("x", layer).start()
        vec_grads[:, 5:6] = row_sums(sums[3])
        if not later:
            lax.fori_loop(0, blocks, last_body, 0)
            emit(1, out, 0)
            save("h", 1).wait()
            load_h(layer, turned(0)).start()
            res[...] = low[...].astype(F32)
            for piece in range(CHUNKS + 1):
                z_finish(piece)
                finish_gather(0, piece)
                if piece < 8 or piece == VECTORS:
                    finish_gather(1, piece)
        else:
            load("slope").wait()

        mlp_back(layer, at_turns({0: (b(8),), 1: (b(9), b(10), b(11))}))
        if later:
            load("n2").wait()
        drain = at_turns({0: (a(4),), 1: (a(5),), 2: (a(6), a(7), c(8))})
        outer(layer, UP, n2, slope, 0, 1536, nothing, drain)
        flip_weights(w, wt, layer, OUT, 384)

        def hidden_in(index, layer=layer):
            turn = lax.rem(index + (1 - t) * (blocks // 2), blocks)

            @pl.when(turn + 1 < blocks)
            def _():
                load_h(layer, turned(turn + 1)).start()

            load_h(layer, index).wait()
            slot = lax.rem(index, 2)
            return lambda span: h_in[slot, span, :]

        def hidden_put(span, cols, total):
            res[span, cols] = total
            rounded = total.astype(BF)
            low[span, cols] = rounded
            sums[2, span, :] += fold(rounded.astype(F32))

        drain = at_turns({0: (b(4), c(9)), 1: (b(5), c(10)), 2: (b(6), c(11)), 3: (b(7),)})
        norm_back(layer, 0, 1, hidden_in, hidden_put, nothing, drain)

        def context_back(index, carry):
            cols = pair_of(index)
            dctx[:, cols] = mm(wt[0:384, :], low[:, cols]).astype(BF)
            return carry

        lax.fori_loop(0, blocks // 2, context_back, 0)
        vec_grads[:, 1:2] = row_sums(sums[0])
        vec_grads[:, 4:5] = row_sums(sums[1])
        vec_grads[:, 3:4] = row_sums(sums[2])
        if later:
            for name in ("ctx", "qkv", "lse"):
                load(name).wait()
        store_grads(layer, OUT, 384, mmt(low[...], ctx[...]))
        step_a(layer, 3)
        drain = at_turns({0: (c(4),), 1: (c(5),), 2: (b(3), c(6)), 3: (c(7),)})
        attend_back(0, 4, 0, 256, drain)
        if later:
            load("n1").wait()
        wt[0:768, :] = whole(w, layer, QKV, 768)

        for first, many in ((0, 512), (512, 256)):
            value = mmt(n1[...], slope[first : first + many, :])
            store_grads(layer, QKV + first, many, value[0:width, :])
            keep_sums(first, value)
        step_a(layer, 0)
        step_a(layer, 1)
        attend_back(4, 2, 768, 128, at_turns({0: (b(0), c(3)), 1: (b(1),)}))

        def first_body(index, carry, layer=layer):
            cols = pair_of(index)
            term = mm(wt[0:768, :], slope[0:768, cols])
            term = term + mm(whole(w, layer, QKV + 768, WIDE), slope[768:1152, cols])
            send_pair(1, index, 5 + 2 * layer, term)
            return carry

        lax.fori_loop(0, blocks // 2, first_body, 0)
        value = mmt(n1[...], slope[768:1152, :])
        store_grads(layer, QKV + 768, WIDE, value[0:width, :])
        keep_sums(768, value)
        step_a(layer, 2)
        step_c(layer, 0)
        collect_biases()
        if layer == 1:
            for name in ("slope", "n1", "n2", "ctx", "qkv", "lse"):
                load(name).start()
        load("x", layer).wait()

        @pl.when(s == layer)
        def _():
            local, away = result_copies(out, 0)
            local.wait()
            away.wait_send()

        def rows_x(index):
            return lambda span: act[span, block_of(index)].astype(F32)

        def rows_put(span, cols, total, layer=layer):
            rounded = total.astype(BF)
            low[span, cols] = rounded
            if layer == 1:
                res[span, cols] = rounded.astype(F32)
                sums[2, span, :] += fold(rounded.astype(F32))

        def rows_out(index, layer=layer):
            @pl.when(s == layer)
            def _():
                stage[block_of(index), :] = low[:, block_of(index)].T
                local, away = grad_copies(index)

                @pl.when(index // (blocks // 2) == t)
                def _():
                    local.start()

                if layer == 0:

                    @pl.when(index // (blocks // 2) != t)
                    def _():
                        away.start()

        drain = at_turns({0: (c(1),), 1: (b(2),), 3: (c(2),)})
        norm_back(layer, 1, 0, rows_x, rows_put, rows_out, drain)
        if layer == 1:
            load("act").start()
        vec_grads[:, 0:1] = row_sums(sums[0])
        vec_grads[:, 2:3] = row_sums(sums[1])
        sums[3] = sums[2]
        store_grads(layer, VEC, 128, vec_grads[...])
        step_a(layer, VECTORS)

    step_b(0, VECTORS)

    @pl.when(s == 1)
    def _():
        for place_in in range(blocks // 2):
            _, away = grad_copies((1 - t) * (blocks // 2) + place_in)
            away.start()

    step_c(0, VECTORS)

    def finish_scatter(piece):
        for layer in range(2):

            @pl.when(secondary)
            def _():
                gya_copy(layer, piece).wait_send()
                gxb_copy(layer, piece).wait_send()
                gx_copy(layer, piece).wait_send()

            @pl.when(primary)
            def _():
                gy_copy(layer, piece).wait_send()
                copies, _ = gz_copies(layer, piece)

                @pl.when(s != layer)
                def _():
                    copies[0].wait_send()

                for copy in copies[1:]:
                    copy.wait_send()

    for piece in range(CHUNKS + 1):
        finish_scatter(piece)
        for line in range(LINES):
            await_bytes(landed_part(piece).at[line], gz_recv.at[piece, line])

    _, away = result_copies(out, 0)
    away.wait_recv()
    for index in range(blocks // 2):
        local, away = grad_copies(index)
        local.wait()
        away.wait()


def layers_call(share, clips, cotangent, shards, dims):
    width, frames, hidden_units, heads_width = dims
    rows = width // GROUPS
    sem = pltpu.SemaphoreType.DMA
    free = pltpu.SemaphoreType.REGULAR
    packed = (2, LINES, 2, rows, END)
    blocks = frames // BLOCK
    shape = jax.ShapeDtypeStruct
    outs = [
        shape((1,) + clips.shape, BF),
        shape((1,) + clips.shape, BF),
        shape((LINES, rows, QKV - VEC), BF),
        shape((LINES, rows, OUT - QKV), BF),
        shape((LINES, rows, UP - OUT), BF),
        shape((LINES, rows, DOWN - UP), BF),
        shape((LINES, rows, END - DOWN), BF),
        shape(clips.shape[1:], BF),
        shape((2, width, frames), BF),
        shape((2, width, frames), F32),
        shape((width, frames), BF),
        shape((width, frames), BF),
        shape((3 * heads_width, frames), BF),
        shape((heads_width, frames), BF),
        shape((8, frames), F32),
        shape((hidden_units, frames), BF),
        shape((hidden_units, frames), BF),
    ]
    scratch = [
        pltpu.VMEM(packed, BF),
        pltpu.VMEM((width, frames), F32),
        pltpu.VMEM((hidden_units, frames), BF),
        pltpu.VMEM((hidden_units, frames), BF),
        pltpu.VMEM((width + ONES, frames), BF),
        pltpu.VMEM((width + ONES, frames), BF),
        pltpu.VMEM((width, frames), BF),
        pltpu.VMEM((3 * heads_width, frames), BF),
        pltpu.VMEM((heads_width, frames), BF),
        pltpu.VMEM((heads_width, frames), BF),
        pltpu.VMEM((8, frames), F32),
        pltpu.VMEM((2, width, BLOCK), F32),
        pltpu.VMEM((hidden_units, width), BF),
        pltpu.VMEM((2, blocks, width, BLOCK), BF),
        pltpu.VMEM((2, blocks, width, BLOCK), BF),
        pltpu.VMEM((width, 128), F32),
        pltpu.VMEM((width, 128), F32),
        pltpu.VMEM((4, width, 128), F32),
        pltpu.VMEM((2 * heads_width + hidden_units, 128), F32),
        pltpu.VMEM((frames, width), BF),
        pltpu.VMEM((rows, END), BF),
        pltpu.VMEM((LINES, rows, END), BF),
        pltpu.VMEM((LINES, rows - SPLIT, END), BF),
        pltpu.VMEM((LINES, rows, END), BF),
    ]
    scratch += [sem((CHUNKS + 1, LINES)), sem((2, CHUNKS + 1, LINES))]
    scratch += [sem((2, CHUNKS + 1))] * 8
    scratch += [sem((2, CHUNKS + 1, LINES)), sem((CHUNKS + 1, LINES))]
    scratch += [sem((2, CHUNKS + 1))] * 8
    scratch += [
        sem((8, blocks)),
        sem((8, blocks)),
        sem((10,)),
        sem((5,)),
        sem((6,)),
        sem((3,)),
        sem((3, blocks // 2)),
        sem((9, 2)),
        sem((9,)),
        sem((2,)),
    ]
    scratch += [free((CHUNKS + 1,))] * 4
    anywhere = pl.BlockSpec(memory_space=pl.ANY)
    inside = pl.BlockSpec(memory_space=pltpu.VMEM)
    return pl.pallas_call(
        functools.partial(layers_kernel, share),
        out_shape=outs,
        in_specs=[anywhere] * 2 + [inside] * 4 + [anywhere] * (len(shards) - 4),
        out_specs=[anywhere] * len(outs),
        scratch_shapes=scratch,
        compiler_params=pltpu.CompilerParams(
            collective_id=0, has_side_effects=True, vmem_limit_bytes=VMEM_LIMIT
        ),
        cost_estimate=pl.CostEstimate(
            flops=60_000_000_000, bytes_accessed=60_000_000, transcendentals=0
        ),
    )(clips, cotangent, *shards)


def group_piece(value, axis, share):
    if share == 1:
        return value
    size = value.shape[axis] * share
    group = lax.axis_index("dp") // share
    full = lax.all_gather(value, "dp", axis=axis, tiled=True)
    return lax.dynamic_slice_in_dim(full, group * size, size, axis)


def own_part(value, axis, share, parts, index):
    size = value.shape[axis] // parts
    if parts == 1:
        return value
    return lax.dynamic_slice_in_dim(value, index * size, size, axis)


def on_device(share, clips, cotangent, ln_gains, row_biases, w_qkv, b_qv, w_o, w_up, b_ff, w_down):
    width = clips.shape[2]
    rows = width // GROUPS
    dims = (width, 2 * clips.shape[1], w_up.shape[2], w_o.shape[1])
    ln_gains = group_piece(ln_gains, 2, share)
    row_biases = group_piece(row_biases, 2, share)
    w_qkv = group_piece(w_qkv, 2, share)
    b_qv = group_piece(b_qv, 3, share)
    w_o = group_piece(w_o, 2, share)
    w_up = group_piece(w_up, 1, share)
    b_ff = group_piece(b_ff, 2, share)
    w_down = group_piece(w_down, 2, share)
    shards = (
        ln_gains,
        row_biases,
        jnp.transpose(b_qv, (0, 2, 1, 3)),
        jnp.swapaxes(b_ff, 1, 2),
        w_qkv,
        jnp.swapaxes(w_o, 1, 2),
        w_up,
        jnp.swapaxes(w_down, 1, 2),
    )
    section_out, section_in_grad, *landed = layers_call(share, clips, cotangent, shards, dims)
    rest = lax.axis_index("dp") % share
    side = lax.axis_index("tensor")

    def joined(value):
        total = jnp.sum(value.astype(F32), 0)
        if share == 1:
            return total
        group = lax.axis_index("dp") // share
        padded = jnp.zeros((width, total.shape[1]), F32)
        padded = lax.dynamic_update_slice_in_dim(padded, total, group * rows, 0)
        return lax.dynamic_slice_in_dim(lax.psum(padded, "dp"), group * rows, rows, 0)

    def mine(value):
        return own_part(joined(value), 0, share, share, rest)

    vectors = joined(landed[0])
    vec = own_part(own_part(vectors, 0, share, share, rest), 0, share, 2, side)
    heads_grad = vectors[0:8, HEAD_LANE : HEAD_LANE + 12].T.reshape(6, 2, 8).transpose(1, 0, 2)
    units_grad = vectors[0:8, UNIT_LANE : UNIT_LANE + 24].T
    qkv_grad = {"q": [], "k": [], "v": []}
    for first, many, kind, _ in PARTS:
        qkv_grad[kind].append(mine(landed[1][:, :, first : first + many]))
    return (
        section_out,
        section_in_grad,
        vec[:, 0:2].T[None],
        vec[:, 2:6].T[None],
        jnp.stack([jnp.concatenate(qkv_grad[kind], 1) for kind in "qkv"])[None],
        own_part(heads_grad, 2, share, share, rest)[None],
        mine(landed[2]).T[None],
        mine(landed[3])[None],
        own_part(units_grad, 1, share, share, rest)[None],
        mine(landed[4]).T[None],
    )


def solution(mesh):
    placed = (
        P("dp", "tensor", None),
        P("dp", "tensor", None),
        P("section", None, "dp"),
        P("section", None, "dp"),
        P("section", None, "dp", "tensor"),
        P("section", None, "tensor", "dp"),
        P("section", "tensor", "dp"),
        P("section", "dp", "tensor"),
        P("section", "tensor", "dp"),
        P("section", "tensor", "dp"),
    )
    share = mesh.shape["dp"] // GROUPS
    return jax.shard_map(
        functools.partial(on_device, share),
        mesh=mesh,
        in_specs=placed,
        out_specs=(
            P("section", "dp", "tensor", None),
            P("section", "dp", "tensor", None),
            P("section", None, ("dp", "tensor")),
            P("section", None, ("dp", "tensor")),
            P("section", None, "dp", "tensor"),
            P("section", None, "tensor", "dp"),
            P("section", "tensor", "dp"),
            P("section", "dp", "tensor"),
            P("section", "tensor", "dp"),
            P("section", "tensor", "dp"),
        ),
        check_vma=False,
    )
```

```python
import functools

import jax
import jax.numpy as jnp
from jax import lax
from jax.experimental import pallas as pl
from jax.experimental.pallas import tpu as pltpu
from jax.sharding import PartitionSpec as P

BF = jnp.bfloat16
F32 = jnp.float32
MESH = pl.DeviceIdType.MESH
EPSILON = 1e-05
HEAD = 64
GROUPS = 8
LINES = 4
BLOCK = 256
PAIR = 2 * BLOCK
ROWS = 64
ONES = 16
VMEM_LIMIT = 62 * 1024 * 1024

VEC = 0
QKV = 128
OUT = 1280
UP = 1664
DOWN = 3200
END = 4736
GATHER_SPLITS = (64, 48)
SPLIT = 48
WIDE = 384
CHUNKS = 12


PARTS = (
    (0, 256, "q", 0),
    (256, 256, "k", 0),
    (512, 256, "v", 384),
    (768, 128, "q", 256),
    (896, 128, "k", 256),
    (1024, 128, "v", 640),
)


HEAD_LANE = 8
UNIT_LANE = 20


def head_lane(kind, head):
    return HEAD_LANE + 2 * head + kind


def mm(left, right):
    return jnp.dot(left, right, preferred_element_type=F32)


def mmt(left, right):
    return lax.dot_general(left, right, (((1,), (1,)), ((), ())), preferred_element_type=F32)


class Place:
    def __init__(self, share):
        self.s = lax.axis_index("section")
        self.d = lax.axis_index("dp")
        self.t = lax.axis_index("tensor")
        group = self.d // share
        self.rest = self.d - group * share
        self.share = share
        self.e = group // 2
        self.y = group - self.e * 2
        self.primary = self.s == self.t
        self.core = (1 - self.s, self.d, self.t)
        self.across = (self.s, self.d, 1 - self.t)
        self.beside = (self.s, self.row_of(self.e, 1 - self.y), self.t)

    def row_of(self, line, y):
        return (line * 2 + y) * self.share + self.rest

    def line(self, step):
        return lax.rem(self.e + step, LINES)

    def greet(self):
        barrier = pltpu.get_barrier_semaphore()
        peers = [self.core, self.across, self.beside]
        for step in range(1, LINES):
            for section in range(2):
                peers.append((section, self.row_of(self.line(step), self.y), self.t))
        for peer in peers:
            pl.semaphore_signal(barrier, inc=1, device_id=peer, device_id_type=MESH)
        pl.semaphore_wait(barrier, len(peers))


def remote(src, dst, send_sem, recv_sem, device):
    return pltpu.make_async_remote_copy(
        src_ref=src,
        dst_ref=dst,
        send_sem=send_sem,
        recv_sem=recv_sem,
        device_id=device,
        device_id_type=MESH,
    )


def await_bytes(ref, sem):
    pltpu.make_async_copy(ref, ref, sem).wait()


def chunks_of(count, size=ROWS):
    return [slice(first, first + size) for first in range(0, count, size)]


def by_eights(value):
    return value.reshape(value.shape[0] // 8, 8, value.shape[1])


def stack_sum(value):
    return jnp.sum(by_eights(value), 0)


def stack_max(value):
    return jnp.max(by_eights(value), 0)


def mean_of(parts, count):
    return jnp.sum(parts, 0, keepdims=True) / count


def norm_stats(read, count):
    total = jnp.zeros((8, BLOCK), F32)
    for span in chunks_of(count):
        total = total + stack_sum(read(span))
    mean = mean_of(total, count)
    square = jnp.zeros((8, BLOCK), F32)
    for span in chunks_of(count):
        centred = read(span) - mean
        square = square + stack_sum(centred * centred)
    return mean, lax.rsqrt(mean_of(square, count) + EPSILON)


def gelu_parts(values):
    bell = jnp.exp(-0.5 * values * values)
    reach = jnp.abs(values) * 0.7071067811865476
    inv = 1.0 / (1.0 + 0.3275911 * reach)
    poly = inv * (
        0.254829592
        + inv * (-0.284496736 + inv * (1.421413741 + inv * (-1.453152027 + inv * 1.061405429)))
    )
    tail = 0.5 * poly * bell
    cdf = jnp.where(values >= 0.0, 1.0 - tail, tail)
    return values * cdf, cdf + values * bell * 0.3989422804014327


def fold(value):
    return value[:, 0:128] + value[:, 128:256]


def block_of(index):
    return pl.ds(pl.multiple_of(index * BLOCK, BLOCK), BLOCK)


def pair_of(index):
    return pl.ds(pl.multiple_of(index * PAIR, PAIR), PAIR)


def flip_weights(w, wt, layer, start, width, target=0):
    def body(index, carry):
        cols = pl.ds(pl.multiple_of(start + index * 128, 128), 128)
        rows = pl.ds(pl.multiple_of(target + index * 128, 128), 128)
        tile = w[layer, :, :, :, cols]
        wt[rows, :] = tile.reshape(tile.shape[0] * tile.shape[1] * tile.shape[2], 128).T
        return carry

    lax.fori_loop(0, width // 128, body, 0)


def whole(w, layer, start, width):
    tile = w[layer, :, :, :, start : start + width]
    return tile.reshape(tile.shape[0] * tile.shape[1] * tile.shape[2], width)


def spread_biases(vecs, spread, rows):
    def body(group, carry):
        at = pl.ds(pl.multiple_of(group * rows, 8), 8)
        for kind in range(2):
            for head in range(6):
                to = pl.ds(pl.multiple_of(kind * 384 + head * HEAD + group * 8, 8), 8)
                lane = head_lane(kind, head)
                spread[to, 6:7] = vecs[at, lane : lane + 1]
        for unit in range(24):
            to = pl.ds(pl.multiple_of(768 + unit * HEAD + group * 8, 8), 8)
            lane = UNIT_LANE + unit
            spread[to, 6:7] = vecs[at, lane : lane + 1]
        return carry

    lax.fori_loop(0, GROUPS, body, 0)


def layers_kernel(
    share,
    clips,
    cot,
    gains_in,
    biases_in,
    heads_in,
    units_in,
    qkv_in,
    out_in,
    up_in,
    down_in,
    out,
    in_grad,
    landed_vec,
    landed_qkv,
    landed_out,
    landed_up,
    landed_down,
    cot_other,
    x_hbm,
    h_hbm,
    n1_hbm,
    n2_hbm,
    qkv_hbm,
    ctx_hbm,
    lse_hbm,
    act_hbm,
    slope_hbm,
    w,
    res,
    act,
    slope,
    n1,
    n2,
    low,
    qkv,
    ctx,
    dctx,
    lse,
    h_in,
    wt,
    send,
    recv,
    vecs,
    vec_grads,
    sums,
    spread,
    stage,
    shard,
    land_a,
    land_b,
    land_y,
    z_send,
    z_recv,
    x_send,
    x_recv,
    xb_send,
    xb_recv,
    y_send,
    y_recv,
    ya_send,
    ya_recv,
    gz_send,
    gz_recv,
    gx_send,
    gx_recv,
    gxb_send,
    gxb_recv,
    gy_send,
    gy_recv,
    gya_send,
    gya_recv,
    e_send,
    e_recv,
    own_sem,
    in_sem,
    cot_sem,
    out_sem,
    grad_sem,
    save_sem,
    load_sem,
    h_sem,
    ya_free,
    xb_free,
    x_free,
    y_free,
):
    place = Place(share)
    s, t, e, y = place.s, place.t, place.e, place.y
    primary, secondary = place.primary, jnp.logical_not(place.primary)
    width, frames = res.shape
    blocks = frames // BLOCK
    half = frames // 2
    quarter = half // 2
    rows = w.shape[3]
    low_rows = pl.ds(0, SPLIT)
    high_rows = pl.ds(SPLIT, rows - SPLIT)
    mine = pl.ds(pl.multiple_of(t * half, half), half)
    theirs = pl.ds(pl.multiple_of((1 - t) * half, half), half)

    own_loads = []
    for number, (first, many, kind, bias) in enumerate(PARTS):
        own_loads.append(
            pltpu.make_async_copy(
                qkv_in.at[0, "qkv".index(kind), :, pl.ds(bias % WIDE, many)],
                shard.at[:, pl.ds(QKV + first, many)],
                own_sem.at[1 + number],
            )
        )
    own_up = pltpu.make_async_copy(up_in.at[0], shard.at[:, pl.ds(UP, DOWN - UP)], own_sem.at[7])
    own_out = pltpu.make_async_copy(out_in.at[0], shard.at[:, pl.ds(OUT, UP - OUT)], own_sem.at[8])
    own_down = pltpu.make_async_copy(
        down_in.at[0], shard.at[:, pl.ds(DOWN, END - DOWN)], own_sem.at[9]
    )
    for copy in own_loads + [own_out, own_up, own_down]:
        copy.start()
    spread[0:32, :] = jnp.zeros((32, 128), F32)
    vec_grads[0:rows, :] = jnp.zeros((rows, 128), F32)
    spread[0:2, 0:rows] = gains_in[0].astype(F32)
    spread[2:6, 0:rows] = biases_in[0].astype(F32)
    for head in range(6):
        spread[8 + 2 * head : 10 + 2 * head, 0:8] = heads_in[0, head].astype(F32)
    vec_grads[0:rows, 0:8] = spread[0:8, :].T[0:rows, :]
    vec_grads[0:8, HEAD_LANE : HEAD_LANE + 12] = spread[8:24, :].T[0:8, 0:12]
    vec_grads[0:8, UNIT_LANE : UNIT_LANE + 24] = units_in[0].astype(F32)
    shard[:, VEC:QKV] = vec_grads[0:rows, :].astype(BF)

    place.greet()

    VECTORS = CHUNKS

    def piece_cols(piece):
        if isinstance(piece, int) and piece == VECTORS:
            return pl.ds(VEC, QKV)
        return pl.ds(pl.multiple_of(QKV + piece * WIDE, 128), WIDE)

    def gather_rows(piece):
        split = GATHER_SPLITS[piece % 2]
        return pl.ds(0, split), pl.ds(split, rows - split)

    def pieces_of(step):
        layer, piece = step // CHUNKS, step % CHUNKS
        return layer, (VECTORS, piece) if piece == 0 else (piece,)

    def z_copies(piece):
        cols = piece_cols(piece)
        copies = []
        for step in range(LINES):
            copies.append(
                remote(
                    shard.at[:, cols],
                    w.at[s, e, y, :, cols],
                    z_send.at[piece, step],
                    z_recv.at[s, piece, e],
                    (t, place.row_of(place.line(step), y), t),
                )
            )
        local = pltpu.make_async_copy(
            shard.at[:, cols], w.at[s, e, y, :, cols], z_recv.at[s, piece, e]
        )
        return copies, local

    def z_start(step):
        layer, pieces = pieces_of(step)

        @pl.when(s == layer)
        def _():
            for piece in pieces:
                copies, local = z_copies(piece)

                @pl.when(primary)
                def _():
                    local.start()

                @pl.when(secondary)
                def _():
                    copies[0].start()

                for copy in copies[1:]:
                    copy.start()

    def z_finish(piece):
        copies, _ = z_copies(piece)

        @pl.when(secondary)
        def _():
            copies[0].wait_send()

        for copy in copies[1:]:
            copy.wait_send()

    def x_copy(layer, piece):
        part = w.at[layer, :, y, :, piece_cols(piece)]
        return remote(part, part, x_send.at[layer, piece], x_recv.at[layer, piece], place.across)

    def y_copy(layer, piece):
        part = w.at[layer, :, y, :, piece_cols(piece)]
        return remote(part, part, y_send.at[layer, piece], y_recv.at[layer, piece], place.beside)

    def xb_copy(layer, piece):
        part = w.at[layer, :, 1 - y, gather_rows(piece)[1], piece_cols(piece)]
        return remote(part, part, xb_send.at[layer, piece], xb_recv.at[layer, piece], place.across)

    def ya_copy(layer, piece):
        part = w.at[layer, :, y, gather_rows(piece)[0], piece_cols(piece)]
        return remote(part, part, ya_send.at[layer, piece], ya_recv.at[layer, piece], place.beside)

    def step_z(step):
        layer, pieces = pieces_of(step)

        @pl.when(primary)
        def _():
            for piece in pieces:
                cols = piece_cols(piece)
                for line in range(LINES):
                    await_bytes(w.at[layer, line, y, :, cols], z_recv.at[layer, piece, line])
                x_copy(layer, piece).start()
                y_copy(layer, piece).start()

    def step_plane(step):
        layer, pieces = pieces_of(step)

        @pl.when(primary)
        def _():
            for piece in pieces:
                await_bytes(w.at[layer, :, 1 - y, :, piece_cols(piece)], y_recv.at[layer, piece])
                xb_copy(layer, piece).start()

        @pl.when(secondary)
        def _():
            for piece in pieces:
                await_bytes(w.at[layer, :, y, :, piece_cols(piece)], x_recv.at[layer, piece])
                ya_copy(layer, piece).start()

    def tick(step):
        if step + 3 < 2 * CHUNKS:
            step_z(step + 3)
        if step + 8 < 2 * CHUNKS:
            z_start(step + 8)
        step_plane(step)

    def complete(*steps):
        @pl.when(secondary)
        def _():
            for step in steps:
                layer, pieces = pieces_of(step)
                for piece in pieces:
                    cols = piece_cols(piece)
                    first, second = gather_rows(piece)
                    await_bytes(w.at[layer, :, 1 - y, second, cols], xb_recv.at[layer, piece])
                    await_bytes(w.at[layer, :, 1 - y, first, cols], ya_recv.at[layer, piece])

    def at_turns(turns):
        def beside(index):
            for turn, steps in turns.items():

                @pl.when(index == turn)
                def _():
                    for step in steps:
                        step()

        return beside

    def ticks(turns):
        return at_turns({turn: (functools.partial(tick, step),) for turn, step in turns.items()})

    kept = {
        "x": (n2.at[pl.ds(0, width), :], x_hbm),
        "h": (res, h_hbm),
        "n1": (n1.at[pl.ds(0, width), :], n1_hbm),
        "n2": (n2.at[pl.ds(0, width), :], n2_hbm),
        "qkv": (qkv, qkv_hbm),
        "ctx": (ctx, ctx_hbm),
        "lse": (lse, lse_hbm),
        "act": (act, act_hbm),
        "slope": (slope, slope_hbm),
    }
    names = tuple(kept)

    def save(name, layer):
        src, dst = kept[name]
        if name in ("x", "h"):
            dst = dst.at[layer]
        return pltpu.make_async_copy(src, dst, save_sem.at[names.index(name), layer])

    def load(name, layer=0):
        dst, src = kept[name]
        if name == "x":
            dst, src = act.at[pl.ds(0, width), :], src.at[layer]
        return pltpu.make_async_copy(src, dst, load_sem.at[names.index(name)])

    def load_h(layer, index):
        slot = lax.rem(index, 2)
        return pltpu.make_async_copy(
            h_hbm.at[layer, :, block_of(index)], h_in.at[slot], h_sem.at[slot]
        )

    my_quarter = pl.ds(s * quarter, quarter)
    my_rows = pl.ds(pl.multiple_of((1 - t) * half + s * quarter, quarter), quarter)

    def clip_across():
        there = pl.ds(pl.multiple_of(t * half + s * quarter, quarter), quarter)
        return remote(
            clips.at[1 - t, my_quarter, :],
            stage.at[there, :],
            in_sem.at[0],
            in_sem.at[1],
            place.across,
        )

    def clip_core():
        part = stage.at[my_rows, :]
        return remote(part, part, in_sem.at[2], in_sem.at[3], place.core)

    def cot_across():
        return remote(
            cot.at[1 - t, my_quarter, :],
            cot_other.at[my_quarter, :],
            cot_sem.at[0],
            cot_sem.at[1],
            place.across,
        )

    def cot_core():
        part = cot_other.at[my_quarter, :]
        return remote(part, part, cot_sem.at[2], cot_sem.at[3], place.core)

    def exchange(kind, index, slot):
        return remote(
            send.at[kind, index],
            recv.at[kind, index],
            e_send.at[slot, index],
            e_recv.at[slot, index],
            place.core,
        )

    def result_copies(ref, first):
        local = pltpu.make_async_copy(stage.at[mine, :], ref.at[0, t], out_sem.at[first])
        away = remote(
            stage.at[theirs, :],
            ref.at[0, t],
            out_sem.at[first + 1],
            out_sem.at[first + 2],
            place.across,
        )
        return local, away

    def grad_copies(index):
        place_in = lax.rem(index, blocks // 2)
        part = in_grad.at[0, t, pl.ds(pl.multiple_of(place_in * BLOCK, BLOCK), BLOCK), :]
        src = stage.at[block_of(index), :]
        local = pltpu.make_async_copy(src, part, grad_sem.at[0, place_in])
        away = remote(
            src, part, grad_sem.at[1, place_in], grad_sem.at[2, place_in], place.across
        )
        return local, away

    def emit(layer, ref, first):
        @pl.when(s == layer)
        def _():
            for copy in result_copies(ref, first):
                copy.start()

    for copy in own_loads:
        copy.wait()
    for step in range(3):
        z_start(step)
    n1[width:, :] = jnp.ones((ONES, frames), BF)
    n2[width:, :] = jnp.ones((ONES, frames), BF)
    own_clip = pltpu.make_async_copy(clips.at[t], stage.at[mine, :], in_sem.at[4])
    own_clip.start()
    clip_across().start()
    own_out.wait()
    own_up.wait()
    own_down.wait()
    for step in (3, 4):
        z_start(step)

    def take_clip(first):
        def body(index, carry):
            at = pl.ds(pl.multiple_of(first + index * BLOCK, BLOCK), BLOCK)
            tile = stage[at, :].T
            n2[0:width, at] = tile
            res[:, at] = tile.astype(F32)
            return carry

        lax.fori_loop(0, half // BLOCK, body, 0)

    own_clip.wait()
    take_clip(t * half)
    clip_across().wait()
    clip_core().start()
    step_z(0)
    z_start(5)
    step_z(1)
    z_start(6)
    clip_core().wait()
    take_clip((1 - t) * half)
    save("x", 0).start()
    step_plane(0)
    step_z(2)
    z_start(7)
    step_plane(1)
    step_z(3)
    z_start(8)
    step_plane(2)
    cot_across().start()
    step_z(4)
    z_start(9)
    step_z(5)
    z_start(10)

    def project(pair):
        for index in (2 * pair, 2 * pair + 1):
            cols = block_of(index)
            mean, scale = norm_stats(lambda span: res[span, cols], width)
            for span in chunks_of(width):
                hat = (res[span, cols] - mean) * scale
                n1[span, cols] = (hat * vecs[span, 0:1] + vecs[span, 2:3]).astype(BF)
        cols = pair_of(pair)
        for first, many, kind, bias in PARTS:
            value = mm(wt[first : first + many, :], n1[0:width, cols])
            for span in chunks_of(many):
                part = value[span, :]
                if kind != "k":
                    part = part + spread[bias + span.start : bias + span.stop, 6:7]
                if kind == "q":
                    part = part * 0.125
                qkv[first + span.start : first + span.stop, cols] = part.astype(BF)

    def send_pair(kind, pair, slot, value):
        for part in range(2):
            index = 2 * pair + part
            send[kind, index] = value[:, part * BLOCK : (part + 1) * BLOCK].astype(BF)
            exchange(kind, index, slot).start()

    def head_rows(head, first):
        return pl.ds(pl.multiple_of(first + head * HEAD, HEAD), HEAD)

    def attend(layer, turns, later_turns):
        def heads_of(first_head, base, stride, beside):
            def one_head(index_in, carry):
                head = first_head + index_in
                q_rows = head_rows(index_in, base)
                k_rows = head_rows(index_in, base + stride)
                v_rows = head_rows(index_in, base + 2 * stride)
                c_rows = head_rows(head, 0)
                keys = qkv[k_rows, :].T
                for index in range(blocks):
                    cols = slice(index * BLOCK, (index + 1) * BLOCK)
                    queries = qkv[q_rows, cols]
                    tiles = []
                    top = None
                    for tile in chunks_of(frames, BLOCK):
                        scores = mm(keys[tile, :], queries)
                        for span in chunks_of(BLOCK):
                            peak = stack_max(scores[span, :])
                            top = peak if top is None else jnp.maximum(top, peak)
                        tiles.append(scores)
                    top = jnp.max(top, 0, keepdims=True)
                    total = jnp.zeros((8, BLOCK), F32)
                    mixed = jnp.zeros((HEAD, BLOCK), F32)
                    for tile, scores in zip(chunks_of(frames, BLOCK), tiles):
                        soft = []
                        for span in chunks_of(BLOCK):
                            part = jnp.exp(scores[span, :] - top)
                            total = total + stack_sum(part)
                            soft.append(part.astype(BF))
                        mixed = mixed + mm(qkv[v_rows, tile], jnp.concatenate(soft, 0))
                    total = jnp.sum(total, 0, keepdims=True)
                    ctx[c_rows, cols] = (mixed / total).astype(BF)
                    lse[pl.ds(head, 1), cols] = top + jnp.log(total)
                beside(index_in)
                return carry

            return one_head

        lax.fori_loop(0, 4, heads_of(0, 0, 256, ticks(turns)), 0)
        lax.fori_loop(0, 2, heads_of(4, 768, 128, ticks(later_turns)), 0)

    def out_project(layer, turns):
        beside = ticks(turns)

        def body(index, carry):
            part = mm(whole(w, layer, OUT, 384), ctx[:, pair_of(index)])
            send_pair(0, index, 2 * layer, part)
            beside(index)
            return carry

        lax.fori_loop(0, blocks // 2, body, 0)

    def middle_norm(layer, turns):
        beside = ticks(turns)

        def body(index, carry):
            cols = block_of(index)
            exchange(0, index, 2 * layer).wait()
            for span in chunks_of(width):
                added = send[0, index, span, :].astype(F32) + recv[0, index, span, :].astype(F32)
                res[span, cols] = res[span, cols] + added + vecs[span, 3:4]
            mean, scale = norm_stats(lambda span: res[span, cols], width)
            for span in chunks_of(width):
                hat = (res[span, cols] - mean) * scale
                n2[span, cols] = (hat * vecs[span, 1:2] + vecs[span, 4:5]).astype(BF)
            beside(index)
            return carry

        lax.fori_loop(0, blocks, body, 0)

    def hidden_part(layer, part):
        flip_weights(w, wt, layer, UP + part * WIDE, WIDE, part * WIDE)
        units = slice(part * WIDE, (part + 1) * WIDE)

        def body(index, carry):
            cols = pair_of(index)
            pre = mm(wt[units, :], n2[0:width, cols])
            for span in chunks_of(WIDE):
                first = part * WIDE + span.start
                bias = spread[768 + first : 768 + first + ROWS, 6:7]
                value, steep = gelu_parts(pre[span, :] + bias)
                act[first : first + ROWS, cols] = value.astype(BF)
                slope[first : first + ROWS, cols] = steep.astype(BF)
            return carry

        lax.fori_loop(0, blocks // 2, body, 0)

    def down_project(layer, turns):
        beside = ticks(turns)

        def body(index, carry):
            part = mm(whole(w, layer, DOWN, 1536), act[:, pair_of(index)])
            send_pair(1, index, 2 * layer + 1, part)
            beside(index)
            return carry

        lax.fori_loop(0, blocks // 2, body, 0)

    def layer_end(layer, index, span):
        added = send[1, index, span, :].astype(F32) + recv[1, index, span, :].astype(F32)
        return (res[span, block_of(index)] + added + vecs[span, 5:6]).astype(BF)

    def take_vectors(layer):
        vecs[...] = whole(w, layer, VEC, 128).astype(F32)
        spread_biases(vecs, spread, rows)

    def project_all(layer, turns):
        beside = ticks(turns)
        flip_weights(w, wt, layer, QKV, 1152)

        def body(index, carry):
            project(index)
            beside(index)
            return carry

        lax.fori_loop(0, blocks // 2, body, 0)
        if layer == 0:
            save("n1", 0).start()
            save("qkv", 0).start()

    complete(0, 1, 2)
    take_vectors(0)
    project_all(0, {0: 3, 1: 4})
    cot_across().wait()
    cot_core().start()
    own_cot = pltpu.make_async_copy(cot.at[t], stage.at[mine, :], cot_sem.at[5])
    own_cot.start()
    attend(0, {0: 5, 2: 6}, {0: 7})
    save("ctx", 0).start()
    save("lse", 0).start()
    cot_core().wait()
    load_cot = pltpu.make_async_copy(cot_other, stage.at[theirs, :], cot_sem.at[4])
    load_cot.start()
    complete(3)
    out_project(0, {1: 8})
    load_cot.wait()
    own_cot.wait()

    sums[3] = jnp.zeros_like(sums[3])

    def take_cot(index, carry):
        low[:, block_of(index)] = stage[block_of(index), :].T
        for span in chunks_of(width):
            sums[3, span, :] += fold(low[span, block_of(index)].astype(F32))
        return carry

    lax.fori_loop(0, blocks, take_cot, 0)
    save("x", 0).wait()
    middle_norm(0, {1: 9})
    save("h", 0).start()
    save("n2", 0).start()
    for part in range(4):
        complete(4 + part)
        hidden_part(0, part)
        tick(10 + part)
    save("act", 0).start()
    save("slope", 0).start()
    complete(8, 9, 10, 11)
    down_project(0, {1: 14})
    for name in ("n1", "qkv", "h", "n2"):
        save(name, 0).wait()

    def finish_body(index, carry):
        exchange(1, index, 1).wait()
        cols = block_of(index)
        for span in chunks_of(width):
            rows_out = layer_end(0, index, span)
            n2[span, cols] = rows_out
            res[span, cols] = rows_out.astype(F32)

        @pl.when(s == 0)
        def _():
            stage[cols, :] = n2[0:width, cols].T

        return carry

    lax.fori_loop(0, blocks, finish_body, 0)
    save("x", 1).start()
    complete(12, 13, 14)
    take_vectors(1)
    project_all(1, {0: 15, 1: 16})
    save("ctx", 0).wait()
    save("lse", 0).wait()
    attend(1, {0: 17, 2: 18}, {0: 19})
    complete(15)
    out_project(1, {1: 20})
    save("x", 1).wait()
    middle_norm(1, {1: 21})
    save("h", 1).start()
    save("act", 0).wait()
    save("slope", 0).wait()
    for part in range(4):
        complete(16 + part)
        hidden_part(1, part)
        if part < 2:
            tick(22 + part)
    for part in range(4):
        complete(20 + part)
        flip_weights(w, wt, 1, DOWN + part * WIDE, WIDE, part * WIDE)
    emit(0, out, 0)
    down_project(1, {})

    def gya_copy(layer, piece):
        cols = piece_cols(piece)
        return remote(
            w.at[layer, :, 1 - y, low_rows, cols],
            land_a.at[:, low_rows, cols],
            gya_send.at[layer, piece],
            gya_recv.at[layer, piece],
            place.beside,
        )

    def gxb_copy(layer, piece):
        cols = piece_cols(piece)
        return remote(
            w.at[layer, :, 1 - y, high_rows, cols],
            land_b.at[:, :, cols],
            gxb_send.at[layer, piece],
            gxb_recv.at[layer, piece],
            place.across,
        )

    def gx_copy(layer, piece):
        cols = piece_cols(piece)
        return remote(
            w.at[layer, :, y, :, cols],
            land_a.at[:, :, cols],
            gx_send.at[layer, piece],
            gx_recv.at[layer, piece],
            place.across,
        )

    def gy_copy(layer, piece):
        cols = piece_cols(piece)
        return remote(
            w.at[layer, :, 1 - y, :, cols],
            land_y.at[:, :, cols],
            gy_send.at[layer, piece],
            gy_recv.at[layer, piece],
            place.beside,
        )

    def landed_part(piece):
        if piece == VECTORS:
            return landed_vec
        ref, first = (
            (landed_qkv, 0)
            if piece < 3
            else (landed_out, 3)
            if piece < 4
            else (landed_up, 4)
            if piece < 8
            else (landed_down, 8)
        )
        return ref.at[:, :, pl.ds((piece - first) * WIDE, WIDE)]

    def gz_copies(layer, piece):
        cols = piece_cols(piece)
        target = landed_part(piece)
        copies = []
        for step in range(LINES):
            line = place.line(step)
            copies.append(
                remote(
                    w.at[layer, line, y, :, cols],
                    target.at[e],
                    gz_send.at[layer, piece, step],
                    gz_recv.at[piece, e],
                    (layer, place.row_of(line, y), t),
                )
            )
        local = pltpu.make_async_copy(
            w.at[layer, e, y, :, cols], target.at[e], gz_recv.at[piece, e]
        )
        return copies, local

    def add_rows(layer, piece, which, span, lands):
        cols = piece_cols(piece)
        first, count = span
        for line in range(LINES):
            total = w[layer, line, which, pl.ds(first, count), cols].astype(F32)
            for land, offset in lands:
                total = total + land[line, pl.ds(offset, count), cols].astype(F32)
            w[layer, line, which, pl.ds(first, count), cols] = total.astype(BF)

    def signal(sem, layer, piece, device):
        if layer == 1:
            pl.semaphore_signal(sem.at[piece], inc=1, device_id=device, device_id_type=MESH)

    def credit(sem, layer, piece):
        if layer == 0:
            pl.semaphore_wait(sem.at[piece], 1)

    def step_a(layer, piece):
        @pl.when(secondary)
        def _():
            credit(ya_free, layer, piece)
            gya_copy(layer, piece).start()
            credit(xb_free, layer, piece)
            gxb_copy(layer, piece).start()

    def step_b(layer, piece):
        cols = piece_cols(piece)

        @pl.when(secondary)
        def _():
            await_bytes(land_a.at[:, low_rows, cols], gya_recv.at[layer, piece])
            add_rows(layer, piece, y, (0, SPLIT), [(land_a, 0)])
            signal(ya_free, layer, piece, place.beside)
            credit(x_free, layer, piece)
            gx_copy(layer, piece).start()

        @pl.when(primary)
        def _():
            await_bytes(land_b.at[:, :, cols], gxb_recv.at[layer, piece])
            add_rows(layer, piece, 1 - y, (SPLIT, rows - SPLIT), [(land_b, 0)])
            signal(xb_free, layer, piece, place.across)
            credit(y_free, layer, piece)
            gy_copy(layer, piece).start()

    def step_c(layer, piece):
        cols = piece_cols(piece)

        @pl.when(primary)
        def _():
            await_bytes(land_a.at[:, :, cols], gx_recv.at[layer, piece])
            await_bytes(land_y.at[:, :, cols], gy_recv.at[layer, piece])
            add_rows(layer, piece, y, (0, rows), [(land_a, 0), (land_y, 0)])
            signal(x_free, layer, piece, place.across)
            signal(y_free, layer, piece, place.beside)
            copies, local = gz_copies(layer, piece)

            @pl.when(s == layer)
            def _():
                local.start()

            @pl.when(s != layer)
            def _():
                copies[0].start()

            for copy in copies[1:]:
                copy.start()

    def store_grads(layer, start, count, value):
        w[layer, :, :, :, pl.ds(start, count)] = value.astype(BF).reshape(
            w.shape[1], w.shape[2], rows, count
        )

    def mlp_back(layer, beside):
        def body(index, carry):
            cols = pair_of(index)
            for part in range(4):
                units = slice(part * WIDE, (part + 1) * WIDE)
                grad = mm(wt[units, :], low[:, cols])
                for span in chunks_of(WIDE):
                    rows_in = slice(units.start + span.start, units.start + span.stop)
                    steep = slope[rows_in, cols].astype(F32)
                    slope[rows_in, cols] = (grad[span, :] * steep).astype(BF)
            term = mm(whole(w, layer, UP, 1536), slope[:, cols])
            send_pair(0, index, 4 + 2 * layer, term)
            beside(index)
            return carry

        lax.fori_loop(0, blocks // 2, body, 0)

    def outer(layer, start, left, right, first, many, before, beside):
        def body(index, carry):
            before(index)
            base = index * PAIR
            span = pl.ds(pl.multiple_of(first + base, 128), PAIR)
            value = mmt(left[...], right[span, :])
            store_grads(layer, pl.multiple_of(start + base, 128), PAIR, value[0:width, :])
            if left.shape[0] > width:
                to = pl.ds(pl.multiple_of(768 + base, BLOCK), PAIR)
                spread[to, 0:8] = value[width : width + 8, :].T
            beside(index)
            return carry

        lax.fori_loop(0, many // PAIR, body, 0)

    def turned(turn):
        return lax.rem(turn + (1 - t) * (blocks // 2), blocks)

    def norm_back(layer, kind, gain_lane, source, put, finish, beside):
        sums[0:3] = jnp.zeros((3, width, 128), F32)

        def body(turn, carry):
            index = turned(turn)
            cols = block_of(index)
            read = source(index)
            mean, scale = norm_stats(read, width)
            exchange(kind, index, 4 + 2 * layer + kind).wait()
            first = jnp.zeros((8, BLOCK), F32)
            second = jnp.zeros((8, BLOCK), F32)

            def terms(span):
                hat = (read(span) - mean) * scale
                grad = send[kind, index, span, :].astype(F32)
                grad = grad + recv[kind, index, span, :].astype(F32)
                return hat, grad, grad * vecs[span, gain_lane : gain_lane + 1]

            for span in chunks_of(width):
                hat, grad, scaled = terms(span)
                sums[0, span, :] += fold(grad * hat)
                sums[1, span, :] += fold(grad)
                first = first + stack_sum(scaled)
                second = second + stack_sum(scaled * hat)
            level = mean_of(first, width)
            slant = mean_of(second, width)
            for span in chunks_of(width):
                hat, _, scaled = terms(span)
                put(span, cols, res[span, cols] + scale * (scaled - level - hat * slant))
            finish(index)
            beside(turn)
            return carry

        lax.fori_loop(0, blocks, body, 0)

    def row_sums(value):
        return jnp.sum(value, 1, keepdims=True)

    def attend_back(first_head, many, base, stride, beside):
        def one_head(index_in, carry):
            head = first_head + index_in
            q_rows = head_rows(index_in, base)
            k_rows = head_rows(index_in, base + stride)
            v_rows = head_rows(index_in, base + 2 * stride)
            c_rows = head_rows(head, 0)
            keys = qkv[k_rows, :].T
            values = qkv[v_rows, :].T
            flat_queries = qkv[q_rows, :].T
            flat_grads = dctx[c_rows, :].T
            level = lse[pl.ds(head, 1), :]
            inner = jnp.sum(
                dctx[c_rows, :].astype(F32) * ctx[c_rows, :].astype(F32), 0, keepdims=True
            )
            step = jnp.zeros((HEAD, frames), F32)
            for tile in chunks_of(frames, BLOCK):
                soft = []
                score_grad = []
                for cols in chunks_of(frames, BLOCK):
                    scores = mm(keys[tile, :], qkv[q_rows, cols])
                    soft_grad = mm(values[tile, :], dctx[c_rows, cols])
                    soft_parts = []
                    grad_parts = []
                    for part in chunks_of(BLOCK):
                        strength = jnp.exp(scores[part, :] - level[:, cols])
                        soft_parts.append(strength.astype(BF))
                        strength = strength * (soft_grad[part, :] - inner[:, cols])
                        grad_parts.append(strength.astype(BF))
                    soft.append(jnp.concatenate(soft_parts, 0))
                    score_grad.append(jnp.concatenate(grad_parts, 0))
                soft = jnp.concatenate(soft, 1)
                score_grad = jnp.concatenate(score_grad, 1)
                step = step + mm(qkv[k_rows, tile], score_grad)
                slope[k_rows, tile] = mm(score_grad, flat_queries).astype(BF).T
                slope[v_rows, tile] = mm(soft, flat_grads).astype(BF).T
            slope[q_rows, :] = (step * 0.125).astype(BF)
            beside(index_in)
            return carry

        lax.fori_loop(0, many, one_head, 0)

    def keep_sums(first, value):
        for start, many, kind, bias in PARTS:
            offset = start - first
            if kind != "k" and 0 <= offset < value.shape[1]:
                spread[bias : bias + many, 0:8] = value[
                    width : width + 8, offset : offset + many
                ].T

    def collect_biases():
        def body(group, carry):
            to = pl.ds(pl.multiple_of(group * rows, 8), 8)
            for kind in range(2):
                for head in range(6):
                    at = pl.ds(pl.multiple_of(kind * 384 + head * HEAD + group * 8, 8), 8)
                    lane = head_lane(kind, head)
                    vec_grads[to, lane : lane + 1] = spread[at, 6:7]
            for unit in range(24):
                at = pl.ds(pl.multiple_of(768 + unit * HEAD + group * 8, 8), 8)
                lane = UNIT_LANE + unit
                vec_grads[to, lane : lane + 1] = spread[at, 6:7]
            return carry

        lax.fori_loop(0, GROUPS, body, 0)

    def nothing(index):
        del index

    def finish_gather(layer, piece):
        @pl.when(primary)
        def _():
            x_copy(layer, piece).wait_send()
            y_copy(layer, piece).wait_send()
            xb_copy(layer, piece).wait_send()

        @pl.when(secondary)
        def _():
            ya_copy(layer, piece).wait_send()

    def send_first_grad():
        @pl.when(s == 1)
        def _():
            for place_in in range(blocks // 2):
                _, away = grad_copies((1 - t) * (blocks // 2) + place_in)
                away.start()

    def last_body(index, carry):
        exchange(1, index, 3).wait()

        @pl.when(s == 1)
        def _():
            for span in chunks_of(width, 128):
                stage[block_of(index), span] = layer_end(1, index, span).T

        return carry

    for layer in (1, 0):
        later = layer == 0
        if later:
            load_h(layer, turned(0)).start()
            load("act").wait()
            vecs[...] = whole(w, layer, VEC, 128).astype(F32)
            flip_weights(w, wt, layer, DOWN, 1536)
        vec_grads[...] = jnp.zeros_like(vec_grads)

        def a(piece, layer=layer):
            return lambda: step_a(layer, piece)

        def b(piece, layer=layer):
            return lambda: step_b(layer, piece)

        def c(piece, layer=layer):
            return lambda: step_c(layer, piece)

        if later:
            before = nothing
            early = at_turns(
                {
                    0: (a(8),),
                    1: (a(9), lambda: step_b(1, VECTORS)),
                    2: (a(10), a(11)),
                }
            )
        else:
            waits = [functools.partial(finish_gather, 1, piece) for piece in (8, 9, 10, 11)]
            before = at_turns({0: waits[:2], 1: waits[2:3], 2: waits[3:]})
            early = at_turns({0: (a(8),), 1: (a(9),), 2: (a(10), a(11))})
        outer(layer, DOWN, low, act, 0, 1536, before, early)
        load("x", layer).start()
        vec_grads[:, 5:6] = row_sums(sums[3])
        if not later:
            lax.fori_loop(0, blocks, last_body, 0)
            emit(1, out, 0)
            save("h", 1).wait()
            load_h(layer, turned(0)).start()
            res[...] = low[...].astype(F32)
            for piece in range(CHUNKS + 1):
                z_finish(piece)
                finish_gather(0, piece)
                if piece < 8 or piece == VECTORS:
                    finish_gather(1, piece)
        else:
            load("slope").wait()

        mlp_back(layer, at_turns({0: (b(8),)}))
        if later:
            load("n2").wait()
        left = (lambda: step_c(1, VECTORS),) if later else ()
        drain = at_turns({0: (a(4),) + left, 1: (a(5), b(9)), 2: (a(6), a(7))})
        outer(layer, UP, n2, slope, 0, 1536, nothing, drain)
        flip_weights(w, wt, layer, OUT, 384)

        def hidden_in(index, layer=layer):
            turn = lax.rem(index + (1 - t) * (blocks // 2), blocks)

            @pl.when(turn + 1 < blocks)
            def _():
                load_h(layer, turned(turn + 1)).start()

            load_h(layer, index).wait()
            slot = lax.rem(index, 2)
            return lambda span: h_in[slot, span, :]

        def hidden_put(span, cols, total):
            res[span, cols] = total
            rounded = total.astype(BF)
            low[span, cols] = rounded
            sums[2, span, :] += fold(rounded.astype(F32))

        drain = at_turns({0: (b(10),), 1: (b(11),), 2: (b(4), b(5)), 3: (c(8),)})
        norm_back(layer, 0, 1, hidden_in, hidden_put, nothing, drain)

        def context_back(index, carry):
            cols = pair_of(index)
            dctx[:, cols] = mm(wt[0:384, :], low[:, cols]).astype(BF)
            return carry

        lax.fori_loop(0, blocks // 2, context_back, 0)
        vec_grads[:, 1:2] = row_sums(sums[0])
        vec_grads[:, 4:5] = row_sums(sums[1])
        vec_grads[:, 3:4] = row_sums(sums[2])
        if later:
            for name in ("ctx", "qkv", "lse"):
                load(name).wait()
        store_grads(layer, OUT, 384, mmt(low[...], ctx[...]))
        step_a(layer, 3)
        over = (send_first_grad,) if later else ()
        drain = at_turns({0: (c(9),), 1: (b(6), c(10), c(11)) + over, 2: (c(4), c(5))})
        attend_back(0, 4, 0, 256, drain)
        if later:
            load("n1").wait()
        wt[0:768, :] = whole(w, layer, QKV, 768)

        for first, many in ((0, 512), (512, 256)):
            value = mmt(n1[...], slope[first : first + many, :])
            store_grads(layer, QKV + first, many, value[0:width, :])
            keep_sums(first, value)
        step_a(layer, 0)
        step_a(layer, 1)
        step_b(layer, 7)
        step_b(layer, 3)
        step_c(layer, 6)
        attend_back(4, 2, 768, 128, nothing)

        def first_body(index, carry, layer=layer):
            cols = pair_of(index)
            term = mm(wt[0:768, :], slope[0:768, cols])
            term = term + mm(whole(w, layer, QKV + 768, WIDE), slope[768:1152, cols])
            send_pair(1, index, 5 + 2 * layer, term)
            return carry

        lax.fori_loop(0, blocks // 2, first_body, 0)
        step_b(layer, 0)
        step_c(layer, 7)
        value = mmt(n1[...], slope[768:1152, :])
        store_grads(layer, QKV + 768, WIDE, value[0:width, :])
        keep_sums(768, value)
        step_a(layer, 2)
        step_b(layer, 1)
        step_c(layer, 3)
        collect_biases()
        if layer == 1:
            for name in ("slope", "n1", "n2", "ctx", "qkv", "lse"):
                load(name).start()
        load("x", layer).wait()

        @pl.when(s == layer)
        def _():
            local, away = result_copies(out, 0)
            local.wait()
            away.wait_send()

        def rows_x(index):
            return lambda span: act[span, block_of(index)].astype(F32)

        def rows_put(span, cols, total, layer=layer):
            rounded = total.astype(BF)
            low[span, cols] = rounded
            if layer == 1:
                res[span, cols] = rounded.astype(F32)
                sums[2, span, :] += fold(rounded.astype(F32))

        def rows_out(index, layer=layer):
            @pl.when(s == layer)
            def _():
                stage[block_of(index), :] = low[:, block_of(index)].T
                local, away = grad_copies(index)

                @pl.when(index // (blocks // 2) == t)
                def _():
                    local.start()

                if layer == 0:

                    @pl.when(index // (blocks // 2) != t)
                    def _():
                        away.start()

        drain = at_turns({0: (b(2), c(0)), 2: (c(1),)})
        norm_back(layer, 1, 0, rows_x, rows_put, rows_out, drain)
        if layer == 1:
            load("act").start()
        vec_grads[:, 0:1] = row_sums(sums[0])
        vec_grads[:, 2:3] = row_sums(sums[1])
        sums[3] = sums[2]
        store_grads(layer, VEC, 128, vec_grads[...])
        step_a(layer, VECTORS)
        step_c(layer, 2)

    step_b(0, VECTORS)

    step_c(0, VECTORS)

    def finish_scatter(piece):
        for layer in range(2):

            @pl.when(secondary)
            def _():
                gya_copy(layer, piece).wait_send()
                gxb_copy(layer, piece).wait_send()
                gx_copy(layer, piece).wait_send()

            @pl.when(primary)
            def _():
                gy_copy(layer, piece).wait_send()
                copies, _ = gz_copies(layer, piece)

                @pl.when(s != layer)
                def _():
                    copies[0].wait_send()

                for copy in copies[1:]:
                    copy.wait_send()

    for piece in range(CHUNKS + 1):
        finish_scatter(piece)
        for line in range(LINES):
            await_bytes(landed_part(piece).at[line], gz_recv.at[piece, line])

    _, away = result_copies(out, 0)
    away.wait_recv()
    for index in range(blocks // 2):
        local, away = grad_copies(index)
        local.wait()
        away.wait()


def layers_call(share, clips, cotangent, shards, dims):
    width, frames, hidden_units, heads_width = dims
    rows = width // GROUPS
    sem = pltpu.SemaphoreType.DMA
    free = pltpu.SemaphoreType.REGULAR
    packed = (2, LINES, 2, rows, END)
    blocks = frames // BLOCK
    shape = jax.ShapeDtypeStruct
    outs = [
        shape((1,) + clips.shape, BF),
        shape((1,) + clips.shape, BF),
        shape((LINES, rows, QKV - VEC), BF),
        shape((LINES, rows, OUT - QKV), BF),
        shape((LINES, rows, UP - OUT), BF),
        shape((LINES, rows, DOWN - UP), BF),
        shape((LINES, rows, END - DOWN), BF),
        shape(clips.shape[1:], BF),
        shape((2, width, frames), BF),
        shape((2, width, frames), F32),
        shape((width, frames), BF),
        shape((width, frames), BF),
        shape((3 * heads_width, frames), BF),
        shape((heads_width, frames), BF),
        shape((8, frames), F32),
        shape((hidden_units, frames), BF),
        shape((hidden_units, frames), BF),
    ]
    scratch = [
        pltpu.VMEM(packed, BF),
        pltpu.VMEM((width, frames), F32),
        pltpu.VMEM((hidden_units, frames), BF),
        pltpu.VMEM((hidden_units, frames), BF),
        pltpu.VMEM((width + ONES, frames), BF),
        pltpu.VMEM((width + ONES, frames), BF),
        pltpu.VMEM((width, frames), BF),
        pltpu.VMEM((3 * heads_width, frames), BF),
        pltpu.VMEM((heads_width, frames), BF),
        pltpu.VMEM((heads_width, frames), BF),
        pltpu.VMEM((8, frames), F32),
        pltpu.VMEM((2, width, BLOCK), F32),
        pltpu.VMEM((hidden_units, width), BF),
        pltpu.VMEM((2, blocks, width, BLOCK), BF),
        pltpu.VMEM((2, blocks, width, BLOCK), BF),
        pltpu.VMEM((width, 128), F32),
        pltpu.VMEM((width, 128), F32),
        pltpu.VMEM((4, width, 128), F32),
        pltpu.VMEM((2 * heads_width + hidden_units, 128), F32),
        pltpu.VMEM((frames, width), BF),
        pltpu.VMEM((rows, END), BF),
        pltpu.VMEM((LINES, rows, END), BF),
        pltpu.VMEM((LINES, rows - SPLIT, END), BF),
        pltpu.VMEM((LINES, rows, END), BF),
    ]
    scratch += [sem((CHUNKS + 1, LINES)), sem((2, CHUNKS + 1, LINES))]
    scratch += [sem((2, CHUNKS + 1))] * 8
    scratch += [sem((2, CHUNKS + 1, LINES)), sem((CHUNKS + 1, LINES))]
    scratch += [sem((2, CHUNKS + 1))] * 8
    scratch += [
        sem((8, blocks)),
        sem((8, blocks)),
        sem((10,)),
        sem((5,)),
        sem((6,)),
        sem((3,)),
        sem((3, blocks // 2)),
        sem((9, 2)),
        sem((9,)),
        sem((2,)),
    ]
    scratch += [free((CHUNKS + 1,))] * 4
    anywhere = pl.BlockSpec(memory_space=pl.ANY)
    inside = pl.BlockSpec(memory_space=pltpu.VMEM)
    return pl.pallas_call(
        functools.partial(layers_kernel, share),
        out_shape=outs,
        in_specs=[anywhere] * 2 + [inside] * 4 + [anywhere] * (len(shards) - 4),
        out_specs=[anywhere] * len(outs),
        scratch_shapes=scratch,
        compiler_params=pltpu.CompilerParams(
            collective_id=0, has_side_effects=True, vmem_limit_bytes=VMEM_LIMIT
        ),
        cost_estimate=pl.CostEstimate(
            flops=60_000_000_000, bytes_accessed=60_000_000, transcendentals=0
        ),
    )(clips, cotangent, *shards)


def group_piece(value, axis, share):
    if share == 1:
        return value
    size = value.shape[axis] * share
    group = lax.axis_index("dp") // share
    full = lax.all_gather(value, "dp", axis=axis, tiled=True)
    return lax.dynamic_slice_in_dim(full, group * size, size, axis)


def own_part(value, axis, share, parts, index):
    size = value.shape[axis] // parts
    if parts == 1:
        return value
    return lax.dynamic_slice_in_dim(value, index * size, size, axis)


def on_device(share, clips, cotangent, ln_gains, row_biases, w_qkv, b_qv, w_o, w_up, b_ff, w_down):
    width = clips.shape[2]
    rows = width // GROUPS
    dims = (width, 2 * clips.shape[1], w_up.shape[2], w_o.shape[1])
    ln_gains = group_piece(ln_gains, 2, share)
    row_biases = group_piece(row_biases, 2, share)
    w_qkv = group_piece(w_qkv, 2, share)
    b_qv = group_piece(b_qv, 3, share)
    w_o = group_piece(w_o, 2, share)
    w_up = group_piece(w_up, 1, share)
    b_ff = group_piece(b_ff, 2, share)
    w_down = group_piece(w_down, 2, share)
    shards = (
        ln_gains,
        row_biases,
        jnp.transpose(b_qv, (0, 2, 1, 3)),
        jnp.swapaxes(b_ff, 1, 2),
        w_qkv,
        jnp.swapaxes(w_o, 1, 2),
        w_up,
        jnp.swapaxes(w_down, 1, 2),
    )
    section_out, section_in_grad, *landed = layers_call(share, clips, cotangent, shards, dims)
    rest = lax.axis_index("dp") % share
    side = lax.axis_index("tensor")

    def joined(value):
        total = jnp.sum(value.astype(F32), 0)
        if share == 1:
            return total
        group = lax.axis_index("dp") // share
        padded = jnp.zeros((width, total.shape[1]), F32)
        padded = lax.dynamic_update_slice_in_dim(padded, total, group * rows, 0)
        return lax.dynamic_slice_in_dim(lax.psum(padded, "dp"), group * rows, rows, 0)

    def mine(value):
        return own_part(joined(value), 0, share, share, rest)

    vectors = joined(landed[0])
    vec = own_part(own_part(vectors, 0, share, share, rest), 0, share, 2, side)
    heads_grad = vectors[0:8, HEAD_LANE : HEAD_LANE + 12].T.reshape(6, 2, 8).transpose(1, 0, 2)
    units_grad = vectors[0:8, UNIT_LANE : UNIT_LANE + 24].T
    qkv_grad = {"q": [], "k": [], "v": []}
    for first, many, kind, _ in PARTS:
        qkv_grad[kind].append(mine(landed[1][:, :, first : first + many]))
    return (
        section_out,
        section_in_grad,
        vec[:, 0:2].T[None],
        vec[:, 2:6].T[None],
        jnp.stack([jnp.concatenate(qkv_grad[kind], 1) for kind in "qkv"])[None],
        own_part(heads_grad, 2, share, share, rest)[None],
        mine(landed[2]).T[None],
        mine(landed[3])[None],
        own_part(units_grad, 1, share, share, rest)[None],
        mine(landed[4]).T[None],
    )


def solution(mesh):
    placed = (
        P("dp", "tensor", None),
        P("dp", "tensor", None),
        P("section", None, "dp"),
        P("section", None, "dp"),
        P("section", None, "dp", "tensor"),
        P("section", None, "tensor", "dp"),
        P("section", "tensor", "dp"),
        P("section", "dp", "tensor"),
        P("section", "tensor", "dp"),
        P("section", "tensor", "dp"),
    )
    share = mesh.shape["dp"] // GROUPS
    return jax.shard_map(
        functools.partial(on_device, share),
        mesh=mesh,
        in_specs=placed,
        out_specs=(
            P("section", "dp", "tensor", None),
            P("section", "dp", "tensor", None),
            P("section", None, ("dp", "tensor")),
            P("section", None, ("dp", "tensor")),
            P("section", None, "dp", "tensor"),
            P("section", None, "tensor", "dp"),
            P("section", "tensor", "dp"),
            P("section", "dp", "tensor"),
            P("section", "tensor", "dp"),
            P("section", "tensor", "dp"),
        ),
        check_vma=False,
    )
```

```python
import functools

import jax
import jax.numpy as jnp
from jax import lax
from jax.experimental import pallas as pl
from jax.experimental.pallas import tpu as pltpu
from jax.sharding import PartitionSpec as P

BF = jnp.bfloat16
F32 = jnp.float32
MESH = pl.DeviceIdType.MESH
EPSILON = 1e-05
HEAD = 64
GROUPS = 8
LINES = 4
BLOCK = 256
PAIR = 2 * BLOCK
ROWS = 64
ONES = 16
VMEM_LIMIT = 62 * 1024 * 1024

VEC = 0
QKV = 128
OUT = 1280
UP = 1664
DOWN = 3200
END = 4736
GATHER_SPLITS = (64, 48)
SPLIT = 64
WIDE = 384
CHUNKS = 12


PARTS = (
    (0, 256, "q", 0),
    (256, 256, "k", 0),
    (512, 256, "v", 384),
    (768, 128, "q", 256),
    (896, 128, "k", 256),
    (1024, 128, "v", 640),
)


HEAD_LANE = 8
UNIT_LANE = 20


def head_lane(kind, head):
    return HEAD_LANE + 2 * head + kind


def mm(left, right):
    return jnp.dot(left, right, preferred_element_type=F32)


def mmt(left, right):
    return lax.dot_general(left, right, (((1,), (1,)), ((), ())), preferred_element_type=F32)


class Place:
    def __init__(self, share):
        self.s = lax.axis_index("section")
        self.d = lax.axis_index("dp")
        self.t = lax.axis_index("tensor")
        group = self.d // share
        self.rest = self.d - group * share
        self.share = share
        self.e = group // 2
        self.y = group - self.e * 2
        self.primary = self.s == self.t
        self.core = (1 - self.s, self.d, self.t)
        self.across = (self.s, self.d, 1 - self.t)
        self.beside = (self.s, self.row_of(self.e, 1 - self.y), self.t)

    def row_of(self, line, y):
        return (line * 2 + y) * self.share + self.rest

    def line(self, step):
        return lax.rem(self.e + step, LINES)

    def greet(self):
        barrier = pltpu.get_barrier_semaphore()
        peers = [self.core, self.across, self.beside]
        for step in range(1, LINES):
            for section in range(2):
                peers.append((section, self.row_of(self.line(step), self.y), self.t))
        for peer in peers:
            pl.semaphore_signal(barrier, inc=1, device_id=peer, device_id_type=MESH)
        pl.semaphore_wait(barrier, len(peers))


def remote(src, dst, send_sem, recv_sem, device):
    return pltpu.make_async_remote_copy(
        src_ref=src,
        dst_ref=dst,
        send_sem=send_sem,
        recv_sem=recv_sem,
        device_id=device,
        device_id_type=MESH,
    )


def await_bytes(ref, sem):
    pltpu.make_async_copy(ref, ref, sem).wait()


def chunks_of(count, size=ROWS):
    return [slice(first, first + size) for first in range(0, count, size)]


def by_eights(value):
    return value.reshape(value.shape[0] // 8, 8, value.shape[1])


def stack_sum(value):
    return jnp.sum(by_eights(value), 0)


def stack_max(value):
    return jnp.max(by_eights(value), 0)


def mean_of(parts, count):
    return jnp.sum(parts, 0, keepdims=True) / count


def norm_stats(read, count):
    total = jnp.zeros((8, BLOCK), F32)
    for span in chunks_of(count):
        total = total + stack_sum(read(span))
    mean = mean_of(total, count)
    square = jnp.zeros((8, BLOCK), F32)
    for span in chunks_of(count):
        centred = read(span) - mean
        square = square + stack_sum(centred * centred)
    return mean, lax.rsqrt(mean_of(square, count) + EPSILON)


def gelu_parts(values):
    bell = jnp.exp(-0.5 * values * values)
    reach = jnp.abs(values) * 0.7071067811865476
    inv = 1.0 / (1.0 + 0.3275911 * reach)
    poly = inv * (
        0.254829592
        + inv * (-0.284496736 + inv * (1.421413741 + inv * (-1.453152027 + inv * 1.061405429)))
    )
    tail = 0.5 * poly * bell
    cdf = jnp.where(values >= 0.0, 1.0 - tail, tail)
    return values * cdf, cdf + values * bell * 0.3989422804014327


def fold(value):
    return value[:, 0:128] + value[:, 128:256]


def block_of(index):
    return pl.ds(pl.multiple_of(index * BLOCK, BLOCK), BLOCK)


def pair_of(index):
    return pl.ds(pl.multiple_of(index * PAIR, PAIR), PAIR)


def flip_weights(w, wt, layer, start, width, target=0):
    def body(index, carry):
        cols = pl.ds(pl.multiple_of(start + index * 128, 128), 128)
        rows = pl.ds(pl.multiple_of(target + index * 128, 128), 128)
        tile = w[layer, :, :, :, cols]
        wt[rows, :] = tile.reshape(tile.shape[0] * tile.shape[1] * tile.shape[2], 128).T
        return carry

    lax.fori_loop(0, width // 128, body, 0)


def whole(w, layer, start, width):
    tile = w[layer, :, :, :, start : start + width]
    return tile.reshape(tile.shape[0] * tile.shape[1] * tile.shape[2], width)


def spread_biases(vecs, spread, rows):
    def body(group, carry):
        at = pl.ds(pl.multiple_of(group * rows, 8), 8)
        for kind in range(2):
            for head in range(6):
                to = pl.ds(pl.multiple_of(kind * 384 + head * HEAD + group * 8, 8), 8)
                lane = head_lane(kind, head)
                spread[to, 6:7] = vecs[at, lane : lane + 1]
        for unit in range(24):
            to = pl.ds(pl.multiple_of(768 + unit * HEAD + group * 8, 8), 8)
            lane = UNIT_LANE + unit
            spread[to, 6:7] = vecs[at, lane : lane + 1]
        return carry

    lax.fori_loop(0, GROUPS, body, 0)


def layers_kernel(
    share,
    clips,
    cot,
    gains_in,
    biases_in,
    heads_in,
    units_in,
    qkv_in,
    out_in,
    up_in,
    down_in,
    out,
    in_grad,
    landed_vec,
    landed_qkv,
    landed_out,
    landed_up,
    landed_down,
    cot_other,
    x_hbm,
    h_hbm,
    n1_hbm,
    n2_hbm,
    qkv_hbm,
    ctx_hbm,
    lse_hbm,
    act_hbm,
    slope_hbm,
    w,
    res,
    act,
    slope,
    n1,
    n2,
    low,
    qkv,
    ctx,
    dctx,
    lse,
    h_in,
    wt,
    send,
    recv,
    vecs,
    vec_grads,
    sums,
    spread,
    stage,
    shard,
    land_a,
    land_b,
    land_y,
    z_send,
    z_recv,
    x_send,
    x_recv,
    xb_send,
    xb_recv,
    y_send,
    y_recv,
    ya_send,
    ya_recv,
    gz_send,
    gz_recv,
    gx_send,
    gx_recv,
    gxb_send,
    gxb_recv,
    gy_send,
    gy_recv,
    gya_send,
    gya_recv,
    e_send,
    e_recv,
    own_sem,
    in_sem,
    cot_sem,
    out_sem,
    grad_sem,
    save_sem,
    load_sem,
    h_sem,
    ya_free,
    xb_free,
    x_free,
    y_free,
):
    place = Place(share)
    s, t, e, y = place.s, place.t, place.e, place.y
    primary, secondary = place.primary, jnp.logical_not(place.primary)
    width, frames = res.shape
    blocks = frames // BLOCK
    half = frames // 2
    quarter = half // 2
    rows = w.shape[3]
    low_rows = pl.ds(0, SPLIT)
    high_rows = pl.ds(SPLIT, rows - SPLIT)
    mine = pl.ds(pl.multiple_of(t * half, half), half)
    theirs = pl.ds(pl.multiple_of((1 - t) * half, half), half)

    own_loads = []
    for number, (first, many, kind, bias) in enumerate(PARTS):
        own_loads.append(
            pltpu.make_async_copy(
                qkv_in.at[0, "qkv".index(kind), :, pl.ds(bias % WIDE, many)],
                shard.at[:, pl.ds(QKV + first, many)],
                own_sem.at[1 + number],
            )
        )
    own_up = pltpu.make_async_copy(up_in.at[0], shard.at[:, pl.ds(UP, DOWN - UP)], own_sem.at[7])
    own_out = pltpu.make_async_copy(out_in.at[0], shard.at[:, pl.ds(OUT, UP - OUT)], own_sem.at[8])
    own_down = pltpu.make_async_copy(
        down_in.at[0], shard.at[:, pl.ds(DOWN, END - DOWN)], own_sem.at[9]
    )
    for copy in own_loads + [own_out, own_up, own_down]:
        copy.start()
    spread[0:32, :] = jnp.zeros((32, 128), F32)
    vec_grads[0:rows, :] = jnp.zeros((rows, 128), F32)
    spread[0:2, 0:rows] = gains_in[0].astype(F32)
    spread[2:6, 0:rows] = biases_in[0].astype(F32)
    for head in range(6):
        spread[8 + 2 * head : 10 + 2 * head, 0:8] = heads_in[0, head].astype(F32)
    vec_grads[0:rows, 0:8] = spread[0:8, :].T[0:rows, :]
    vec_grads[0:8, HEAD_LANE : HEAD_LANE + 12] = spread[8:24, :].T[0:8, 0:12]
    vec_grads[0:8, UNIT_LANE : UNIT_LANE + 24] = units_in[0].astype(F32)
    shard[:, VEC:QKV] = vec_grads[0:rows, :].astype(BF)

    place.greet()

    VECTORS = CHUNKS

    def piece_cols(piece):
        if isinstance(piece, int) and piece == VECTORS:
            return pl.ds(VEC, QKV)
        return pl.ds(pl.multiple_of(QKV + piece * WIDE, 128), WIDE)

    def gather_rows(piece):
        split = GATHER_SPLITS[piece % 2]
        return pl.ds(0, split), pl.ds(split, rows - split)

    def pieces_of(step):
        layer, piece = step // CHUNKS, step % CHUNKS
        return layer, (VECTORS, piece) if piece == 0 else (piece,)

    def z_copies(piece):
        cols = piece_cols(piece)
        copies = []
        for step in range(LINES):
            copies.append(
                remote(
                    shard.at[:, cols],
                    w.at[s, e, y, :, cols],
                    z_send.at[piece, step],
                    z_recv.at[s, piece, e],
                    (t, place.row_of(place.line(step), y), t),
                )
            )
        local = pltpu.make_async_copy(
            shard.at[:, cols], w.at[s, e, y, :, cols], z_recv.at[s, piece, e]
        )
        return copies, local

    def z_start(step):
        layer, pieces = pieces_of(step)

        @pl.when(s == layer)
        def _():
            for piece in pieces:
                copies, local = z_copies(piece)

                @pl.when(primary)
                def _():
                    local.start()

                @pl.when(secondary)
                def _():
                    copies[0].start()

                for copy in copies[1:]:
                    copy.start()

    def z_finish(piece):
        copies, _ = z_copies(piece)

        @pl.when(secondary)
        def _():
            copies[0].wait_send()

        for copy in copies[1:]:
            copy.wait_send()

    def x_copy(layer, piece):
        part = w.at[layer, :, y, :, piece_cols(piece)]
        return remote(part, part, x_send.at[layer, piece], x_recv.at[layer, piece], place.across)

    def y_copy(layer, piece):
        part = w.at[layer, :, y, :, piece_cols(piece)]
        return remote(part, part, y_send.at[layer, piece], y_recv.at[layer, piece], place.beside)

    def xb_copy(layer, piece):
        part = w.at[layer, :, 1 - y, gather_rows(piece)[1], piece_cols(piece)]
        return remote(part, part, xb_send.at[layer, piece], xb_recv.at[layer, piece], place.across)

    def ya_copy(layer, piece):
        part = w.at[layer, :, y, gather_rows(piece)[0], piece_cols(piece)]
        return remote(part, part, ya_send.at[layer, piece], ya_recv.at[layer, piece], place.beside)

    def step_z(step):
        layer, pieces = pieces_of(step)

        @pl.when(primary)
        def _():
            for piece in pieces:
                cols = piece_cols(piece)
                for line in range(LINES):
                    await_bytes(w.at[layer, line, y, :, cols], z_recv.at[layer, piece, line])
                x_copy(layer, piece).start()
                y_copy(layer, piece).start()

    def step_plane(step):
        layer, pieces = pieces_of(step)

        @pl.when(primary)
        def _():
            for piece in pieces:
                await_bytes(w.at[layer, :, 1 - y, :, piece_cols(piece)], y_recv.at[layer, piece])
                xb_copy(layer, piece).start()

        @pl.when(secondary)
        def _():
            for piece in pieces:
                await_bytes(w.at[layer, :, y, :, piece_cols(piece)], x_recv.at[layer, piece])
                ya_copy(layer, piece).start()

    def tick(step):
        if step + 3 < 2 * CHUNKS:
            step_z(step + 3)
        if step + 8 < 2 * CHUNKS:
            z_start(step + 8)
        step_plane(step)

    def complete(*steps):
        @pl.when(secondary)
        def _():
            for step in steps:
                layer, pieces = pieces_of(step)
                for piece in pieces:
                    cols = piece_cols(piece)
                    first, second = gather_rows(piece)
                    await_bytes(w.at[layer, :, 1 - y, second, cols], xb_recv.at[layer, piece])
                    await_bytes(w.at[layer, :, 1 - y, first, cols], ya_recv.at[layer, piece])

    def at_turns(turns):
        def beside(index):
            for turn, steps in turns.items():

                @pl.when(index == turn)
                def _():
                    for step in steps:
                        step()

        return beside

    def ticks(turns):
        return at_turns({turn: (functools.partial(tick, step),) for turn, step in turns.items()})

    kept = {
        "x": (n2.at[pl.ds(0, width), :], x_hbm),
        "h": (res, h_hbm),
        "n1": (n1.at[pl.ds(0, width), :], n1_hbm),
        "n2": (n2.at[pl.ds(0, width), :], n2_hbm),
        "qkv": (qkv, qkv_hbm),
        "ctx": (ctx, ctx_hbm),
        "lse": (lse, lse_hbm),
        "act": (act, act_hbm),
        "slope": (slope, slope_hbm),
    }
    names = tuple(kept)

    def save(name, layer):
        src, dst = kept[name]
        if name in ("x", "h"):
            dst = dst.at[layer]
        return pltpu.make_async_copy(src, dst, save_sem.at[names.index(name), layer])

    def load(name, layer=0):
        dst, src = kept[name]
        if name == "x":
            dst, src = act.at[pl.ds(0, width), :], src.at[layer]
        return pltpu.make_async_copy(src, dst, load_sem.at[names.index(name)])

    def load_h(layer, index):
        slot = lax.rem(index, 2)
        return pltpu.make_async_copy(
            h_hbm.at[layer, :, block_of(index)], h_in.at[slot], h_sem.at[slot]
        )

    my_quarter = pl.ds(s * quarter, quarter)
    my_rows = pl.ds(pl.multiple_of((1 - t) * half + s * quarter, quarter), quarter)

    def clip_across():
        there = pl.ds(pl.multiple_of(t * half + s * quarter, quarter), quarter)
        return remote(
            clips.at[1 - t, my_quarter, :],
            stage.at[there, :],
            in_sem.at[0],
            in_sem.at[1],
            place.across,
        )

    def clip_core():
        part = stage.at[my_rows, :]
        return remote(part, part, in_sem.at[2], in_sem.at[3], place.core)

    def cot_across():
        return remote(
            cot.at[1 - t, my_quarter, :],
            cot_other.at[my_quarter, :],
            cot_sem.at[0],
            cot_sem.at[1],
            place.across,
        )

    def cot_core():
        part = cot_other.at[my_quarter, :]
        return remote(part, part, cot_sem.at[2], cot_sem.at[3], place.core)

    def exchange(kind, index, slot):
        return remote(
            send.at[kind, index],
            recv.at[kind, index],
            e_send.at[slot, index],
            e_recv.at[slot, index],
            place.core,
        )

    def result_copies(ref, first):
        local = pltpu.make_async_copy(stage.at[mine, :], ref.at[0, t], out_sem.at[first])
        away = remote(
            stage.at[theirs, :],
            ref.at[0, t],
            out_sem.at[first + 1],
            out_sem.at[first + 2],
            place.across,
        )
        return local, away

    def grad_copies(index):
        place_in = lax.rem(index, blocks // 2)
        part = in_grad.at[0, t, pl.ds(pl.multiple_of(place_in * BLOCK, BLOCK), BLOCK), :]
        src = stage.at[block_of(index), :]
        local = pltpu.make_async_copy(src, part, grad_sem.at[0, place_in])
        away = remote(
            src, part, grad_sem.at[1, place_in], grad_sem.at[2, place_in], place.across
        )
        return local, away

    def emit(layer, ref, first):
        @pl.when(s == layer)
        def _():
            for copy in result_copies(ref, first):
                copy.start()

    for copy in own_loads:
        copy.wait()
    for step in range(3):
        z_start(step)
    n1[width:, :] = jnp.ones((ONES, frames), BF)
    n2[width:, :] = jnp.ones((ONES, frames), BF)
    own_clip = pltpu.make_async_copy(clips.at[t], stage.at[mine, :], in_sem.at[4])
    own_clip.start()
    clip_across().start()
    own_out.wait()
    own_up.wait()
    own_down.wait()
    for step in (3, 4):
        z_start(step)

    def take_clip(first):
        def body(index, carry):
            at = pl.ds(pl.multiple_of(first + index * BLOCK, BLOCK), BLOCK)
            tile = stage[at, :].T
            n2[0:width, at] = tile
            res[:, at] = tile.astype(F32)
            return carry

        lax.fori_loop(0, half // BLOCK, body, 0)

    own_clip.wait()
    take_clip(t * half)
    clip_across().wait()
    clip_core().start()
    step_z(0)
    z_start(5)
    step_z(1)
    z_start(6)
    clip_core().wait()
    take_clip((1 - t) * half)
    save("x", 0).start()
    step_plane(0)
    step_z(2)
    z_start(7)
    step_plane(1)
    step_z(3)
    z_start(8)
    step_plane(2)
    cot_across().start()
    step_z(4)
    z_start(9)
    step_z(5)
    z_start(10)

    def project(pair):
        for index in (2 * pair, 2 * pair + 1):
            cols = block_of(index)
            mean, scale = norm_stats(lambda span: res[span, cols], width)
            for span in chunks_of(width):
                hat = (res[span, cols] - mean) * scale
                n1[span, cols] = (hat * vecs[span, 0:1] + vecs[span, 2:3]).astype(BF)
        cols = pair_of(pair)
        for first, many, kind, bias in PARTS:
            value = mm(wt[first : first + many, :], n1[0:width, cols])
            for span in chunks_of(many):
                part = value[span, :]
                if kind != "k":
                    part = part + spread[bias + span.start : bias + span.stop, 6:7]
                if kind == "q":
                    part = part * 0.125
                qkv[first + span.start : first + span.stop, cols] = part.astype(BF)

    def send_pair(kind, pair, slot, value):
        for part in range(2):
            index = 2 * pair + part
            send[kind, index] = value[:, part * BLOCK : (part + 1) * BLOCK].astype(BF)
            exchange(kind, index, slot).start()

    def head_rows(head, first):
        return pl.ds(pl.multiple_of(first + head * HEAD, HEAD), HEAD)

    def attend(layer, turns, later_turns):
        def heads_of(first_head, base, stride, beside):
            def one_head(index_in, carry):
                head = first_head + index_in
                q_rows = head_rows(index_in, base)
                k_rows = head_rows(index_in, base + stride)
                v_rows = head_rows(index_in, base + 2 * stride)
                c_rows = head_rows(head, 0)
                keys = qkv[k_rows, :].T
                for index in range(blocks):
                    cols = slice(index * BLOCK, (index + 1) * BLOCK)
                    queries = qkv[q_rows, cols]
                    tiles = []
                    top = None
                    for tile in chunks_of(frames, BLOCK):
                        scores = mm(keys[tile, :], queries)
                        for span in chunks_of(BLOCK):
                            peak = stack_max(scores[span, :])
                            top = peak if top is None else jnp.maximum(top, peak)
                        tiles.append(scores)
                    top = jnp.max(top, 0, keepdims=True)
                    total = jnp.zeros((8, BLOCK), F32)
                    mixed = jnp.zeros((HEAD, BLOCK), F32)
                    for tile, scores in zip(chunks_of(frames, BLOCK), tiles):
                        soft = []
                        for span in chunks_of(BLOCK):
                            part = jnp.exp(scores[span, :] - top)
                            total = total + stack_sum(part)
                            soft.append(part.astype(BF))
                        mixed = mixed + mm(qkv[v_rows, tile], jnp.concatenate(soft, 0))
                    total = jnp.sum(total, 0, keepdims=True)
                    ctx[c_rows, cols] = (mixed / total).astype(BF)
                    lse[pl.ds(head, 1), cols] = top + jnp.log(total)
                beside(index_in)
                return carry

            return one_head

        lax.fori_loop(0, 4, heads_of(0, 0, 256, ticks(turns)), 0)
        lax.fori_loop(0, 2, heads_of(4, 768, 128, ticks(later_turns)), 0)

    def out_project(layer, turns):
        beside = ticks(turns)

        def body(index, carry):
            part = mm(whole(w, layer, OUT, 384), ctx[:, pair_of(index)])
            send_pair(0, index, 2 * layer, part)
            beside(index)
            return carry

        lax.fori_loop(0, blocks // 2, body, 0)

    def middle_norm(layer, turns):
        beside = ticks(turns)

        def body(index, carry):
            cols = block_of(index)
            exchange(0, index, 2 * layer).wait()
            for span in chunks_of(width):
                added = send[0, index, span, :].astype(F32) + recv[0, index, span, :].astype(F32)
                res[span, cols] = res[span, cols] + added + vecs[span, 3:4]
            mean, scale = norm_stats(lambda span: res[span, cols], width)
            for span in chunks_of(width):
                hat = (res[span, cols] - mean) * scale
                n2[span, cols] = (hat * vecs[span, 1:2] + vecs[span, 4:5]).astype(BF)
            beside(index)
            return carry

        lax.fori_loop(0, blocks, body, 0)

    def hidden_part(layer, part):
        flip_weights(w, wt, layer, UP + part * WIDE, WIDE, part * WIDE)
        units = slice(part * WIDE, (part + 1) * WIDE)

        def body(index, carry):
            cols = pair_of(index)
            pre = mm(wt[units, :], n2[0:width, cols])
            for span in chunks_of(WIDE):
                first = part * WIDE + span.start
                bias = spread[768 + first : 768 + first + ROWS, 6:7]
                value, steep = gelu_parts(pre[span, :] + bias)
                act[first : first + ROWS, cols] = value.astype(BF)
                slope[first : first + ROWS, cols] = steep.astype(BF)
            return carry

        lax.fori_loop(0, blocks // 2, body, 0)

    def down_project(layer, turns):
        beside = ticks(turns)

        def body(index, carry):
            part = mm(whole(w, layer, DOWN, 1536), act[:, pair_of(index)])
            send_pair(1, index, 2 * layer + 1, part)
            beside(index)
            return carry

        lax.fori_loop(0, blocks // 2, body, 0)

    def layer_end(layer, index, span):
        added = send[1, index, span, :].astype(F32) + recv[1, index, span, :].astype(F32)
        return (res[span, block_of(index)] + added + vecs[span, 5:6]).astype(BF)

    def take_vectors(layer):
        vecs[...] = whole(w, layer, VEC, 128).astype(F32)
        spread_biases(vecs, spread, rows)

    def project_all(layer, turns):
        beside = ticks(turns)
        flip_weights(w, wt, layer, QKV, 1152)

        def body(index, carry):
            project(index)
            beside(index)
            return carry

        lax.fori_loop(0, blocks // 2, body, 0)
        if layer == 0:
            save("n1", 0).start()
            save("qkv", 0).start()

    complete(0, 1, 2)
    take_vectors(0)
    project_all(0, {0: 3, 1: 4})
    cot_across().wait()
    cot_core().start()
    own_cot = pltpu.make_async_copy(cot.at[t], stage.at[mine, :], cot_sem.at[5])
    own_cot.start()
    attend(0, {0: 5, 2: 6}, {0: 7})
    save("ctx", 0).start()
    save("lse", 0).start()
    cot_core().wait()
    load_cot = pltpu.make_async_copy(cot_other, stage.at[theirs, :], cot_sem.at[4])
    load_cot.start()
    complete(3)
    out_project(0, {1: 8})
    load_cot.wait()
    own_cot.wait()

    sums[3] = jnp.zeros_like(sums[3])

    def take_cot(index, carry):
        low[:, block_of(index)] = stage[block_of(index), :].T
        for span in chunks_of(width):
            sums[3, span, :] += fold(low[span, block_of(index)].astype(F32))
        return carry

    lax.fori_loop(0, blocks, take_cot, 0)
    save("x", 0).wait()
    middle_norm(0, {1: 9})
    save("h", 0).start()
    save("n2", 0).start()
    for part in range(4):
        complete(4 + part)
        hidden_part(0, part)
        tick(10 + part)
    save("act", 0).start()
    save("slope", 0).start()
    complete(8, 9, 10, 11)
    down_project(0, {1: 14})
    for name in ("n1", "qkv", "h", "n2"):
        save(name, 0).wait()

    def finish_body(index, carry):
        exchange(1, index, 1).wait()
        cols = block_of(index)
        for span in chunks_of(width):
            rows_out = layer_end(0, index, span)
            n2[span, cols] = rows_out
            res[span, cols] = rows_out.astype(F32)

        @pl.when(s == 0)
        def _():
            stage[cols, :] = n2[0:width, cols].T

        return carry

    lax.fori_loop(0, blocks, finish_body, 0)
    save("x", 1).start()
    complete(12, 13, 14)
    take_vectors(1)
    project_all(1, {0: 15, 1: 16})
    save("ctx", 0).wait()
    save("lse", 0).wait()
    attend(1, {0: 17, 2: 18}, {0: 19})
    complete(15)
    out_project(1, {1: 20})
    save("x", 1).wait()
    middle_norm(1, {1: 21})
    save("h", 1).start()
    save("act", 0).wait()
    save("slope", 0).wait()
    for part in range(4):
        complete(16 + part)
        hidden_part(1, part)
        if part < 2:
            tick(22 + part)
    for part in range(4):
        complete(20 + part)
        flip_weights(w, wt, 1, DOWN + part * WIDE, WIDE, part * WIDE)
    emit(0, out, 0)
    down_project(1, {})

    def gya_copy(layer, piece):
        cols = piece_cols(piece)
        return remote(
            w.at[layer, :, 1 - y, low_rows, cols],
            land_a.at[:, low_rows, cols],
            gya_send.at[layer, piece],
            gya_recv.at[layer, piece],
            place.beside,
        )

    def gxb_copy(layer, piece):
        cols = piece_cols(piece)
        return remote(
            w.at[layer, :, 1 - y, high_rows, cols],
            land_b.at[:, :, cols],
            gxb_send.at[layer, piece],
            gxb_recv.at[layer, piece],
            place.across,
        )

    def gx_copy(layer, piece):
        cols = piece_cols(piece)
        return remote(
            w.at[layer, :, y, :, cols],
            land_a.at[:, :, cols],
            gx_send.at[layer, piece],
            gx_recv.at[layer, piece],
            place.across,
        )

    def gy_copy(layer, piece):
        cols = piece_cols(piece)
        return remote(
            w.at[layer, :, 1 - y, :, cols],
            land_y.at[:, :, cols],
            gy_send.at[layer, piece],
            gy_recv.at[layer, piece],
            place.beside,
        )

    def landed_part(piece):
        if piece == VECTORS:
            return landed_vec
        ref, first = (
            (landed_qkv, 0)
            if piece < 3
            else (landed_out, 3)
            if piece < 4
            else (landed_up, 4)
            if piece < 8
            else (landed_down, 8)
        )
        return ref.at[:, :, pl.ds((piece - first) * WIDE, WIDE)]

    def gz_copies(layer, piece):
        cols = piece_cols(piece)
        target = landed_part(piece)
        copies = []
        for step in range(LINES):
            line = place.line(step)
            copies.append(
                remote(
                    w.at[layer, line, y, :, cols],
                    target.at[e],
                    gz_send.at[layer, piece, step],
                    gz_recv.at[piece, e],
                    (layer, place.row_of(line, y), t),
                )
            )
        local = pltpu.make_async_copy(
            w.at[layer, e, y, :, cols], target.at[e], gz_recv.at[piece, e]
        )
        return copies, local

    def add_rows(layer, piece, which, span, lands):
        cols = piece_cols(piece)
        first, count = span
        for line in range(LINES):
            added = [land[line, pl.ds(offset, count), cols] for land, offset in lands]
            total = added[0] if len(added) == 1 else added[0] + added[1]
            w[layer, line, which, pl.ds(first, count), cols] += total

    def signal(sem, layer, piece, device):
        if layer == 1:
            pl.semaphore_signal(sem.at[piece], inc=1, device_id=device, device_id_type=MESH)

    def credit(sem, layer, piece):
        if layer == 0:
            pl.semaphore_wait(sem.at[piece], 1)

    def step_a(layer, piece):
        @pl.when(secondary)
        def _():
            credit(ya_free, layer, piece)
            gya_copy(layer, piece).start()
            credit(xb_free, layer, piece)
            gxb_copy(layer, piece).start()

    def step_b(layer, piece):
        cols = piece_cols(piece)

        @pl.when(secondary)
        def _():
            await_bytes(land_a.at[:, low_rows, cols], gya_recv.at[layer, piece])
            add_rows(layer, piece, y, (0, SPLIT), [(land_a, 0)])
            signal(ya_free, layer, piece, place.beside)
            credit(x_free, layer, piece)
            gx_copy(layer, piece).start()

        @pl.when(primary)
        def _():
            await_bytes(land_b.at[:, :, cols], gxb_recv.at[layer, piece])
            add_rows(layer, piece, 1 - y, (SPLIT, rows - SPLIT), [(land_b, 0)])
            signal(xb_free, layer, piece, place.across)
            credit(y_free, layer, piece)
            gy_copy(layer, piece).start()

    def step_c(layer, piece):
        cols = piece_cols(piece)

        @pl.when(primary)
        def _():
            await_bytes(land_a.at[:, :, cols], gx_recv.at[layer, piece])
            await_bytes(land_y.at[:, :, cols], gy_recv.at[layer, piece])
            add_rows(layer, piece, y, (0, rows), [(land_a, 0), (land_y, 0)])
            signal(x_free, layer, piece, place.across)
            signal(y_free, layer, piece, place.beside)
            copies, local = gz_copies(layer, piece)

            @pl.when(s == layer)
            def _():
                local.start()

            @pl.when(s != layer)
            def _():
                copies[0].start()

            for copy in copies[1:]:
                copy.start()

    def store_grads(layer, start, count, value):
        w[layer, :, :, :, pl.ds(start, count)] = value.astype(BF).reshape(
            w.shape[1], w.shape[2], rows, count
        )

    def mlp_back(layer, beside):
        def body(index, carry):
            cols = pair_of(index)
            for part in range(4):
                units = slice(part * WIDE, (part + 1) * WIDE)
                grad = mm(wt[units, :], low[:, cols])
                for span in chunks_of(WIDE):
                    rows_in = slice(units.start + span.start, units.start + span.stop)
                    steep = slope[rows_in, cols].astype(F32)
                    slope[rows_in, cols] = (grad[span, :] * steep).astype(BF)
            term = mm(whole(w, layer, UP, 1536), slope[:, cols])
            send_pair(0, index, 4 + 2 * layer, term)
            beside(index)
            return carry

        lax.fori_loop(0, blocks // 2, body, 0)

    def outer(layer, start, left, right, first, many, before, beside):
        def body(index, carry):
            before(index)
            base = index * PAIR
            span = pl.ds(pl.multiple_of(first + base, 128), PAIR)
            value = mmt(left[...], right[span, :])
            store_grads(layer, pl.multiple_of(start + base, 128), PAIR, value[0:width, :])
            if left.shape[0] > width:
                to = pl.ds(pl.multiple_of(768 + base, BLOCK), PAIR)
                spread[to, 0:8] = value[width : width + 8, :].T
            beside(index)
            return carry

        lax.fori_loop(0, many // PAIR, body, 0)

    def turned(turn):
        return lax.rem(turn + (1 - t) * (blocks // 2), blocks)

    def norm_back(layer, kind, gain_lane, source, put, finish, beside):
        sums[0:3] = jnp.zeros((3, width, 128), F32)

        def body(turn, carry):
            index = turned(turn)
            cols = block_of(index)
            read = source(index)
            mean, scale = norm_stats(read, width)
            exchange(kind, index, 4 + 2 * layer + kind).wait()
            first = jnp.zeros((8, BLOCK), F32)
            second = jnp.zeros((8, BLOCK), F32)

            def terms(span):
                hat = (read(span) - mean) * scale
                grad = send[kind, index, span, :].astype(F32)
                grad = grad + recv[kind, index, span, :].astype(F32)
                return hat, grad, grad * vecs[span, gain_lane : gain_lane + 1]

            for span in chunks_of(width):
                hat, grad, scaled = terms(span)
                sums[0, span, :] += fold(grad * hat)
                sums[1, span, :] += fold(grad)
                first = first + stack_sum(scaled)
                second = second + stack_sum(scaled * hat)
            level = mean_of(first, width)
            slant = mean_of(second, width)
            for span in chunks_of(width):
                hat, _, scaled = terms(span)
                put(span, cols, res[span, cols] + scale * (scaled - level - hat * slant))
            finish(index)
            beside(turn)
            return carry

        lax.fori_loop(0, blocks, body, 0)

    def row_sums(value):
        return jnp.sum(value, 1, keepdims=True)

    def attend_back(first_head, many, base, stride, beside):
        def one_head(index_in, carry):
            head = first_head + index_in
            q_rows = head_rows(index_in, base)
            k_rows = head_rows(index_in, base + stride)
            v_rows = head_rows(index_in, base + 2 * stride)
            c_rows = head_rows(head, 0)
            keys = qkv[k_rows, :].T
            values = qkv[v_rows, :].T
            flat_queries = qkv[q_rows, :].T
            flat_grads = dctx[c_rows, :].T
            level = lse[pl.ds(head, 1), :]
            inner = jnp.sum(
                dctx[c_rows, :].astype(F32) * ctx[c_rows, :].astype(F32), 0, keepdims=True
            )
            step = jnp.zeros((HEAD, frames), F32)
            for tile in chunks_of(frames, BLOCK):
                soft = []
                score_grad = []
                for cols in chunks_of(frames, BLOCK):
                    scores = mm(keys[tile, :], qkv[q_rows, cols])
                    soft_grad = mm(values[tile, :], dctx[c_rows, cols])
                    soft_parts = []
                    grad_parts = []
                    for part in chunks_of(BLOCK):
                        strength = jnp.exp(scores[part, :] - level[:, cols])
                        soft_parts.append(strength.astype(BF))
                        strength = strength * (soft_grad[part, :] - inner[:, cols])
                        grad_parts.append(strength.astype(BF))
                    soft.append(jnp.concatenate(soft_parts, 0))
                    score_grad.append(jnp.concatenate(grad_parts, 0))
                soft = jnp.concatenate(soft, 1)
                score_grad = jnp.concatenate(score_grad, 1)
                step = step + mm(qkv[k_rows, tile], score_grad)
                slope[k_rows, tile] = mm(score_grad, flat_queries).astype(BF).T
                slope[v_rows, tile] = mm(soft, flat_grads).astype(BF).T
            slope[q_rows, :] = (step * 0.125).astype(BF)
            beside(index_in)
            return carry

        lax.fori_loop(0, many, one_head, 0)

    def keep_sums(first, value):
        for start, many, kind, bias in PARTS:
            offset = start - first
            if kind != "k" and 0 <= offset < value.shape[1]:
                spread[bias : bias + many, 0:8] = value[
                    width : width + 8, offset : offset + many
                ].T

    def collect_biases():
        def body(group, carry):
            to = pl.ds(pl.multiple_of(group * rows, 8), 8)
            for kind in range(2):
                for head in range(6):
                    at = pl.ds(pl.multiple_of(kind * 384 + head * HEAD + group * 8, 8), 8)
                    lane = head_lane(kind, head)
                    vec_grads[to, lane : lane + 1] = spread[at, 6:7]
            for unit in range(24):
                at = pl.ds(pl.multiple_of(768 + unit * HEAD + group * 8, 8), 8)
                lane = UNIT_LANE + unit
                vec_grads[to, lane : lane + 1] = spread[at, 6:7]
            return carry

        lax.fori_loop(0, GROUPS, body, 0)

    def nothing(index):
        del index

    def finish_gather(layer, piece):
        @pl.when(primary)
        def _():
            x_copy(layer, piece).wait_send()
            y_copy(layer, piece).wait_send()
            xb_copy(layer, piece).wait_send()

        @pl.when(secondary)
        def _():
            ya_copy(layer, piece).wait_send()

    def send_first_grad():
        @pl.when(s == 1)
        def _():
            for place_in in range(blocks // 2):
                _, away = grad_copies((1 - t) * (blocks // 2) + place_in)
                away.start()

    def last_body(index, carry):
        exchange(1, index, 3).wait()

        @pl.when(s == 1)
        def _():
            for span in chunks_of(width, 128):
                stage[block_of(index), span] = layer_end(1, index, span).T

        return carry

    for layer in (1, 0):
        later = layer == 0
        if later:
            load_h(layer, turned(0)).start()
            load("act").wait()
            vecs[...] = whole(w, layer, VEC, 128).astype(F32)
            flip_weights(w, wt, layer, DOWN, 1536)
        vec_grads[...] = jnp.zeros_like(vec_grads)

        def a(piece, layer=layer):
            return lambda: step_a(layer, piece)

        def b(piece, layer=layer):
            return lambda: step_b(layer, piece)

        def c(piece, layer=layer):
            return lambda: step_c(layer, piece)

        if later:
            before = nothing
            early = at_turns(
                {
                    0: (a(8),),
                    1: (a(9), lambda: step_b(1, VECTORS)),
                    2: (a(10), a(11)),
                }
            )
        else:
            waits = [functools.partial(finish_gather, 1, piece) for piece in (8, 9, 10, 11)]
            before = at_turns({0: waits[:2], 1: waits[2:3], 2: waits[3:]})
            early = at_turns({0: (a(8),), 1: (a(9),), 2: (a(10), a(11))})
        outer(layer, DOWN, low, act, 0, 1536, before, early)
        load("x", layer).start()
        vec_grads[:, 5:6] = row_sums(sums[3])
        if not later:
            lax.fori_loop(0, blocks, last_body, 0)
            emit(1, out, 0)
            save("h", 1).wait()
            load_h(layer, turned(0)).start()
            res[...] = low[...].astype(F32)
            for piece in range(CHUNKS + 1):
                z_finish(piece)
                finish_gather(0, piece)
                if piece < 8 or piece == VECTORS:
                    finish_gather(1, piece)
        else:
            load("slope").wait()

        mlp_back(layer, at_turns({0: (b(8),)}))
        if later:
            load("n2").wait()
        left = (lambda: step_c(1, VECTORS),) if later else ()
        drain = at_turns({0: (a(4),) + left, 1: (a(5), b(9)), 2: (a(6), a(7))})
        outer(layer, UP, n2, slope, 0, 1536, nothing, drain)
        flip_weights(w, wt, layer, OUT, 384)

        def hidden_in(index, layer=layer):
            turn = lax.rem(index + (1 - t) * (blocks // 2), blocks)

            @pl.when(turn + 1 < blocks)
            def _():
                load_h(layer, turned(turn + 1)).start()

            load_h(layer, index).wait()
            slot = lax.rem(index, 2)
            return lambda span: h_in[slot, span, :]

        def hidden_put(span, cols, total):
            res[span, cols] = total
            rounded = total.astype(BF)
            low[span, cols] = rounded
            sums[2, span, :] += fold(rounded.astype(F32))

        drain = at_turns({0: (b(10),), 1: (b(11),), 2: (b(4), b(5)), 3: (c(8),)})
        norm_back(layer, 0, 1, hidden_in, hidden_put, nothing, drain)

        def context_back(index, carry):
            cols = pair_of(index)
            dctx[:, cols] = mm(wt[0:384, :], low[:, cols]).astype(BF)
            return carry

        lax.fori_loop(0, blocks // 2, context_back, 0)
        vec_grads[:, 1:2] = row_sums(sums[0])
        vec_grads[:, 4:5] = row_sums(sums[1])
        vec_grads[:, 3:4] = row_sums(sums[2])
        if later:
            for name in ("ctx", "qkv", "lse"):
                load(name).wait()
        store_grads(layer, OUT, 384, mmt(low[...], ctx[...]))
        step_a(layer, 3)
        over = (send_first_grad,) if later else ()
        drain = at_turns({0: (c(9),), 1: (b(6), c(10), c(11)) + over, 2: (c(4), c(5))})
        attend_back(0, 4, 0, 256, drain)
        if later:
            load("n1").wait()
        wt[0:768, :] = whole(w, layer, QKV, 768)

        for first, many in ((0, 512), (512, 256)):
            value = mmt(n1[...], slope[first : first + many, :])
            store_grads(layer, QKV + first, many, value[0:width, :])
            keep_sums(first, value)
        step_a(layer, 0)
        step_a(layer, 1)
        step_b(layer, 7)
        step_b(layer, 3)
        step_c(layer, 6)
        attend_back(4, 2, 768, 128, nothing)

        def first_body(index, carry, layer=layer):
            cols = pair_of(index)
            term = mm(wt[0:768, :], slope[0:768, cols])
            term = term + mm(whole(w, layer, QKV + 768, WIDE), slope[768:1152, cols])
            send_pair(1, index, 5 + 2 * layer, term)
            return carry

        lax.fori_loop(0, blocks // 2, first_body, 0)
        step_b(layer, 0)
        step_c(layer, 7)
        value = mmt(n1[...], slope[768:1152, :])
        store_grads(layer, QKV + 768, WIDE, value[0:width, :])
        keep_sums(768, value)
        step_a(layer, 2)
        step_b(layer, 1)
        step_c(layer, 3)
        collect_biases()
        if layer == 1:
            for name in ("slope", "n1", "n2", "ctx", "qkv", "lse"):
                load(name).start()
        load("x", layer).wait()

        @pl.when(s == layer)
        def _():
            local, away = result_copies(out, 0)
            local.wait()
            away.wait_send()

        def rows_x(index):
            return lambda span: act[span, block_of(index)].astype(F32)

        def rows_put(span, cols, total, layer=layer):
            rounded = total.astype(BF)
            low[span, cols] = rounded
            if layer == 1:
                res[span, cols] = rounded.astype(F32)
                sums[2, span, :] += fold(rounded.astype(F32))

        def rows_out(index, layer=layer):
            @pl.when(s == layer)
            def _():
                stage[block_of(index), :] = low[:, block_of(index)].T
                local, away = grad_copies(index)

                @pl.when(index // (blocks // 2) == t)
                def _():
                    local.start()

                if layer == 0:

                    @pl.when(index // (blocks // 2) != t)
                    def _():
                        away.start()

        drain = at_turns({0: (b(2), c(0)), 2: (c(1),)})
        norm_back(layer, 1, 0, rows_x, rows_put, rows_out, drain)
        if layer == 1:
            load("act").start()
        vec_grads[:, 0:1] = row_sums(sums[0])
        vec_grads[:, 2:3] = row_sums(sums[1])
        sums[3] = sums[2]
        store_grads(layer, VEC, 128, vec_grads[...])
        step_a(layer, VECTORS)
        step_c(layer, 2)

    step_b(0, VECTORS)

    step_c(0, VECTORS)

    def finish_scatter(piece):
        for layer in range(2):

            @pl.when(secondary)
            def _():
                gya_copy(layer, piece).wait_send()
                gxb_copy(layer, piece).wait_send()
                gx_copy(layer, piece).wait_send()

            @pl.when(primary)
            def _():
                gy_copy(layer, piece).wait_send()
                copies, _ = gz_copies(layer, piece)

                @pl.when(s != layer)
                def _():
                    copies[0].wait_send()

                for copy in copies[1:]:
                    copy.wait_send()

    for piece in range(CHUNKS + 1):
        finish_scatter(piece)
        for line in range(LINES):
            await_bytes(landed_part(piece).at[line], gz_recv.at[piece, line])

    _, away = result_copies(out, 0)
    away.wait_recv()
    for index in range(blocks // 2):
        local, away = grad_copies(index)
        local.wait()
        away.wait()


def layers_call(share, clips, cotangent, shards, dims):
    width, frames, hidden_units, heads_width = dims
    rows = width // GROUPS
    sem = pltpu.SemaphoreType.DMA
    free = pltpu.SemaphoreType.REGULAR
    packed = (2, LINES, 2, rows, END)
    blocks = frames // BLOCK
    shape = jax.ShapeDtypeStruct
    outs = [
        shape((1,) + clips.shape, BF),
        shape((1,) + clips.shape, BF),
        shape((LINES, rows, QKV - VEC), BF),
        shape((LINES, rows, OUT - QKV), BF),
        shape((LINES, rows, UP - OUT), BF),
        shape((LINES, rows, DOWN - UP), BF),
        shape((LINES, rows, END - DOWN), BF),
        shape(clips.shape[1:], BF),
        shape((2, width, frames), BF),
        shape((2, width, frames), F32),
        shape((width, frames), BF),
        shape((width, frames), BF),
        shape((3 * heads_width, frames), BF),
        shape((heads_width, frames), BF),
        shape((8, frames), F32),
        shape((hidden_units, frames), BF),
        shape((hidden_units, frames), BF),
    ]
    scratch = [
        pltpu.VMEM(packed, BF),
        pltpu.VMEM((width, frames), F32),
        pltpu.VMEM((hidden_units, frames), BF),
        pltpu.VMEM((hidden_units, frames), BF),
        pltpu.VMEM((width + ONES, frames), BF),
        pltpu.VMEM((width + ONES, frames), BF),
        pltpu.VMEM((width, frames), BF),
        pltpu.VMEM((3 * heads_width, frames), BF),
        pltpu.VMEM((heads_width, frames), BF),
        pltpu.VMEM((heads_width, frames), BF),
        pltpu.VMEM((8, frames), F32),
        pltpu.VMEM((2, width, BLOCK), F32),
        pltpu.VMEM((hidden_units, width), BF),
        pltpu.VMEM((2, blocks, width, BLOCK), BF),
        pltpu.VMEM((2, blocks, width, BLOCK), BF),
        pltpu.VMEM((width, 128), F32),
        pltpu.VMEM((width, 128), F32),
        pltpu.VMEM((4, width, 128), F32),
        pltpu.VMEM((2 * heads_width + hidden_units, 128), F32),
        pltpu.VMEM((frames, width), BF),
        pltpu.VMEM((rows, END), BF),
        pltpu.VMEM((LINES, rows, END), BF),
        pltpu.VMEM((LINES, rows - SPLIT, END), BF),
        pltpu.VMEM((LINES, rows, END), BF),
    ]
    scratch += [sem((CHUNKS + 1, LINES)), sem((2, CHUNKS + 1, LINES))]
    scratch += [sem((2, CHUNKS + 1))] * 8
    scratch += [sem((2, CHUNKS + 1, LINES)), sem((CHUNKS + 1, LINES))]
    scratch += [sem((2, CHUNKS + 1))] * 8
    scratch += [
        sem((8, blocks)),
        sem((8, blocks)),
        sem((10,)),
        sem((5,)),
        sem((6,)),
        sem((3,)),
        sem((3, blocks // 2)),
        sem((9, 2)),
        sem((9,)),
        sem((2,)),
    ]
    scratch += [free((CHUNKS + 1,))] * 4
    anywhere = pl.BlockSpec(memory_space=pl.ANY)
    inside = pl.BlockSpec(memory_space=pltpu.VMEM)
    return pl.pallas_call(
        functools.partial(layers_kernel, share),
        out_shape=outs,
        in_specs=[anywhere] * 2 + [inside] * 4 + [anywhere] * (len(shards) - 4),
        out_specs=[anywhere] * len(outs),
        scratch_shapes=scratch,
        compiler_params=pltpu.CompilerParams(
            collective_id=0, has_side_effects=True, vmem_limit_bytes=VMEM_LIMIT
        ),
        cost_estimate=pl.CostEstimate(
            flops=60_000_000_000, bytes_accessed=60_000_000, transcendentals=0
        ),
    )(clips, cotangent, *shards)


def group_piece(value, axis, share):
    if share == 1:
        return value
    size = value.shape[axis] * share
    group = lax.axis_index("dp") // share
    full = lax.all_gather(value, "dp", axis=axis, tiled=True)
    return lax.dynamic_slice_in_dim(full, group * size, size, axis)


def own_part(value, axis, share, parts, index):
    size = value.shape[axis] // parts
    if parts == 1:
        return value
    return lax.dynamic_slice_in_dim(value, index * size, size, axis)


def on_device(share, clips, cotangent, ln_gains, row_biases, w_qkv, b_qv, w_o, w_up, b_ff, w_down):
    width = clips.shape[2]
    rows = width // GROUPS
    dims = (width, 2 * clips.shape[1], w_up.shape[2], w_o.shape[1])
    ln_gains = group_piece(ln_gains, 2, share)
    row_biases = group_piece(row_biases, 2, share)
    w_qkv = group_piece(w_qkv, 2, share)
    b_qv = group_piece(b_qv, 3, share)
    w_o = group_piece(w_o, 2, share)
    w_up = group_piece(w_up, 1, share)
    b_ff = group_piece(b_ff, 2, share)
    w_down = group_piece(w_down, 2, share)
    shards = (
        ln_gains,
        row_biases,
        jnp.transpose(b_qv, (0, 2, 1, 3)),
        jnp.swapaxes(b_ff, 1, 2),
        w_qkv,
        jnp.swapaxes(w_o, 1, 2),
        w_up,
        jnp.swapaxes(w_down, 1, 2),
    )
    section_out, section_in_grad, *landed = layers_call(share, clips, cotangent, shards, dims)
    rest = lax.axis_index("dp") % share
    side = lax.axis_index("tensor")

    def joined(value):
        total = jnp.sum(value.astype(F32), 0)
        if share == 1:
            return total
        group = lax.axis_index("dp") // share
        padded = jnp.zeros((width, total.shape[1]), F32)
        padded = lax.dynamic_update_slice_in_dim(padded, total, group * rows, 0)
        return lax.dynamic_slice_in_dim(lax.psum(padded, "dp"), group * rows, rows, 0)

    def mine(value):
        return own_part(joined(value), 0, share, share, rest)

    vectors = joined(landed[0])
    turned = own_part(own_part(vectors.T, 1, share, share, rest), 1, share, 2, side)
    heads_grad = vectors[0:8, HEAD_LANE : HEAD_LANE + 12].T.reshape(6, 2, 8).transpose(1, 0, 2)
    units_grad = vectors[0:8, UNIT_LANE : UNIT_LANE + 24].T
    qkv_grad = {"q": [], "k": [], "v": []}
    for first, many, kind, _ in PARTS:
        qkv_grad[kind].append(mine(landed[1][:, :, first : first + many]))
    return (
        section_out,
        section_in_grad,
        turned[0:2][None],
        turned[2:6][None],
        jnp.stack([jnp.concatenate(qkv_grad[kind], 1) for kind in "qkv"])[None],
        own_part(heads_grad, 2, share, share, rest)[None],
        mine(landed[2]).T[None],
        mine(landed[3])[None],
        own_part(units_grad, 1, share, share, rest)[None],
        mine(landed[4]).T[None],
    )


def solution(mesh):
    placed = (
        P("dp", "tensor", None),
        P("dp", "tensor", None),
        P("section", None, "dp"),
        P("section", None, "dp"),
        P("section", None, "dp", "tensor"),
        P("section", None, "tensor", "dp"),
        P("section", "tensor", "dp"),
        P("section", "dp", "tensor"),
        P("section", "tensor", "dp"),
        P("section", "tensor", "dp"),
    )
    share = mesh.shape["dp"] // GROUPS
    return jax.shard_map(
        functools.partial(on_device, share),
        mesh=mesh,
        in_specs=placed,
        out_specs=(
            P("section", "dp", "tensor", None),
            P("section", "dp", "tensor", None),
            P("section", None, ("dp", "tensor")),
            P("section", None, ("dp", "tensor")),
            P("section", None, "dp", "tensor"),
            P("section", None, "tensor", "dp"),
            P("section", "tensor", "dp"),
            P("section", "dp", "tensor"),
            P("section", "tensor", "dp"),
            P("section", "tensor", "dp"),
        ),
        check_vma=False,
    )
```

```python
import functools

import jax
import jax.numpy as jnp
from jax import lax
from jax.experimental import pallas as pl
from jax.experimental.pallas import tpu as pltpu
from jax.sharding import PartitionSpec as P

BF = jnp.bfloat16
F32 = jnp.float32
MESH = pl.DeviceIdType.MESH
EPSILON = 1e-05
HEAD = 64
GROUPS = 8
LINES = 4
BLOCK = 256
PAIR = 2 * BLOCK
ROWS = 64
ONES = 16
VMEM_LIMIT = 62 * 1024 * 1024

VEC = 0
QKV = 128
OUT = 1280
UP = 1664
DOWN = 3200
END = 4736
GATHER_SPLITS = (64, 48)
SPLIT = 64
WIDE = 384
CHUNKS = 12


PARTS = (
    (0, 256, "q", 0),
    (256, 256, "k", 0),
    (512, 256, "v", 384),
    (768, 128, "q", 256),
    (896, 128, "k", 256),
    (1024, 128, "v", 640),
)


HEAD_LANE = 8
UNIT_LANE = 20


def head_lane(kind, head):
    return HEAD_LANE + 2 * head + kind


def mm(left, right):
    return jnp.dot(left, right, preferred_element_type=F32)


def mmt(left, right):
    return lax.dot_general(left, right, (((1,), (1,)), ((), ())), preferred_element_type=F32)


class Place:
    def __init__(self, share):
        self.s = lax.axis_index("section")
        self.d = lax.axis_index("dp")
        self.t = lax.axis_index("tensor")
        group = self.d // share
        self.rest = self.d - group * share
        self.share = share
        self.e = group // 2
        self.y = group - self.e * 2
        self.primary = self.s == self.t
        self.core = (1 - self.s, self.d, self.t)
        self.across = (self.s, self.d, 1 - self.t)
        self.beside = (self.s, self.row_of(self.e, 1 - self.y), self.t)

    def row_of(self, line, y):
        return (line * 2 + y) * self.share + self.rest

    def line(self, step):
        return lax.rem(self.e + step, LINES)

    def greet(self):
        barrier = pltpu.get_barrier_semaphore()
        peers = [self.core, self.across, self.beside]
        for step in range(1, LINES):
            for section in range(2):
                peers.append((section, self.row_of(self.line(step), self.y), self.t))
        for peer in peers:
            pl.semaphore_signal(barrier, inc=1, device_id=peer, device_id_type=MESH)
        pl.semaphore_wait(barrier, len(peers))


def remote(src, dst, send_sem, recv_sem, device):
    return pltpu.make_async_remote_copy(
        src_ref=src,
        dst_ref=dst,
        send_sem=send_sem,
        recv_sem=recv_sem,
        device_id=device,
        device_id_type=MESH,
    )


def await_bytes(ref, sem):
    pltpu.make_async_copy(ref, ref, sem).wait()


def chunks_of(count, size=ROWS):
    return [slice(first, first + size) for first in range(0, count, size)]


def by_eights(value):
    return value.reshape(value.shape[0] // 8, 8, value.shape[1])


def stack_sum(value):
    return jnp.sum(by_eights(value), 0)


def stack_max(value):
    return jnp.max(by_eights(value), 0)


def mean_of(parts, count):
    return jnp.sum(parts, 0, keepdims=True) / count


def norm_stats(read, count):
    total = jnp.zeros((8, BLOCK), F32)
    for span in chunks_of(count):
        total = total + stack_sum(read(span))
    mean = mean_of(total, count)
    square = jnp.zeros((8, BLOCK), F32)
    for span in chunks_of(count):
        centred = read(span) - mean
        square = square + stack_sum(centred * centred)
    return mean, lax.rsqrt(mean_of(square, count) + EPSILON)


def gelu_parts(values):
    bell = jnp.exp(-0.5 * values * values)
    reach = jnp.abs(values) * 0.7071067811865476
    inv = 1.0 / (1.0 + 0.3275911 * reach)
    poly = inv * (
        0.254829592
        + inv * (-0.284496736 + inv * (1.421413741 + inv * (-1.453152027 + inv * 1.061405429)))
    )
    tail = 0.5 * poly * bell
    cdf = jnp.where(values >= 0.0, 1.0 - tail, tail)
    return values * cdf, cdf + values * bell * 0.3989422804014327


def fold(value):
    return value[:, 0:128] + value[:, 128:256]


def block_of(index):
    return pl.ds(pl.multiple_of(index * BLOCK, BLOCK), BLOCK)


def pair_of(index):
    return pl.ds(pl.multiple_of(index * PAIR, PAIR), PAIR)


def flip_weights(w, wt, layer, start, width, target=0):
    def body(index, carry):
        cols = pl.ds(pl.multiple_of(start + index * 128, 128), 128)
        rows = pl.ds(pl.multiple_of(target + index * 128, 128), 128)
        tile = w[layer, :, :, :, cols]
        wt[rows, :] = tile.reshape(tile.shape[0] * tile.shape[1] * tile.shape[2], 128).T
        return carry

    lax.fori_loop(0, width // 128, body, 0)


def whole(w, layer, start, width):
    tile = w[layer, :, :, :, start : start + width]
    return tile.reshape(tile.shape[0] * tile.shape[1] * tile.shape[2], width)


def spread_biases(vecs, spread, rows):
    def body(group, carry):
        at = pl.ds(pl.multiple_of(group * rows, 8), 8)
        for kind in range(2):
            for head in range(6):
                to = pl.ds(pl.multiple_of(kind * 384 + head * HEAD + group * 8, 8), 8)
                lane = head_lane(kind, head)
                spread[to, 6:7] = vecs[at, lane : lane + 1]
        for unit in range(24):
            to = pl.ds(pl.multiple_of(768 + unit * HEAD + group * 8, 8), 8)
            lane = UNIT_LANE + unit
            spread[to, 6:7] = vecs[at, lane : lane + 1]
        return carry

    lax.fori_loop(0, GROUPS, body, 0)


def layers_kernel(
    share,
    clips,
    cot,
    gains_in,
    biases_in,
    heads_in,
    units_in,
    qkv_in,
    out_in,
    up_in,
    down_in,
    out,
    in_grad,
    landed_vec,
    landed_qkv,
    landed_out,
    landed_up,
    landed_down,
    cot_other,
    x_hbm,
    h_hbm,
    n1_hbm,
    n2_hbm,
    qkv_hbm,
    ctx_hbm,
    lse_hbm,
    act_hbm,
    slope_hbm,
    w,
    res,
    act,
    slope,
    n1,
    n2,
    low,
    qkv,
    ctx,
    dctx,
    lse,
    h_in,
    wt,
    send,
    recv,
    vecs,
    vec_grads,
    sums,
    spread,
    stage,
    shard,
    land_a,
    land_b,
    land_y,
    z_send,
    z_recv,
    x_send,
    x_recv,
    xb_send,
    xb_recv,
    y_send,
    y_recv,
    ya_send,
    ya_recv,
    gz_send,
    gz_recv,
    gx_send,
    gx_recv,
    gxb_send,
    gxb_recv,
    gy_send,
    gy_recv,
    gya_send,
    gya_recv,
    e_send,
    e_recv,
    own_sem,
    in_sem,
    cot_sem,
    out_sem,
    grad_sem,
    save_sem,
    load_sem,
    h_sem,
    ya_free,
    xb_free,
    x_free,
    y_free,
):
    place = Place(share)
    s, t, e, y = place.s, place.t, place.e, place.y
    primary, secondary = place.primary, jnp.logical_not(place.primary)
    width, frames = res.shape
    blocks = frames // BLOCK
    half = frames // 2
    quarter = half // 2
    rows = w.shape[3]
    low_rows = pl.ds(0, SPLIT)
    high_rows = pl.ds(SPLIT, rows - SPLIT)
    mine = pl.ds(pl.multiple_of(t * half, half), half)
    theirs = pl.ds(pl.multiple_of((1 - t) * half, half), half)

    own_loads = []
    for number, (first, many, kind, bias) in enumerate(PARTS):
        own_loads.append(
            pltpu.make_async_copy(
                qkv_in.at[0, "qkv".index(kind), :, pl.ds(bias % WIDE, many)],
                shard.at[:, pl.ds(QKV + first, many)],
                own_sem.at[1 + number],
            )
        )
    own_up = pltpu.make_async_copy(up_in.at[0], shard.at[:, pl.ds(UP, DOWN - UP)], own_sem.at[7])
    own_out = pltpu.make_async_copy(out_in.at[0], shard.at[:, pl.ds(OUT, UP - OUT)], own_sem.at[8])
    own_down = pltpu.make_async_copy(
        down_in.at[0], shard.at[:, pl.ds(DOWN, END - DOWN)], own_sem.at[9]
    )
    for copy in own_loads + [own_out, own_up, own_down]:
        copy.start()
    spread[0:32, :] = jnp.zeros((32, 128), F32)
    vec_grads[0:rows, :] = jnp.zeros((rows, 128), F32)
    spread[0:2, 0:rows] = gains_in[0].astype(F32)
    spread[2:6, 0:rows] = biases_in[0].astype(F32)
    for head in range(6):
        spread[8 + 2 * head : 10 + 2 * head, 0:8] = heads_in[0, head].astype(F32)
    vec_grads[0:rows, 0:8] = spread[0:8, :].T[0:rows, :]
    vec_grads[0:8, HEAD_LANE : HEAD_LANE + 12] = spread[8:24, :].T[0:8, 0:12]
    vec_grads[0:8, UNIT_LANE : UNIT_LANE + 24] = units_in[0].astype(F32)
    shard[:, VEC:QKV] = vec_grads[0:rows, :].astype(BF)

    place.greet()

    VECTORS = CHUNKS

    def piece_cols(piece):
        if isinstance(piece, int) and piece == VECTORS:
            return pl.ds(VEC, QKV)
        return pl.ds(pl.multiple_of(QKV + piece * WIDE, 128), WIDE)

    def gather_rows(piece):
        split = GATHER_SPLITS[piece % 2]
        return pl.ds(0, split), pl.ds(split, rows - split)

    def pieces_of(step):
        layer, piece = step // CHUNKS, step % CHUNKS
        return layer, (VECTORS, piece) if piece == 0 else (piece,)

    def z_copies(piece):
        cols = piece_cols(piece)
        copies = []
        for step in range(LINES):
            copies.append(
                remote(
                    shard.at[:, cols],
                    w.at[s, e, y, :, cols],
                    z_send.at[piece, step],
                    z_recv.at[s, piece, e],
                    (t, place.row_of(place.line(step), y), t),
                )
            )
        local = pltpu.make_async_copy(
            shard.at[:, cols], w.at[s, e, y, :, cols], z_recv.at[s, piece, e]
        )
        return copies, local

    def z_start(step):
        layer, pieces = pieces_of(step)

        @pl.when(s == layer)
        def _():
            for piece in pieces:
                copies, local = z_copies(piece)

                @pl.when(primary)
                def _():
                    local.start()

                @pl.when(secondary)
                def _():
                    copies[0].start()

                for copy in copies[1:]:
                    copy.start()

    def z_finish(piece):
        copies, _ = z_copies(piece)

        @pl.when(secondary)
        def _():
            copies[0].wait_send()

        for copy in copies[1:]:
            copy.wait_send()

    def x_copy(layer, piece):
        part = w.at[layer, :, y, :, piece_cols(piece)]
        return remote(part, part, x_send.at[layer, piece], x_recv.at[layer, piece], place.across)

    def y_copy(layer, piece):
        part = w.at[layer, :, y, :, piece_cols(piece)]
        return remote(part, part, y_send.at[layer, piece], y_recv.at[layer, piece], place.beside)

    def xb_copy(layer, piece):
        part = w.at[layer, :, 1 - y, gather_rows(piece)[1], piece_cols(piece)]
        return remote(part, part, xb_send.at[layer, piece], xb_recv.at[layer, piece], place.across)

    def ya_copy(layer, piece):
        part = w.at[layer, :, y, gather_rows(piece)[0], piece_cols(piece)]
        return remote(part, part, ya_send.at[layer, piece], ya_recv.at[layer, piece], place.beside)

    def step_z(step):
        layer, pieces = pieces_of(step)

        @pl.when(primary)
        def _():
            for piece in pieces:
                cols = piece_cols(piece)
                for line in range(LINES):
                    await_bytes(w.at[layer, line, y, :, cols], z_recv.at[layer, piece, line])
                x_copy(layer, piece).start()
                y_copy(layer, piece).start()

    def step_plane(step):
        layer, pieces = pieces_of(step)

        @pl.when(primary)
        def _():
            for piece in pieces:
                await_bytes(w.at[layer, :, 1 - y, :, piece_cols(piece)], y_recv.at[layer, piece])
                xb_copy(layer, piece).start()

        @pl.when(secondary)
        def _():
            for piece in pieces:
                await_bytes(w.at[layer, :, y, :, piece_cols(piece)], x_recv.at[layer, piece])
                ya_copy(layer, piece).start()

    def tick(step):
        if step + 3 < 2 * CHUNKS:
            step_z(step + 3)
        if step + 8 < 2 * CHUNKS:
            z_start(step + 8)
        step_plane(step)

    def complete(*steps):
        @pl.when(secondary)
        def _():
            for step in steps:
                layer, pieces = pieces_of(step)
                for piece in pieces:
                    cols = piece_cols(piece)
                    first, second = gather_rows(piece)
                    await_bytes(w.at[layer, :, 1 - y, second, cols], xb_recv.at[layer, piece])
                    await_bytes(w.at[layer, :, 1 - y, first, cols], ya_recv.at[layer, piece])

    def at_turns(turns):
        def beside(index):
            for turn, steps in turns.items():

                @pl.when(index == turn)
                def _():
                    for step in steps:
                        step()

        return beside

    def ticks(turns):
        return at_turns({turn: (functools.partial(tick, step),) for turn, step in turns.items()})

    kept = {
        "x": (n2.at[pl.ds(0, width), :], x_hbm),
        "h": (res, h_hbm),
        "n1": (n1.at[pl.ds(0, width), :], n1_hbm),
        "n2": (n2.at[pl.ds(0, width), :], n2_hbm),
        "qkv": (qkv, qkv_hbm),
        "ctx": (ctx, ctx_hbm),
        "lse": (lse, lse_hbm),
        "act": (act, act_hbm),
        "slope": (slope, slope_hbm),
    }
    names = tuple(kept)

    def save(name, layer):
        src, dst = kept[name]
        if name in ("x", "h"):
            dst = dst.at[layer]
        return pltpu.make_async_copy(src, dst, save_sem.at[names.index(name), layer])

    def load(name, layer=0):
        dst, src = kept[name]
        if name == "x":
            dst, src = act.at[pl.ds(0, width), :], src.at[layer]
        return pltpu.make_async_copy(src, dst, load_sem.at[names.index(name)])

    def load_h(layer, index):
        slot = lax.rem(index, 2)
        return pltpu.make_async_copy(
            h_hbm.at[layer, :, block_of(index)], h_in.at[slot], h_sem.at[slot]
        )

    my_quarter = pl.ds(s * quarter, quarter)
    my_rows = pl.ds(pl.multiple_of((1 - t) * half + s * quarter, quarter), quarter)

    def clip_across():
        there = pl.ds(pl.multiple_of(t * half + s * quarter, quarter), quarter)
        return remote(
            clips.at[1 - t, my_quarter, :],
            stage.at[there, :],
            in_sem.at[0],
            in_sem.at[1],
            place.across,
        )

    def clip_core():
        part = stage.at[my_rows, :]
        return remote(part, part, in_sem.at[2], in_sem.at[3], place.core)

    def cot_across():
        return remote(
            cot.at[1 - t, my_quarter, :],
            cot_other.at[my_quarter, :],
            cot_sem.at[0],
            cot_sem.at[1],
            place.across,
        )

    def cot_core():
        part = cot_other.at[my_quarter, :]
        return remote(part, part, cot_sem.at[2], cot_sem.at[3], place.core)

    def exchange(kind, index, slot):
        return remote(
            send.at[kind, index],
            recv.at[kind, index],
            e_send.at[slot, index],
            e_recv.at[slot, index],
            place.core,
        )

    def result_copies(ref, first):
        local = pltpu.make_async_copy(stage.at[mine, :], ref.at[0, t], out_sem.at[first])
        away = remote(
            stage.at[theirs, :],
            ref.at[0, t],
            out_sem.at[first + 1],
            out_sem.at[first + 2],
            place.across,
        )
        return local, away

    def grad_copies(index):
        place_in = lax.rem(index, blocks // 2)
        part = in_grad.at[0, t, pl.ds(pl.multiple_of(place_in * BLOCK, BLOCK), BLOCK), :]
        src = stage.at[block_of(index), :]
        local = pltpu.make_async_copy(src, part, grad_sem.at[0, place_in])
        away = remote(
            src, part, grad_sem.at[1, place_in], grad_sem.at[2, place_in], place.across
        )
        return local, away

    def emit(layer, ref, first):
        @pl.when(s == layer)
        def _():
            for copy in result_copies(ref, first):
                copy.start()

    for copy in own_loads:
        copy.wait()
    for step in range(3):
        z_start(step)
    n1[width:, :] = jnp.ones((ONES, frames), BF)
    n2[width:, :] = jnp.ones((ONES, frames), BF)
    own_clip = pltpu.make_async_copy(clips.at[t], stage.at[mine, :], in_sem.at[4])
    own_clip.start()
    clip_across().start()
    own_out.wait()
    own_up.wait()
    own_down.wait()
    for step in (3, 4):
        z_start(step)

    def take_clip(first):
        def body(index, carry):
            at = pl.ds(pl.multiple_of(first + index * BLOCK, BLOCK), BLOCK)
            tile = stage[at, :].T
            n2[0:width, at] = tile
            res[:, at] = tile.astype(F32)
            return carry

        lax.fori_loop(0, half // BLOCK, body, 0)

    own_clip.wait()
    take_clip(t * half)
    clip_across().wait()
    clip_core().start()
    step_z(0)
    z_start(5)
    step_z(1)
    z_start(6)
    clip_core().wait()
    take_clip((1 - t) * half)
    save("x", 0).start()
    step_plane(0)
    step_z(2)
    z_start(7)
    step_plane(1)
    step_z(3)
    z_start(8)
    step_plane(2)
    cot_across().start()
    step_z(4)
    z_start(9)
    step_z(5)
    z_start(10)

    def project(pair):
        for index in (2 * pair, 2 * pair + 1):
            cols = block_of(index)
            mean, scale = norm_stats(lambda span: res[span, cols], width)
            for span in chunks_of(width):
                hat = (res[span, cols] - mean) * scale
                n1[span, cols] = (hat * vecs[span, 0:1] + vecs[span, 2:3]).astype(BF)
        cols = pair_of(pair)
        for first, many, kind, bias in PARTS:
            value = mm(wt[first : first + many, :], n1[0:width, cols])
            for span in chunks_of(many):
                part = value[span, :]
                if kind != "k":
                    part = part + spread[bias + span.start : bias + span.stop, 6:7]
                if kind == "q":
                    part = part * 0.125
                qkv[first + span.start : first + span.stop, cols] = part.astype(BF)

    def send_pair(kind, pair, slot, value):
        for part in range(2):
            index = 2 * pair + part
            send[kind, index] = value[:, part * BLOCK : (part + 1) * BLOCK].astype(BF)
            exchange(kind, index, slot).start()

    def head_rows(head, first):
        return pl.ds(pl.multiple_of(first + head * HEAD, HEAD), HEAD)

    def attend(layer, turns, later_turns):
        def heads_of(first_head, base, stride, beside):
            def one_head(index_in, carry):
                head = first_head + index_in
                q_rows = head_rows(index_in, base)
                k_rows = head_rows(index_in, base + stride)
                v_rows = head_rows(index_in, base + 2 * stride)
                c_rows = head_rows(head, 0)
                keys = qkv[k_rows, :].T
                for index in range(blocks):
                    cols = slice(index * BLOCK, (index + 1) * BLOCK)
                    queries = qkv[q_rows, cols]
                    tiles = []
                    top = None
                    for tile in chunks_of(frames, BLOCK):
                        scores = mm(keys[tile, :], queries)
                        for span in chunks_of(BLOCK):
                            peak = stack_max(scores[span, :])
                            top = peak if top is None else jnp.maximum(top, peak)
                        tiles.append(scores)
                    top = jnp.max(top, 0, keepdims=True)
                    total = jnp.zeros((8, BLOCK), F32)
                    mixed = jnp.zeros((HEAD, BLOCK), F32)
                    for tile, scores in zip(chunks_of(frames, BLOCK), tiles):
                        soft = []
                        for span in chunks_of(BLOCK):
                            part = jnp.exp(scores[span, :] - top)
                            total = total + stack_sum(part)
                            soft.append(part.astype(BF))
                        mixed = mixed + mm(qkv[v_rows, tile], jnp.concatenate(soft, 0))
                    total = jnp.sum(total, 0, keepdims=True)
                    ctx[c_rows, cols] = (mixed / total).astype(BF)
                    lse[pl.ds(head, 1), cols] = top + jnp.log(total)
                beside(index_in)
                return carry

            return one_head

        lax.fori_loop(0, 4, heads_of(0, 0, 256, ticks(turns)), 0)
        lax.fori_loop(0, 2, heads_of(4, 768, 128, ticks(later_turns)), 0)

    def out_project(layer, turns):
        beside = ticks(turns)

        def body(index, carry):
            part = mm(whole(w, layer, OUT, 384), ctx[:, pair_of(index)])
            send_pair(0, index, 2 * layer, part)
            beside(index)
            return carry

        lax.fori_loop(0, blocks // 2, body, 0)

    def middle_norm(layer, turns):
        beside = ticks(turns)

        def body(index, carry):
            cols = block_of(index)
            exchange(0, index, 2 * layer).wait()
            for span in chunks_of(width):
                added = send[0, index, span, :].astype(F32) + recv[0, index, span, :].astype(F32)
                res[span, cols] = res[span, cols] + added + vecs[span, 3:4]
            mean, scale = norm_stats(lambda span: res[span, cols], width)
            for span in chunks_of(width):
                hat = (res[span, cols] - mean) * scale
                n2[span, cols] = (hat * vecs[span, 1:2] + vecs[span, 4:5]).astype(BF)
            beside(index)
            return carry

        lax.fori_loop(0, blocks, body, 0)

    def hidden_part(layer, part):
        flip_weights(w, wt, layer, UP + part * WIDE, WIDE, part * WIDE)
        units = slice(part * WIDE, (part + 1) * WIDE)

        def body(index, carry):
            cols = pair_of(index)
            pre = mm(wt[units, :], n2[0:width, cols])
            for span in chunks_of(WIDE):
                first = part * WIDE + span.start
                bias = spread[768 + first : 768 + first + ROWS, 6:7]
                value, steep = gelu_parts(pre[span, :] + bias)
                act[first : first + ROWS, cols] = value.astype(BF)
                slope[first : first + ROWS, cols] = steep.astype(BF)
            return carry

        lax.fori_loop(0, blocks // 2, body, 0)

    def down_project(layer, turns):
        beside = ticks(turns)

        def body(index, carry):
            part = mm(whole(w, layer, DOWN, 1536), act[:, pair_of(index)])
            send_pair(1, index, 2 * layer + 1, part)
            beside(index)
            return carry

        lax.fori_loop(0, blocks // 2, body, 0)

    def layer_end(layer, index, span):
        added = send[1, index, span, :].astype(F32) + recv[1, index, span, :].astype(F32)
        return (res[span, block_of(index)] + added + vecs[span, 5:6]).astype(BF)

    def take_vectors(layer):
        vecs[...] = whole(w, layer, VEC, 128).astype(F32)
        spread_biases(vecs, spread, rows)

    def project_all(layer, turns):
        beside = ticks(turns)
        flip_weights(w, wt, layer, QKV, 1152)

        def body(index, carry):
            project(index)
            beside(index)
            return carry

        lax.fori_loop(0, blocks // 2, body, 0)
        if layer == 0:
            save("n1", 0).start()
            save("qkv", 0).start()

    complete(0, 1, 2)
    take_vectors(0)
    project_all(0, {0: 3, 1: 4})
    cot_across().wait()
    cot_core().start()
    own_cot = pltpu.make_async_copy(cot.at[t], stage.at[mine, :], cot_sem.at[5])
    own_cot.start()
    attend(0, {0: 5, 2: 6}, {0: 7})
    save("ctx", 0).start()
    save("lse", 0).start()
    cot_core().wait()
    load_cot = pltpu.make_async_copy(cot_other, stage.at[theirs, :], cot_sem.at[4])
    load_cot.start()
    complete(3)
    out_project(0, {1: 8})
    load_cot.wait()
    own_cot.wait()

    sums[3] = jnp.zeros_like(sums[3])

    def take_cot(index, carry):
        low[:, block_of(index)] = stage[block_of(index), :].T
        for span in chunks_of(width):
            sums[3, span, :] += fold(low[span, block_of(index)].astype(F32))
        return carry

    lax.fori_loop(0, blocks, take_cot, 0)
    save("x", 0).wait()
    middle_norm(0, {1: 9})
    save("h", 0).start()
    save("n2", 0).start()
    for part in range(4):
        complete(4 + part)
        hidden_part(0, part)
        tick(10 + part)
    save("act", 0).start()
    save("slope", 0).start()
    complete(8, 9, 10, 11)
    down_project(0, {1: 14})
    for name in ("n1", "qkv", "h", "n2"):
        save(name, 0).wait()

    def finish_body(index, carry):
        exchange(1, index, 1).wait()
        cols = block_of(index)
        for span in chunks_of(width):
            rows_out = layer_end(0, index, span)
            n2[span, cols] = rows_out
            res[span, cols] = rows_out.astype(F32)

        @pl.when(s == 0)
        def _():
            stage[cols, :] = n2[0:width, cols].T

        return carry

    lax.fori_loop(0, blocks, finish_body, 0)
    save("x", 1).start()
    complete(12, 13, 14)
    take_vectors(1)
    project_all(1, {0: 15, 1: 16})
    save("ctx", 0).wait()
    save("lse", 0).wait()
    attend(1, {0: 17, 2: 18}, {0: 19})
    complete(15)
    out_project(1, {1: 20})
    save("x", 1).wait()
    middle_norm(1, {1: 21})
    save("h", 1).start()
    save("act", 0).wait()
    save("slope", 0).wait()
    for part in range(4):
        complete(16 + part)
        hidden_part(1, part)
        if part < 2:
            tick(22 + part)
    for part in range(4):
        complete(20 + part)
        flip_weights(w, wt, 1, DOWN + part * WIDE, WIDE, part * WIDE)
    emit(0, out, 0)
    down_project(1, {})

    def gya_copy(layer, piece):
        cols = piece_cols(piece)
        return remote(
            w.at[layer, :, 1 - y, low_rows, cols],
            land_a.at[:, low_rows, cols],
            gya_send.at[layer, piece],
            gya_recv.at[layer, piece],
            place.beside,
        )

    def gxb_copy(layer, piece):
        cols = piece_cols(piece)
        return remote(
            w.at[layer, :, 1 - y, high_rows, cols],
            land_b.at[:, :, cols],
            gxb_send.at[layer, piece],
            gxb_recv.at[layer, piece],
            place.across,
        )

    def gx_copy(layer, piece):
        cols = piece_cols(piece)
        return remote(
            w.at[layer, :, y, :, cols],
            land_a.at[:, :, cols],
            gx_send.at[layer, piece],
            gx_recv.at[layer, piece],
            place.across,
        )

    def gy_copy(layer, piece):
        cols = piece_cols(piece)
        return remote(
            w.at[layer, :, 1 - y, :, cols],
            land_y.at[:, :, cols],
            gy_send.at[layer, piece],
            gy_recv.at[layer, piece],
            place.beside,
        )

    def landed_part(piece):
        if piece == VECTORS:
            return landed_vec
        ref, first = (
            (landed_qkv, 0)
            if piece < 3
            else (landed_out, 3)
            if piece < 4
            else (landed_up, 4)
            if piece < 8
            else (landed_down, 8)
        )
        return ref.at[:, :, pl.ds((piece - first) * WIDE, WIDE)]

    def gz_copies(layer, piece):
        cols = piece_cols(piece)
        target = landed_part(piece)
        copies = []
        for step in range(LINES):
            line = place.line(step)
            copies.append(
                remote(
                    w.at[layer, line, y, :, cols],
                    target.at[e],
                    gz_send.at[layer, piece, step],
                    gz_recv.at[piece, e],
                    (layer, place.row_of(line, y), t),
                )
            )
        local = pltpu.make_async_copy(
            w.at[layer, e, y, :, cols], target.at[e], gz_recv.at[piece, e]
        )
        return copies, local

    def add_rows(layer, piece, which, span, lands):
        cols = piece_cols(piece)
        first, count = span
        for line in range(LINES):
            added = [land[line, pl.ds(offset, count), cols] for land, offset in lands]
            total = added[0] if len(added) == 1 else added[0] + added[1]
            w[layer, line, which, pl.ds(first, count), cols] += total

    def signal(sem, layer, piece, device):
        if layer == 1:
            pl.semaphore_signal(sem.at[piece], inc=1, device_id=device, device_id_type=MESH)

    def credit(sem, layer, piece):
        if layer == 0:
            pl.semaphore_wait(sem.at[piece], 1)

    def step_a(layer, piece):
        @pl.when(secondary)
        def _():
            credit(ya_free, layer, piece)
            gya_copy(layer, piece).start()
            credit(xb_free, layer, piece)
            gxb_copy(layer, piece).start()

    def step_b(layer, piece):
        cols = piece_cols(piece)

        @pl.when(secondary)
        def _():
            await_bytes(land_a.at[:, low_rows, cols], gya_recv.at[layer, piece])
            add_rows(layer, piece, y, (0, SPLIT), [(land_a, 0)])
            signal(ya_free, layer, piece, place.beside)
            credit(x_free, layer, piece)
            gx_copy(layer, piece).start()

        @pl.when(primary)
        def _():
            await_bytes(land_b.at[:, :, cols], gxb_recv.at[layer, piece])
            add_rows(layer, piece, 1 - y, (SPLIT, rows - SPLIT), [(land_b, 0)])
            signal(xb_free, layer, piece, place.across)
            credit(y_free, layer, piece)
            gy_copy(layer, piece).start()

    def step_c(layer, piece):
        cols = piece_cols(piece)

        @pl.when(primary)
        def _():
            await_bytes(land_a.at[:, :, cols], gx_recv.at[layer, piece])
            await_bytes(land_y.at[:, :, cols], gy_recv.at[layer, piece])
            add_rows(layer, piece, y, (0, rows), [(land_a, 0), (land_y, 0)])
            signal(x_free, layer, piece, place.across)
            signal(y_free, layer, piece, place.beside)
            copies, local = gz_copies(layer, piece)

            @pl.when(s == layer)
            def _():
                local.start()

            @pl.when(s != layer)
            def _():
                copies[0].start()

            for copy in copies[1:]:
                copy.start()

    def store_grads(layer, start, count, value):
        w[layer, :, :, :, pl.ds(start, count)] = value.astype(BF).reshape(
            w.shape[1], w.shape[2], rows, count
        )

    def mlp_back(layer, beside):
        def body(index, carry):
            cols = pair_of(index)
            for part in range(4):
                units = slice(part * WIDE, (part + 1) * WIDE)
                grad = mm(wt[units, :], low[:, cols])
                for span in chunks_of(WIDE):
                    rows_in = slice(units.start + span.start, units.start + span.stop)
                    steep = slope[rows_in, cols].astype(F32)
                    slope[rows_in, cols] = (grad[span, :] * steep).astype(BF)
            term = mm(whole(w, layer, UP, 1536), slope[:, cols])
            send_pair(0, index, 4 + 2 * layer, term)
            beside(index)
            return carry

        lax.fori_loop(0, blocks // 2, body, 0)

    def outer(layer, start, left, right, first, many, before, beside):
        def body(index, carry):
            before(index)
            base = index * PAIR
            span = pl.ds(pl.multiple_of(first + base, 128), PAIR)
            value = mmt(left[...], right[span, :])
            store_grads(layer, pl.multiple_of(start + base, 128), PAIR, value[0:width, :])
            if left.shape[0] > width:
                to = pl.ds(pl.multiple_of(768 + base, BLOCK), PAIR)
                spread[to, 0:8] = value[width : width + 8, :].T
            beside(index)
            return carry

        lax.fori_loop(0, many // PAIR, body, 0)

    def turned(turn):
        return lax.rem(turn + (1 - t) * (blocks // 2), blocks)

    def norm_back(layer, kind, gain_lane, source, put, finish, beside):
        sums[0:3] = jnp.zeros((3, width, 128), F32)

        def body(turn, carry):
            index = turned(turn)
            cols = block_of(index)
            read = source(index)
            mean, scale = norm_stats(read, width)
            exchange(kind, index, 4 + 2 * layer + kind).wait()
            first = jnp.zeros((8, BLOCK), F32)
            second = jnp.zeros((8, BLOCK), F32)

            def terms(span):
                hat = (read(span) - mean) * scale
                grad = send[kind, index, span, :].astype(F32)
                grad = grad + recv[kind, index, span, :].astype(F32)
                return hat, grad, grad * vecs[span, gain_lane : gain_lane + 1]

            for span in chunks_of(width):
                hat, grad, scaled = terms(span)
                sums[0, span, :] += fold(grad * hat)
                sums[1, span, :] += fold(grad)
                first = first + stack_sum(scaled)
                second = second + stack_sum(scaled * hat)
            level = mean_of(first, width)
            slant = mean_of(second, width)
            for span in chunks_of(width):
                hat, _, scaled = terms(span)
                put(span, cols, res[span, cols] + scale * (scaled - level - hat * slant))
            finish(index)
            beside(turn)
            return carry

        lax.fori_loop(0, blocks, body, 0)

    def row_sums(value):
        return jnp.sum(value, 1, keepdims=True)

    def attend_back(first_head, many, base, stride, beside):
        def one_head(index_in, carry):
            head = first_head + index_in
            q_rows = head_rows(index_in, base)
            k_rows = head_rows(index_in, base + stride)
            v_rows = head_rows(index_in, base + 2 * stride)
            c_rows = head_rows(head, 0)
            keys = qkv[k_rows, :].T
            values = qkv[v_rows, :].T
            flat_queries = qkv[q_rows, :].T
            flat_grads = dctx[c_rows, :].T
            level = lse[pl.ds(head, 1), :]
            inner = jnp.sum(
                dctx[c_rows, :].astype(F32) * ctx[c_rows, :].astype(F32), 0, keepdims=True
            )
            step = jnp.zeros((HEAD, frames), F32)
            for tile in chunks_of(frames, BLOCK):
                soft = []
                score_grad = []
                for cols in chunks_of(frames, BLOCK):
                    scores = mm(keys[tile, :], qkv[q_rows, cols])
                    soft_grad = mm(values[tile, :], dctx[c_rows, cols])
                    soft_parts = []
                    grad_parts = []
                    for part in chunks_of(BLOCK):
                        strength = jnp.exp(scores[part, :] - level[:, cols])
                        soft_parts.append(strength.astype(BF))
                        strength = strength * (soft_grad[part, :] - inner[:, cols])
                        grad_parts.append(strength.astype(BF))
                    soft.append(jnp.concatenate(soft_parts, 0))
                    score_grad.append(jnp.concatenate(grad_parts, 0))
                soft = jnp.concatenate(soft, 1)
                score_grad = jnp.concatenate(score_grad, 1)
                step = step + mm(qkv[k_rows, tile], score_grad)
                slope[k_rows, tile] = mm(score_grad, flat_queries).astype(BF).T
                slope[v_rows, tile] = mm(soft, flat_grads).astype(BF).T
            slope[q_rows, :] = (step * 0.125).astype(BF)
            beside(index_in)
            return carry

        lax.fori_loop(0, many, one_head, 0)

    def keep_sums(first, value):
        for start, many, kind, bias in PARTS:
            offset = start - first
            if kind != "k" and 0 <= offset < value.shape[1]:
                spread[bias : bias + many, 0:8] = value[
                    width : width + 8, offset : offset + many
                ].T

    def collect_biases():
        def body(group, carry):
            to = pl.ds(pl.multiple_of(group * rows, 8), 8)
            for kind in range(2):
                for head in range(6):
                    at = pl.ds(pl.multiple_of(kind * 384 + head * HEAD + group * 8, 8), 8)
                    lane = head_lane(kind, head)
                    vec_grads[to, lane : lane + 1] = spread[at, 6:7]
            for unit in range(24):
                at = pl.ds(pl.multiple_of(768 + unit * HEAD + group * 8, 8), 8)
                lane = UNIT_LANE + unit
                vec_grads[to, lane : lane + 1] = spread[at, 6:7]
            return carry

        lax.fori_loop(0, GROUPS, body, 0)

    def nothing(index):
        del index

    def finish_gather(layer, piece):
        @pl.when(primary)
        def _():
            x_copy(layer, piece).wait_send()
            y_copy(layer, piece).wait_send()
            xb_copy(layer, piece).wait_send()

        @pl.when(secondary)
        def _():
            ya_copy(layer, piece).wait_send()

    def send_first_grad():
        @pl.when(s == 1)
        def _():
            for place_in in range(blocks // 2):
                _, away = grad_copies((1 - t) * (blocks // 2) + place_in)
                away.start()

    def last_body(index, carry):
        exchange(1, index, 3).wait()

        @pl.when(s == 1)
        def _():
            for span in chunks_of(width, 128):
                stage[block_of(index), span] = layer_end(1, index, span).T

        return carry

    for layer in (1, 0):
        later = layer == 0
        if later:
            load_h(layer, turned(0)).start()
            for piece in range(CHUNKS + 1):
                finish_gather(0, piece)
            load("act").wait()
            vecs[...] = whole(w, layer, VEC, 128).astype(F32)
            flip_weights(w, wt, layer, DOWN, 1536)
        vec_grads[...] = jnp.zeros_like(vec_grads)

        def a(piece, layer=layer):
            return lambda: step_a(layer, piece)

        def b(piece, layer=layer):
            return lambda: step_b(layer, piece)

        def c(piece, layer=layer):
            return lambda: step_c(layer, piece)

        if later:
            before = nothing
            early = at_turns(
                {
                    0: (a(8),),
                    1: (a(9), lambda: step_b(1, VECTORS)),
                    2: (a(10), a(11)),
                }
            )
        else:
            waits = [functools.partial(finish_gather, 1, piece) for piece in (8, 9, 10, 11)]
            before = at_turns({0: waits[:2], 1: waits[2:3], 2: waits[3:]})
            early = at_turns({0: (a(8),), 1: (a(9),), 2: (a(10), a(11))})
        outer(layer, DOWN, low, act, 0, 1536, before, early)
        load("x", layer).start()
        vec_grads[:, 5:6] = row_sums(sums[3])
        if not later:
            lax.fori_loop(0, blocks, last_body, 0)
            emit(1, out, 0)
            save("h", 1).wait()
            load_h(layer, turned(0)).start()
            res[...] = low[...].astype(F32)
            for piece in (*range(8), VECTORS):
                finish_gather(1, piece)
        else:
            load("slope").wait()

        mlp_back(layer, at_turns({0: (b(8),)}))
        if later:
            load("n2").wait()
        left = (lambda: step_c(1, VECTORS),) if later else ()
        drain = at_turns({0: (a(4),) + left, 1: (a(5), b(9)), 2: (a(6), a(7))})
        outer(layer, UP, n2, slope, 0, 1536, nothing, drain)
        flip_weights(w, wt, layer, OUT, 384)

        def hidden_in(index, layer=layer):
            turn = lax.rem(index + (1 - t) * (blocks // 2), blocks)

            @pl.when(turn + 1 < blocks)
            def _():
                load_h(layer, turned(turn + 1)).start()

            load_h(layer, index).wait()
            slot = lax.rem(index, 2)
            return lambda span: h_in[slot, span, :]

        def hidden_put(span, cols, total):
            res[span, cols] = total
            rounded = total.astype(BF)
            low[span, cols] = rounded
            sums[2, span, :] += fold(rounded.astype(F32))

        drain = at_turns({0: (b(10),), 1: (b(11),), 2: (b(4), b(5)), 3: (c(8),)})
        norm_back(layer, 0, 1, hidden_in, hidden_put, nothing, drain)

        def context_back(index, carry):
            cols = pair_of(index)
            dctx[:, cols] = mm(wt[0:384, :], low[:, cols]).astype(BF)
            return carry

        lax.fori_loop(0, blocks // 2, context_back, 0)
        vec_grads[:, 1:2] = row_sums(sums[0])
        vec_grads[:, 4:5] = row_sums(sums[1])
        vec_grads[:, 3:4] = row_sums(sums[2])
        if later:
            for name in ("ctx", "qkv", "lse"):
                load(name).wait()
        store_grads(layer, OUT, 384, mmt(low[...], ctx[...]))
        step_a(layer, 3)
        over = (send_first_grad,) if later else ()
        drain = at_turns({0: (c(9),), 1: (b(6), c(10), c(11)) + over, 2: (c(4), c(5))})
        attend_back(0, 4, 0, 256, drain)
        if later:
            load("n1").wait()
        wt[0:768, :] = whole(w, layer, QKV, 768)

        for first, many in ((0, 512), (512, 256)):
            value = mmt(n1[...], slope[first : first + many, :])
            store_grads(layer, QKV + first, many, value[0:width, :])
            keep_sums(first, value)
        step_a(layer, 0)
        step_a(layer, 1)
        step_b(layer, 7)
        step_b(layer, 3)
        step_c(layer, 6)
        attend_back(4, 2, 768, 128, nothing)

        def first_body(index, carry, layer=layer):
            cols = pair_of(index)
            term = mm(wt[0:768, :], slope[0:768, cols])
            term = term + mm(whole(w, layer, QKV + 768, WIDE), slope[768:1152, cols])
            send_pair(1, index, 5 + 2 * layer, term)
            return carry

        lax.fori_loop(0, blocks // 2, first_body, 0)
        step_b(layer, 0)
        step_c(layer, 7)
        value = mmt(n1[...], slope[768:1152, :])
        store_grads(layer, QKV + 768, WIDE, value[0:width, :])
        keep_sums(768, value)
        step_a(layer, 2)
        step_b(layer, 1)
        step_c(layer, 3)
        collect_biases()
        if layer == 1:
            for name in ("slope", "n1", "n2", "ctx", "qkv", "lse"):
                load(name).start()
        load("x", layer).wait()

        @pl.when(s == layer)
        def _():
            local, away = result_copies(out, 0)
            local.wait()
            away.wait_send()

        def rows_x(index):
            return lambda span: act[span, block_of(index)].astype(F32)

        def rows_put(span, cols, total, layer=layer):
            rounded = total.astype(BF)
            low[span, cols] = rounded
            if layer == 1:
                res[span, cols] = rounded.astype(F32)
                sums[2, span, :] += fold(rounded.astype(F32))

        def rows_out(index, layer=layer):
            @pl.when(s == layer)
            def _():
                stage[block_of(index), :] = low[:, block_of(index)].T
                local, away = grad_copies(index)

                @pl.when(index // (blocks // 2) == t)
                def _():
                    local.start()

                if layer == 0:

                    @pl.when(index // (blocks // 2) != t)
                    def _():
                        away.start()

        drain = at_turns({0: (b(2), c(0)), 2: (c(1),)})
        norm_back(layer, 1, 0, rows_x, rows_put, rows_out, drain)
        if layer == 1:
            load("act").start()
        vec_grads[:, 0:1] = row_sums(sums[0])
        vec_grads[:, 2:3] = row_sums(sums[1])
        sums[3] = sums[2]
        store_grads(layer, VEC, 128, vec_grads[...])
        step_a(layer, VECTORS)
        step_c(layer, 2)

    step_b(0, VECTORS)

    step_c(0, VECTORS)

    def finish_scatter(piece):
        for layer in range(2):

            @pl.when(secondary)
            def _():
                gya_copy(layer, piece).wait_send()
                gxb_copy(layer, piece).wait_send()
                gx_copy(layer, piece).wait_send()

            @pl.when(primary)
            def _():
                gy_copy(layer, piece).wait_send()
                copies, _ = gz_copies(layer, piece)

                @pl.when(s != layer)
                def _():
                    copies[0].wait_send()

                for copy in copies[1:]:
                    copy.wait_send()

    for piece in range(CHUNKS + 1):
        z_finish(piece)
        finish_scatter(piece)
        for line in range(LINES):
            await_bytes(landed_part(piece).at[line], gz_recv.at[piece, line])

    _, away = result_copies(out, 0)
    away.wait_recv()
    for index in range(blocks // 2):
        local, away = grad_copies(index)
        local.wait()
        away.wait()


def layers_call(share, clips, cotangent, shards, dims):
    width, frames, hidden_units, heads_width = dims
    rows = width // GROUPS
    sem = pltpu.SemaphoreType.DMA
    free = pltpu.SemaphoreType.REGULAR
    packed = (2, LINES, 2, rows, END)
    blocks = frames // BLOCK
    shape = jax.ShapeDtypeStruct
    outs = [
        shape((1,) + clips.shape, BF),
        shape((1,) + clips.shape, BF),
        shape((LINES, rows, QKV - VEC), BF),
        shape((LINES, rows, OUT - QKV), BF),
        shape((LINES, rows, UP - OUT), BF),
        shape((LINES, rows, DOWN - UP), BF),
        shape((LINES, rows, END - DOWN), BF),
        shape(clips.shape[1:], BF),
        shape((2, width, frames), BF),
        shape((2, width, frames), F32),
        shape((width, frames), BF),
        shape((width, frames), BF),
        shape((3 * heads_width, frames), BF),
        shape((heads_width, frames), BF),
        shape((8, frames), F32),
        shape((hidden_units, frames), BF),
        shape((hidden_units, frames), BF),
    ]
    scratch = [
        pltpu.VMEM(packed, BF),
        pltpu.VMEM((width, frames), F32),
        pltpu.VMEM((hidden_units, frames), BF),
        pltpu.VMEM((hidden_units, frames), BF),
        pltpu.VMEM((width + ONES, frames), BF),
        pltpu.VMEM((width + ONES, frames), BF),
        pltpu.VMEM((width, frames), BF),
        pltpu.VMEM((3 * heads_width, frames), BF),
        pltpu.VMEM((heads_width, frames), BF),
        pltpu.VMEM((heads_width, frames), BF),
        pltpu.VMEM((8, frames), F32),
        pltpu.VMEM((2, width, BLOCK), F32),
        pltpu.VMEM((hidden_units, width), BF),
        pltpu.VMEM((2, blocks, width, BLOCK), BF),
        pltpu.VMEM((2, blocks, width, BLOCK), BF),
        pltpu.VMEM((width, 128), F32),
        pltpu.VMEM((width, 128), F32),
        pltpu.VMEM((4, width, 128), F32),
        pltpu.VMEM((2 * heads_width + hidden_units, 128), F32),
        pltpu.VMEM((frames, width), BF),
        pltpu.VMEM((rows, END), BF),
        pltpu.VMEM((LINES, rows, END), BF),
        pltpu.VMEM((LINES, rows - SPLIT, END), BF),
        pltpu.VMEM((LINES, rows, END), BF),
    ]
    scratch += [sem((CHUNKS + 1, LINES)), sem((2, CHUNKS + 1, LINES))]
    scratch += [sem((2, CHUNKS + 1))] * 8
    scratch += [sem((2, CHUNKS + 1, LINES)), sem((CHUNKS + 1, LINES))]
    scratch += [sem((2, CHUNKS + 1))] * 8
    scratch += [
        sem((8, blocks)),
        sem((8, blocks)),
        sem((10,)),
        sem((5,)),
        sem((6,)),
        sem((3,)),
        sem((3, blocks // 2)),
        sem((9, 2)),
        sem((9,)),
        sem((2,)),
    ]
    scratch += [free((CHUNKS + 1,))] * 4
    anywhere = pl.BlockSpec(memory_space=pl.ANY)
    inside = pl.BlockSpec(memory_space=pltpu.VMEM)
    return pl.pallas_call(
        functools.partial(layers_kernel, share),
        out_shape=outs,
        in_specs=[anywhere] * 2 + [inside] * 4 + [anywhere] * (len(shards) - 4),
        out_specs=[anywhere] * len(outs),
        scratch_shapes=scratch,
        compiler_params=pltpu.CompilerParams(
            collective_id=0, has_side_effects=True, vmem_limit_bytes=VMEM_LIMIT
        ),
        cost_estimate=pl.CostEstimate(
            flops=60_000_000_000, bytes_accessed=60_000_000, transcendentals=0
        ),
    )(clips, cotangent, *shards)


def group_piece(value, axis, share):
    if share == 1:
        return value
    size = value.shape[axis] * share
    group = lax.axis_index("dp") // share
    full = lax.all_gather(value, "dp", axis=axis, tiled=True)
    return lax.dynamic_slice_in_dim(full, group * size, size, axis)


def own_part(value, axis, share, parts, index):
    size = value.shape[axis] // parts
    if parts == 1:
        return value
    return lax.dynamic_slice_in_dim(value, index * size, size, axis)


def on_device(share, clips, cotangent, ln_gains, row_biases, w_qkv, b_qv, w_o, w_up, b_ff, w_down):
    width = clips.shape[2]
    rows = width // GROUPS
    dims = (width, 2 * clips.shape[1], w_up.shape[2], w_o.shape[1])
    ln_gains = group_piece(ln_gains, 2, share)
    row_biases = group_piece(row_biases, 2, share)
    w_qkv = group_piece(w_qkv, 2, share)
    b_qv = group_piece(b_qv, 3, share)
    w_o = group_piece(w_o, 2, share)
    w_up = group_piece(w_up, 1, share)
    b_ff = group_piece(b_ff, 2, share)
    w_down = group_piece(w_down, 2, share)
    shards = (
        ln_gains,
        row_biases,
        jnp.transpose(b_qv, (0, 2, 1, 3)),
        jnp.swapaxes(b_ff, 1, 2),
        w_qkv,
        jnp.swapaxes(w_o, 1, 2),
        w_up,
        jnp.swapaxes(w_down, 1, 2),
    )
    section_out, section_in_grad, *landed = layers_call(share, clips, cotangent, shards, dims)
    rest = lax.axis_index("dp") % share
    side = lax.axis_index("tensor")

    def joined(value):
        total = jnp.sum(value.astype(F32), 0)
        if share == 1:
            return total
        group = lax.axis_index("dp") // share
        padded = jnp.zeros((width, total.shape[1]), F32)
        padded = lax.dynamic_update_slice_in_dim(padded, total, group * rows, 0)
        return lax.dynamic_slice_in_dim(lax.psum(padded, "dp"), group * rows, rows, 0)

    def mine(value):
        return own_part(joined(value), 0, share, share, rest)

    vectors = joined(landed[0])
    turned = own_part(own_part(vectors.T, 1, share, share, rest), 1, share, 2, side)
    heads_grad = vectors[0:8, HEAD_LANE : HEAD_LANE + 12].T.reshape(6, 2, 8).transpose(1, 0, 2)
    units_grad = vectors[0:8, UNIT_LANE : UNIT_LANE + 24].T
    qkv_grad = {"q": [], "k": [], "v": []}
    for first, many, kind, _ in PARTS:
        qkv_grad[kind].append(mine(landed[1][:, :, first : first + many]))
    return (
        section_out,
        section_in_grad,
        turned[0:2][None],
        turned[2:6][None],
        jnp.stack([jnp.concatenate(qkv_grad[kind], 1) for kind in "qkv"])[None],
        own_part(heads_grad, 2, share, share, rest)[None],
        mine(landed[2]).T[None],
        mine(landed[3])[None],
        own_part(units_grad, 1, share, share, rest)[None],
        mine(landed[4]).T[None],
    )


def solution(mesh):
    placed = (
        P("dp", "tensor", None),
        P("dp", "tensor", None),
        P("section", None, "dp"),
        P("section", None, "dp"),
        P("section", None, "dp", "tensor"),
        P("section", None, "tensor", "dp"),
        P("section", "tensor", "dp"),
        P("section", "dp", "tensor"),
        P("section", "tensor", "dp"),
        P("section", "tensor", "dp"),
    )
    share = mesh.shape["dp"] // GROUPS
    return jax.shard_map(
        functools.partial(on_device, share),
        mesh=mesh,
        in_specs=placed,
        out_specs=(
            P("section", "dp", "tensor", None),
            P("section", "dp", "tensor", None),
            P("section", None, ("dp", "tensor")),
            P("section", None, ("dp", "tensor")),
            P("section", None, "dp", "tensor"),
            P("section", None, "tensor", "dp"),
            P("section", "tensor", "dp"),
            P("section", "dp", "tensor"),
            P("section", "tensor", "dp"),
            P("section", "tensor", "dp"),
        ),
        check_vma=False,
    )
```
